32 devices in a mesh: dp: 8 (over y, x, core), mp: 4 (over z).
Axes of the slice: x: 2, y: 2, z: 4, core: 2. Of those that a mesh axis runs over, the one named last changes fastest.
Arguments:
- tokens: bfloat16 [8, 2048, 1024], P('dp', 'mp'), may hold values from -6 to 6
- w_qkv: bfloat16 [1024, 3, 1024], P(None, None, 'mp'), may hold values from -0.1875 to 0.1875
- w_out: bfloat16 [1024, 1024], P('mp'), may hold values from -0.1875 to 0.1875
- w_up: bfloat16 [1024, 4096], P(None, 'mp'), may hold values from -0.1875 to 0.1875
- w_down: bfloat16 [4096, 1024], P('mp'), may hold values from -0.09375 to 0.09375
- norm_gains: float32 [4, 1024], replicated, may hold values from 0.5 to 1.5
- norm_shifts: float32 [4, 1024], replicated, may hold values from -1 to 1
- cotangent: bfloat16 [8, 2048, 1024], P('dp', 'mp'), may hold values from -6 to 6
- corpus_ids: int32 [8], P('dp'), may hold values from 0 to 7
- corpus_weight: float32 [8], replicated, may hold values from 0.25 to 4
Outputs:
- output: bfloat16 [8, 2048, 1024], P('dp', 'mp')
- input_grad: float32 [8, 2048, 1024], P('dp', 'mp')
- qkv_grad: float32 [1024, 3, 1024], P(None, None, 'mp')
- out_grad: float32 [1024, 1024], P('mp')
- up_grad: float32 [1024, 4096], P(None, 'mp')
- down_grad: float32 [4096, 1024], P('mp')
- gain_grad: float32 [4, 1024], replicated
- shift_grad: float32 [4, 1024], replicated
The draws below stay inside these ranges and needn't reach their ends.
Inputs may be any that keep to these rules, and one draw needn't show every extreme that they name: `corpus_ids`: each entry names one of the 8 corpora.
All inputs are finite; a program needn't handle non-finite values.
Results may differ from the reference program's by a relative error of at most 0.018.
Values may be sent and summed in bfloat16 or wider, within the bound.
A program may use at most 256 MiB of HBM per device.

```python
import math
import jax
import jax.numpy as jnp
from jax import lax

D = 1024
HEADS = 16
HEAD_DIM = 64
FF = 4096
SEQ = 2048
BLOCK = 512
CORPORA = 8
ROWS = 8


def touch_ends(array, stream_key, smallest, high):
    spot = [jax.random.randint(jax.random.fold_in(stream_key, axis), (), 0, length) for axis, length in enumerate(array.shape)]
    widest = array.shape.index(max(array.shape))
    neighbour = spot[:widest] + [(spot[widest] + 1) % array.shape[widest]] + spot[widest + 1:]
    return array.at[tuple(spot)].set(smallest).at[tuple(neighbour)].set(high)


def shard_levels(stream_key, dims, cuts, low, top_value):
    loudness = 1.0
    for dim, parts in cuts:
        draws = jax.random.uniform(jax.random.fold_in(jax.random.fold_in(stream_key, 6), dim), (parts,), jnp.float32, low / len(cuts), top_value / len(cuts))
        loudness = loudness * jnp.repeat(jnp.exp(draws), dims[dim] // parts).reshape((-1,) + (1,) * (len(dims) - 1 - dim))
    return loudness


def scatter_about(stream_key, extent, scale, reach, shards=(), kind=jnp.bfloat16):
    array = jax.random.normal(stream_key, extent, jnp.float32) * scale
    if len(shards) > 0:
        array = shard_levels(stream_key, extent, shards, -0.22, 0.18) * array
    return jnp.clip(array, min=-reach, max=reach).astype(kind)


def setup_inputs(seed: int = 0) -> dict:
    seeds = jax.random.split(jax.random.key(seed), 11)
    return {
        "tokens": scatter_about(seeds[0], (ROWS, SEQ, D), 1.0, 6.0, ((0, 8), (1, 4))),
        "w_qkv": scatter_about(seeds[1], (D, 3, D), D ** -0.5, 0.1875, ((2, 4),)),
        "w_out": scatter_about(seeds[2], (D, D), D ** -0.5, 0.1875, ((0, 4),)),
        "w_up": scatter_about(seeds[3], (D, FF), D ** -0.5, 0.1875, ((1, 4),)),
        "w_down": scatter_about(seeds[4], (FF, D), FF ** -0.5, 0.09375, ((0, 4),)),
        "norm_gains": jnp.clip(1.0 + 0.1 * jax.random.normal(seeds[5], (4, D), jnp.float32), 0.5, 1.5),
        "norm_shifts": scatter_about(seeds[6], (4, D), 0.2, 1.0, (), jnp.float32),
        "cotangent": scatter_about(seeds[7], (ROWS, SEQ, D), 1.0, 6.0, ((0, 8), (1, 4))),
        "corpus_ids": touch_ends(jax.random.randint(seeds[8], (ROWS,), 0, CORPORA), jax.random.fold_in(seeds[8], 1), 0, CORPORA - 1).astype(jnp.int32),
        "corpus_weight": jnp.clip(jnp.exp(jax.random.uniform(seeds[9], (CORPORA,), jnp.float32, math.log(0.25), math.log(4.0))), 0.25, 4.0),
    }


@jax.custom_vjp
def low(v):
    return lax.optimization_barrier(v.astype(jnp.bfloat16)).astype(jnp.float32)

@jax.custom_vjp
def low_back(v):
    return v

def low_keep(v):
    return (low(v), None)

def low_pass(kept, grad):
    return (grad,)

def back_keep(v):
    return (v, None)

def back_low(kept, grad):
    return (low(grad),)
low.defvjp(low_keep, low_pass)
low_back.defvjp(back_keep, back_low)

def matmul(left, right):
    return jnp.dot(left, right, precision=lax.Precision.HIGHEST)

def layer_norm(value, gain, shift):
    center = value - lax.optimization_barrier(jnp.mean(value, axis=-1, keepdims=True))
    spread = lax.optimization_barrier(jnp.mean(center * center, axis=-1, keepdims=True))
    return center * lax.rsqrt(spread + 1e-05) * gain + shift

def rotary_tables(length, half):
    steps = jnp.arange(half, dtype=jnp.float32) / half
    freqs = 10000.0 ** (-steps)
    angles = jnp.arange(length, dtype=jnp.float32)[:, None] * freqs[None, :]
    return (jnp.cos(angles), jnp.sin(angles))

def rotate(value, cosine, sine):
    half = value.shape[-1] // 2
    first = value[..., :half]
    second = value[..., half:]
    cos_b = cosine[:, None, :]
    sin_b = sine[:, None, :]
    return jnp.concatenate([first * cos_b - second * sin_b, second * cos_b + first * sin_b], axis=-1)

def attention(queries, keys, values):
    length = queries.shape[0]
    blocks = queries.reshape(length // BLOCK, BLOCK, HEADS, HEAD_DIM)
    starts = jnp.arange(length // BLOCK, dtype=jnp.int32) * BLOCK
    key_pos = jnp.arange(length, dtype=jnp.int32)

    def one_block(item):
        rows, start = item
        raw = jnp.einsum('qhe,khe->hqk', rows, keys, precision=lax.Precision.HIGHEST)
        scores = low_back(raw)
        query_pos = start + jnp.arange(BLOCK, dtype=jnp.int32)
        allowed = key_pos[None, :] <= query_pos[:, None]
        scores = jnp.where(allowed[None], scores, -1e+30)
        probs = low(jax.nn.softmax(scores, axis=-1))
        return jnp.einsum('hqk,khe->qhe', probs, values, precision=lax.Precision.HIGHEST)
    result = lax.map(jax.checkpoint(one_block), (blocks, starts))
    return result.reshape(length, HEADS * HEAD_DIM)

def layer(resid, params):
    w_qkv, w_out, w_up, w_down, gains, shifts = params
    cosine, sine = rotary_tables(SEQ, HEAD_DIM // 2)
    normed_a = low(layer_norm(resid, gains[0], shifts[0]))
    mixed = low_back(matmul(normed_a, w_qkv.reshape(D, 3 * D)))
    query_raw = mixed[:, :D].reshape(SEQ, HEADS, HEAD_DIM)
    key_raw = mixed[:, D:2 * D].reshape(SEQ, HEADS, HEAD_DIM)
    value_raw = mixed[:, 2 * D:].reshape(SEQ, HEADS, HEAD_DIM)
    queries = low(HEAD_DIM ** (-0.5) * rotate(query_raw, cosine, sine))
    keys = low(rotate(key_raw, cosine, sine))
    values = low(value_raw)
    attended = low(low_back(attention(queries, keys, values)))
    branch_a = low_back(matmul(attended, w_out))
    middle = resid + layer_norm(branch_a, gains[1], shifts[1])
    normed_f = low(layer_norm(middle, gains[2], shifts[2]))
    hidden = low_back(matmul(normed_f, w_up))
    active = low(jax.nn.gelu(hidden))
    branch_f = low_back(matmul(active, w_down))
    return middle + layer_norm(branch_f, gains[3], shifts[3])

def reference(tokens, w_qkv, w_out, w_up, w_down, norm_gains, norm_shifts, cotangent, corpus_ids, corpus_weight):
    params = (w_qkv.astype(jnp.float32), w_out.astype(jnp.float32), w_up.astype(jnp.float32), w_down.astype(jnp.float32), norm_gains.astype(jnp.float32), norm_shifts.astype(jnp.float32))
    row_weight = corpus_weight.astype(jnp.float32)[corpus_ids]

    def step(totals, item):
        sequence, grad_seed, weight = item
        final, pull = jax.vjp(layer, sequence.astype(jnp.float32), params)
        grad_in, grads = pull(grad_seed.astype(jnp.float32) * weight)
        totals = jax.tree.map(lambda left, right: left + right, totals, grads)
        return (totals, (final.astype(jnp.bfloat16), grad_in))
    zeros = jax.tree.map(jnp.zeros_like, params)
    totals, (output, input_grad) = lax.scan(step, zeros, (tokens, cotangent, row_weight))
    return (output, input_grad, totals[0], totals[1], totals[2], totals[3], totals[4], totals[5])
```

```python
import functools

import jax
import jax.numpy as jnp
from jax import lax
from jax.experimental import pallas as pl
from jax.experimental.pallas import tpu as pltpu
from jax.sharding import Mesh, PartitionSpec as P

HEAD_DIM = 64
BLOCK = 512
EPS = 1e-05
LOG2E = 1.4426950408889634
NN = (((1,), (0,)), ((), ()))
NT = (((1,), (1,)), ((), ()))
TN = (((0,), (0,)), ((), ()))
f32 = jnp.float32
bf16 = jnp.bfloat16


def head_lanes(shape, head):
    return lax.broadcasted_iota(jnp.int32, shape, 1) // HEAD_DIM == head


def swap_halves(value, sign):
    half = HEAD_DIM // 2
    width = value.shape[1]
    first = (lax.broadcasted_iota(jnp.int32, value.shape, 1) // half) % 2 == 0
    return jnp.where(
        first, sign * pltpu.roll(value, width - half, 1), -sign * pltpu.roll(value, half, 1)
    )


def qkv_kernel(place_ref, x_ref, w_ref, gain_ref, shift_ref, cos_ref, sin_ref, *refs):
    q_ref, k_ref, v_ref, normed_ref = refs[-4:]
    width = q_ref.shape[1]
    value = x_ref[...].astype(f32)
    center = value - jnp.mean(value, axis=1, keepdims=True)
    inverse = lax.rsqrt(jnp.mean(center * center, axis=1, keepdims=True) + EPS)
    normed = (center * inverse * gain_ref[...] + shift_ref[...]).astype(bf16)
    normed_ref[...] = normed
    mixed = jnp.dot(normed, w_ref[...], preferred_element_type=f32)
    cosine, sine = cos_ref[...], sin_ref[...]
    query, key = mixed[:, :width], mixed[:, width : 2 * width]
    query = HEAD_DIM ** (-0.5) * (query * cosine + swap_halves(query, -1.0) * sine)
    q_ref[...] = query.astype(bf16)
    k_ref[...] = (key * cosine + swap_halves(key, -1.0) * sine).astype(bf16)
    v_ref[...] = mixed[:, 2 * width :].astype(bf16)


def project(place, x, w, gain, shift, cosine, sine, length, filled, rows=256):
    part, depth = x.shape
    width = w.shape[1] // 3
    steps = part // rows

    def there(i, place_ref):
        return (place_ref[0] * steps + i, 0)

    def whole(i, place_ref):
        return (0, 0)

    return pl.pallas_call(
        qkv_kernel,
        out_shape=tuple(
            jax.ShapeDtypeStruct((length, n), bf16) for n in (width, width, width, depth)
        ),
        grid_spec=pltpu.PrefetchScalarGridSpec(
            num_scalar_prefetch=1,
            grid=(steps,),
            in_specs=[
                pl.BlockSpec((rows, depth), lambda i, place_ref: (i, 0)),
                pl.BlockSpec(w.shape, whole),
                pl.BlockSpec((1, depth), whole),
                pl.BlockSpec((1, depth), whole),
                pl.BlockSpec((rows, width), there),
                pl.BlockSpec((rows, width), there),
            ]
            + [pl.BlockSpec(memory_space=pl.ANY)] * len(filled),
            out_specs=tuple(pl.BlockSpec((rows, n), there) for n in (width, width, width, depth)),
        ),
        input_output_aliases={7 + i: i for i in range(len(filled))},
        compiler_params=pltpu.CompilerParams(vmem_limit_bytes=40 * 2**20),
        cost_estimate=pl.CostEstimate(
            flops=2 * part * depth * 3 * width, bytes_accessed=5 * 2**20, transcendentals=0
        ),
    )(place, x, w, gain, shift, cosine, sine, *filled)


def forward_kernel(q_ref, k_ref, v_ref, o_ref, lse_ref, *, rows, blocks):
    width = q_ref.shape[1]
    heads = width // HEAD_DIM

    def branch(last):
        n = (last + 1) * rows
        acc = jnp.zeros((rows, width), f32)
        logs = jnp.zeros((rows, width), f32)
        for h in range(heads):
            mine = head_lanes((rows, width), h)
            qm = jnp.where(mine, q_ref[...], jnp.zeros((), bf16))
            s = lax.dot_general(qm, k_ref[:n], NT, preferred_element_type=f32)
            row = lax.broadcasted_iota(jnp.int32, (rows, rows), 0)
            column = lax.broadcasted_iota(jnp.int32, (rows, rows), 1)
            tail = jnp.where(column <= row, s[:, n - rows :], -1e30)
            top = jnp.max(tail, axis=1, keepdims=True)
            if last:
                top = jnp.maximum(top, jnp.max(s[:, : n - rows], axis=1, keepdims=True))
            top = top * LOG2E
            vm = jnp.where(head_lanes((n, width), h), v_ref[:n], jnp.ones((), bf16))
            low = jnp.exp2(tail * LOG2E - top).astype(bf16)
            out = lax.dot_general(low, vm[n - rows :], NN, preferred_element_type=f32)
            if last:
                low = jnp.exp2(s[:, : n - rows] * LOG2E - top).astype(bf16)
                out = out + lax.dot_general(low, vm[: n - rows], NN, preferred_element_type=f32)
            total = pltpu.roll(out, HEAD_DIM, 1)
            acc = jnp.where(mine, out / total, acc)
            logs = jnp.where(mine, top + jnp.log2(total), logs)
        o_ref[...] = acc.astype(bf16)
        lane = lax.broadcasted_iota(jnp.int32, (8, width), 1)
        pick = (lane == HEAD_DIM * lax.broadcasted_iota(jnp.int32, (8, width), 0)).astype(f32)
        lse_ref[...] = lax.dot_general(
            pick, logs, NT, precision=lax.Precision.HIGHEST, preferred_element_type=f32
        )

    for i in range(blocks):
        pl.when(pl.program_id(0) == i)(functools.partial(branch, i))


def attend_forward(q, k, v, rows=BLOCK):
    length, width = q.shape
    blocks = length // rows
    return pl.pallas_call(
        functools.partial(forward_kernel, rows=rows, blocks=blocks),
        grid=(blocks,),
        out_shape=(
            jax.ShapeDtypeStruct((length, width), bf16),
            jax.ShapeDtypeStruct((8, length), f32),
        ),
        in_specs=[
            pl.BlockSpec((rows, width), lambda i: (i, 0)),
            pl.BlockSpec((length, width), lambda i: (0, 0)),
            pl.BlockSpec((length, width), lambda i: (0, 0)),
        ],
        out_specs=(
            pl.BlockSpec((rows, width), lambda i: (i, 0)),
            pl.BlockSpec((8, rows), lambda i: (0, i)),
        ),
        compiler_params=pltpu.CompilerParams(vmem_limit_bytes=48 * 2**20),
        cost_estimate=pl.CostEstimate(
            flops=20_000_000_000, bytes_accessed=6 * 2**20, transcendentals=0
        ),
    )(q, k, v)


def backward_kernel(
    q_ref, k_ref, v_ref, o_ref, do_ref, lse_ref, cos_ref, sin_ref, out_ref, dq, delta, *, rows
):
    length, width = q_ref.shape
    heads = width // HEAD_DIM
    blocks = length // rows
    lane_head = lax.broadcasted_iota(jnp.int32, (8, width), 1) // HEAD_DIM
    marks = (lane_head == lax.broadcasted_iota(jnp.int32, (8, width), 0)).astype(f32)

    def span(i):
        return pl.ds(pl.multiple_of(i * rows, rows), rows)

    @pl.loop(0, blocks)
    def _(i):
        product = do_ref[span(i)].astype(f32) * o_ref[span(i)].astype(f32)
        delta[:, span(i)] = lax.dot_general(
            marks, product, NT, precision=lax.Precision.HIGHEST, preferred_element_type=f32
        )

    dq[...] = jnp.zeros_like(dq)

    def tile(i, j, diagonal):
        at = span(i)
        keys, values = k_ref[span(j)], v_ref[span(j)]
        queries, grads = q_ref[at], do_ref[at]
        dk = jnp.zeros((rows, width), f32)
        dv = jnp.zeros((rows, width), f32)
        dqi = dq[at]
        zero = jnp.zeros((), bf16)
        for h in range(heads):
            mine = head_lanes((rows, width), h)
            qm = jnp.where(mine, queries, zero)
            dom = jnp.where(mine, grads, zero)
            km = jnp.where(mine, keys, zero)
            st = lax.dot_general(keys, qm, NT, preferred_element_type=f32)
            pt = jnp.exp2(st * LOG2E - lse_ref[h : h + 1, at])
            if diagonal:
                key = lax.broadcasted_iota(jnp.int32, (rows, rows), 0)
                query = lax.broadcasted_iota(jnp.int32, (rows, rows), 1)
                pt = jnp.where(key <= query, pt, 0.0)
            dpt = lax.dot_general(values, dom, NT, preferred_element_type=f32)
            dst = (pt * (dpt - delta[h : h + 1, at])).astype(bf16)
            dv = dv + jnp.dot(pt.astype(bf16), dom, preferred_element_type=f32)
            dk = dk + jnp.dot(dst, qm, preferred_element_type=f32)
            dqi = dqi + lax.dot_general(dst, km, TN, preferred_element_type=f32)
        dq[at] = dqi
        return dk, dv

    def turn_back(grad, at):
        return grad * cos_ref[at] + swap_halves(grad, 1.0) * sin_ref[at]

    @pl.loop(0, blocks)
    def _(j):
        def more(i, carry):
            dk, dv = tile(i, j, False)
            return carry[0] + dk, carry[1] + dv

        dk, dv = lax.fori_loop(j + 1, blocks, more, tile(j, j, True))
        out_ref[span(j), width : 2 * width] = turn_back(dk, span(j)).astype(bf16)
        out_ref[span(j), 2 * width :] = dv.astype(bf16)

    @pl.loop(0, blocks)
    def _(i):
        turned = turn_back(dq[span(i)], span(i))
        out_ref[span(i), :width] = (HEAD_DIM ** (-0.5) * turned).astype(bf16)


def attend_backward(q, k, v, o, do, lse, cosine, sine, rows=BLOCK):
    length, width = q.shape
    vmem = pl.BlockSpec(memory_space=pltpu.VMEM)
    return pl.pallas_call(
        functools.partial(backward_kernel, rows=rows),
        out_shape=jax.ShapeDtypeStruct((length, 3 * width), bf16),
        in_specs=[vmem] * 8,
        out_specs=vmem,
        scratch_shapes=[pltpu.VMEM((length, width), f32), pltpu.VMEM((8, length), f32)],
        compiler_params=pltpu.CompilerParams(vmem_limit_bytes=56 * 2**20),
        cost_estimate=pl.CostEstimate(
            flops=45_000_000_000, bytes_accessed=12 * 2**20, transcendentals=0
        ),
    )(q, k, v, o, do, lse, cosine, sine)


def norm_forward(value, gain, shift):
    center = value - jnp.mean(value, axis=-1, keepdims=True)
    inverse = lax.rsqrt(jnp.mean(center * center, axis=-1, keepdims=True) + EPS)
    unit = center * inverse
    return (unit * gain + shift, unit, inverse)


def norm_backward(grad, unit, inverse, gain):
    scaled = grad * gain
    back = inverse * (
        scaled
        - jnp.mean(scaled, axis=-1, keepdims=True)
        - unit * jnp.mean(scaled * unit, axis=-1, keepdims=True)
    )
    return (back, jnp.sum(grad * unit, axis=0), jnp.sum(grad, axis=0))


def rotary_tables(length, width):
    half = HEAD_DIM // 2
    lane = jnp.arange(width, dtype=jnp.int32) % half
    freqs = 10000.0 ** (-(lane.astype(f32) / half))
    angles = jnp.arange(length, dtype=f32)[:, None] * freqs[None, :]
    return (jnp.cos(angles), jnp.sin(angles))


SWAP = [(0, 1), (1, 0)]


def dot(left, right, dims=NN):
    return lax.dot_general(left, right, dims, preferred_element_type=f32)


def across(value, axis):
    return lax.ppermute(value, axis, SWAP)


def turn(value):
    return lax.ppermute(value, ("b", "h"), [(0, 0), (1, 2), (2, 1), (3, 3)])


def quad_swap(value, far_b, far_l):
    mask = 2 * far_b + far_l
    return lax.ppermute(value, ("b", "l"), [(i, i ^ mask) for i in range(4)])


def gather_axis(value, axis, dim=0):
    other = across(value, axis)
    first = lax.axis_index(axis) == 0
    return jnp.where(
        first, jnp.concatenate([value, other], dim), jnp.concatenate([other, value], dim)
    )


def scatter_axis(value, axis):
    low, high = jnp.split(value.astype(f32), 2, axis=0)
    first = lax.axis_index(axis) == 0
    kept = jnp.where(first, low, high)
    sent = jnp.where(first, high, low).astype(bf16)
    return kept + across(sent, axis).astype(f32)


def on_device(
    tokens,
    w_qkv,
    w_out,
    w_up,
    w_down,
    norm_gains,
    norm_shifts,
    cotangent,
    corpus_ids,
    corpus_weight,
    *,
    groups,
):
    _, part, depth = tokens.shape
    cols = w_qkv.shape[2]
    units = w_up.shape[1]
    core, half, near = lax.axis_index("b"), lax.axis_index("h"), lax.axis_index("l")
    length = 4 * part
    place = 2 * core + near
    group = jnp.int32(0)
    for axis in groups:
        group = 2 * group + lax.axis_index(axis)
    n_groups = 2 ** len(groups)
    stack = ("h", "l")
    cosine, sine = rotary_tables(length, cols)
    gains = [norm_gains[i : i + 1] for i in range(4)]
    shifts = [norm_shifts[i : i + 1] for i in range(4)]

    resid_low = turn(tokens[0])
    w_attn = turn(w_qkv.reshape(depth, 3 * cols))
    near_block = across(resid_low, "l")
    blocks = [resid_low, across(resid_low, "b"), near_block, across(near_block, "b")]

    slice_out = cols // (2 * n_groups)
    out_piece = lax.dynamic_slice_in_dim(w_out, (2 * group + core) * slice_out, slice_out, 0)
    out_whole = lax.all_gather(out_piece, stack + groups + ("b",), axis=0, tiled=True)
    slice_unit = units // (2 * n_groups)
    unit_at = (core * n_groups + group) * slice_unit
    up_piece = lax.dynamic_slice_in_dim(w_up, unit_at, slice_unit, 1)
    down_piece = lax.dynamic_slice_in_dim(w_down, unit_at, slice_unit, 0)
    up_half = lax.all_gather(up_piece, stack + groups, axis=1, tiled=True)
    down_half = lax.all_gather(down_piece, stack + groups, axis=0, tiled=True)

    filled = ()
    for mask, block in zip((0, 2, 1, 3), blocks):
        filled = project(
            jnp.reshape(place ^ mask, (1,)),
            block,
            w_attn,
            gains[0],
            shifts[0],
            cosine,
            sine,
            length,
            filled,
        )
    q, k, v, whole_a = filled
    attended, lse = attend_forward(q, k, v)

    def block_of(value, mask):
        return lax.dynamic_slice_in_dim(value, (place ^ mask) * part, part, 0)

    def out_rows(mask):
        return lax.dynamic_slice_in_dim(out_whole, (place ^ mask) * cols, cols, 0)

    heads = {0: block_of(attended, 0)}
    for mask in (1, 3, 2):
        heads[mask] = quad_swap(block_of(attended, mask), mask // 2, mask % 2)
    branch_a = sum(dot(heads[mask], out_rows(mask)) for mask in (0, 2, 1, 3))

    resid = resid_low.astype(f32)
    normed_a, unit_0, inverse_0 = norm_forward(resid, gains[0], shifts[0])
    out_a, unit_1, inverse_1 = norm_forward(branch_a, gains[1], shifts[1])
    middle = resid + out_a
    normed_f, unit_2, inverse_2 = norm_forward(middle, gains[2], shifts[2])
    own_f = normed_f.astype(bf16)
    pair_f = jnp.concatenate([own_f, across(own_f, "b")], axis=0)
    hidden = dot(pair_f, up_half)
    cube = 0.7978845608028654 * (hidden + 0.044715 * hidden * hidden * hidden)
    bend = jnp.tanh(cube)
    active = (0.5 * hidden * (1.0 + bend)).astype(bf16)
    slope = 0.5 * (1.0 + bend) + 0.5 * hidden * (1.0 - bend * bend) * 0.7978845608028654 * (
        1.0 + 3 * 0.044715 * hidden * hidden
    )
    slope = slope.astype(bf16)
    branch_f = dot(active[part:], down_half).astype(bf16)
    branch_f = dot(active[:part], down_half) + across(branch_f, "b").astype(f32)
    out_f, unit_3, inverse_3 = norm_forward(branch_f, gains[3], shifts[3])
    output = turn((middle + out_f).astype(bf16))

    picks = (
        corpus_ids[:, None] == jnp.arange(corpus_weight.shape[0], dtype=jnp.int32)[None, :]
    ).astype(f32)
    row_scale = turn(jnp.dot(picks, corpus_weight, precision=lax.Precision.HIGHEST))
    grad_final = turn(cotangent[0]).astype(f32) * row_scale[:, None]
    back_3, gain_3, shift_3 = norm_backward(grad_final, unit_3, inverse_3, gains[3])
    own_g = back_3.astype(bf16)
    pair_g = jnp.concatenate([own_g, across(own_g, "b")], axis=0)
    grad_active = dot(pair_g, down_half, NT)
    grad_hidden = (slope.astype(f32) * grad_active).astype(bf16)
    down_grad = dot(active, pair_g, TN).astype(bf16)
    up_grad = dot(pair_f, grad_hidden, TN).astype(bf16)
    down_sum = lax.psum_scatter(down_grad, stack + groups, scatter_dimension=0, tiled=True)
    up_sum = lax.psum_scatter(up_grad, stack + groups, scatter_dimension=1, tiled=True)
    down_grad = lax.all_gather(down_sum, ("b",) + groups, axis=0, tiled=True).astype(f32)
    up_grad = lax.all_gather(up_sum, ("b",) + groups, axis=1, tiled=True).astype(f32)

    grad_f = dot(grad_hidden[part:], up_half, NT).astype(bf16)
    grad_f = dot(grad_hidden[:part], up_half, NT) + across(grad_f, "b").astype(f32)
    back_2, gain_2, shift_2 = norm_backward(grad_f, unit_2, inverse_2, gains[2])
    grad_middle = grad_final + back_2
    back_1, gain_1, shift_1 = norm_backward(grad_middle, unit_1, inverse_1, gains[1])
    grad_a = back_1.astype(bf16)
    grad_attended = jnp.zeros((length, cols), bf16)
    for mask in (3, 1, 2, 0):
        sent = dot(grad_a, out_rows(mask), NT).astype(bf16)
        if mask:
            sent = quad_swap(sent, mask // 2, mask % 2)
        grad_attended = lax.dynamic_update_slice_in_dim(
            grad_attended, sent, (place ^ mask) * part, 0
        )
    out_grad = jnp.zeros((4 * cols, depth), bf16)
    for mask in range(4):
        out_grad = lax.dynamic_update_slice_in_dim(
            out_grad, dot(heads[mask], grad_a, TN).astype(bf16), (place ^ mask) * cols, 0
        )
    out_sum = lax.psum_scatter(
        out_grad, stack + groups + ("b",), scatter_dimension=0, tiled=True
    )
    out_grad = lax.all_gather(out_sum, groups + ("b",), axis=0, tiled=True).astype(f32)

    grad_mixed = attend_backward(q, k, v, attended, grad_attended, lse, cosine, sine)

    pair = 2 * part
    sent = lax.dynamic_slice_in_dim(grad_mixed, (1 - core) * pair, pair, 0)
    from_core = across(dot(sent, w_attn, NT).astype(bf16), "b")
    sent = dot(block_of(grad_mixed, 1), w_attn, NT)
    sent = sent + lax.dynamic_slice_in_dim(from_core, (1 - near) * part, part, 0).astype(f32)
    from_near = across(sent.astype(bf16), "l")
    grad_normed_a = dot(block_of(grad_mixed, 0), w_attn, NT)
    grad_normed_a = grad_normed_a + lax.dynamic_slice_in_dim(
        from_core, near * part, part, 0
    ).astype(f32)
    grad_normed_a = grad_normed_a + from_near.astype(f32)

    qkv_grad = dot(whole_a, grad_mixed, TN)
    for axis in groups:
        qkv_grad = scatter_axis(qkv_grad, axis)
    qkv_grad = turn(qkv_grad.astype(bf16))
    qkv_grad = scatter_axis(qkv_grad, "b").astype(bf16)
    qkv_grad = gather_axis(qkv_grad, "b")
    for axis in reversed(groups):
        qkv_grad = gather_axis(qkv_grad, axis)
    qkv_grad = qkv_grad.astype(f32).reshape(depth, 3, cols)

    back_0, gain_0, shift_0 = norm_backward(grad_normed_a, unit_0, inverse_0, gains[0])
    input_grad = turn((grad_middle + back_0).astype(bf16)).astype(f32)
    norm_grads = jnp.stack([gain_0, gain_1, gain_2, gain_3, shift_0, shift_1, shift_2, shift_3])
    norm_grads = lax.psum(norm_grads, groups + ("b",) + stack)
    return (
        output[None],
        input_grad[None],
        qkv_grad,
        out_grad,
        up_grad,
        down_grad,
        norm_grads[:4],
        norm_grads[4:],
    )


def solution(mesh):
    rows, parts = mesh.shape["dp"], mesh.shape["mp"]
    bits = (rows // 2).bit_length() - 1
    assert parts == 4 and rows == 2 ** (bits + 1)
    groups = tuple(f"g{i}" for i in range(bits))
    fine = Mesh(mesh.devices.reshape((2,) * (bits + 3)), groups + ("b", "h", "l"))
    dp, mp = groups + ("b",), ("h", "l")
    placed = (
        P(dp, mp, None),
        P(None, None, mp),
        P(mp, None),
        P(None, mp),
        P(mp, None),
        P(),
        P(),
        P(dp, mp, None),
        P(dp),
        P(),
    )
    return jax.shard_map(
        functools.partial(on_device, groups=groups),
        mesh=fine,
        in_specs=placed,
        out_specs=(
            P(dp, mp, None),
            P(dp, mp, None),
            P(None, None, mp),
            P(mp, None),
            P(None, mp),
            P(mp, None),
            P(),
            P(),
        ),
        check_vma=False,
    )
```

```python
import functools

import jax
import jax.numpy as jnp
import numpy as np
from jax import lax
from jax.experimental import pallas as pl
from jax.experimental.pallas import tpu as pltpu
from jax.sharding import Mesh, PartitionSpec as P

HEAD_DIM = 64
BLOCK = 512
EPS = 1e-05
LOG2E = 1.4426950408889634
NN = (((1,), (0,)), ((), ()))
NT = (((1,), (1,)), ((), ()))
TN = (((0,), (0,)), ((), ()))
f32 = jnp.float32
bf16 = jnp.bfloat16


def head_lanes(shape, head):
    return lax.broadcasted_iota(jnp.int32, shape, 1) // HEAD_DIM == head


def swap_halves(value, sign):
    half = HEAD_DIM // 2
    width = value.shape[1]
    first = (lax.broadcasted_iota(jnp.int32, value.shape, 1) // half) % 2 == 0
    return jnp.where(
        first, sign * pltpu.roll(value, width - half, 1), -sign * pltpu.roll(value, half, 1)
    )


def qkv_kernel(place_ref, x_ref, w_ref, gain_ref, shift_ref, cos_ref, sin_ref, *refs):
    q_ref, k_ref, v_ref, normed_ref = refs[-4:]
    width = q_ref.shape[1]
    value = x_ref[...].astype(f32)
    center = value - jnp.mean(value, axis=1, keepdims=True)
    inverse = lax.rsqrt(jnp.mean(center * center, axis=1, keepdims=True) + EPS)
    normed = (center * inverse * gain_ref[...] + shift_ref[...]).astype(bf16)
    normed_ref[...] = normed
    mixed = jnp.dot(normed, w_ref[...], preferred_element_type=f32)
    cosine, sine = cos_ref[...], sin_ref[...]
    query, key = mixed[:, :width], mixed[:, width : 2 * width]
    query = HEAD_DIM ** (-0.5) * (query * cosine + swap_halves(query, -1.0) * sine)
    q_ref[...] = query.astype(bf16)
    k_ref[...] = (key * cosine + swap_halves(key, -1.0) * sine).astype(bf16)
    v_ref[...] = mixed[:, 2 * width :].astype(bf16)


def project(place, x, w, gain, shift, cosine, sine, length, filled, rows=256):
    part, depth = x.shape
    width = w.shape[1] // 3
    steps = part // rows

    def there(i, place_ref):
        return (place_ref[0] * steps + i, 0)

    def whole(i, place_ref):
        return (0, 0)

    return pl.pallas_call(
        qkv_kernel,
        out_shape=tuple(
            jax.ShapeDtypeStruct((length, n), bf16) for n in (width, width, width, depth)
        ),
        grid_spec=pltpu.PrefetchScalarGridSpec(
            num_scalar_prefetch=1,
            grid=(steps,),
            in_specs=[
                pl.BlockSpec((rows, depth), lambda i, place_ref: (i, 0)),
                pl.BlockSpec(w.shape, whole),
                pl.BlockSpec((1, depth), whole),
                pl.BlockSpec((1, depth), whole),
                pl.BlockSpec((rows, width), there),
                pl.BlockSpec((rows, width), there),
            ]
            + [pl.BlockSpec(memory_space=pl.ANY)] * len(filled),
            out_specs=tuple(pl.BlockSpec((rows, n), there) for n in (width, width, width, depth)),
        ),
        input_output_aliases={7 + i: i for i in range(len(filled))},
        compiler_params=pltpu.CompilerParams(vmem_limit_bytes=40 * 2**20),
        cost_estimate=pl.CostEstimate(
            flops=2 * part * depth * 3 * width, bytes_accessed=5 * 2**20, transcendentals=0
        ),
    )(place, x, w, gain, shift, cosine, sine, *filled)


def forward_kernel(q_ref, k_ref, v_ref, o_ref, lse_ref, *, rows, blocks):
    width = q_ref.shape[1]
    heads = width // HEAD_DIM

    def branch(last):
        n = (last + 1) * rows
        acc = jnp.zeros((rows, width), f32)
        logs = jnp.zeros((rows, width), f32)
        for h in range(heads):
            mine = head_lanes((rows, width), h)
            qm = jnp.where(mine, q_ref[...], jnp.zeros((), bf16))
            s = lax.dot_general(qm, k_ref[:n], NT, preferred_element_type=f32)
            row = lax.broadcasted_iota(jnp.int32, (rows, rows), 0)
            column = lax.broadcasted_iota(jnp.int32, (rows, rows), 1)
            tail = jnp.where(column <= row, s[:, n - rows :], -1e30)
            top = jnp.max(tail, axis=1, keepdims=True)
            if last:
                top = jnp.maximum(top, jnp.max(s[:, : n - rows], axis=1, keepdims=True))
            top = top * LOG2E
            vm = jnp.where(head_lanes((n, width), h), v_ref[:n], jnp.ones((), bf16))
            low = jnp.exp2(tail * LOG2E - top).astype(bf16)
            out = lax.dot_general(low, vm[n - rows :], NN, preferred_element_type=f32)
            if last:
                low = jnp.exp2(s[:, : n - rows] * LOG2E - top).astype(bf16)
                out = out + lax.dot_general(low, vm[: n - rows], NN, preferred_element_type=f32)
            total = pltpu.roll(out, HEAD_DIM, 1)
            acc = jnp.where(mine, out / total, acc)
            logs = jnp.where(mine, top + jnp.log2(total), logs)
        o_ref[...] = acc.astype(bf16)
        lane = lax.broadcasted_iota(jnp.int32, (8, width), 1)
        pick = (lane == HEAD_DIM * lax.broadcasted_iota(jnp.int32, (8, width), 0)).astype(f32)
        lse_ref[...] = lax.dot_general(
            pick, logs, NT, precision=lax.Precision.HIGHEST, preferred_element_type=f32
        )

    for i in range(blocks):
        pl.when(pl.program_id(0) == i)(functools.partial(branch, i))


def attend_forward(q, k, v, rows=BLOCK):
    length, width = q.shape
    blocks = length // rows
    return pl.pallas_call(
        functools.partial(forward_kernel, rows=rows, blocks=blocks),
        grid=(blocks,),
        out_shape=(
            jax.ShapeDtypeStruct((length, width), bf16),
            jax.ShapeDtypeStruct((8, length), f32),
        ),
        in_specs=[
            pl.BlockSpec((rows, width), lambda i: (i, 0)),
            pl.BlockSpec((length, width), lambda i: (0, 0)),
            pl.BlockSpec((length, width), lambda i: (0, 0)),
        ],
        out_specs=(
            pl.BlockSpec((rows, width), lambda i: (i, 0)),
            pl.BlockSpec((8, rows), lambda i: (0, i)),
        ),
        compiler_params=pltpu.CompilerParams(vmem_limit_bytes=48 * 2**20),
        cost_estimate=pl.CostEstimate(
            flops=20_000_000_000, bytes_accessed=6 * 2**20, transcendentals=0
        ),
    )(q, k, v)


MESH = pl.DeviceIdType.MESH


class Copies:
    def __init__(self, send, recv):
        self.send, self.recv, self.made = send, recv, {}

    def start(self, name, source, target, device):
        n = len(self.made)
        copy = pltpu.make_async_remote_copy(
            src_ref=source,
            dst_ref=target,
            send_sem=self.send.at[n],
            recv_sem=self.recv.at[n],
            device_id=device,
            device_id_type=MESH,
        )
        self.made[name] = copy
        copy.start()

    def arrived(self, name):
        self.made[name].wait_recv()

    def drain(self):
        for copy in self.made.values():
            copy.wait_send()


def flip(axis):
    return {axis: 1 - lax.axis_index(axis)}


def next_layer(step):
    at = lax.rem(2 * lax.axis_index("h") + lax.axis_index("l") + step, 4)
    return {"h": at // 2, "l": lax.rem(at, 2)}


def greet(groups):
    barrier = pltpu.get_barrier_semaphore()
    friends = [flip(axis) for axis in groups + ("b",)] + [next_layer(1), next_layer(3)]
    for friend in friends:
        pl.semaphore_signal(barrier, inc=1, device_id=friend, device_id_type=MESH)
    pl.semaphore_wait(barrier, len(friends))


def add_into(total, term, rows=16):
    lead, count = total.shape[:-2], total.shape[-2]
    step = min(rows, count)

    @pl.loop(0, count // step)
    def _(i):
        at = pl.ds(pl.multiple_of(i * step, step), step)
        for index in np.ndindex(*lead):
            total[index + (at,)] = (
                total[index + (at,)].astype(f32) + term[index + (at,)].astype(f32)
            ).astype(bf16)


def sums_kernel(*refs, groups, rows):
    (
        q_ref, k_ref, v_ref, o_ref, do_ref, lse_ref, cos_ref, sin_ref,
        up_ref, out_ref, down_ref,
        mixed_ref, up_all, out_all, down_all,
        dq, dk, dv, delta,
        *rest,
    ) = refs
    bits = len(groups)
    terms = (up_ref, out_ref, down_ref)
    results = (up_all, out_all, down_all)
    partial = [[rest[3 * s + a] for s in range(bits)] for a in range(3)]
    rest = rest[3 * bits :]
    passing, (send, recv, local) = rest[:3], rest[3:]
    copies = Copies(send, recv)
    place = [lax.axis_index(axis) for axis in groups]
    layer = 2 * lax.axis_index("h") + lax.axis_index("l")
    core = lax.axis_index("b")
    orders = [tuple(range(bits)), tuple(range(bits)), tuple(reversed(range(bits)))]

    def shard(k):
        return lax.rem(layer + 4 - k, 4)

    def index(order, stage, side):
        at = []
        for axis in range(bits):
            when = order.index(axis)
            if when < stage:
                at.append(place[axis])
            elif when == stage:
                at.append(place[axis] if side == 0 else 1 - place[axis])
            else:
                at.append(slice(None))
        return tuple(at)

    def inner(order, stage, side):
        at = []
        for axis in range(bits):
            when = order.index(axis)
            if when == stage:
                at.append(place[axis] if side == 0 else 1 - place[axis])
            elif when > stage:
                at.append(slice(None))
        return tuple(at)

    def source(a, k, stage, side):
        order = orders[a]
        if stage == 0:
            return terms[a].at[(shard(k),) + index(order, 0, side)]
        return partial[a][stage - 1].at[(k % 4,) + inner(order, stage, side)]

    def plane_send(k, stage):
        for a in range(3):
            copies.start(
                ("plane", a, k, stage),
                source(a, k, stage, 1),
                partial[a][stage].at[k % 4],
                flip(groups[orders[a][stage]]),
            )

    def plane_add(k, stage):
        for a in range(3):
            copies.arrived(("plane", a, k, stage))
            add_into(partial[a][stage].at[k % 4], source(a, k, stage, 0))

    def ring_send(step):
        for a in range(3):
            held = partial[a][bits - 1].at[1] if step == 1 else passing[a].at[step - 2]
            copies.start(("ring", a, step), held, passing[a].at[step - 1], next_layer(1))

    def ring_add(step):
        for a in range(3):
            copies.arrived(("ring", a, step))
            add_into(passing[a].at[step - 1], partial[a][bits - 1].at[(step + 1) % 4])

    def gather_send(stage):
        for a in range(3):
            order = orders[a]
            at = tuple(
                place[axis] if order.index(axis) >= stage else slice(None) for axis in range(bits)
            )
            held = passing[a].at[2] if stage == 0 else results[a].at[(core,) + at]
            copies.start(
                ("gather", a, stage), held, results[a].at[(core,) + at], flip(groups[order[stage]])
            )

    def core_send(stage):
        for a in range(3):
            order = orders[a]
            at = []
            for axis in range(bits):
                when = order.index(axis)
                if stage == 0 or when > stage - 1:
                    at.append(place[axis])
                elif when == stage - 1:
                    at.append(1 - place[axis])
                else:
                    at.append(slice(None))
            spot = results[a].at[(core,) + tuple(at)]
            held = passing[a].at[2] if stage == 0 else spot
            copies.start(("core", a, stage), held, spot, flip("b"))

    greet(groups)
    length, width = q_ref.shape
    heads = width // HEAD_DIM
    blocks = length // rows
    lane_head = lax.broadcasted_iota(jnp.int32, (8, width), 1) // HEAD_DIM
    marks = (lane_head == lax.broadcasted_iota(jnp.int32, (8, width), 0)).astype(f32)
    for k in (1, 2):
        plane_send(k, 0)

    def span(i):
        return pl.ds(pl.multiple_of(i * rows, rows), rows)

    @pl.loop(0, blocks)
    def _(i):
        product = do_ref[span(i)].astype(f32) * o_ref[span(i)].astype(f32)
        delta[:, span(i)] = lax.dot_general(
            marks, product, NT, precision=lax.Precision.HIGHEST, preferred_element_type=f32
        )

    for total in (dq, dk, dv):
        total[...] = jnp.zeros_like(total)

    def tile(i, j):
        at, to = span(i), span(j)
        keys, values = k_ref[to], v_ref[to]
        queries, grads = q_ref[at], do_ref[at]
        dkj, dvj, dqi = dk[to], dv[to], dq[at]
        zero = jnp.zeros((), bf16)
        key = j * rows + lax.broadcasted_iota(jnp.int32, (rows, rows), 0)
        query = i * rows + lax.broadcasted_iota(jnp.int32, (rows, rows), 1)
        allowed = key <= query
        for h in range(heads):
            mine = head_lanes((rows, width), h)
            qm = jnp.where(mine, queries, zero)
            dom = jnp.where(mine, grads, zero)
            km = jnp.where(mine, keys, zero)
            st = lax.dot_general(keys, qm, NT, preferred_element_type=f32)
            pt = jnp.where(allowed, jnp.exp2(st * LOG2E - lse_ref[h : h + 1, at]), 0.0)
            dpt = lax.dot_general(values, dom, NT, preferred_element_type=f32)
            dst = (pt * (dpt - delta[h : h + 1, at])).astype(bf16)
            dvj = dvj + jnp.dot(pt.astype(bf16), dom, preferred_element_type=f32)
            dkj = dkj + jnp.dot(dst, qm, preferred_element_type=f32)
            dqi = dqi + lax.dot_general(dst, km, TN, preferred_element_type=f32)
        dq[at], dk[to], dv[to] = dqi, dkj, dvj

    def tiles(low, high):
        @pl.loop(low, high)
        def _(t):
            i = jnp.int32(0)
            for n in range(1, blocks):
                i = i + (t >= n * (n + 1) // 2).astype(jnp.int32)
            tile(i, t - i * (i + 1) // 2)

    count = blocks * (blocks + 1) // 2
    tiles(0, 3 * count // 10)
    plane_add(1, 0)
    if bits > 1:
        plane_send(1, 1)
    plane_send(3, 0)
    tiles(3 * count // 10, 8 * count // 10)
    plane_add(2, 0)
    if bits > 1:
        plane_send(2, 1)
    plane_send(4, 0)
    tiles(8 * count // 10, count)

    def turn_back(grad, at):
        return grad * cos_ref[at] + swap_halves(grad, 1.0) * sin_ref[at]

    @pl.loop(0, blocks)
    def _(i):
        at = span(i)
        mixed_ref[at, :width] = (HEAD_DIM ** (-0.5) * turn_back(dq[at], at)).astype(bf16)
        mixed_ref[at, width : 2 * width] = turn_back(dk[at], at).astype(bf16)
        mixed_ref[at, 2 * width :] = dv[at].astype(bf16)

    for stage in range(1, bits):
        for k in (1, 2):
            plane_add(k, stage)
            if stage + 1 < bits:
                plane_send(k, stage + 1)
    ring_send(1)
    plane_add(3, 0)
    if bits > 1:
        plane_send(3, 1)
    ring_add(1)
    ring_send(2)
    plane_add(4, 0)
    if bits > 1:
        plane_send(4, 1)
    for stage in range(1, bits):
        plane_add(3, stage)
        if stage + 1 < bits:
            plane_send(3, stage + 1)
    ring_add(2)
    ring_send(3)
    for stage in range(1, bits):
        plane_add(4, stage)
        if stage + 1 < bits:
            plane_send(4, stage + 1)
    ring_add(3)
    core_send(0)
    own = [
        pltpu.make_async_copy(
            passing[a].at[2], results[a].at[(core,) + tuple(place)], local.at[a]
        )
        for a in range(3)
    ]
    gather_send(0)
    for copy in own:
        copy.start()
    for copy in own:
        copy.wait()
    for stage in range(bits):
        for a in range(3):
            copies.arrived(("gather", a, stage))
        if stage + 1 < bits:
            gather_send(stage + 1)
        core_send(stage + 1)
    for stage in range(bits + 1):
        for a in range(3):
            copies.arrived(("core", a, stage))
    copies.drain()


def attend_and_sum(q, k, v, o, do, lse, cosine, sine, up, out, down, groups, rows=BLOCK):
    length, width = q.shape
    bits = len(groups)
    terms = (up, out, down)
    vmem = pl.BlockSpec(memory_space=pltpu.VMEM)
    anywhere = pl.BlockSpec(memory_space=pl.ANY)
    scratch = [pltpu.VMEM((length, width), f32)] * 3 + [pltpu.VMEM((8, length), f32)]
    for stage in range(bits):
        for term in terms:
            kept = (2,) * (bits - 1 - stage)
            scratch.append(pltpu.VMEM((4,) + kept + term.shape[-2:], bf16))
    for term in terms:
        scratch.append(pltpu.VMEM((3,) + term.shape[-2:], bf16))
    n = 3 * (4 * bits + 3 + bits + bits + 1)
    scratch += [pltpu.SemaphoreType.DMA((n,)), pltpu.SemaphoreType.DMA((n,))]
    scratch += [pltpu.SemaphoreType.DMA((3,))]
    return pl.pallas_call(
        functools.partial(sums_kernel, groups=groups, rows=rows),
        out_shape=(jax.ShapeDtypeStruct((length, 3 * width), bf16),)
        + tuple(jax.ShapeDtypeStruct((2,) + term.shape[1:], bf16) for term in terms),
        in_specs=[vmem] * 11,
        out_specs=(vmem,) + (anywhere,) * 3,
        scratch_shapes=scratch,
        compiler_params=pltpu.CompilerParams(
            vmem_limit_bytes=60 * 2**20, collective_id=1, has_side_effects=True
        ),
        cost_estimate=pl.CostEstimate(
            flops=100_000_000_000, bytes_accessed=32 * 2**20, transcendentals=0
        ),
    )(q, k, v, o, do, lse, cosine, sine, up, out, down)


def norm_forward(value, gain, shift):
    center = value - jnp.mean(value, axis=-1, keepdims=True)
    inverse = lax.rsqrt(jnp.mean(center * center, axis=-1, keepdims=True) + EPS)
    unit = center * inverse
    return (unit * gain + shift, unit, inverse)


def norm_backward(grad, unit, inverse, gain):
    scaled = grad * gain
    back = inverse * (
        scaled
        - jnp.mean(scaled, axis=-1, keepdims=True)
        - unit * jnp.mean(scaled * unit, axis=-1, keepdims=True)
    )
    return (back, jnp.sum(grad * unit, axis=0), jnp.sum(grad, axis=0))


def rotary_tables(length, width):
    half = HEAD_DIM // 2
    lane = jnp.arange(width, dtype=jnp.int32) % half
    freqs = 10000.0 ** (-(lane.astype(f32) / half))
    angles = jnp.arange(length, dtype=f32)[:, None] * freqs[None, :]
    return (jnp.cos(angles), jnp.sin(angles))


SWAP = [(0, 1), (1, 0)]


def dot(left, right, dims=NN):
    return lax.dot_general(left, right, dims, preferred_element_type=f32)


def across(value, axis):
    return lax.ppermute(value, axis, SWAP)


def turn(value):
    return lax.ppermute(value, ("b", "h"), [(0, 0), (1, 2), (2, 1), (3, 3)])


def quad_swap(value, far_b, far_l):
    mask = 2 * far_b + far_l
    return lax.ppermute(value, ("b", "l"), [(i, i ^ mask) for i in range(4)])


def gather_axis(value, axis, dim=0):
    other = across(value, axis)
    first = lax.axis_index(axis) == 0
    return jnp.where(
        first, jnp.concatenate([value, other], dim), jnp.concatenate([other, value], dim)
    )


def scatter_axis(value, axis):
    low, high = jnp.split(value.astype(f32), 2, axis=0)
    first = lax.axis_index(axis) == 0
    kept = jnp.where(first, low, high)
    sent = jnp.where(first, high, low).astype(bf16)
    return kept + across(sent, axis).astype(f32)


def on_device(
    tokens,
    w_qkv,
    w_out,
    w_up,
    w_down,
    norm_gains,
    norm_shifts,
    cotangent,
    corpus_ids,
    corpus_weight,
    *,
    groups,
):
    _, part, depth = tokens.shape
    cols = w_qkv.shape[2]
    units = w_up.shape[1]
    core, half, near = lax.axis_index("b"), lax.axis_index("h"), lax.axis_index("l")
    length = 4 * part
    place = 2 * core + near
    group = jnp.int32(0)
    for axis in groups:
        group = 2 * group + lax.axis_index(axis)
    n_groups = 2 ** len(groups)
    stack = ("h", "l")
    cosine, sine = rotary_tables(length, cols)
    gains = [norm_gains[i : i + 1] for i in range(4)]
    shifts = [norm_shifts[i : i + 1] for i in range(4)]

    resid_low = turn(tokens[0])
    w_attn = turn(w_qkv.reshape(depth, 3 * cols))
    near_block = across(resid_low, "l")
    blocks = [resid_low, across(resid_low, "b"), near_block, across(near_block, "b")]

    slice_out = cols // (2 * n_groups)
    out_piece = lax.dynamic_slice_in_dim(w_out, (2 * group + core) * slice_out, slice_out, 0)
    out_whole = lax.all_gather(out_piece, stack + groups + ("b",), axis=0, tiled=True)
    slice_unit = units // (2 * n_groups)
    unit_at = (core * n_groups + group) * slice_unit
    up_piece = lax.dynamic_slice_in_dim(w_up, unit_at, slice_unit, 1)
    down_piece = lax.dynamic_slice_in_dim(w_down, unit_at, slice_unit, 0)
    up_half = lax.all_gather(up_piece, stack + groups, axis=1, tiled=True)
    down_half = lax.all_gather(down_piece, stack + groups, axis=0, tiled=True)

    filled = ()
    for mask, block in zip((0, 2, 1, 3), blocks):
        filled = project(
            jnp.reshape(place ^ mask, (1,)),
            block,
            w_attn,
            gains[0],
            shifts[0],
            cosine,
            sine,
            length,
            filled,
        )
    q, k, v, whole_a = filled
    attended, lse = attend_forward(q, k, v)

    def block_of(value, mask):
        return lax.dynamic_slice_in_dim(value, (place ^ mask) * part, part, 0)

    def out_rows(mask):
        return lax.dynamic_slice_in_dim(out_whole, (place ^ mask) * cols, cols, 0)

    heads = {0: block_of(attended, 0)}
    for mask in (1, 3, 2):
        heads[mask] = quad_swap(block_of(attended, mask), mask // 2, mask % 2)
    branch_a = sum(dot(heads[mask], out_rows(mask)) for mask in (0, 2, 1, 3))

    resid = resid_low.astype(f32)
    normed_a, unit_0, inverse_0 = norm_forward(resid, gains[0], shifts[0])
    out_a, unit_1, inverse_1 = norm_forward(branch_a, gains[1], shifts[1])
    middle = resid + out_a
    normed_f, unit_2, inverse_2 = norm_forward(middle, gains[2], shifts[2])
    own_f = normed_f.astype(bf16)
    pair_f = jnp.concatenate([own_f, across(own_f, "b")], axis=0)
    hidden = dot(pair_f, up_half)
    cube = 0.7978845608028654 * (hidden + 0.044715 * hidden * hidden * hidden)
    bend = jnp.tanh(cube)
    active = (0.5 * hidden * (1.0 + bend)).astype(bf16)
    slope = 0.5 * (1.0 + bend) + 0.5 * hidden * (1.0 - bend * bend) * 0.7978845608028654 * (
        1.0 + 3 * 0.044715 * hidden * hidden
    )
    slope = slope.astype(bf16)
    branch_f = dot(active[part:], down_half).astype(bf16)
    branch_f = dot(active[:part], down_half) + across(branch_f, "b").astype(f32)
    out_f, unit_3, inverse_3 = norm_forward(branch_f, gains[3], shifts[3])
    output = turn((middle + out_f).astype(bf16))

    picks = (
        corpus_ids[:, None] == jnp.arange(corpus_weight.shape[0], dtype=jnp.int32)[None, :]
    ).astype(f32)
    row_scale = turn(jnp.dot(picks, corpus_weight, precision=lax.Precision.HIGHEST))
    grad_final = turn(cotangent[0]).astype(f32) * row_scale[:, None]
    back_3, gain_3, shift_3 = norm_backward(grad_final, unit_3, inverse_3, gains[3])
    own_g = back_3.astype(bf16)
    pair_g = jnp.concatenate([own_g, across(own_g, "b")], axis=0)
    grad_active = dot(pair_g, down_half, NT)
    grad_hidden = (slope.astype(f32) * grad_active).astype(bf16)
    down_grad = dot(active, pair_g, TN).astype(bf16)
    up_grad = dot(grad_hidden, pair_f, TN).astype(bf16)

    grad_f = dot(grad_hidden[part:], up_half, NT).astype(bf16)
    grad_f = dot(grad_hidden[:part], up_half, NT) + across(grad_f, "b").astype(f32)
    back_2, gain_2, shift_2 = norm_backward(grad_f, unit_2, inverse_2, gains[2])
    grad_middle = grad_final + back_2
    back_1, gain_1, shift_1 = norm_backward(grad_middle, unit_1, inverse_1, gains[1])
    grad_a = back_1.astype(bf16)
    grad_attended = jnp.zeros((length, cols), bf16)
    for mask in (3, 1, 2, 0):
        sent = dot(grad_a, out_rows(mask), NT).astype(bf16)
        if mask:
            sent = quad_swap(sent, mask // 2, mask % 2)
        grad_attended = lax.dynamic_update_slice_in_dim(
            grad_attended, sent, (place ^ mask) * part, 0
        )
    out_grad = jnp.zeros((4 * cols, depth), bf16)
    for mask in range(4):
        out_grad = lax.dynamic_update_slice_in_dim(
            out_grad, dot(heads[mask], grad_a, TN).astype(bf16), (place ^ mask) * cols, 0
        )
    out_grad = out_grad.reshape(4, 2, cols // 2, depth)
    sent = lax.dynamic_index_in_dim(out_grad, 1 - core, 1, False)
    kept = lax.dynamic_index_in_dim(out_grad, core, 1, False)
    out_grad = (kept.astype(f32) + across(sent, "b").astype(f32)).astype(bf16)
    slots = (2,) * len(groups)

    def pieces(value):
        return value.reshape((4,) + slots + (value.size // (4 * n_groups * depth), depth))

    grad_mixed, up_grad, out_grad, down_grad = attend_and_sum(
        q,
        k,
        v,
        attended,
        grad_attended,
        lse,
        cosine,
        sine,
        pieces(up_grad),
        pieces(out_grad),
        pieces(down_grad),
        groups,
    )
    up_grad = up_grad.reshape(units, depth).T.astype(f32)
    out_grad = out_grad.reshape(cols, depth).astype(f32)
    down_grad = down_grad.reshape(units, depth).astype(f32)

    pair = 2 * part
    sent = lax.dynamic_slice_in_dim(grad_mixed, (1 - core) * pair, pair, 0)
    from_core = across(dot(sent, w_attn, NT).astype(bf16), "b")
    sent = dot(block_of(grad_mixed, 1), w_attn, NT)
    sent = sent + lax.dynamic_slice_in_dim(from_core, (1 - near) * part, part, 0).astype(f32)
    from_near = across(sent.astype(bf16), "l")
    grad_normed_a = dot(block_of(grad_mixed, 0), w_attn, NT)
    grad_normed_a = grad_normed_a + lax.dynamic_slice_in_dim(
        from_core, near * part, part, 0
    ).astype(f32)
    grad_normed_a = grad_normed_a + from_near.astype(f32)

    qkv_grad = dot(whole_a, grad_mixed, TN)
    for axis in groups:
        qkv_grad = scatter_axis(qkv_grad, axis)
    qkv_grad = turn(qkv_grad.astype(bf16))
    qkv_grad = scatter_axis(qkv_grad, "b").astype(bf16)
    qkv_grad = gather_axis(qkv_grad, "b")
    for axis in reversed(groups):
        qkv_grad = gather_axis(qkv_grad, axis)
    qkv_grad = qkv_grad.astype(f32).reshape(depth, 3, cols)

    back_0, gain_0, shift_0 = norm_backward(grad_normed_a, unit_0, inverse_0, gains[0])
    input_grad = turn((grad_middle + back_0).astype(bf16)).astype(f32)
    norm_grads = jnp.stack([gain_0, gain_1, gain_2, gain_3, shift_0, shift_1, shift_2, shift_3])
    norm_grads = lax.psum(norm_grads, groups + ("b",) + stack)
    return (
        output[None],
        input_grad[None],
        qkv_grad,
        out_grad,
        up_grad,
        down_grad,
        norm_grads[:4],
        norm_grads[4:],
    )


def solution(mesh):
    rows, parts = mesh.shape["dp"], mesh.shape["mp"]
    bits = (rows // 2).bit_length() - 1
    assert parts == 4 and rows == 2 ** (bits + 1)
    groups = tuple(f"g{i}" for i in range(bits))
    fine = Mesh(mesh.devices.reshape((2,) * (bits + 3)), groups + ("b", "h", "l"))
    dp, mp = groups + ("b",), ("h", "l")
    placed = (
        P(dp, mp, None),
        P(None, None, mp),
        P(mp, None),
        P(None, mp),
        P(mp, None),
        P(),
        P(),
        P(dp, mp, None),
        P(dp),
        P(),
    )
    return jax.shard_map(
        functools.partial(on_device, groups=groups),
        mesh=fine,
        in_specs=placed,
        out_specs=(
            P(dp, mp, None),
            P(dp, mp, None),
            P(None, None, mp),
            P(mp, None),
            P(None, mp),
            P(mp, None),
            P(),
            P(),
        ),
        check_vma=False,
    )
```

```python
import functools

import jax
import jax.numpy as jnp
import numpy as np
from jax import lax
from jax.experimental import pallas as pl
from jax.experimental.pallas import tpu as pltpu
from jax.sharding import Mesh, PartitionSpec as P

HEAD_DIM = 64
BLOCK = 512
EPS = 1e-05
LOG2E = 1.4426950408889634
NN = (((1,), (0,)), ((), ()))
NT = (((1,), (1,)), ((), ()))
TN = (((0,), (0,)), ((), ()))
f32 = jnp.float32
bf16 = jnp.bfloat16


def head_lanes(shape, head):
    return lax.broadcasted_iota(jnp.int32, shape, 1) // HEAD_DIM == head


def swap_halves(value, sign):
    half = HEAD_DIM // 2
    width = value.shape[1]
    first = (lax.broadcasted_iota(jnp.int32, value.shape, 1) // half) % 2 == 0
    return jnp.where(
        first, sign * pltpu.roll(value, width - half, 1), -sign * pltpu.roll(value, half, 1)
    )


MESH = pl.DeviceIdType.MESH


class Copies:
    def __init__(self, send, recv):
        self.send, self.recv, self.made = send, recv, {}

    def describe(self, name):
        n, build = self.made[name]
        source, target, device = build()
        return pltpu.make_async_remote_copy(
            src_ref=source,
            dst_ref=target,
            send_sem=self.send.at[n],
            recv_sem=self.recv.at[n],
            device_id=device,
            device_id_type=MESH,
        )

    def plan(self, name, build):
        self.made[name] = (len(self.made), build)

    def start(self, name, build=None):
        if build is not None:
            self.plan(name, build)
        self.describe(name).start()

    def arrived(self, name):
        self.describe(name).wait_recv()

    def sent(self, name):
        self.describe(name).wait_send()

    def drain(self, but=()):
        for name in self.made:
            if name not in but:
                self.sent(name)


def flip(axis):
    return {axis: 1 - lax.axis_index(axis)}


def next_layer(step):
    at = lax.rem(2 * lax.axis_index("h") + lax.axis_index("l") + step, 4)
    return {"h": at // 2, "l": lax.rem(at, 2)}


def greet(groups):
    barrier = pltpu.get_barrier_semaphore()
    friends = [flip(axis) for axis in groups + ("b",)] + [next_layer(1), next_layer(3)]
    for friend in friends:
        pl.semaphore_signal(barrier, inc=1, device_id=friend, device_id_type=MESH)
    pl.semaphore_wait(barrier, len(friends))


def add_into(total, term, rows=16):
    lead, count = total.shape[:-2], total.shape[-2]
    step = min(rows, count)

    @pl.loop(0, count // step)
    def _(i):
        at = pl.ds(pl.multiple_of(i * step, step), step)
        for index in np.ndindex(*lead):
            total[index + (at,)] = (
                total[index + (at,)].astype(f32) + term[index + (at,)].astype(f32)
            ).astype(bf16)


def sums_kernel(*refs, groups, rows):
    (
        q_ref, k_ref, v_ref, o_ref, do_ref, lse_ref, cos_ref, sin_ref,
        up_ref, out_ref, down_ref,
        mixed_ref, up_all, out_all, down_all,
        dq, dk, dv, delta,
        *rest,
    ) = refs
    bits = len(groups)
    terms = (up_ref, out_ref, down_ref)
    results = (up_all, out_all, down_all)
    partial = [[rest[3 * s + a] for s in range(bits)] for a in range(3)]
    rest = rest[3 * bits :]
    passing, (send, recv, local) = rest[:3], rest[3:]
    copies = Copies(send, recv)
    place = [lax.axis_index(axis) for axis in groups]
    layer = 2 * lax.axis_index("h") + lax.axis_index("l")
    core = lax.axis_index("b")
    orders = [tuple(range(bits)), tuple(range(bits)), tuple(reversed(range(bits)))]

    def shard(k):
        return lax.rem(layer + 4 - k, 4)

    def index(order, stage, side):
        at = []
        for axis in range(bits):
            when = order.index(axis)
            if when < stage:
                at.append(place[axis])
            elif when == stage:
                at.append(place[axis] if side == 0 else 1 - place[axis])
            else:
                at.append(slice(None))
        return tuple(at)

    def inner(order, stage, side):
        at = []
        for axis in range(bits):
            when = order.index(axis)
            if when == stage:
                at.append(place[axis] if side == 0 else 1 - place[axis])
            elif when > stage:
                at.append(slice(None))
        return tuple(at)

    def source(a, k, stage, side):
        order = orders[a]
        if stage == 0:
            return terms[a].at[(shard(k),) + index(order, 0, side)]
        return partial[a][stage - 1].at[(k % 4,) + inner(order, stage, side)]

    def plane_send(k, stage):
        for a in range(3):
            copies.start(
                ("plane", a, k, stage),
                lambda a=a: (
                    source(a, k, stage, 1),
                    partial[a][stage].at[k % 4],
                    flip(groups[orders[a][stage]]),
                ),
            )

    def plane_add(k, stage):
        for a in range(3):
            copies.arrived(("plane", a, k, stage))
            add_into(partial[a][stage].at[k % 4], source(a, k, stage, 0))

    def ring_send(step):
        for a in range(3):
            held = partial[a][bits - 1].at[1] if step == 1 else passing[a].at[step - 2]
            target = passing[a].at[step - 1]
            copies.start(
                ("ring", a, step), lambda held=held, target=target: (held, target, next_layer(1))
            )

    def ring_add(step):
        for a in range(3):
            copies.arrived(("ring", a, step))
            add_into(passing[a].at[step - 1], partial[a][bits - 1].at[(step + 1) % 4])

    def gather_send(stage):
        for a in range(3):
            order = orders[a]
            at = tuple(
                place[axis] if order.index(axis) >= stage else slice(None) for axis in range(bits)
            )
            held = passing[a].at[2] if stage == 0 else results[a].at[(core,) + at]
            spot = results[a].at[(core,) + at]
            axis = groups[order[stage]]
            copies.start(
                ("gather", a, stage),
                lambda held=held, spot=spot, axis=axis: (held, spot, flip(axis)),
            )

    def core_send(stage):
        for a in range(3):
            order = orders[a]
            at = []
            for axis in range(bits):
                when = order.index(axis)
                if stage == 0 or when > stage - 1:
                    at.append(place[axis])
                elif when == stage - 1:
                    at.append(1 - place[axis])
                else:
                    at.append(slice(None))
            spot = results[a].at[(core,) + tuple(at)]
            held = passing[a].at[2] if stage == 0 else spot
            copies.start(("core", a, stage), lambda held=held, spot=spot: (held, spot, flip("b")))

    greet(groups)
    length, width = q_ref.shape
    heads = width // HEAD_DIM
    blocks = length // rows
    lane_head = lax.broadcasted_iota(jnp.int32, (8, width), 1) // HEAD_DIM
    marks = (lane_head == lax.broadcasted_iota(jnp.int32, (8, width), 0)).astype(f32)
    for k in (1, 2):
        plane_send(k, 0)

    def span(i):
        return pl.ds(pl.multiple_of(i * rows, rows), rows)

    @pl.loop(0, blocks)
    def _(i):
        product = do_ref[span(i)].astype(f32) * o_ref[span(i)].astype(f32)
        delta[:, span(i)] = lax.dot_general(
            marks, product, NT, precision=lax.Precision.HIGHEST, preferred_element_type=f32
        )

    for total in (dq, dk, dv):
        total[...] = jnp.zeros_like(total)

    def tile(i, j):
        at, to = span(i), span(j)
        keys, values = k_ref[to], v_ref[to]
        queries, grads = q_ref[at], do_ref[at]
        dkj, dvj, dqi = dk[to], dv[to], dq[at]
        zero = jnp.zeros((), bf16)
        key = j * rows + lax.broadcasted_iota(jnp.int32, (rows, rows), 0)
        query = i * rows + lax.broadcasted_iota(jnp.int32, (rows, rows), 1)
        allowed = key <= query
        for h in range(heads):
            mine = head_lanes((rows, width), h)
            qm = jnp.where(mine, queries, zero)
            dom = jnp.where(mine, grads, zero)
            km = jnp.where(mine, keys, zero)
            st = lax.dot_general(keys, qm, NT, preferred_element_type=f32)
            pt = jnp.where(allowed, jnp.exp2(st * LOG2E - lse_ref[h : h + 1, at]), 0.0)
            dpt = lax.dot_general(values, dom, NT, preferred_element_type=f32)
            dst = (pt * (dpt - delta[h : h + 1, at])).astype(bf16)
            dvj = dvj + jnp.dot(pt.astype(bf16), dom, preferred_element_type=f32)
            dkj = dkj + jnp.dot(dst, qm, preferred_element_type=f32)
            dqi = dqi + lax.dot_general(dst, km, TN, preferred_element_type=f32)
        dq[at], dk[to], dv[to] = dqi, dkj, dvj

    def tiles(low, high):
        @pl.loop(low, high)
        def _(t):
            i = jnp.int32(0)
            for n in range(1, blocks):
                i = i + (t >= n * (n + 1) // 2).astype(jnp.int32)
            tile(i, t - i * (i + 1) // 2)

    count = blocks * (blocks + 1) // 2
    tiles(0, 3 * count // 10)
    plane_add(1, 0)
    if bits > 1:
        plane_send(1, 1)
    plane_send(3, 0)
    tiles(3 * count // 10, 8 * count // 10)
    plane_add(2, 0)
    if bits > 1:
        plane_send(2, 1)
    plane_send(4, 0)
    tiles(8 * count // 10, count)

    def turn_back(grad, at):
        cosine = jnp.concatenate([cos_ref[at]] * (width // 128), axis=1)
        sine = jnp.concatenate([sin_ref[at]] * (width // 128), axis=1)
        return grad * cosine + swap_halves(grad, 1.0) * sine

    @pl.loop(0, blocks)
    def _(i):
        at = span(i)
        mixed_ref[at, :width] = (HEAD_DIM ** (-0.5) * turn_back(dq[at], at)).astype(bf16)
        mixed_ref[at, width : 2 * width] = turn_back(dk[at], at).astype(bf16)
        mixed_ref[at, 2 * width :] = dv[at].astype(bf16)

    for stage in range(1, bits):
        for k in (1, 2):
            plane_add(k, stage)
            if stage + 1 < bits:
                plane_send(k, stage + 1)
    ring_send(1)
    plane_add(3, 0)
    if bits > 1:
        plane_send(3, 1)
    ring_add(1)
    ring_send(2)
    plane_add(4, 0)
    if bits > 1:
        plane_send(4, 1)
    for stage in range(1, bits):
        plane_add(3, stage)
        if stage + 1 < bits:
            plane_send(3, stage + 1)
    ring_add(2)
    ring_send(3)
    for stage in range(1, bits):
        plane_add(4, stage)
        if stage + 1 < bits:
            plane_send(4, stage + 1)
    ring_add(3)
    core_send(0)
    own = [
        pltpu.make_async_copy(
            passing[a].at[2], results[a].at[(core,) + tuple(place)], local.at[a]
        )
        for a in range(3)
    ]
    gather_send(0)
    for copy in own:
        copy.start()
    for copy in own:
        copy.wait()
    for stage in range(bits):
        for a in range(3):
            copies.arrived(("gather", a, stage))
        if stage + 1 < bits:
            gather_send(stage + 1)
        core_send(stage + 1)
    for stage in range(bits + 1):
        for a in range(3):
            copies.arrived(("core", a, stage))
    copies.drain()


def attend_and_sum(q, k, v, o, do, lse, cosine, sine, up, out, down, groups, rows=BLOCK):
    length, width = q.shape
    bits = len(groups)
    terms = (up, out, down)
    vmem = pl.BlockSpec(memory_space=pltpu.VMEM)
    anywhere = pl.BlockSpec(memory_space=pl.ANY)
    scratch = [pltpu.VMEM((length, width), f32)] * 3 + [pltpu.VMEM((8, length), f32)]
    for stage in range(bits):
        for term in terms:
            kept = (2,) * (bits - 1 - stage)
            scratch.append(pltpu.VMEM((4,) + kept + term.shape[-2:], bf16))
    for term in terms:
        scratch.append(pltpu.VMEM((3,) + term.shape[-2:], bf16))
    n = 3 * (4 * bits + 3 + bits + bits + 1)
    scratch += [pltpu.SemaphoreType.DMA((n,)), pltpu.SemaphoreType.DMA((n,))]
    scratch += [pltpu.SemaphoreType.DMA((3,))]
    return pl.pallas_call(
        functools.partial(sums_kernel, groups=groups, rows=rows),
        out_shape=(jax.ShapeDtypeStruct((length, 3 * width), bf16),)
        + tuple(jax.ShapeDtypeStruct((2,) + term.shape[1:], bf16) for term in terms),
        in_specs=[vmem] * 11,
        out_specs=(vmem,) + (anywhere,) * 3,
        scratch_shapes=scratch,
        compiler_params=pltpu.CompilerParams(
            vmem_limit_bytes=60 * 2**20, collective_id=1, has_side_effects=True
        ),
        cost_estimate=pl.CostEstimate(
            flops=100_000_000_000, bytes_accessed=32 * 2**20, transcendentals=0
        ),
    )(q, k, v, o, do, lse, cosine, sine, up, out, down)

def exclusive(a, b):
    return a + b - 2 * a * b


def forward_branch(last, heads, rows, q_ref, k_ref, v_ref, o_ref, lse_ref):
    width = q_ref.shape[1]
    n = (last + 1) * rows
    block = pl.ds(last * rows, rows)
    acc = jnp.zeros((rows, width), f32)
    logs = jnp.zeros((rows, width), f32)
    for h in range(heads):
        mine = head_lanes((rows, width), h)
        qm = jnp.where(mine, q_ref[block], jnp.zeros((), bf16))
        s = lax.dot_general(qm, k_ref[:n], NT, preferred_element_type=f32)
        row = lax.broadcasted_iota(jnp.int32, (rows, rows), 0)
        column = lax.broadcasted_iota(jnp.int32, (rows, rows), 1)
        tail = jnp.where(column <= row, s[:, n - rows :], -1e30)
        top = jnp.max(tail, axis=1, keepdims=True)
        if last:
            top = jnp.maximum(top, jnp.max(s[:, : n - rows], axis=1, keepdims=True))
        top = top * LOG2E
        vm = jnp.where(head_lanes((n, width), h), v_ref[:n], jnp.ones((), bf16))
        low = jnp.exp2(tail * LOG2E - top).astype(bf16)
        out = lax.dot_general(low, vm[n - rows :], NN, preferred_element_type=f32)
        if last:
            low = jnp.exp2(s[:, : n - rows] * LOG2E - top).astype(bf16)
            out = out + lax.dot_general(low, vm[: n - rows], NN, preferred_element_type=f32)
        total = pltpu.roll(out, HEAD_DIM, 1)
        acc = jnp.where(mine, out / total, acc)
        logs = jnp.where(mine, top + jnp.log2(total), logs)
    o_ref[block] = acc.astype(bf16)
    lane = lax.broadcasted_iota(jnp.int32, (8, width), 1)
    pick = (lane == HEAD_DIM * lax.broadcasted_iota(jnp.int32, (8, width), 0)).astype(f32)
    lse_ref[:, block] = lax.dot_general(
        pick, logs, NT, precision=lax.Precision.HIGHEST, preferred_element_type=f32
    )


def front_kernel(*refs, groups, chunks):
    (
        tok_ref, cot_ref, wq_ref, up_ref, out_ref, down_ref, gain_ref, shift_ref, cos_ref, sin_ref,
        q_ref, k_ref, v_ref, whole_ref, o_ref, lse_ref,
        heads_ref, tok_home, cot_home, w_home, up_all, out_all, down_all,
        row, w_att, send, recv, local, head_send, head_recv,
    ) = refs
    bits = len(groups)
    part = tok_ref.shape[0]
    depth = tok_ref.shape[1]
    width = q_ref.shape[1]
    heads = width // HEAD_DIM
    core, half, near = lax.axis_index("b"), lax.axis_index("h"), lax.axis_index("l")
    group = [lax.axis_index(axis) for axis in groups]
    layer = 2 * half + near
    place = 2 * core + near
    stays = core == half
    moves = core != half
    partner = {"b": half, "h": core}
    copies = Copies(send, recv)
    locals_made, here = [], []

    def copy_here(source, target):
        copy = pltpu.make_async_copy(source, target, local.at[len(locals_made)])
        locals_made.append(copy)
        here.append(copy)
        copy.start()

    barrier = pltpu.get_barrier_semaphore()
    friends = [flip(axis) for axis in groups + ("b",)] + [next_layer(1), next_layer(3)]
    friends += [flip("l"), {"b": 1 - core, "l": 1 - near}]
    for friend in friends:
        pl.semaphore_signal(barrier, inc=1, device_id=friend, device_id_type=MESH)

    @pl.when(moves)
    def _():
        pl.semaphore_signal(barrier, inc=1, device_id=partner, device_id_type=MESH)
        pl.semaphore_wait(barrier, len(friends) + 1)

    @pl.when(stays)
    def _():
        pl.semaphore_wait(barrier, len(friends))

    size = part // chunks

    def piece(c):
        return pl.ds(c * size, size)

    own = [
        pltpu.make_async_copy(tok_ref.at[piece(c)], row.at[place, piece(c)], local.at[c])
        for c in range(chunks)
    ]
    locals_made.extend(own)
    turned = [("turn", c) for c in range(chunks)]
    for c in range(chunks):
        copies.plan(
            turned[c],
            lambda c=c: (tok_ref.at[piece(c)], row.at[layer, piece(c)], partner),
        )
    w_here = pltpu.make_async_copy(wq_ref, w_att, local.at[len(locals_made)])
    locals_made.append(w_here)
    copies.plan("wturn", lambda: (wq_ref.at[tuple(group)], w_att.at[tuple(group)], partner))
    cot_here = pltpu.make_async_copy(cot_ref, cot_home, local.at[len(locals_made)])
    locals_made.append(cot_here)
    copies.plan("cot", lambda: (cot_ref, cot_home, partner))

    @pl.when(moves)
    def _():
        for c in range(chunks):
            copies.start(turned[c])
        copies.start("wturn")

    @pl.when(stays)
    def _():
        for c in range(chunks):
            own[c].start()
        w_here.start()

    weights = (up_ref, out_ref, down_ref)
    orders = [tuple(range(bits)), tuple(range(bits)), tuple(reversed(range(bits)))]
    slab = up_ref.shape[-1] // 2

    def slot(a, shard, at):
        if a == 0:
            return up_all.at[at + (slice(None), pl.ds(pl.multiple_of(shard * slab, slab), slab))]
        if a == 1:
            return out_all.at[(shard, core) + at]
        return down_all.at[(shard,) + at]

    def held(a, at):
        if a == 0:
            return up_ref.at[at + (slice(None), pl.ds(pl.multiple_of(core * slab, slab), slab))]
        return weights[a].at[(core,) + at]

    def shard(k):
        return lax.rem(layer + 4 - k, 4)

    def ring_send(step):
        for a in range(3):

            def build(a=a):
                at = tuple(group)
                spot = slot(a, shard(step - 1), at)
                return (held(a, at) if step == 1 else spot, spot, next_layer(1))

            copies.start(("ring", a, step), build)

    def ring_wait(step):
        for a in range(3):
            copies.arrived(("ring", a, step))

    def plane_send(k, stage):
        for a in range(3):

            def build(a=a):
                order = orders[a]
                at = tuple(
                    group[axis] if order.index(axis) >= stage else slice(None)
                    for axis in range(bits)
                )
                spot = slot(a, shard(k), at)
                return (spot, spot, flip(groups[order[stage]]))

            copies.start(("plane", a, k, stage), build)

    def plane_wait(k, stage):
        for a in range(3):
            copies.arrived(("plane", a, k, stage))

    def core_send(k):
        def build():
            spot = slot(1, shard(k), (slice(None),) * bits)
            return (spot, spot, flip("b"))

        copies.start(("core", k), build)

    for a in range(3):
        everything = (slice(None),) * bits
        if a == 1:
            copy_here(out_ref, out_all.at[layer])
        else:
            copy_here(held(a, everything), slot(a, layer, everything))

    for c in range(chunks):
        pl.when(moves)(functools.partial(copies.arrived, turned[c]))
        pl.when(stays)(own[c].wait)
        for name, axis in (("near", "l"), ("core own", "b")):
            copies.start(
                (name, c),
                lambda c=c, axis=axis: (
                    row.at[place, piece(c)],
                    row.at[place, piece(c)],
                    flip(axis),
                ),
            )
    copy_here(row.at[place], tok_home)

    @pl.when(stays)
    def _():
        w_here.wait()

    parts = [pl.ds(i * (w_att.shape[-2] // 2), w_att.shape[-2] // 2) for i in range(2)]
    w_orders = [orders[0], orders[2]]
    for stage in range(bits):
        for i in range(2):

            def build(stage=stage, i=i):
                order = w_orders[i]
                at = tuple(
                    group[axis] if order.index(axis) >= stage else slice(None)
                    for axis in range(bits)
                )
                spot = w_att.at[at + (parts[i],)]
                return (spot, spot, flip(groups[order[stage]]))

            copies.plan(("w", stage, i), build)

    @pl.when(moves)
    def _():
        copies.arrived("wturn")
        for stage in range(bits):
            for i in range(2):
                copies.start(("w", stage, i))
            for i in range(2):
                copies.arrived(("w", stage, i))

    copy_here(w_att, w_home)
    near_block = 2 * core + 1 - near

    def pass_on():
        for c in range(chunks):
            copies.arrived(("near", c))
            copies.start(
                ("core near", c),
                lambda c=c: (row.at[near_block, piece(c)], row.at[near_block, piece(c)], flip("b")),
            )
        ring_send(1)

    def wait_all(name):
        def run():
            for c in range(chunks):
                copies.arrived((name, c))

        return run

    @pl.loop(0, 4)
    def _(r):
        far_core, far_near = lax.rem(r, 2), r // 2
        block = 2 * exclusive(core, far_core) + exclusive(near, far_near)
        pl.when(r == 1)(wait_all("core own"))
        pl.when(r == 2)(pass_on)
        pl.when(r == 3)(wait_all("core near"))

        @pl.loop(0, 2)
        def _(c):
            rows = part // 2
            inside = pl.ds(pl.multiple_of(c * rows, rows), rows)
            at = pl.ds(pl.multiple_of(block * part + c * rows, rows), rows)
            value = row[block, inside].astype(f32)
            center = value - jnp.mean(value, axis=1, keepdims=True)
            inverse = lax.rsqrt(jnp.mean(center * center, axis=1, keepdims=True) + EPS)
            normed = (center * inverse * gain_ref[...] + shift_ref[...]).astype(bf16)
            whole_ref[at] = normed
            w = w_att[...].reshape(depth, 3 * width)
            mixed = jnp.dot(normed, w, preferred_element_type=f32)
            cosine = jnp.concatenate([cos_ref[at]] * (width // 128), axis=1)
            sine = jnp.concatenate([sin_ref[at]] * (width // 128), axis=1)
            query, key = mixed[:, :width], mixed[:, width : 2 * width]
            query = HEAD_DIM ** (-0.5) * (query * cosine + swap_halves(query, -1.0) * sine)
            q_ref[at] = query.astype(bf16)
            k_ref[at] = (key * cosine + swap_halves(key, -1.0) * sine).astype(bf16)
            v_ref[at] = mixed[:, 2 * width :].astype(bf16)

    def head_copy(mask):
        far_core, far_near = mask // 2, lax.rem(mask, 2)
        to_core, to_near = exclusive(core, far_core), exclusive(near, far_near)
        block = 2 * to_core + to_near
        rows = pl.ds(pl.multiple_of(block * part, part), part)
        columns = pl.ds(pl.multiple_of(place * width, width), width)
        return pltpu.make_async_remote_copy(
            src_ref=o_ref.at[rows],
            dst_ref=heads_ref.at[:, columns],
            send_sem=head_send.at[mask],
            recv_sem=head_recv.at[mask],
            device_id={"b": to_core, "l": to_near},
            device_id_type=MESH,
        )

    def forward_weights():
        ring_wait(1)
        ring_send(2)
        plane_send(1, 0)

    @pl.loop(0, 4)
    def _(r):
        far_core, far_near = 1 - lax.rem(r, 2), 1 - r // 2
        mask = 2 * far_core + far_near
        block = 2 * exclusive(core, far_core) + exclusive(near, far_near)
        pl.when(r == 2)(forward_weights)
        for i in range(4):
            pl.when(block == i)(
                functools.partial(
                    forward_branch, i, heads, part, q_ref, k_ref, v_ref, o_ref, lse_ref
                )
            )

        @pl.when(r < 3)
        def _():
            head_copy(mask).start()

    copy_here(
        o_ref.at[pl.ds(pl.multiple_of(place * part, part), part)],
        heads_ref.at[:, pl.ds(pl.multiple_of(place * width, width), width)],
    )

    @pl.when(moves)
    def _():
        copies.start("cot")

    @pl.when(stays)
    def _():
        cot_here.start()

    for k in (1, 2, 3):
        if k > 1:
            plane_send(k, 0)
        for stage in range(bits):
            plane_wait(k, stage)
            if stage + 1 < bits:
                plane_send(k, stage + 1)
            if stage == 0 and k < 3:
                ring_wait(k + 1)
                if k < 2:
                    ring_send(k + 2)
        core_send(k)
    for mask in (1, 2, 3):
        copy = head_copy(jnp.int32(mask))
        copy.wait_send()
        copy.wait_recv()
    for k in (1, 2, 3):
        copies.arrived(("core", k))
    sometimes = turned + ["wturn", "cot"] + [("w", s, i) for s in range(bits) for i in range(2)]

    @pl.when(moves)
    def _():
        copies.arrived("cot")
        for name in sometimes:
            copies.sent(name)

    @pl.when(stays)
    def _():
        cot_here.wait()

    for copy in here:
        copy.wait()
    copies.drain(sometimes)


def front(tok, cot, wq, up, out, down, gain, shift, cosine, sine, groups, chunks=2):
    part, depth = tok.shape
    length = 4 * part
    width = wq.shape[-1] // 3
    bits = len(groups)
    vmem = pl.BlockSpec(memory_space=pltpu.VMEM)
    anywhere = pl.BlockSpec(memory_space=pl.ANY)

    def shape(*dims):
        return jax.ShapeDtypeStruct(dims, bf16)

    n = 2 * chunks + 2 + 3 * chunks + 2 * bits + 3 * 3 + 9 * bits + 3 + 4
    return pl.pallas_call(
        functools.partial(front_kernel, groups=groups, chunks=chunks),
        out_shape=(
            shape(length, width),
            shape(length, width),
            shape(length, width),
            shape(length, depth),
            shape(length, width),
            jax.ShapeDtypeStruct((8, length), f32),
            shape(part, depth),
            shape(part, depth),
            shape(part, depth),
            shape(*wq.shape),
            shape(*up.shape[:-1], 2 * up.shape[-1]),
            shape(4, *out.shape),
            shape(4, *down.shape[1:]),
        ),
        in_specs=[anywhere] * 6 + [vmem] * 4,
        out_specs=(vmem,) * 6 + (anywhere,) * 7,
        scratch_shapes=[
            pltpu.VMEM((4, part, depth), bf16),
            pltpu.VMEM(wq.shape, bf16),
            pltpu.SemaphoreType.DMA((n,)),
            pltpu.SemaphoreType.DMA((n,)),
            pltpu.SemaphoreType.DMA((16,)),
            pltpu.SemaphoreType.DMA((4,)),
            pltpu.SemaphoreType.DMA((4,)),
        ],
        compiler_params=pltpu.CompilerParams(
            vmem_limit_bytes=58 * 2**20, collective_id=2, has_side_effects=True
        ),
        cost_estimate=pl.CostEstimate(
            flops=100_000_000_000, bytes_accessed=32 * 2**20, transcendentals=0
        ),
    )(tok, cot, wq, up, out, down, gain, shift, cosine, sine)


def norm_forward(value, gain, shift):
    center = value - jnp.mean(value, axis=-1, keepdims=True)
    inverse = lax.rsqrt(jnp.mean(center * center, axis=-1, keepdims=True) + EPS)
    unit = center * inverse
    return (unit * gain + shift, unit, inverse)


def norm_backward(grad, unit, inverse, gain):
    scaled = grad * gain
    back = inverse * (
        scaled
        - jnp.mean(scaled, axis=-1, keepdims=True)
        - unit * jnp.mean(scaled * unit, axis=-1, keepdims=True)
    )
    return (back, jnp.sum(grad * unit, axis=0), jnp.sum(grad, axis=0))


def rotary_tables(length, width):
    half = HEAD_DIM // 2
    steps = (np.arange(width) % half).astype(np.float32) / np.float32(half)
    freqs = np.float32(10000.0) ** (-steps)
    angles = np.arange(length, dtype=np.float32)[:, None] * freqs[None, :]
    return (jnp.asarray(np.cos(angles)), jnp.asarray(np.sin(angles)))


SWAP = [(0, 1), (1, 0)]


def dot(left, right, dims=NN):
    return lax.dot_general(left, right, dims, preferred_element_type=f32)


def across(value, axis):
    return lax.ppermute(value, axis, SWAP)


def turn(value):
    return lax.ppermute(value, ("b", "h"), [(0, 0), (1, 2), (2, 1), (3, 3)])


def quad_swap(value, far_b, far_l):
    mask = 2 * far_b + far_l
    return lax.ppermute(value, ("b", "l"), [(i, i ^ mask) for i in range(4)])


def gather_axis(value, axis, dim=0):
    other = across(value, axis)
    first = lax.axis_index(axis) == 0
    return jnp.where(
        first, jnp.concatenate([value, other], dim), jnp.concatenate([other, value], dim)
    )


def scatter_axis(value, axis):
    low, high = jnp.split(value.astype(f32), 2, axis=0)
    first = lax.axis_index(axis) == 0
    kept = jnp.where(first, low, high)
    sent = jnp.where(first, high, low).astype(bf16)
    return kept + across(sent, axis).astype(f32)


def on_device(
    tokens,
    w_qkv,
    w_out,
    w_up,
    w_down,
    norm_gains,
    norm_shifts,
    cotangent,
    corpus_ids,
    corpus_weight,
    *,
    groups,
):
    _, part, depth = tokens.shape
    cols = w_qkv.shape[2]
    units = w_up.shape[1]
    core, half, near = lax.axis_index("b"), lax.axis_index("h"), lax.axis_index("l")
    length = 4 * part
    place = 2 * core + near
    group = jnp.int32(0)
    for axis in groups:
        group = 2 * group + lax.axis_index(axis)
    n_groups = 2 ** len(groups)
    stack = ("h", "l")
    cosine, sine = rotary_tables(length, 128)
    gains = [norm_gains[i : i + 1] for i in range(4)]
    shifts = [norm_shifts[i : i + 1] for i in range(4)]

    slots = (2,) * len(groups)
    q, k, v, whole_a, attended, lse, heads, resid_low, cotangent_low, w_attn, up_half, out_whole, down_half = front(
        tokens[0],
        cotangent[0],
        w_qkv.reshape(slots + (depth // n_groups, 3 * cols)),
        w_up.reshape(slots + (depth // n_groups, units)),
        w_out.reshape((2,) + slots + (cols // (2 * n_groups), depth)),
        w_down.reshape((2,) + slots + (units // (2 * n_groups), depth)),
        gains[0],
        shifts[0],
        cosine,
        sine,
        groups,
    )
    up_half = up_half.reshape(depth, 2 * units)
    out_whole = out_whole.reshape(4 * cols, depth)
    down_half = down_half.reshape(2 * units, depth)
    w_attn = w_attn.reshape(depth, 3 * cols)

    def block_of(value, mask):
        return lax.dynamic_slice_in_dim(value, (place ^ mask) * part, part, 0)

    def out_rows(mask):
        return lax.dynamic_slice_in_dim(out_whole, (place ^ mask) * cols, cols, 0)

    branch_a = dot(heads, out_whole)

    resid = resid_low.astype(f32)
    normed_a, unit_0, inverse_0 = norm_forward(resid, gains[0], shifts[0])
    out_a, unit_1, inverse_1 = norm_forward(branch_a, gains[1], shifts[1])
    middle = resid + out_a
    normed_f, unit_2, inverse_2 = norm_forward(middle, gains[2], shifts[2])
    own_f = normed_f.astype(bf16)
    pair_f = jnp.concatenate([own_f, across(own_f, "b")], axis=0)
    hidden = dot(pair_f, up_half)
    cube = 0.7978845608028654 * (hidden + 0.044715 * hidden * hidden * hidden)
    bend = jnp.tanh(cube)
    active = (0.5 * hidden * (1.0 + bend)).astype(bf16)
    slope = 0.5 * (1.0 + bend) + 0.5 * hidden * (1.0 - bend * bend) * 0.7978845608028654 * (
        1.0 + 3 * 0.044715 * hidden * hidden
    )
    slope = slope.astype(bf16)
    branch_f = dot(active[part:], down_half).astype(bf16)
    branch_f = dot(active[:part], down_half) + across(branch_f, "b").astype(f32)
    out_f, unit_3, inverse_3 = norm_forward(branch_f, gains[3], shifts[3])
    output = turn((middle + out_f).astype(bf16))

    picks = (
        corpus_ids[:, None] == jnp.arange(corpus_weight.shape[0], dtype=jnp.int32)[None, :]
    ).astype(f32)
    row_scale = turn(jnp.dot(picks, corpus_weight, precision=lax.Precision.HIGHEST))
    grad_final = cotangent_low.astype(f32) * row_scale[:, None]
    back_3, gain_3, shift_3 = norm_backward(grad_final, unit_3, inverse_3, gains[3])
    own_g = back_3.astype(bf16)
    pair_g = jnp.concatenate([own_g, across(own_g, "b")], axis=0)
    grad_active = dot(pair_g, down_half, NT)
    grad_hidden = (slope.astype(f32) * grad_active).astype(bf16)
    down_grad = dot(active, pair_g, TN).astype(bf16)
    up_grad = dot(grad_hidden, pair_f, TN).astype(bf16)

    grad_f = dot(grad_hidden[part:], up_half, NT).astype(bf16)
    grad_f = dot(grad_hidden[:part], up_half, NT) + across(grad_f, "b").astype(f32)
    back_2, gain_2, shift_2 = norm_backward(grad_f, unit_2, inverse_2, gains[2])
    grad_middle = grad_final + back_2
    back_1, gain_1, shift_1 = norm_backward(grad_middle, unit_1, inverse_1, gains[1])
    grad_a = back_1.astype(bf16)
    grad_attended = jnp.zeros((length, cols), bf16)
    for mask in (3, 1, 2, 0):
        sent = dot(grad_a, out_rows(mask), NT).astype(bf16)
        if mask:
            sent = quad_swap(sent, mask // 2, mask % 2)
        grad_attended = lax.dynamic_update_slice_in_dim(
            grad_attended, sent, (place ^ mask) * part, 0
        )
    out_grad = dot(heads, grad_a, TN).astype(bf16)
    out_grad = out_grad.reshape(4, 2, cols // 2, depth)
    sent = lax.dynamic_index_in_dim(out_grad, 1 - core, 1, False)
    kept = lax.dynamic_index_in_dim(out_grad, core, 1, False)
    out_grad = (kept.astype(f32) + across(sent, "b").astype(f32)).astype(bf16)
    def pieces(value):
        return value.reshape((4,) + slots + (value.size // (4 * n_groups * depth), depth))

    grad_mixed, up_grad, out_grad, down_grad = attend_and_sum(
        q,
        k,
        v,
        attended,
        grad_attended,
        lse,
        cosine,
        sine,
        pieces(up_grad),
        pieces(out_grad),
        pieces(down_grad),
        groups,
    )
    up_grad = up_grad.reshape(units, depth).T.astype(f32)
    out_grad = out_grad.reshape(cols, depth).astype(f32)
    down_grad = down_grad.reshape(units, depth).astype(f32)

    pair = 2 * part
    sent = lax.dynamic_slice_in_dim(grad_mixed, (1 - core) * pair, pair, 0)
    from_core = across(dot(sent, w_attn, NT).astype(bf16), "b")
    sent = dot(block_of(grad_mixed, 1), w_attn, NT)
    sent = sent + lax.dynamic_slice_in_dim(from_core, (1 - near) * part, part, 0).astype(f32)
    from_near = across(sent.astype(bf16), "l")
    grad_normed_a = dot(block_of(grad_mixed, 0), w_attn, NT)
    grad_normed_a = grad_normed_a + lax.dynamic_slice_in_dim(
        from_core, near * part, part, 0
    ).astype(f32)
    grad_normed_a = grad_normed_a + from_near.astype(f32)

    qkv_grad = dot(whole_a, grad_mixed, TN)
    for axis in groups:
        qkv_grad = scatter_axis(qkv_grad, axis)
    qkv_grad = turn(qkv_grad.astype(bf16))
    qkv_grad = scatter_axis(qkv_grad, "b").astype(bf16)
    qkv_grad = gather_axis(qkv_grad, "b")
    for axis in reversed(groups):
        qkv_grad = gather_axis(qkv_grad, axis)
    qkv_grad = qkv_grad.astype(f32).reshape(depth, 3, cols)

    back_0, gain_0, shift_0 = norm_backward(grad_normed_a, unit_0, inverse_0, gains[0])
    input_grad = turn((grad_middle + back_0).astype(bf16)).astype(f32)
    norm_grads = jnp.stack([gain_0, gain_1, gain_2, gain_3, shift_0, shift_1, shift_2, shift_3])
    norm_grads = lax.psum(norm_grads, groups + ("b",) + stack)
    return (
        output[None],
        input_grad[None],
        qkv_grad,
        out_grad,
        up_grad,
        down_grad,
        norm_grads[:4],
        norm_grads[4:],
    )


def solution(mesh):
    rows, parts = mesh.shape["dp"], mesh.shape["mp"]
    bits = (rows // 2).bit_length() - 1
    assert parts == 4 and rows == 2 ** (bits + 1)
    groups = tuple(f"g{i}" for i in range(bits))
    fine = Mesh(mesh.devices.reshape((2,) * (bits + 3)), groups + ("b", "h", "l"))
    dp, mp = groups + ("b",), ("h", "l")
    placed = (
        P(dp, mp, None),
        P(None, None, mp),
        P(mp, None),
        P(None, mp),
        P(mp, None),
        P(),
        P(),
        P(dp, mp, None),
        P(dp),
        P(),
    )
    return jax.shard_map(
        functools.partial(on_device, groups=groups),
        mesh=fine,
        in_specs=placed,
        out_specs=(
            P(dp, mp, None),
            P(dp, mp, None),
            P(None, None, mp),
            P(mp, None),
            P(None, mp),
            P(mp, None),
            P(),
            P(),
        ),
        check_vma=False,
    )
```

```python
import functools

import jax
import jax.numpy as jnp
import numpy as np
from jax import lax
from jax.experimental import pallas as pl
from jax.experimental.pallas import tpu as pltpu
from jax.sharding import Mesh, PartitionSpec as P

HEAD_DIM = 64
BLOCK = 512
EPS = 1e-05
LOG2E = 1.4426950408889634
NN = (((1,), (0,)), ((), ()))
NT = (((1,), (1,)), ((), ()))
TN = (((0,), (0,)), ((), ()))
f32 = jnp.float32
bf16 = jnp.bfloat16


def head_lanes(shape, head):
    return lax.broadcasted_iota(jnp.int32, shape, 1) // HEAD_DIM == head


def swap_halves(value, sign):
    half = HEAD_DIM // 2
    width = value.shape[1]
    first = (lax.broadcasted_iota(jnp.int32, value.shape, 1) // half) % 2 == 0
    return jnp.where(
        first, sign * pltpu.roll(value, width - half, 1), -sign * pltpu.roll(value, half, 1)
    )


MESH = pl.DeviceIdType.MESH


class Copies:
    def __init__(self, send, recv):
        self.send, self.recv, self.made = send, recv, {}

    def describe(self, name):
        n, build = self.made[name]
        source, target, device = build()
        return pltpu.make_async_remote_copy(
            src_ref=source,
            dst_ref=target,
            send_sem=self.send.at[n],
            recv_sem=self.recv.at[n],
            device_id=device,
            device_id_type=MESH,
        )

    def plan(self, name, build):
        self.made[name] = (len(self.made), build)

    def start(self, name, build=None):
        if build is not None:
            self.plan(name, build)
        self.describe(name).start()

    def arrived(self, name):
        self.describe(name).wait_recv()

    def sent(self, name):
        self.describe(name).wait_send()

    def drain(self, but=()):
        for name in self.made:
            if name not in but:
                self.sent(name)


def flip(axis):
    return {axis: 1 - lax.axis_index(axis)}


def next_layer(step):
    at = lax.rem(2 * lax.axis_index("h") + lax.axis_index("l") + step, 4)
    return {"h": at // 2, "l": lax.rem(at, 2)}


def add_into(total, term, rows=16):
    lead, count = total.shape[:-2], total.shape[-2]
    step = min(rows, count)

    @pl.loop(0, count // step)
    def _(i):
        at = pl.ds(pl.multiple_of(i * step, step), step)
        for index in np.ndindex(*lead):
            total[index + (at,)] = (
                total[index + (at,)].astype(f32) + term[index + (at,)].astype(f32)
            ).astype(bf16)


def exclusive(a, b):
    return a + b - 2 * a * b


def forward_branch(last, heads, rows, q_ref, k_ref, v_ref, o_ref, lse_ref):
    width = q_ref.shape[1]
    n = (last + 1) * rows
    block = pl.ds(last * rows, rows)
    acc = jnp.zeros((rows, width), f32)
    logs = jnp.zeros((rows, width), f32)
    for h in range(heads):
        mine = head_lanes((rows, width), h)
        qm = jnp.where(mine, q_ref[block], jnp.zeros((), bf16))
        s = lax.dot_general(qm, k_ref[:n], NT, preferred_element_type=f32)
        row = lax.broadcasted_iota(jnp.int32, (rows, rows), 0)
        column = lax.broadcasted_iota(jnp.int32, (rows, rows), 1)
        tail = jnp.where(column <= row, s[:, n - rows :], -1e30)
        top = jnp.max(tail, axis=1, keepdims=True)
        if last:
            top = jnp.maximum(top, jnp.max(s[:, : n - rows], axis=1, keepdims=True))
        top = top * LOG2E
        vm = jnp.where(head_lanes((n, width), h), v_ref[:n], jnp.ones((), bf16))
        low = jnp.exp2(tail * LOG2E - top).astype(bf16)
        out = lax.dot_general(low, vm[n - rows :], NN, preferred_element_type=f32)
        if last:
            low = jnp.exp2(s[:, : n - rows] * LOG2E - top).astype(bf16)
            out = out + lax.dot_general(low, vm[: n - rows], NN, preferred_element_type=f32)
        total = pltpu.roll(out, HEAD_DIM, 1)
        acc = jnp.where(mine, out / total, acc)
        logs = jnp.where(mine, top + jnp.log2(total), logs)
    o_ref[block] = acc.astype(bf16)
    lane = lax.broadcasted_iota(jnp.int32, (8, width), 1)
    pick = (lane == HEAD_DIM * lax.broadcasted_iota(jnp.int32, (8, width), 0)).astype(f32)
    lse_ref[:, block] = lax.dot_general(
        pick, logs, NT, precision=lax.Precision.HIGHEST, preferred_element_type=f32
    )


def front_kernel(*refs, groups, chunks):
    (
        tok_ref, cot_ref, wq_ref, up_ref, out_ref, down_ref, gain_ref, shift_ref, cos_ref, sin_ref,
        q_ref, k_ref, v_ref, whole_ref, o_ref, lse_ref,
        heads_ref, tok_home, cot_home, w_home, up_all, out_all, down_all,
        row, w_att, send, recv, local, head_send, head_recv,
    ) = refs
    bits = len(groups)
    part = tok_ref.shape[0]
    depth = tok_ref.shape[1]
    width = q_ref.shape[1]
    heads = width // HEAD_DIM
    core, half, near = lax.axis_index("b"), lax.axis_index("h"), lax.axis_index("l")
    group = [lax.axis_index(axis) for axis in groups]
    layer = 2 * half + near
    place = 2 * core + near
    stays = core == half
    moves = core != half
    partner = {"b": half, "h": core}
    copies = Copies(send, recv)
    locals_made, here = [], []

    def copy_here(source, target):
        copy = pltpu.make_async_copy(source, target, local.at[len(locals_made)])
        locals_made.append(copy)
        here.append(copy)
        copy.start()

    barrier = pltpu.get_barrier_semaphore()
    friends = [flip(axis) for axis in groups + ("b",)] + [next_layer(1), next_layer(3)]
    friends += [flip("l"), {"b": 1 - core, "l": 1 - near}]
    for friend in friends:
        pl.semaphore_signal(barrier, inc=1, device_id=friend, device_id_type=MESH)

    @pl.when(moves)
    def _():
        pl.semaphore_signal(barrier, inc=1, device_id=partner, device_id_type=MESH)
        pl.semaphore_wait(barrier, len(friends) + 1)

    @pl.when(stays)
    def _():
        pl.semaphore_wait(barrier, len(friends))

    size = part // chunks

    def piece(c):
        return pl.ds(c * size, size)

    own = [
        pltpu.make_async_copy(tok_ref.at[piece(c)], row.at[place, piece(c)], local.at[c])
        for c in range(chunks)
    ]
    locals_made.extend(own)
    turned = [("turn", c) for c in range(chunks)]
    for c in range(chunks):
        copies.plan(
            turned[c],
            lambda c=c: (tok_ref.at[piece(c)], row.at[layer, piece(c)], partner),
        )
    w_here = pltpu.make_async_copy(wq_ref, w_att, local.at[len(locals_made)])
    locals_made.append(w_here)
    copies.plan("wturn", lambda: (wq_ref.at[tuple(group)], w_att.at[tuple(group)], partner))
    cot_here = pltpu.make_async_copy(cot_ref, cot_home, local.at[len(locals_made)])
    locals_made.append(cot_here)
    copies.plan("cot", lambda: (cot_ref, cot_home, partner))

    @pl.when(moves)
    def _():
        for c in range(chunks):
            copies.start(turned[c])
        copies.start("wturn")

    @pl.when(stays)
    def _():
        for c in range(chunks):
            own[c].start()
        w_here.start()

    weights = (up_ref, out_ref, down_ref)
    orders = [tuple(range(bits)), tuple(range(bits)), tuple(reversed(range(bits)))]
    slab = up_ref.shape[-1] // 2

    def slot(a, shard, at):
        if a == 0:
            return up_all.at[at + (slice(None), pl.ds(pl.multiple_of(shard * slab, slab), slab))]
        if a == 1:
            return out_all.at[(shard, core) + at]
        return down_all.at[(shard,) + at]

    def held(a, at):
        if a == 0:
            return up_ref.at[at + (slice(None), pl.ds(pl.multiple_of(core * slab, slab), slab))]
        return weights[a].at[(core,) + at]

    def shard(k):
        return lax.rem(layer + 4 - k, 4)

    def ring_send(step):
        for a in range(3):

            def build(a=a):
                at = tuple(group)
                spot = slot(a, shard(step - 1), at)
                return (held(a, at) if step == 1 else spot, spot, next_layer(1))

            copies.start(("ring", a, step), build)

    def ring_wait(step):
        for a in range(3):
            copies.arrived(("ring", a, step))

    def plane_send(k, stage):
        for a in range(3):

            def build(a=a):
                order = orders[a]
                at = tuple(
                    group[axis] if order.index(axis) >= stage else slice(None)
                    for axis in range(bits)
                )
                spot = slot(a, shard(k), at)
                return (spot, spot, flip(groups[order[stage]]))

            copies.start(("plane", a, k, stage), build)

    def plane_wait(k, stage):
        for a in range(3):
            copies.arrived(("plane", a, k, stage))

    def core_send(k):
        def build():
            spot = slot(1, shard(k), (slice(None),) * bits)
            return (spot, spot, flip("b"))

        copies.start(("core", k), build)

    for a in range(3):
        everything = (slice(None),) * bits
        if a == 1:
            copy_here(out_ref, out_all.at[layer])
        else:
            copy_here(held(a, everything), slot(a, layer, everything))

    for c in range(chunks):
        pl.when(moves)(functools.partial(copies.arrived, turned[c]))
        pl.when(stays)(own[c].wait)
        for name, axis in (("near", "l"), ("core own", "b")):
            copies.start(
                (name, c),
                lambda c=c, axis=axis: (
                    row.at[place, piece(c)],
                    row.at[place, piece(c)],
                    flip(axis),
                ),
            )
    copy_here(row.at[place], tok_home)

    @pl.when(stays)
    def _():
        w_here.wait()

    parts = [pl.ds(i * (w_att.shape[-2] // 2), w_att.shape[-2] // 2) for i in range(2)]
    w_orders = [orders[0], orders[2]]
    for stage in range(bits):
        for i in range(2):

            def build(stage=stage, i=i):
                order = w_orders[i]
                at = tuple(
                    group[axis] if order.index(axis) >= stage else slice(None)
                    for axis in range(bits)
                )
                spot = w_att.at[at + (parts[i],)]
                return (spot, spot, flip(groups[order[stage]]))

            copies.plan(("w", stage, i), build)

    @pl.when(moves)
    def _():
        copies.arrived("wturn")
        for stage in range(bits):
            for i in range(2):
                copies.start(("w", stage, i))
            for i in range(2):
                copies.arrived(("w", stage, i))

    copy_here(w_att, w_home)
    near_block = 2 * core + 1 - near

    def pass_on():
        for c in range(chunks):
            copies.arrived(("near", c))
            copies.start(
                ("core near", c),
                lambda c=c: (row.at[near_block, piece(c)], row.at[near_block, piece(c)], flip("b")),
            )
        ring_send(1)

    def wait_all(name):
        def run():
            for c in range(chunks):
                copies.arrived((name, c))

        return run

    @pl.loop(0, 4)
    def _(r):
        far_core, far_near = lax.rem(r, 2), r // 2
        block = 2 * exclusive(core, far_core) + exclusive(near, far_near)
        pl.when(r == 1)(wait_all("core own"))
        pl.when(r == 2)(pass_on)
        pl.when(r == 3)(wait_all("core near"))

        @pl.loop(0, 2)
        def _(c):
            rows = part // 2
            inside = pl.ds(pl.multiple_of(c * rows, rows), rows)
            at = pl.ds(pl.multiple_of(block * part + c * rows, rows), rows)
            value = row[block, inside].astype(f32)
            center = value - jnp.mean(value, axis=1, keepdims=True)
            inverse = lax.rsqrt(jnp.mean(center * center, axis=1, keepdims=True) + EPS)
            normed = (center * inverse * gain_ref[...] + shift_ref[...]).astype(bf16)
            whole_ref[at] = normed
            w = w_att[...].reshape(depth, 3 * width)
            mixed = jnp.dot(normed, w, preferred_element_type=f32)
            cosine = jnp.concatenate([cos_ref[at]] * (width // 128), axis=1)
            sine = jnp.concatenate([sin_ref[at]] * (width // 128), axis=1)
            query, key = mixed[:, :width], mixed[:, width : 2 * width]
            query = HEAD_DIM ** (-0.5) * (query * cosine + swap_halves(query, -1.0) * sine)
            q_ref[at] = query.astype(bf16)
            k_ref[at] = (key * cosine + swap_halves(key, -1.0) * sine).astype(bf16)
            v_ref[at] = mixed[:, 2 * width :].astype(bf16)

    def head_copy(mask):
        far_core, far_near = mask // 2, lax.rem(mask, 2)
        to_core, to_near = exclusive(core, far_core), exclusive(near, far_near)
        block = 2 * to_core + to_near
        rows = pl.ds(pl.multiple_of(block * part, part), part)
        columns = pl.ds(pl.multiple_of(place * width, width), width)
        return pltpu.make_async_remote_copy(
            src_ref=o_ref.at[rows],
            dst_ref=heads_ref.at[:, columns],
            send_sem=head_send.at[mask],
            recv_sem=head_recv.at[mask],
            device_id={"b": to_core, "l": to_near},
            device_id_type=MESH,
        )

    def forward_weights():
        ring_wait(1)
        ring_send(2)
        plane_send(1, 0)

    @pl.loop(0, 4)
    def _(r):
        far_core, far_near = 1 - lax.rem(r, 2), 1 - r // 2
        mask = 2 * far_core + far_near
        block = 2 * exclusive(core, far_core) + exclusive(near, far_near)
        pl.when(r == 2)(forward_weights)
        for i in range(4):
            pl.when(block == i)(
                functools.partial(
                    forward_branch, i, heads, part, q_ref, k_ref, v_ref, o_ref, lse_ref
                )
            )

        @pl.when(r < 3)
        def _():
            head_copy(mask).start()

    copy_here(
        o_ref.at[pl.ds(pl.multiple_of(place * part, part), part)],
        heads_ref.at[:, pl.ds(pl.multiple_of(place * width, width), width)],
    )

    @pl.when(moves)
    def _():
        copies.start("cot")

    @pl.when(stays)
    def _():
        cot_here.start()

    for k in (1, 2, 3):
        if k > 1:
            plane_send(k, 0)
        for stage in range(bits):
            plane_wait(k, stage)
            if stage + 1 < bits:
                plane_send(k, stage + 1)
            if stage == 0 and k < 3:
                ring_wait(k + 1)
                if k < 2:
                    ring_send(k + 2)
        core_send(k)
    for mask in (1, 2, 3):
        copy = head_copy(jnp.int32(mask))
        copy.wait_send()
        copy.wait_recv()
    for k in (1, 2, 3):
        copies.arrived(("core", k))
    sometimes = turned + ["wturn", "cot"] + [("w", s, i) for s in range(bits) for i in range(2)]

    @pl.when(moves)
    def _():
        copies.arrived("cot")
        for name in sometimes:
            copies.sent(name)

    @pl.when(stays)
    def _():
        cot_here.wait()

    for copy in here:
        copy.wait()
    copies.drain(sometimes)


def front(tok, cot, wq, up, out, down, gain, shift, cosine, sine, groups, chunks=2):
    part, depth = tok.shape
    length = 4 * part
    width = wq.shape[-1] // 3
    bits = len(groups)
    vmem = pl.BlockSpec(memory_space=pltpu.VMEM)
    anywhere = pl.BlockSpec(memory_space=pl.ANY)

    def shape(*dims):
        return jax.ShapeDtypeStruct(dims, bf16)

    n = 2 * chunks + 2 + 3 * chunks + 2 * bits + 3 * 3 + 9 * bits + 3 + 4
    return pl.pallas_call(
        functools.partial(front_kernel, groups=groups, chunks=chunks),
        out_shape=(
            shape(length, width),
            shape(length, width),
            shape(length, width),
            shape(length, depth),
            shape(length, width),
            jax.ShapeDtypeStruct((8, length), f32),
            shape(part, depth),
            shape(part, depth),
            shape(part, depth),
            shape(*wq.shape),
            shape(*up.shape[:-1], 2 * up.shape[-1]),
            shape(4, *out.shape),
            shape(4, *down.shape[1:]),
        ),
        in_specs=[anywhere] * 6 + [vmem] * 4,
        out_specs=(vmem,) * 6 + (anywhere,) * 7,
        scratch_shapes=[
            pltpu.VMEM((4, part, depth), bf16),
            pltpu.VMEM(wq.shape, bf16),
            pltpu.SemaphoreType.DMA((n,)),
            pltpu.SemaphoreType.DMA((n,)),
            pltpu.SemaphoreType.DMA((16,)),
            pltpu.SemaphoreType.DMA((4,)),
            pltpu.SemaphoreType.DMA((4,)),
        ],
        compiler_params=pltpu.CompilerParams(
            vmem_limit_bytes=58 * 2**20, collective_id=2, has_side_effects=True
        ),
        cost_estimate=pl.CostEstimate(
            flops=100_000_000_000, bytes_accessed=32 * 2**20, transcendentals=0
        ),
    )(tok, cot, wq, up, out, down, gain, shift, cosine, sine)

def back_kernel(*refs, groups, rows, chunks):
    (
        q_ref, k_ref, v_ref, o_ref, lse_ref, cos_ref, sin_ref, gain_ref, norms_ref,
        da_ref, up_ref, out_ref, down_ref, whole_ref, w_ref, resid_ref, middle_ref,
        norms_out, grad_home, qkv_all, up_all, out_all, down_all,
        do, dq, dk, dv, delta, mixed, whole, w, resid, middle,
        sent, from_core, from_near, grad_x, grad_low, qkv_sum, qkv_core, norm_sum, norm_in,
        *rest,
    ) = refs
    bits = len(groups)
    terms = (up_ref, out_ref, down_ref)
    partial = [[rest[3 * s + a] for s in range(bits)] for a in range(3)]
    rest = rest[3 * bits :]
    passing, staged, rest = rest[:3], rest[3:6], rest[6:]
    qkv_in, (send, recv, local) = rest[:bits], rest[bits:]
    copies = Copies(send, recv)
    group = [lax.axis_index(axis) for axis in groups]
    core, half, near = lax.axis_index("b"), lax.axis_index("h"), lax.axis_index("l")
    layer = 2 * half + near
    place = 2 * core + near
    moves, stays = core != half, core == half
    partner = {"b": half, "h": core}
    orders = [tuple(range(bits)), tuple(range(bits)), tuple(reversed(range(bits)))]
    part, depth = da_ref.shape
    length, width = q_ref.shape
    heads = width // HEAD_DIM
    blocks = length // rows
    slab = up_ref.shape[-1] // 4
    all_local = [0]

    def local_copy(source, target):
        n = all_local[0]
        all_local[0] += 1
        return pltpu.make_async_copy(source, target, local.at[n])

    def columns(which, size):
        return pl.ds(pl.multiple_of(which * size, size), size)

    def shard(k):
        return lax.rem(layer + 4 - k, 4)

    def term(a, k, at):
        if a == 0:
            return up_ref.at[at + (slice(None), columns(shard(k), slab))]
        return terms[a].at[(shard(k),) + at]

    def result(a, at):
        if a == 0:
            return up_all.at[at + (slice(None), columns(core, slab))]
        return (None, out_all, down_all)[a].at[(core,) + at]

    def split(order, stage, side):
        at = []
        for axis in range(bits):
            when = order.index(axis)
            if when == stage:
                at.append(group[axis] if side == 0 else 1 - group[axis])
            elif when > stage:
                at.append(slice(None))
        return tuple(at)

    def source(a, k, stage, side):
        at = split(orders[a], stage, side)
        if stage == 0:
            return term(a, k, at) if side else staged[a].at[k % 2]
        return partial[a][stage - 1].at[(k % 4,) + at]

    loads = {}

    def plane_send(k, stage):
        for a in range(3):
            copies.start(
                ("plane", a, k, stage),
                lambda a=a: (
                    source(a, k, stage, 1),
                    partial[a][stage].at[k % 4],
                    flip(groups[orders[a][stage]]),
                ),
            )
            if stage == 0:
                loads[a, k] = local_copy(term(a, k, split(orders[a], 0, 0)), staged[a].at[k % 2])
                loads[a, k].start()

    def plane_add(k, stage):
        for a in range(3):
            copies.arrived(("plane", a, k, stage))
            if stage == 0:
                loads[a, k].wait()
            add_into(partial[a][stage].at[k % 4], source(a, k, stage, 0))

    def plane_step(k, stage):
        plane_add(k, stage)
        if stage + 1 < bits:
            plane_send(k, stage + 1)

    def ring_send(step):
        for a in range(3):
            held = partial[a][bits - 1].at[1] if step == 1 else passing[a].at[step - 2]
            target = passing[a].at[step - 1]
            copies.start(
                ("ring", a, step), lambda held=held, target=target: (held, target, next_layer(1))
            )

    def ring_add(step):
        for a in range(3):
            copies.arrived(("ring", a, step))
            add_into(passing[a].at[step - 1], partial[a][bits - 1].at[(step + 1) % 4])

    def gather_send(stage):
        for a in range(3):
            order = orders[a]
            at = tuple(
                group[axis] if order.index(axis) >= stage else slice(None) for axis in range(bits)
            )
            held = passing[a].at[2] if stage == 0 else result(a, at)
            spot, axis = result(a, at), groups[order[stage]]
            copies.start(
                ("gather", a, stage),
                lambda held=held, spot=spot, axis=axis: (held, spot, flip(axis)),
            )

    def brought(order, stage):
        at = []
        for axis in range(bits):
            when = order.index(axis)
            if stage == 0 or when > stage - 1:
                at.append(group[axis])
            elif when == stage - 1:
                at.append(1 - group[axis])
            else:
                at.append(slice(None))
        return tuple(at)

    def core_send(stage):
        for a in range(3):
            spot = result(a, brought(orders[a], stage))
            held = passing[a].at[2] if stage == 0 else spot
            copies.start(("core", a, stage), lambda held=held, spot=spot: (held, spot, flip("b")))

    barrier = pltpu.get_barrier_semaphore()
    friends = [flip(axis) for axis in groups + ("b", "h", "l")] + [next_layer(1), next_layer(3)]
    friends += [{"b": 1 - core, "l": 1 - near}]
    for friend in friends:
        pl.semaphore_signal(barrier, inc=1, device_id=friend, device_id_type=MESH)

    @pl.when(moves)
    def _():
        pl.semaphore_signal(barrier, inc=1, device_id=partner, device_id_type=MESH)
        pl.semaphore_wait(barrier, len(friends) + 1)

    @pl.when(stays)
    def _():
        pl.semaphore_wait(barrier, len(friends))

    for mask in (3, 1, 2):
        to_core, to_near = exclusive(core, mask // 2), exclusive(near, mask % 2)

        def build(to_core=to_core, to_near=to_near):
            return (
                da_ref.at[:, columns(2 * to_core + to_near, width)],
                do.at[columns(place, part)],
                {"b": to_core, "l": to_near},
            )

        copies.start(("heads", mask), build)
    own_heads = local_copy(da_ref.at[:, columns(place, width)], do.at[columns(place, part)])
    own_heads.start()
    for k in (1, 2):
        plane_send(k, 0)
    early = [
        local_copy(whole_ref, whole),
        local_copy(w_ref, w),
        local_copy(resid_ref, resid),
        local_copy(middle_ref, middle),
    ]
    for copy in early:
        copy.start()
    for total in (dq, dk, dv):
        total[...] = jnp.zeros_like(total)
    own_heads.wait()
    for mask in (2, 1, 3):
        copies.arrived(("heads", mask))

    lane_head = lax.broadcasted_iota(jnp.int32, (8, width), 1) // HEAD_DIM
    marks = (lane_head == lax.broadcasted_iota(jnp.int32, (8, width), 0)).astype(f32)

    def span(i):
        return pl.ds(pl.multiple_of(i * rows, rows), rows)

    @pl.loop(0, blocks)
    def _(i):
        product = do[span(i)].astype(f32) * o_ref[span(i)].astype(f32)
        delta[:, span(i)] = lax.dot_general(
            marks, product, NT, precision=lax.Precision.HIGHEST, preferred_element_type=f32
        )

    def tile(i, j):
        at, to = span(i), span(j)
        keys, values = k_ref[to], v_ref[to]
        queries, grads = q_ref[at], do[at]
        dkj, dvj, dqi = dk[to], dv[to], dq[at]
        zero = jnp.zeros((), bf16)
        key = j * rows + lax.broadcasted_iota(jnp.int32, (rows, rows), 0)
        query = i * rows + lax.broadcasted_iota(jnp.int32, (rows, rows), 1)
        allowed = key <= query
        for h in range(heads):
            mine = head_lanes((rows, width), h)
            qm = jnp.where(mine, queries, zero)
            dom = jnp.where(mine, grads, zero)
            km = jnp.where(mine, keys, zero)
            st = lax.dot_general(keys, qm, NT, preferred_element_type=f32)
            pt = jnp.where(allowed, jnp.exp2(st * LOG2E - lse_ref[h : h + 1, at]), 0.0)
            dpt = lax.dot_general(values, dom, NT, preferred_element_type=f32)
            dst = (pt * (dpt - delta[h : h + 1, at])).astype(bf16)
            dvj = dvj + jnp.dot(pt.astype(bf16), dom, preferred_element_type=f32)
            dkj = dkj + jnp.dot(dst, qm, preferred_element_type=f32)
            dqi = dqi + lax.dot_general(dst, km, TN, preferred_element_type=f32)
        dq[at], dk[to], dv[to] = dqi, dkj, dvj

    count = blocks * (blocks + 1) // 2

    def first_sums():
        plane_step(1, 0)
        plane_send(3, 0)

    def second_sums():
        plane_step(2, 0)
        plane_send(4, 0)

    plans = {3 * count // 10: first_sums, 7 * count // 10: second_sums}

    def tiles(low, high):
        @pl.loop(low, high)
        def _(t):
            i = jnp.int32(0)
            for n in range(1, blocks):
                i = i + (t >= n * (n + 1) // 2).astype(jnp.int32)
            tile(i, t - i * (i + 1) // 2)

    low = 0
    for when, step in plans.items():
        tiles(low, when)
        step()
        low = when
    tiles(low, count)

    def turn_back(grad, at):
        cosine = jnp.concatenate([cos_ref[at]] * (width // 128), axis=1)
        sine = jnp.concatenate([sin_ref[at]] * (width // 128), axis=1)
        return grad * cosine + swap_halves(grad, 1.0) * sine

    @pl.loop(0, blocks)
    def _(i):
        at = span(i)
        mixed[at, :width] = (HEAD_DIM ** (-0.5) * turn_back(dq[at], at)).astype(bf16)
        mixed[at, width : 2 * width] = turn_back(dk[at], at).astype(bf16)
        mixed[at, 2 * width :] = dv[at].astype(bf16)

    for copy in early:
        copy.wait()
    size = part // chunks

    def input_part(block, c):
        at = pl.ds(pl.multiple_of(block * part + c * size, size), size)
        return lax.dot_general(
            mixed[at], w[...].reshape(depth, 3 * width), NT, preferred_element_type=f32
        )

    def inside(c):
        return pl.ds(pl.multiple_of(c * size, size), size)

    for slot in range(2):
        block = 2 * (1 - core) + (1 - near if slot == 0 else near)

        @pl.loop(0, chunks)
        def _(c):
            sent[slot, inside(c)] = input_part(block, c).astype(bf16)

        copies.start(
            ("x core", slot),
            lambda slot=slot: (sent.at[slot], from_core.at[slot], flip("b")),
        )
    for stage in range(1, bits):
        plane_step(1, stage)
    ring_send(1)
    copies.arrived(("x core", 0))
    for c in range(chunks):
        total = input_part(2 * core + 1 - near, c) + from_core[0, inside(c)].astype(f32)
        sent[2, inside(c)] = total.astype(bf16)
        copies.start(
            ("x near", c),
            lambda c=c: (sent.at[2, inside(c)], from_near.at[inside(c)], flip("l")),
        )
    plane_step(3, 0)
    copies.arrived(("x core", 1))

    @pl.loop(0, chunks)
    def _(c):
        grad_x[inside(c)] = input_part(place, c) + from_core[1, inside(c)].astype(f32)

    quarter = depth // 2**bits
    side = quarter // 2
    for index in np.ndindex(*(2,) * bits):
        first = sum(bit << (bits - 1 - axis) for axis, bit in enumerate(index)) * quarter
        block = lax.dot_general(
            whole[:, first : first + quarter], mixed[...], TN, preferred_element_type=f32
        ).astype(bf16)
        for i in range(2):
            qkv_sum[index + (i,)] = block[i * side : (i + 1) * side]
    q_orders = [orders[0], orders[2]]

    def q_slot(i, stage, side):
        order = q_orders[i]
        at = []
        for axis in range(bits):
            when = order.index(axis)
            if when < stage:
                at.append(group[axis])
            elif when == stage:
                at.append(group[axis] if side == 0 else 1 - group[axis])
            else:
                at.append(slice(None))
        return qkv_sum.at[tuple(at) + (i,)]

    def q_send(stage):
        for i in range(2):
            copies.start(
                ("q", i, stage),
                lambda i=i: (
                    q_slot(i, stage, 1),
                    qkv_in[stage].at[i],
                    flip(groups[q_orders[i][stage]]),
                ),
            )

    def q_add(stage):
        for i in range(2):
            copies.arrived(("q", i, stage))
            add_into(q_slot(i, stage, 0), qkv_in[stage].at[i])

    q_send(0)
    for stage in range(1, bits):
        plane_step(2, stage)
    ring_add(1)
    ring_send(2)
    plane_step(4, 0)

    norm_sum[...] = norms_ref[...]
    fine = min(128, size)
    for c in range(chunks):
        copies.arrived(("x near", c))

        @pl.loop(0, size // fine)
        def _(s):
            at = pl.ds(pl.multiple_of(c * size + s * fine, fine), fine)
            grad = grad_x[at] + from_near[at].astype(f32)
            value = resid[at].astype(f32)
            center = value - jnp.mean(value, axis=1, keepdims=True)
            inverse = lax.rsqrt(jnp.mean(center * center, axis=1, keepdims=True) + EPS)
            unit = center * inverse
            scaled = grad * gain_ref[...]
            back = inverse * (
                scaled
                - jnp.mean(scaled, axis=1, keepdims=True)
                - unit * jnp.mean(scaled * unit, axis=1, keepdims=True)
            )
            grad_low[at] = (middle[at] + back).astype(bf16)
            norm_sum[0:1] += jnp.sum(grad * unit, axis=0, keepdims=True)
            norm_sum[4:5] += jnp.sum(grad, axis=0, keepdims=True)

        copies.plan(
            ("home", c), lambda c=c: (grad_low.at[inside(c)], grad_home.at[inside(c)], partner)
        )
        pl.when(moves)(functools.partial(copies.start, ("home", c)))
    stay = [local_copy(grad_low, grad_home)]
    pl.when(stays)(stay[0].start)

    axes = groups + ("b", "h", "l")

    def norms_send(step):
        copies.start(("norms", step), lambda: (norm_sum, norm_in.at[step], flip(axes[step])))

    def norms_add(step):
        copies.arrived(("norms", step))
        copies.sent(("norms", step))
        norm_sum[...] += norm_in[step]

    norms_send(0)
    q_add(0)
    if bits > 1:
        q_send(1)
    for stage in range(1, bits):
        plane_step(3, stage)
    ring_add(2)
    ring_send(3)
    norms_add(0)
    norms_send(1)
    for stage in range(1, bits):
        q_add(stage)
        if stage + 1 < bits:
            q_send(stage + 1)
    own_q = tuple(group)

    copies.plan("q turn", lambda: (qkv_sum.at[own_q], qkv_core.at[0], partner))
    pl.when(moves)(functools.partial(copies.start, "q turn"))
    norms_add(1)
    norms_send(2)
    for stage in range(1, bits):
        plane_step(4, stage)
    ring_add(3)
    core_send(0)
    own = [local_copy(passing[a].at[2], result(a, tuple(group))) for a in range(3)]
    gather_send(0)
    for copy in own:
        copy.start()
    norms_add(2)
    norms_send(3)

    @pl.when(moves)
    def _():
        copies.arrived("q turn")

    @pl.when(stays)
    def _():
        qkv_core[0] = qkv_sum[own_q]

    copies.start("q core", lambda: (qkv_core.at[0, 1 - core], qkv_core.at[1, 1 - core], flip("b")))
    norms_add(3)
    norms_send(4)
    for copy in own:
        copy.wait()
    copies.arrived("q core")
    add_into(qkv_core.at[1, core], qkv_core.at[0, core])

    def q_spot(at):
        return qkv_all.at[at + (core,)]

    keep_q = local_copy(qkv_core.at[1, core], q_spot(own_q))
    keep_q.start()

    def q_gather(stage):
        at = tuple(group[axis] if axis >= stage else slice(None) for axis in range(bits))
        held = qkv_core.at[1, core] if stage == 0 else q_spot(at)
        copies.start(
            ("q gather", stage), lambda: (held, q_spot(at), flip(groups[stage]))
        )

    def q_core_send(stage):
        spot = q_spot(brought(orders[0], stage))
        held = qkv_core.at[1, core] if stage == 0 else spot
        copies.start(("q both", stage), lambda: (held, spot, flip("b")))

    q_gather(0)
    q_core_send(0)
    keep_q.wait()
    for step in range(4, len(axes)):
        norms_add(step)
        if step + 1 < len(axes):
            norms_send(step + 1)
    for stage in range(bits):
        for a in range(3):
            copies.arrived(("gather", a, stage))
        if stage + 1 < bits:
            gather_send(stage + 1)
        core_send(stage + 1)
        copies.arrived(("q gather", stage))
        if stage + 1 < bits:
            q_gather(stage + 1)
        q_core_send(stage + 1)
    norms_out[...] = norm_sum[...]
    for stage in range(bits + 1):
        for a in range(3):
            copies.arrived(("core", a, stage))
        copies.arrived(("q both", stage))
    sometimes = ["q turn"] + [("home", c) for c in range(chunks)]

    @pl.when(moves)
    def _():
        for c in range(chunks):
            copies.arrived(("home", c))
        for name in sometimes:
            copies.sent(name)

    pl.when(stays)(stay[0].wait)
    copies.drain(sometimes + [("norms", step) for step in range(len(axes))])


def back(
    q, k, v, o, lse, cosine, sine, gain, norms, da, up, out, down, whole, w, resid, middle,
    groups, rows=BLOCK, chunks=2,
):
    length, width = q.shape
    part, depth = da.shape
    bits = len(groups)
    slab = up.shape[-1] // 4
    tails = (up.shape[-2:-1] + (slab,), out.shape[-2:], down.shape[-2:])
    vmem = pl.BlockSpec(memory_space=pltpu.VMEM)
    anywhere = pl.BlockSpec(memory_space=pl.ANY)
    slots = (2,) * bits
    quarter = depth // 2**bits
    q_tail = (quarter // 2, 3 * width)
    scratch = [pltpu.VMEM((length, width), bf16)]
    scratch += [pltpu.VMEM((length, width), f32)] * 3 + [pltpu.VMEM((8, length), f32)]
    scratch += [
        pltpu.VMEM((length, 3 * width), bf16),
        pltpu.VMEM(whole.shape, bf16),
        pltpu.VMEM(w.shape, bf16),
        pltpu.VMEM((part, depth), bf16),
        pltpu.VMEM((part, depth), f32),
        pltpu.VMEM((3, part, depth), bf16),
        pltpu.VMEM((2, part, depth), bf16),
        pltpu.VMEM((part, depth), bf16),
        pltpu.VMEM((part, depth), f32),
        pltpu.VMEM((part, depth), bf16),
        pltpu.VMEM(slots + (2,) + q_tail, bf16),
        pltpu.VMEM((2, 2) + q_tail, bf16),
        pltpu.VMEM((8, depth), f32),
        pltpu.VMEM((bits + 3, 8, depth), f32),
    ]
    for stage in range(bits):
        for tail in tails:
            scratch.append(pltpu.VMEM((4,) + (2,) * (bits - 1 - stage) + tail, bf16))
    scratch += [pltpu.VMEM((3,) + tail, bf16) for tail in tails]
    scratch += [pltpu.VMEM((2,) + (2,) * (bits - 1) + tail, bf16) for tail in tails]
    scratch += [
        pltpu.VMEM((2,) + (2,) * (bits - 1 - stage) + q_tail, bf16) for stage in range(bits)
    ]
    n = 3 + 3 * (4 * bits + 3 + bits + bits + 1)
    n += 2 + chunks + 2 * bits + chunks + (bits + 3) + 2 + bits + bits + 1
    scratch += [pltpu.SemaphoreType.DMA((n,)), pltpu.SemaphoreType.DMA((n,))]
    scratch += [pltpu.SemaphoreType.DMA((1 + 12 + 4 + 1 + 3 + 1,))]
    return pl.pallas_call(
        functools.partial(back_kernel, groups=groups, rows=rows, chunks=chunks),
        out_shape=(
            jax.ShapeDtypeStruct((8, depth), f32),
            jax.ShapeDtypeStruct((part, depth), bf16),
            jax.ShapeDtypeStruct(slots + (2,) + q_tail, bf16),
            jax.ShapeDtypeStruct(slots + (up.shape[-2], 2 * slab), bf16),
            jax.ShapeDtypeStruct((2,) + out.shape[1:], bf16),
            jax.ShapeDtypeStruct((2,) + down.shape[1:], bf16),
        ),
        in_specs=[vmem] * 9 + [anywhere] * 8,
        out_specs=(vmem,) + (anywhere,) * 5,
        scratch_shapes=scratch,
        compiler_params=pltpu.CompilerParams(
            vmem_limit_bytes=63 * 2**20, collective_id=1, has_side_effects=True
        ),
        cost_estimate=pl.CostEstimate(
            flops=100_000_000_000, bytes_accessed=32 * 2**20, transcendentals=0
        ),
    )(q, k, v, o, lse, cosine, sine, gain, norms, da, up, out, down, whole, w, resid, middle)


def norm_forward(value, gain, shift):
    center = value - jnp.mean(value, axis=-1, keepdims=True)
    inverse = lax.rsqrt(jnp.mean(center * center, axis=-1, keepdims=True) + EPS)
    unit = center * inverse
    return (unit * gain + shift, unit, inverse)


def norm_backward(grad, unit, inverse, gain):
    scaled = grad * gain
    back = inverse * (
        scaled
        - jnp.mean(scaled, axis=-1, keepdims=True)
        - unit * jnp.mean(scaled * unit, axis=-1, keepdims=True)
    )
    return (back, jnp.sum(grad * unit, axis=0), jnp.sum(grad, axis=0))


def rotary_tables(length, width):
    half = HEAD_DIM // 2
    steps = (np.arange(width) % half).astype(np.float32) / np.float32(half)
    freqs = np.float32(10000.0) ** (-steps)
    angles = np.arange(length, dtype=np.float32)[:, None] * freqs[None, :]
    return (jnp.asarray(np.cos(angles)), jnp.asarray(np.sin(angles)))


SWAP = [(0, 1), (1, 0)]


def dot(left, right, dims=NN):
    return lax.dot_general(left, right, dims, preferred_element_type=f32)


def across(value, axis):
    return lax.ppermute(value, axis, SWAP)


def turn(value):
    return lax.ppermute(value, ("b", "h"), [(0, 0), (1, 2), (2, 1), (3, 3)])


def on_device(
    tokens,
    w_qkv,
    w_out,
    w_up,
    w_down,
    norm_gains,
    norm_shifts,
    cotangent,
    corpus_ids,
    corpus_weight,
    *,
    groups,
):
    _, part, depth = tokens.shape
    cols = w_qkv.shape[2]
    units = w_up.shape[1]
    core, half, near = lax.axis_index("b"), lax.axis_index("h"), lax.axis_index("l")
    length = 4 * part
    place = 2 * core + near
    group = jnp.int32(0)
    for axis in groups:
        group = 2 * group + lax.axis_index(axis)
    n_groups = 2 ** len(groups)
    stack = ("h", "l")
    cosine, sine = rotary_tables(length, 128)
    gains = [norm_gains[i : i + 1] for i in range(4)]
    shifts = [norm_shifts[i : i + 1] for i in range(4)]

    slots = (2,) * len(groups)
    q, k, v, whole_a, attended, lse, heads, resid_low, cotangent_low, w_attn, up_half, out_whole, down_half = front(
        tokens[0],
        cotangent[0],
        w_qkv.reshape(slots + (depth // n_groups, 3 * cols)),
        w_up.reshape(slots + (depth // n_groups, units)),
        w_out.reshape((2,) + slots + (cols // (2 * n_groups), depth)),
        w_down.reshape((2,) + slots + (units // (2 * n_groups), depth)),
        gains[0],
        shifts[0],
        cosine,
        sine,
        groups,
    )
    up_half = up_half.reshape(depth, 2 * units)
    out_whole = out_whole.reshape(4 * cols, depth)
    down_half = down_half.reshape(2 * units, depth)

    branch_a = dot(heads, out_whole)

    resid = resid_low.astype(f32)
    out_a, unit_1, inverse_1 = norm_forward(branch_a, gains[1], shifts[1])
    middle = resid + out_a
    normed_f, unit_2, inverse_2 = norm_forward(middle, gains[2], shifts[2])
    own_f = normed_f.astype(bf16)
    pair_f = jnp.concatenate([own_f, across(own_f, "b")], axis=0)
    hidden = dot(pair_f, up_half)
    cube = 0.7978845608028654 * (hidden + 0.044715 * hidden * hidden * hidden)
    bend = jnp.tanh(cube)
    active = (0.5 * hidden * (1.0 + bend)).astype(bf16)
    slope = 0.5 * (1.0 + bend) + 0.5 * hidden * (1.0 - bend * bend) * 0.7978845608028654 * (
        1.0 + 3 * 0.044715 * hidden * hidden
    )
    slope = slope.astype(bf16)
    branch_f = dot(active[part:], down_half).astype(bf16)
    branch_f = dot(active[:part], down_half) + across(branch_f, "b").astype(f32)
    out_f, unit_3, inverse_3 = norm_forward(branch_f, gains[3], shifts[3])
    output = turn((middle + out_f).astype(bf16))

    picks = (
        corpus_ids[:, None] == jnp.arange(corpus_weight.shape[0], dtype=jnp.int32)[None, :]
    ).astype(f32)
    row_scale = turn(jnp.dot(picks, corpus_weight, precision=lax.Precision.HIGHEST))
    grad_final = cotangent_low.astype(f32) * row_scale[:, None]
    back_3, gain_3, shift_3 = norm_backward(grad_final, unit_3, inverse_3, gains[3])
    own_g = back_3.astype(bf16)
    pair_g = jnp.concatenate([own_g, across(own_g, "b")], axis=0)
    grad_active = dot(pair_g, down_half, NT)
    grad_hidden = (slope.astype(f32) * grad_active).astype(bf16)
    down_grad = dot(active, pair_g, TN).astype(bf16)
    up_grad = dot(pair_f, grad_hidden, TN).astype(bf16)

    grad_f = dot(grad_hidden[part:], up_half, NT).astype(bf16)
    grad_f = dot(grad_hidden[:part], up_half, NT) + across(grad_f, "b").astype(f32)
    back_2, gain_2, shift_2 = norm_backward(grad_f, unit_2, inverse_2, gains[2])
    grad_middle = grad_final + back_2
    back_1, gain_1, shift_1 = norm_backward(grad_middle, unit_1, inverse_1, gains[1])
    grad_a = back_1.astype(bf16)
    grad_attended = dot(grad_a, out_whole, NT).astype(bf16)
    out_grad = dot(heads, grad_a, TN).astype(bf16)
    out_grad = out_grad.reshape(4, 2, cols // 2, depth)
    sent = lax.dynamic_index_in_dim(out_grad, 1 - core, 1, False)
    kept = lax.dynamic_index_in_dim(out_grad, core, 1, False)
    out_grad = (kept.astype(f32) + across(sent, "b").astype(f32)).astype(bf16)
    def pieces(value):
        return value.reshape((4,) + slots + (value.size // (4 * n_groups * depth), depth))

    none = jnp.zeros_like(gain_1)
    norms = jnp.stack([none, gain_1, gain_2, gain_3, none, shift_1, shift_2, shift_3])
    norm_grads, input_grad, qkv_grad, up_grad, out_grad, down_grad = back(
        q,
        k,
        v,
        attended,
        lse,
        cosine,
        sine,
        gains[0],
        norms,
        grad_attended,
        up_grad.reshape(slots + (depth // n_groups, 2 * units)),
        pieces(out_grad),
        pieces(down_grad),
        whole_a,
        w_attn,
        resid_low,
        grad_middle,
        groups,
    )
    input_grad = input_grad.astype(f32)
    qkv_grad = qkv_grad.reshape(depth, 3, cols).astype(f32)
    up_grad = up_grad.reshape(depth, units).astype(f32)
    out_grad = out_grad.reshape(cols, depth).astype(f32)
    down_grad = down_grad.reshape(units, depth).astype(f32)
    return (
        output[None],
        input_grad[None],
        qkv_grad,
        out_grad,
        up_grad,
        down_grad,
        norm_grads[:4],
        norm_grads[4:],
    )


def solution(mesh):
    rows, parts = mesh.shape["dp"], mesh.shape["mp"]
    bits = (rows // 2).bit_length() - 1
    assert parts == 4 and rows == 2 ** (bits + 1)
    groups = tuple(f"g{i}" for i in range(bits))
    fine = Mesh(mesh.devices.reshape((2,) * (bits + 3)), groups + ("b", "h", "l"))
    dp, mp = groups + ("b",), ("h", "l")
    placed = (
        P(dp, mp, None),
        P(None, None, mp),
        P(mp, None),
        P(None, mp),
        P(mp, None),
        P(),
        P(),
        P(dp, mp, None),
        P(dp),
        P(),
    )
    return jax.shard_map(
        functools.partial(on_device, groups=groups),
        mesh=fine,
        in_specs=placed,
        out_specs=(
            P(dp, mp, None),
            P(dp, mp, None),
            P(None, None, mp),
            P(mp, None),
            P(None, mp),
            P(mp, None),
            P(),
            P(),
        ),
        check_vma=False,
    )
```

```python
import functools

import jax
import jax.numpy as jnp
import numpy as np
from jax import lax
from jax.experimental import pallas as pl
from jax.experimental.pallas import tpu as pltpu
from jax.sharding import Mesh, PartitionSpec as P

HEAD_DIM = 64
BLOCK = 512
EPS = 1e-05
LOG2E = 1.4426950408889634
NN = (((1,), (0,)), ((), ()))
NT = (((1,), (1,)), ((), ()))
TN = (((0,), (0,)), ((), ()))
f32 = jnp.float32
bf16 = jnp.bfloat16


def head_lanes(shape, head):
    return lax.broadcasted_iota(jnp.int32, shape, 1) // HEAD_DIM == head


def swap_halves(value, sign):
    half = HEAD_DIM // 2
    width = value.shape[1]
    first = (lax.broadcasted_iota(jnp.int32, value.shape, 1) // half) % 2 == 0
    return jnp.where(
        first, sign * pltpu.roll(value, width - half, 1), -sign * pltpu.roll(value, half, 1)
    )


MESH = pl.DeviceIdType.MESH
FRONT_PLAN = {
    "own": "ring",
    "near": "one",
    0: "1a",
    1: "two 1b",
    2: "2a three",
    3: "2b 3a",
    "rest": "3b",
}


class Copies:
    def __init__(self, send, recv):
        self.send, self.recv, self.made = send, recv, {}

    def describe(self, name):
        n, build = self.made[name]
        source, target, device = build()
        return pltpu.make_async_remote_copy(
            src_ref=source,
            dst_ref=target,
            send_sem=self.send.at[n],
            recv_sem=self.recv.at[n],
            device_id=device,
            device_id_type=MESH,
        )

    def plan(self, name, build):
        self.made[name] = (len(self.made), build)

    def start(self, name, build=None):
        if build is not None:
            self.plan(name, build)
        self.describe(name).start()

    def arrived(self, name):
        self.describe(name).wait_recv()

    def sent(self, name):
        self.describe(name).wait_send()

    def drain(self, but=()):
        for name in self.made:
            if name not in but:
                self.sent(name)


def flip(axis):
    return {axis: 1 - lax.axis_index(axis)}


def next_layer(step):
    at = lax.rem(2 * lax.axis_index("h") + lax.axis_index("l") + step, 4)
    return {"h": at // 2, "l": lax.rem(at, 2)}


def add_into(total, term, rows=64):
    lead, count = total.shape[:-2], total.shape[-2]
    step = next(n for n in (rows, 32, 16, 8) if count % n == 0)

    @pl.loop(0, count // step)
    def _(i):
        at = pl.ds(pl.multiple_of(i * step, step), step)
        for index in np.ndindex(*lead):
            total[index + (at,)] = (
                total[index + (at,)].astype(f32) + term[index + (at,)].astype(f32)
            ).astype(bf16)


def exclusive(a, b):
    return a + b - 2 * a * b


def forward_branch(last, heads, rows, q_ref, k_ref, v_ref, o_ref, lse_ref):
    width = q_ref.shape[1]
    n = (last + 1) * rows
    block = pl.ds(last * rows, rows)
    acc = jnp.zeros((rows, width), f32)
    logs = jnp.zeros((rows, width), f32)
    for h in range(heads):
        mine = head_lanes((rows, width), h)
        qm = jnp.where(mine, q_ref[block], jnp.zeros((), bf16))
        s = lax.dot_general(qm, k_ref[:n], NT, preferred_element_type=f32)
        row = lax.broadcasted_iota(jnp.int32, (rows, rows), 0)
        column = lax.broadcasted_iota(jnp.int32, (rows, rows), 1)
        tail = jnp.where(column <= row, s[:, n - rows :], -1e30)
        top = jnp.max(tail, axis=1, keepdims=True)
        if last:
            top = jnp.maximum(top, jnp.max(s[:, : n - rows], axis=1, keepdims=True))
        top = top * LOG2E
        vm = jnp.where(head_lanes((n, width), h), v_ref[:n], jnp.ones((), bf16))
        low = jnp.exp2(tail * LOG2E - top).astype(bf16)
        out = lax.dot_general(low, vm[n - rows :], NN, preferred_element_type=f32)
        if last:
            low = jnp.exp2(s[:, : n - rows] * LOG2E - top).astype(bf16)
            out = out + lax.dot_general(low, vm[: n - rows], NN, preferred_element_type=f32)
        total = pltpu.roll(out, HEAD_DIM, 1)
        acc = jnp.where(mine, out / total, acc)
        logs = jnp.where(mine, top + jnp.log2(total), logs)
    o_ref[block] = acc.astype(bf16)
    lane = lax.broadcasted_iota(jnp.int32, (8, width), 1)
    pick = (lane == HEAD_DIM * lax.broadcasted_iota(jnp.int32, (8, width), 0)).astype(f32)
    lse_ref[:, block] = lax.dot_general(
        pick, logs, NT, precision=lax.Precision.HIGHEST, preferred_element_type=f32
    )


def front_kernel(*refs, groups, chunks):
    (
        tok_ref, cot_ref, wq_ref, up_ref, out_ref, down_ref, gain_ref, shift_ref, cos_ref, sin_ref,
        q_ref, k_ref, v_ref, whole_ref, o_ref, lse_ref,
        heads_ref, tok_home, cot_home, w_home, up_all, out_all, down_all,
        row, w_att, bounce_up, bounce_out, bounce_down, bounce_cot,
        send, recv, local, head_send, head_recv,
    ) = refs
    bits = len(groups)
    part = tok_ref.shape[0]
    depth = tok_ref.shape[1]
    width = q_ref.shape[1]
    heads = width // HEAD_DIM
    core, half, near = lax.axis_index("b"), lax.axis_index("h"), lax.axis_index("l")
    group = [lax.axis_index(axis) for axis in groups]
    layer = 2 * half + near
    place = 2 * core + near
    stays = core == half
    moves = core != half
    partner = {"b": half, "h": core}
    copies = Copies(send, recv)
    locals_made, here = [], []

    def copy_here(source, target):
        copy = pltpu.make_async_copy(source, target, local.at[len(locals_made)])
        locals_made.append(copy)
        here.append(copy)
        copy.start()

    barrier = pltpu.get_barrier_semaphore()
    friends = [flip(axis) for axis in groups + ("b",)] + [next_layer(1), next_layer(3)]
    friends += [flip("l"), {"b": 1 - core, "l": 1 - near}]
    for friend in friends:
        pl.semaphore_signal(barrier, inc=1, device_id=friend, device_id_type=MESH)

    @pl.when(moves)
    def _():
        pl.semaphore_signal(barrier, inc=1, device_id=partner, device_id_type=MESH)
        pl.semaphore_wait(barrier, len(friends) + 1)

    @pl.when(stays)
    def _():
        pl.semaphore_wait(barrier, len(friends))

    size = part // chunks

    def piece(c):
        return pl.ds(c * size, size)

    weights = (up_ref, out_ref, down_ref)
    orders = [tuple(range(bits)), tuple(range(bits)), tuple(reversed(range(bits)))]
    slab = up_ref.shape[-1] // 2

    def slot(a, shard, at):
        if a == 0:
            return up_all.at[at + (slice(None), pl.ds(pl.multiple_of(shard * slab, slab), slab))]
        if a == 1:
            return out_all.at[(shard, core) + at]
        return down_all.at[(shard,) + at]

    def held(a, at):
        if a == 0:
            return up_ref.at[at + (slice(None), pl.ds(pl.multiple_of(core * slab, slab), slab))]
        return weights[a].at[(core,) + at]

    def shard(k):
        return lax.rem(layer + 4 - k, 4)

    def ring_send(step):
        for a in range(3):

            def build(a=a):
                at = tuple(group)
                spot = slot(a, shard(step - 1), at)
                return (held(a, at) if step == 1 else spot, spot, next_layer(1))

            copies.start(("ring", a, step), build)

    def ring_wait(step):
        for a in range(3):
            copies.arrived(("ring", a, step))

    def plane_send(k, stage):
        for a in range(3):

            def build(a=a):
                order = orders[a]
                at = tuple(
                    group[axis] if order.index(axis) >= stage else slice(None)
                    for axis in range(bits)
                )
                spot = slot(a, shard(k), at)
                return (spot, spot, flip(groups[order[stage]]))

            copies.start(("plane", a, k, stage), build)

    def plane_wait(k, stage):
        for a in range(3):
            copies.arrived(("plane", a, k, stage))

    def core_send(k):
        def build():
            spot = slot(1, shard(k), (slice(None),) * bits)
            return (spot, spot, flip("b"))

        copies.start(("core", k), build)

    def plane_next(k, stage):
        plane_wait(k, stage)
        if stage + 1 < bits:
            plane_send(k, stage + 1)
        else:
            core_send(k)

    def inner_stages(k):
        for stage in range(1, bits):
            plane_next(k, stage)

    def arrive(k):
        ring_wait(k)
        if k < 3:
            ring_send(k + 1)
        plane_send(k, 0)

    steps = {
        "ring": lambda: ring_send(1),
        "one": lambda: arrive(1),
        "two": lambda: arrive(2),
        "three": lambda: arrive(3),
        "1a": lambda: plane_next(1, 0),
        "1b": lambda: inner_stages(1),
        "2a": lambda: plane_next(2, 0),
        "2b": lambda: inner_stages(2),
        "3a": lambda: plane_next(3, 0),
        "3b": lambda: inner_stages(3),
    }

    def weights_at(point):
        for name in FRONT_PLAN.get(point, "").split():
            steps[name]()

    everything = (slice(None),) * bits
    bounces = [
        (held(0, everything), bounce_up, slot(0, layer, everything)),
        (out_ref, bounce_out, out_all.at[layer]),
        (held(2, everything), bounce_down, slot(2, layer, everything)),
    ]
    inward = []
    for source, buffer, _ in bounces:
        copy = pltpu.make_async_copy(source, buffer, local.at[len(locals_made)])
        locals_made.append(copy)
        inward.append(copy)
        copy.start()

    weights_at("start")
    own = [
        pltpu.make_async_copy(
            tok_ref.at[piece(c)], row.at[place, piece(c)], local.at[len(locals_made) + c]
        )
        for c in range(chunks)
    ]
    locals_made.extend(own)
    turned = [("turn", c) for c in range(chunks)]
    for c in range(chunks):
        copies.plan(
            turned[c],
            lambda c=c: (tok_ref.at[piece(c)], row.at[layer, piece(c)], partner),
        )
    w_here = pltpu.make_async_copy(wq_ref, w_att, local.at[len(locals_made)])
    locals_made.append(w_here)
    copies.plan("wturn", lambda: (wq_ref.at[tuple(group)], w_att.at[tuple(group)], partner))
    cot_in = pltpu.make_async_copy(cot_ref, bounce_cot, local.at[len(locals_made)])
    locals_made.append(cot_in)
    cot_here = pltpu.make_async_copy(bounce_cot, cot_home, local.at[len(locals_made)])
    locals_made.append(cot_here)
    copies.plan("cot", lambda: (cot_ref, cot_home, partner))

    @pl.when(moves)
    def _():
        for c in range(chunks):
            copies.start(turned[c])
        copies.start("wturn")

    @pl.when(stays)
    def _():
        for c in range(chunks):
            own[c].start()
        w_here.start()
        cot_in.start()

    for c in range(chunks):
        pl.when(moves)(functools.partial(copies.arrived, turned[c]))
        pl.when(stays)(own[c].wait)
        for name, axis in (("near", "l"), ("core own", "b")):
            copies.start(
                (name, c),
                lambda c=c, axis=axis: (
                    row.at[place, piece(c)],
                    row.at[place, piece(c)],
                    flip(axis),
                ),
            )
    copy_here(row.at[place], tok_home)
    for copy in inward:
        copy.wait()
    for _, buffer, target in bounces:
        copy_here(buffer, target)
    weights_at("own")

    @pl.when(stays)
    def _():
        w_here.wait()

    parts = [pl.ds(i * (w_att.shape[-2] // 2), w_att.shape[-2] // 2) for i in range(2)]
    w_orders = [orders[0], orders[2]]
    for stage in range(bits):
        for i in range(2):

            def build(stage=stage, i=i):
                order = w_orders[i]
                at = tuple(
                    group[axis] if order.index(axis) >= stage else slice(None)
                    for axis in range(bits)
                )
                spot = w_att.at[at + (parts[i],)]
                return (spot, spot, flip(groups[order[stage]]))

            copies.plan(("w", stage, i), build)

    @pl.when(moves)
    def _():
        copies.arrived("wturn")
        for stage in range(bits):
            for i in range(2):
                copies.start(("w", stage, i))
            for i in range(2):
                copies.arrived(("w", stage, i))

    copy_here(w_att, w_home)
    near_block = 2 * core + 1 - near

    def pass_on():
        for c in range(chunks):
            copies.arrived(("near", c))
            copies.start(
                ("core near", c),
                lambda c=c: (row.at[near_block, piece(c)], row.at[near_block, piece(c)], flip("b")),
            )
        weights_at("near")

    def wait_all(name):
        def run():
            for c in range(chunks):
                copies.arrived((name, c))

        return run

    @pl.loop(0, 4)
    def _(r):
        far_core, far_near = lax.rem(r, 2), r // 2
        block = 2 * exclusive(core, far_core) + exclusive(near, far_near)
        pl.when(r == 1)(wait_all("core own"))
        pl.when(r == 2)(pass_on)
        pl.when(r == 3)(wait_all("core near"))

        @pl.loop(0, 2)
        def _(c):
            rows = part // 2
            inside = pl.ds(pl.multiple_of(c * rows, rows), rows)
            at = pl.ds(pl.multiple_of(block * part + c * rows, rows), rows)
            value = row[block, inside].astype(f32)
            center = value - jnp.mean(value, axis=1, keepdims=True)
            inverse = lax.rsqrt(jnp.mean(center * center, axis=1, keepdims=True) + EPS)
            normed = (center * inverse * gain_ref[...] + shift_ref[...]).astype(bf16)
            whole_ref[at] = normed
            w = w_att[...].reshape(depth, 3 * width)
            mixed = jnp.dot(normed, w, preferred_element_type=f32)
            cosine = jnp.concatenate([cos_ref[at]] * (width // 128), axis=1)
            sine = jnp.concatenate([sin_ref[at]] * (width // 128), axis=1)
            query, key = mixed[:, :width], mixed[:, width : 2 * width]
            query = HEAD_DIM ** (-0.5) * (query * cosine + swap_halves(query, -1.0) * sine)
            q_ref[at] = query.astype(bf16)
            k_ref[at] = (key * cosine + swap_halves(key, -1.0) * sine).astype(bf16)
            v_ref[at] = mixed[:, 2 * width :].astype(bf16)

    def head_copy(mask):
        far_core, far_near = mask // 2, lax.rem(mask, 2)
        to_core, to_near = exclusive(core, far_core), exclusive(near, far_near)
        block = 2 * to_core + to_near
        rows = pl.ds(pl.multiple_of(block * part, part), part)
        columns = pl.ds(pl.multiple_of(place * width, width), width)
        return pltpu.make_async_remote_copy(
            src_ref=o_ref.at[rows],
            dst_ref=heads_ref.at[:, columns],
            send_sem=head_send.at[mask],
            recv_sem=head_recv.at[mask],
            device_id={"b": to_core, "l": to_near},
            device_id_type=MESH,
        )

    @pl.loop(0, 4)
    def _(r):
        far_core, far_near = 1 - lax.rem(r, 2), 1 - r // 2
        mask = 2 * far_core + far_near
        block = 2 * exclusive(core, far_core) + exclusive(near, far_near)
        for n in range(4):
            pl.when(r == n)(functools.partial(weights_at, n))
        for i in range(4):
            pl.when(block == i)(
                functools.partial(
                    forward_branch, i, heads, part, q_ref, k_ref, v_ref, o_ref, lse_ref
                )
            )

        @pl.when(r < 3)
        def _():
            head_copy(mask).start()

    copy_here(
        o_ref.at[pl.ds(pl.multiple_of(place * part, part), part)],
        heads_ref.at[:, pl.ds(pl.multiple_of(place * width, width), width)],
    )

    @pl.when(moves)
    def _():
        copies.start("cot")

    @pl.when(stays)
    def _():
        cot_in.wait()
        cot_here.start()

    weights_at("rest")
    for mask in (1, 2, 3):
        copy = head_copy(jnp.int32(mask))
        copy.wait_send()
        copy.wait_recv()
    for k in (1, 2, 3):
        copies.arrived(("core", k))
    sometimes = turned + ["wturn", "cot"] + [("w", s, i) for s in range(bits) for i in range(2)]

    @pl.when(moves)
    def _():
        copies.arrived("cot")
        for name in sometimes:
            copies.sent(name)

    @pl.when(stays)
    def _():
        cot_here.wait()

    for copy in here:
        copy.wait()
    copies.drain(sometimes)


def front(tok, cot, wq, up, out, down, gain, shift, cosine, sine, groups, chunks=2):
    part, depth = tok.shape
    length = 4 * part
    width = wq.shape[-1] // 3
    bits = len(groups)
    vmem = pl.BlockSpec(memory_space=pltpu.VMEM)
    anywhere = pl.BlockSpec(memory_space=pl.ANY)

    def shape(*dims):
        return jax.ShapeDtypeStruct(dims, bf16)

    n = 2 * chunks + 2 + 3 * chunks + 2 * bits + 3 * 3 + 9 * bits + 3 + 4
    return pl.pallas_call(
        functools.partial(front_kernel, groups=groups, chunks=chunks),
        out_shape=(
            shape(length, width),
            shape(length, width),
            shape(length, width),
            shape(length, depth),
            shape(length, width),
            jax.ShapeDtypeStruct((8, length), f32),
            shape(part, depth),
            shape(part, depth),
            shape(part, depth),
            shape(*wq.shape),
            shape(*up.shape[:-1], 2 * up.shape[-1]),
            shape(4, *out.shape),
            shape(4, *down.shape[1:]),
        ),
        in_specs=[anywhere] * 6 + [vmem] * 4,
        out_specs=(vmem,) * 6 + (anywhere,) * 7,
        scratch_shapes=[
            pltpu.VMEM((4, part, depth), bf16),
            pltpu.VMEM(wq.shape, bf16),
            pltpu.VMEM(up.shape[:-1] + (up.shape[-1] // 2,), bf16),
            pltpu.VMEM(out.shape, bf16),
            pltpu.VMEM(down.shape[1:], bf16),
            pltpu.VMEM((part, depth), bf16),
            pltpu.SemaphoreType.DMA((n,)),
            pltpu.SemaphoreType.DMA((n,)),
            pltpu.SemaphoreType.DMA((32,)),
            pltpu.SemaphoreType.DMA((4,)),
            pltpu.SemaphoreType.DMA((4,)),
        ],
        compiler_params=pltpu.CompilerParams(
            vmem_limit_bytes=58 * 2**20, collective_id=2, has_side_effects=True
        ),
        cost_estimate=pl.CostEstimate(
            flops=100_000_000_000, bytes_accessed=32 * 2**20, transcendentals=0
        ),
    )(tok, cot, wq, up, out, down, gain, shift, cosine, sine)

def back_kernel(*refs, groups, rows, chunks):
    (
        q_ref, k_ref, v_ref, o_ref, lse_ref, cos_ref, sin_ref, gain_ref, norms_ref,
        da_ref, low_ref, inputs_ref, branches_ref, hidden_ref, active_ref, heads_ref, branch_ref,
        whole_ref, w_ref, resid_ref, middle_ref,
        norms_out, grad_home, low_home, qkv_all, up_all, out_all, down_all,
        up_ref, out_ref, down_ref,
        out_part, out_in, up_tile, down_tile, turned,
        do, dq, dk, dv, delta, mixed, whole, w, resid, middle,
        sent, from_core, from_near, grad_x, grad_low, qkv_sum, qkv_core, norm_sum, norm_in,
        *rest,
    ) = refs
    bits = len(groups)
    terms = (up_ref, out_ref, down_ref)
    partial = [[rest[3 * s + a] for s in range(bits)] for a in range(3)]
    rest = rest[3 * bits :]
    passing, staged, rest = rest[:3], rest[3:6], rest[6:]
    qkv_in, (send, recv, local) = rest[:bits], rest[bits:]
    copies = Copies(send, recv)
    group = [lax.axis_index(axis) for axis in groups]
    core, half, near = lax.axis_index("b"), lax.axis_index("h"), lax.axis_index("l")
    layer = 2 * half + near
    place = 2 * core + near
    moves, stays = core != half, core == half
    partner = {"b": half, "h": core}
    orders = [tuple(range(bits)), tuple(range(bits)), tuple(reversed(range(bits)))]
    part, depth = da_ref.shape
    length, width = q_ref.shape
    heads = width // HEAD_DIM
    blocks = length // rows
    slab = up_ref.shape[-1] // 4
    quarter = depth // 2**bits
    all_local = [0]

    def local_copy(source, target):
        n = all_local[0]
        all_local[0] += 1
        return pltpu.make_async_copy(source, target, local.at[n])

    def columns(which, size):
        return pl.ds(pl.multiple_of(which * size, size), size)

    def shard(k):
        return lax.rem(layer + 4 - k, 4)

    def term(a, k, at):
        if a == 0:
            return up_ref.at[at + (slice(None), columns(shard(k), slab))]
        return terms[a].at[(shard(k),) + at]

    def result(a, at):
        if a == 0:
            return up_all.at[at + (slice(None), columns(core, slab))]
        return (None, out_all, down_all)[a].at[(core,) + at]

    def split(order, stage, side):
        at = []
        for axis in range(bits):
            when = order.index(axis)
            if when == stage:
                at.append(group[axis] if side == 0 else 1 - group[axis])
            elif when > stage:
                at.append(slice(None))
        return tuple(at)

    def source(a, k, stage, side):
        at = split(orders[a], stage, side)
        if stage == 0:
            return term(a, k, at) if side else staged[a].at[k % 2]
        return partial[a][stage - 1].at[(k % 4,) + at]

    loads = {}

    def plane_send(k, stage):
        for a in range(3):
            copies.start(
                ("plane", a, k, stage),
                lambda a=a: (
                    source(a, k, stage, 1),
                    partial[a][stage].at[k % 4],
                    flip(groups[orders[a][stage]]),
                ),
            )
            if stage == 0:
                loads[a, k] = local_copy(term(a, k, split(orders[a], 0, 0)), staged[a].at[k % 2])
                loads[a, k].start()

    def plane_add(k, stage):
        for a in range(3):
            copies.arrived(("plane", a, k, stage))
            if stage == 0:
                loads[a, k].wait()
            add_into(partial[a][stage].at[k % 4], source(a, k, stage, 0))

    def plane_step(k, stage):
        plane_add(k, stage)
        if stage + 1 < bits:
            plane_send(k, stage + 1)

    def ring_send(step):
        for a in range(3):
            held = partial[a][bits - 1].at[1] if step == 1 else passing[a].at[step - 2]
            target = passing[a].at[step - 1]
            copies.start(
                ("ring", a, step), lambda held=held, target=target: (held, target, next_layer(1))
            )

    def ring_add(step):
        for a in range(3):
            copies.arrived(("ring", a, step))
            add_into(passing[a].at[step - 1], partial[a][bits - 1].at[(step + 1) % 4])

    def gather_send(stage):
        for a in range(3):
            order = orders[a]
            at = tuple(
                group[axis] if order.index(axis) >= stage else slice(None) for axis in range(bits)
            )
            held = passing[a].at[2] if stage == 0 else result(a, at)
            spot, axis = result(a, at), groups[order[stage]]
            copies.start(
                ("gather", a, stage),
                lambda held=held, spot=spot, axis=axis: (held, spot, flip(axis)),
            )

    def brought(order, stage):
        at = []
        for axis in range(bits):
            when = order.index(axis)
            if stage == 0 or when > stage - 1:
                at.append(group[axis])
            elif when == stage - 1:
                at.append(1 - group[axis])
            else:
                at.append(slice(None))
        return tuple(at)

    def core_send(stage):
        for a in range(3):
            spot = result(a, brought(orders[a], stage))
            held = passing[a].at[2] if stage == 0 else spot
            copies.start(("core", a, stage), lambda held=held, spot=spot: (held, spot, flip("b")))

    barrier = pltpu.get_barrier_semaphore()
    friends = [flip(axis) for axis in groups + ("b", "h", "l")] + [next_layer(1), next_layer(3)]
    friends += [{"b": 1 - core, "l": 1 - near}]
    for friend in friends:
        pl.semaphore_signal(barrier, inc=1, device_id=friend, device_id_type=MESH)

    @pl.when(moves)
    def _():
        pl.semaphore_signal(barrier, inc=1, device_id=partner, device_id_type=MESH)
        pl.semaphore_wait(barrier, len(friends) + 1)

    @pl.when(stays)
    def _():
        pl.semaphore_wait(barrier, len(friends))

    for mask in (3, 1, 2):
        to_core, to_near = exclusive(core, mask // 2), exclusive(near, mask % 2)

        def build(to_core=to_core, to_near=to_near):
            return (
                da_ref.at[:, columns(2 * to_core + to_near, width)],
                do.at[columns(place, part)],
                {"b": to_core, "l": to_near},
            )

        copies.start(("heads", mask), build)
    own_heads = local_copy(da_ref.at[:, columns(place, width)], do.at[columns(place, part)])
    own_heads.start()
    low_in = local_copy(low_ref, grad_low)
    low_here = local_copy(grad_low, low_home)
    copies.plan("low", lambda: (low_ref, low_home, partner))
    pl.when(moves)(functools.partial(copies.start, "low"))
    pl.when(stays)(low_in.start)

    pieces = 2
    thin = slab // pieces
    pair = whole.shape[0] // 2
    units = [local_copy(inputs_ref, whole.at[:pair]), local_copy(branches_ref, whole.at[pair:])]
    units += [local_copy(heads_ref, sent.at[0]), local_copy(branch_ref, sent.at[1])]
    for copy in units:
        copy.start()

    def hidden_load(u):
        spot = columns(pieces * shard(1 + u // pieces) + lax.rem(u, pieces), thin)
        at = columns(lax.rem(u, 3), thin)
        semaphore = hidden_local + 2 * lax.rem(u, 3)
        return (
            pltpu.make_async_copy(
                hidden_ref.at[:, spot], mixed.at[:pair, at], local.at[semaphore]
            ),
            pltpu.make_async_copy(
                active_ref.at[:, spot], mixed.at[pair:, at], local.at[semaphore + 1]
            ),
        )

    hidden_local = all_local[0]
    all_local[0] += 6
    for u in range(2):
        for copy in hidden_load(jnp.int32(u)):
            copy.start()
    for copy in units:
        copy.wait()
    @pl.loop(0, 4)
    def _(s):
        block = lax.dot_general(
            sent[0, :, columns(s, width)], sent[1], TN, preferred_element_type=f32
        ).astype(bf16)
        out_part[s] = block.reshape(out_part.shape[1:])

    @pl.loop(0, 4)
    def _(c):
        turned[columns(c, depth // 4)] = whole[:pair, columns(c, depth // 4)].T

    copies.start("out core", lambda: (out_part.at[:, 1 - core], out_in, flip("b")))
    def shard_gradients(k):
        @pl.loop(0, pieces)
        def _(n):
            u = pieces * (k - 1) + n
            for copy in hidden_load(u):
                copy.wait()

            @pl.when(u + 2 < 4 * pieces)
            def _():
                for copy in hidden_load(u + 2):
                    copy.start()

            buffer = columns(lax.rem(u, 3), thin)

            @pl.loop(0, 2**bits)
            def _(c):
                slot = tuple(lax.rem(c // 2 ** (bits - 1 - i), 2) for i in range(bits))
                up_tile[(n,) + slot] = jnp.dot(
                    turned[columns(c, quarter)],
                    mixed[:pair, buffer],
                    preferred_element_type=f32,
                ).astype(bf16)

            block = lax.dot_general(
                mixed[pair:, buffer], whole[pair:], TN, preferred_element_type=f32
            )
            down_tile[n] = block.astype(bf16).reshape(down_tile.shape[1:])

        if k == 1:
            copies.arrived("out core")

            @pl.loop(0, 4)
            def _(s):
                out_in[s] = (out_in[s].astype(f32) + out_part[s, core].astype(f32)).astype(bf16)

            put = local_copy(out_in, out_ref)
            put.start()
            put.wait()
        made = []
        for u in range(pieces):
            spot = (slice(None),) * (bits + 1) + (columns(pieces * shard(k) + u, thin),)
            made.append(local_copy(up_tile.at[u], up_ref.at[spot]))
            made.append(local_copy(down_tile.at[u], down_ref.at[shard(k), u]))
        for copy in made:
            copy.start()
        for copy in made:
            copy.wait()

    for k in (1, 2, 3, 4):
        shard_gradients(k)
        if k < 3:
            plane_send(k, 0)
    early = [
        local_copy(whole_ref, whole),
        local_copy(w_ref, w),
        local_copy(resid_ref, resid),
        local_copy(middle_ref, middle),
    ]
    for copy in early:
        copy.start()

    @pl.when(stays)
    def _():
        low_in.wait()
        low_here.start()

    for total in (dq, dk, dv):
        total[...] = jnp.zeros_like(total)
    own_heads.wait()
    for mask in (2, 1, 3):
        copies.arrived(("heads", mask))

    lane_head = lax.broadcasted_iota(jnp.int32, (8, width), 1) // HEAD_DIM
    marks = (lane_head == lax.broadcasted_iota(jnp.int32, (8, width), 0)).astype(f32)

    def span(i):
        return pl.ds(pl.multiple_of(i * rows, rows), rows)

    @pl.loop(0, blocks)
    def _(i):
        product = do[span(i)].astype(f32) * o_ref[span(i)].astype(f32)
        delta[:, span(i)] = lax.dot_general(
            marks, product, NT, precision=lax.Precision.HIGHEST, preferred_element_type=f32
        )

    def tile(i, j):
        at, to = span(i), span(j)
        keys, values = k_ref[to], v_ref[to]
        queries, grads = q_ref[at], do[at]
        dkj, dvj, dqi = dk[to], dv[to], dq[at]
        zero = jnp.zeros((), bf16)
        key = j * rows + lax.broadcasted_iota(jnp.int32, (rows, rows), 0)
        query = i * rows + lax.broadcasted_iota(jnp.int32, (rows, rows), 1)
        allowed = key <= query
        for h in range(heads):
            mine = head_lanes((rows, width), h)
            qm = jnp.where(mine, queries, zero)
            dom = jnp.where(mine, grads, zero)
            km = jnp.where(mine, keys, zero)
            st = lax.dot_general(keys, qm, NT, preferred_element_type=f32)
            pt = jnp.where(allowed, jnp.exp2(st * LOG2E - lse_ref[h : h + 1, at]), 0.0)
            dpt = lax.dot_general(values, dom, NT, preferred_element_type=f32)
            dst = (pt * (dpt - delta[h : h + 1, at])).astype(bf16)
            dvj = dvj + jnp.dot(pt.astype(bf16), dom, preferred_element_type=f32)
            dkj = dkj + jnp.dot(dst, qm, preferred_element_type=f32)
            dqi = dqi + lax.dot_general(dst, km, TN, preferred_element_type=f32)
        dq[at], dk[to], dv[to] = dqi, dkj, dvj

    count = blocks * (blocks + 1) // 2

    def last_stages(k):
        for stage in range(1, bits):
            plane_step(k, stage)

    def sums_a():
        plane_step(1, 0)
        plane_send(3, 0)

    def sums_b():
        plane_step(2, 0)
        plane_send(4, 0)

    def sums_c():
        last_stages(1)
        ring_send(1)

    def sums_d():
        plane_step(3, 0)

    def sums_e():
        last_stages(2)
        ring_add(1)
        ring_send(2)

    plans = ((0, sums_a), (2, sums_b), (4, sums_c), (6, sums_d), (8, sums_e))

    def tiles(low, high):
        @pl.loop(low, high)
        def _(t):
            i = jnp.int32(0)
            for n in range(1, blocks):
                i = i + (t >= n * (n + 1) // 2).astype(jnp.int32)
            tile(i, t - i * (i + 1) // 2)

    low = 0
    for when, step in plans:
        when = when * count // 10
        if when > low:
            tiles(low, when)
        step()
        low = when
    tiles(low, count)

    def turn_back(grad, at):
        cosine = jnp.concatenate([cos_ref[at]] * (width // 128), axis=1)
        sine = jnp.concatenate([sin_ref[at]] * (width // 128), axis=1)
        return grad * cosine + swap_halves(grad, 1.0) * sine

    @pl.loop(0, blocks)
    def _(i):
        at = span(i)
        mixed[at, :width] = (HEAD_DIM ** (-0.5) * turn_back(dq[at], at)).astype(bf16)
        mixed[at, width : 2 * width] = turn_back(dk[at], at).astype(bf16)
        mixed[at, 2 * width :] = dv[at].astype(bf16)

    for copy in early:
        copy.wait()
    size = part // chunks

    def input_part(block, c):
        at = pl.ds(pl.multiple_of(block * part + c * size, size), size)
        return lax.dot_general(
            mixed[at], w[...].reshape(depth, 3 * width), NT, preferred_element_type=f32
        )

    def inside(c):
        return pl.ds(pl.multiple_of(c * size, size), size)

    for slot in range(2):
        block = 2 * (1 - core) + (1 - near if slot == 0 else near)

        @pl.loop(0, chunks)
        def _(c):
            sent[slot, inside(c)] = input_part(block, c).astype(bf16)

        copies.start(
            ("x core", slot),
            lambda slot=slot: (sent.at[slot], from_core.at[slot], flip("b")),
        )
    copies.arrived(("x core", 0))
    for c in range(chunks):
        total = input_part(2 * core + 1 - near, c) + from_core[0, inside(c)].astype(f32)
        sent[2, inside(c)] = total.astype(bf16)
        copies.start(
            ("x near", c),
            lambda c=c: (sent.at[2, inside(c)], from_near.at[inside(c)], flip("l")),
        )
    plane_step(4, 0)
    side = quarter // 2
    for index in np.ndindex(*(2,) * bits):
        first = sum(bit << (bits - 1 - axis) for axis, bit in enumerate(index)) * quarter
        block = lax.dot_general(
            whole[:, first : first + quarter], mixed[...], TN, preferred_element_type=f32
        ).astype(bf16)
        for i in range(2):
            qkv_sum[index + (i,)] = block[i * side : (i + 1) * side]
    q_orders = [orders[0], orders[2]]

    def q_slot(i, stage, side):
        order = q_orders[i]
        at = []
        for axis in range(bits):
            when = order.index(axis)
            if when < stage:
                at.append(group[axis])
            elif when == stage:
                at.append(group[axis] if side == 0 else 1 - group[axis])
            else:
                at.append(slice(None))
        return qkv_sum.at[tuple(at) + (i,)]

    def q_send(stage):
        for i in range(2):
            copies.start(
                ("q", i, stage),
                lambda i=i: (
                    q_slot(i, stage, 1),
                    qkv_in[stage].at[i],
                    flip(groups[q_orders[i][stage]]),
                ),
            )

    def q_add(stage):
        for i in range(2):
            copies.arrived(("q", i, stage))
            add_into(q_slot(i, stage, 0), qkv_in[stage].at[i])

    q_send(0)
    last_stages(3)
    ring_add(2)
    ring_send(3)
    copies.arrived(("x core", 1))

    @pl.loop(0, chunks)
    def _(c):
        grad_x[inside(c)] = input_part(place, c) + from_core[1, inside(c)].astype(f32)

    own_q = tuple(group)
    axes = groups + ("b", "h", "l")

    def norms_send(step):
        copies.start(("norms", step), lambda: (norm_sum, norm_in.at[step], flip(axes[step])))

    def norms_add(step):
        copies.arrived(("norms", step))
        copies.sent(("norms", step))
        norm_sum[...] += norm_in[step]

    pl.when(stays)(low_here.wait)
    norm_sum[...] = norms_ref[...]
    fine = min(128, size)

    def home(c):
        copies.arrived(("x near", c))

        @pl.loop(0, size // fine)
        def _(s):
            at = pl.ds(pl.multiple_of(c * size + s * fine, fine), fine)
            grad = grad_x[at] + from_near[at].astype(f32)
            value = resid[at].astype(f32)
            center = value - jnp.mean(value, axis=1, keepdims=True)
            inverse = lax.rsqrt(jnp.mean(center * center, axis=1, keepdims=True) + EPS)
            unit = center * inverse
            scaled = grad * gain_ref[...]
            back = inverse * (
                scaled
                - jnp.mean(scaled, axis=1, keepdims=True)
                - unit * jnp.mean(scaled * unit, axis=1, keepdims=True)
            )
            grad_low[at] = (middle[at] + back).astype(bf16)
            norm_sum[0:1] += jnp.sum(grad * unit, axis=0, keepdims=True)
            norm_sum[4:5] += jnp.sum(grad, axis=0, keepdims=True)

        copies.plan(
            ("home", c), lambda c=c: (grad_low.at[inside(c)], grad_home.at[inside(c)], partner)
        )
        pl.when(moves)(functools.partial(copies.start, ("home", c)))

    def gather_next(stage):
        for a in range(3):
            copies.arrived(("gather", a, stage))
        if stage + 1 < bits:
            gather_send(stage + 1)
        core_send(stage + 1)

    def q_spot(at):
        return qkv_all.at[at + (core,)]

    keep_q = local_copy(qkv_core.at[1, core], q_spot(own_q))
    own = [local_copy(passing[a].at[2], result(a, tuple(group))) for a in range(3)]

    def q_gather(stage):
        at = tuple(group[axis] if axis >= stage else slice(None) for axis in range(bits))
        held = qkv_core.at[1, core] if stage == 0 else q_spot(at)
        copies.start(("q gather", stage), lambda: (held, q_spot(at), flip(groups[stage])))

    def q_core_send(stage):
        spot = q_spot(brought(orders[0], stage))
        held = qkv_core.at[1, core] if stage == 0 else spot
        copies.start(("q both", stage), lambda: (held, spot, flip("b")))

    half_way = chunks // 2
    for c in range(half_way):
        home(c)
    for stage in range(bits):
        q_add(stage)
        if stage + 1 < bits:
            q_send(stage + 1)

    copies.plan("q turn", lambda: (qkv_sum.at[own_q], qkv_core.at[0], partner))
    pl.when(moves)(functools.partial(copies.start, "q turn"))
    last_stages(4)
    ring_add(3)
    core_send(0)
    gather_send(0)
    for copy in own:
        copy.start()
    for c in range(half_way, chunks):
        home(c)
    stay = [local_copy(grad_low, grad_home)]
    pl.when(stays)(stay[0].start)
    norms_send(0)
    for copy in own:
        copy.wait()
    if bits > 0:
        gather_next(0)

    @pl.when(moves)
    def _():
        copies.arrived("q turn")

    @pl.when(stays)
    def _():
        qkv_core[0] = qkv_sum[own_q]

    copies.start("q core", lambda: (qkv_core.at[0, 1 - core], qkv_core.at[1, 1 - core], flip("b")))
    norms_add(0)
    norms_send(1)
    copies.arrived("q core")
    add_into(qkv_core.at[1, core], qkv_core.at[0, core])
    keep_q.start()
    q_gather(0)
    q_core_send(0)
    keep_q.wait()
    norms_add(1)
    norms_send(2)
    for stage in range(1, bits):
        gather_next(stage)
    for stage in range(bits):
        copies.arrived(("q gather", stage))
        if stage + 1 < bits:
            q_gather(stage + 1)
        q_core_send(stage + 1)
    for step in range(2, len(axes)):
        norms_add(step)
        if step + 1 < len(axes):
            norms_send(step + 1)
    norms_out[...] = norm_sum[...]
    for stage in range(bits + 1):
        for a in range(3):
            copies.arrived(("core", a, stage))
        copies.arrived(("q both", stage))
    sometimes = ["q turn", "low"] + [("home", c) for c in range(chunks)]

    @pl.when(moves)
    def _():
        copies.arrived("low")
        for c in range(chunks):
            copies.arrived(("home", c))
        for name in sometimes:
            copies.sent(name)

    pl.when(stays)(stay[0].wait)
    copies.drain(sometimes + [("norms", step) for step in range(len(axes))])


def back(
    q, k, v, o, lse, cosine, sine, gain, norms, da, low, inputs, branches, hidden, active,
    heads, branch, whole, w, resid, middle, groups, rows=BLOCK, chunks=2,
):
    length, width = q.shape
    part, depth = da.shape
    bits = len(groups)
    slots = (2,) * bits
    slab = hidden.shape[1] // 4
    up_shape = slots + (depth // 2**bits, 4 * slab)
    out_shape = (4,) + slots + (width // 2 ** (bits + 1), depth)
    down_shape = (4,) + slots + (slab // 2**bits, depth)
    tails = (up_shape[-2:-1] + (slab,), out_shape[-2:], down_shape[-2:])
    vmem = pl.BlockSpec(memory_space=pltpu.VMEM)
    anywhere = pl.BlockSpec(memory_space=pl.ANY)
    quarter = depth // 2**bits
    q_tail = (quarter // 2, 3 * width)
    thin = slab // 2
    scratch = [
        pltpu.VMEM((4, 2) + out_shape[1:], bf16),
        pltpu.VMEM(out_shape, bf16),
        pltpu.VMEM((2,) + up_shape[:-1] + (thin,), bf16),
        pltpu.VMEM((2,) + down_shape[2:], bf16),
        pltpu.VMEM((depth, length // 2), bf16),
    ]
    scratch += [pltpu.VMEM((length, width), bf16)]
    scratch += [pltpu.VMEM((length, width), f32)] * 3 + [pltpu.VMEM((8, length), f32)]
    scratch += [
        pltpu.VMEM((length, 3 * width), bf16),
        pltpu.VMEM(whole.shape, bf16),
        pltpu.VMEM(w.shape, bf16),
        pltpu.VMEM((part, depth), bf16),
        pltpu.VMEM((part, depth), f32),
        pltpu.VMEM((3, part, depth), bf16),
        pltpu.VMEM((2, part, depth), bf16),
        pltpu.VMEM((part, depth), bf16),
        pltpu.VMEM((part, depth), f32),
        pltpu.VMEM((part, depth), bf16),
        pltpu.VMEM(slots + (2,) + q_tail, bf16),
        pltpu.VMEM((2, 2) + q_tail, bf16),
        pltpu.VMEM((8, depth), f32),
        pltpu.VMEM((bits + 3, 8, depth), f32),
    ]
    for stage in range(bits):
        for tail in tails:
            scratch.append(pltpu.VMEM((4,) + (2,) * (bits - 1 - stage) + tail, bf16))
    scratch += [pltpu.VMEM((3,) + tail, bf16) for tail in tails]
    scratch += [pltpu.VMEM((2,) + (2,) * (bits - 1) + tail, bf16) for tail in tails]
    scratch += [
        pltpu.VMEM((2,) + (2,) * (bits - 1 - stage) + q_tail, bf16) for stage in range(bits)
    ]
    n = 5 + 3 * (4 * bits + 3 + bits + bits + 1)
    n += 2 + chunks + 2 * bits + chunks + (bits + 3) + 2 + bits + bits + 1
    scratch += [pltpu.SemaphoreType.DMA((n,)), pltpu.SemaphoreType.DMA((n,))]
    scratch += [pltpu.SemaphoreType.DMA((64,))]
    return pl.pallas_call(
        functools.partial(back_kernel, groups=groups, rows=rows, chunks=chunks),
        out_shape=(
            jax.ShapeDtypeStruct((8, depth), f32),
            jax.ShapeDtypeStruct((part, depth), bf16),
            jax.ShapeDtypeStruct((part, depth), bf16),
            jax.ShapeDtypeStruct(slots + (2,) + q_tail, bf16),
            jax.ShapeDtypeStruct(up_shape[:-1] + (2 * slab,), bf16),
            jax.ShapeDtypeStruct((2,) + out_shape[1:], bf16),
            jax.ShapeDtypeStruct((2,) + down_shape[1:], bf16),
            jax.ShapeDtypeStruct(up_shape, bf16),
            jax.ShapeDtypeStruct(out_shape, bf16),
            jax.ShapeDtypeStruct(down_shape, bf16),
        ),
        in_specs=[vmem] * 9 + [anywhere] * 12,
        out_specs=(vmem,) + (anywhere,) * 9,
        scratch_shapes=scratch,
        compiler_params=pltpu.CompilerParams(
            vmem_limit_bytes=63 * 2**20, collective_id=1, has_side_effects=True
        ),
        cost_estimate=pl.CostEstimate(
            flops=100_000_000_000, bytes_accessed=32 * 2**20, transcendentals=0
        ),
    )(
        q, k, v, o, lse, cosine, sine, gain, norms, da, low, inputs, branches, hidden, active, heads,
        branch, whole, w, resid, middle,
    )[:7]


def norm_forward(value, gain, shift):
    center = value - jnp.mean(value, axis=-1, keepdims=True)
    inverse = lax.rsqrt(jnp.mean(center * center, axis=-1, keepdims=True) + EPS)
    unit = center * inverse
    return (unit * gain + shift, unit, inverse)


def norm_backward(grad, unit, inverse, gain):
    scaled = grad * gain
    back = inverse * (
        scaled
        - jnp.mean(scaled, axis=-1, keepdims=True)
        - unit * jnp.mean(scaled * unit, axis=-1, keepdims=True)
    )
    return (back, jnp.sum(grad * unit, axis=0), jnp.sum(grad, axis=0))


def rotary_tables(length, width):
    half = HEAD_DIM // 2
    steps = (np.arange(width) % half).astype(np.float32) / np.float32(half)
    freqs = np.float32(10000.0) ** (-steps)
    angles = np.arange(length, dtype=np.float32)[:, None] * freqs[None, :]
    return (jnp.asarray(np.cos(angles)), jnp.asarray(np.sin(angles)))


SWAP = [(0, 1), (1, 0)]


def dot(left, right, dims=NN):
    return lax.dot_general(left, right, dims, preferred_element_type=f32)


def across(value, axis):
    return lax.ppermute(value, axis, SWAP)


def turn(value):
    return lax.ppermute(value, ("b", "h"), [(0, 0), (1, 2), (2, 1), (3, 3)])


def on_device(
    tokens,
    w_qkv,
    w_out,
    w_up,
    w_down,
    norm_gains,
    norm_shifts,
    cotangent,
    corpus_ids,
    corpus_weight,
    *,
    groups,
):
    _, part, depth = tokens.shape
    cols = w_qkv.shape[2]
    units = w_up.shape[1]
    core, half, near = lax.axis_index("b"), lax.axis_index("h"), lax.axis_index("l")
    length = 4 * part
    place = 2 * core + near
    group = jnp.int32(0)
    for axis in groups:
        group = 2 * group + lax.axis_index(axis)
    n_groups = 2 ** len(groups)
    stack = ("h", "l")
    cosine, sine = rotary_tables(length, 128)
    gains = [norm_gains[i : i + 1] for i in range(4)]
    shifts = [norm_shifts[i : i + 1] for i in range(4)]

    slots = (2,) * len(groups)
    q, k, v, whole_a, attended, lse, heads, resid_low, cotangent_low, w_attn, up_half, out_whole, down_half = front(
        tokens[0],
        cotangent[0],
        w_qkv.reshape(slots + (depth // n_groups, 3 * cols)),
        w_up.reshape(slots + (depth // n_groups, units)),
        w_out.reshape((2,) + slots + (cols // (2 * n_groups), depth)),
        w_down.reshape((2,) + slots + (units // (2 * n_groups), depth)),
        gains[0],
        shifts[0],
        cosine,
        sine,
        groups,
    )
    up_half = up_half.reshape(depth, 2 * units)
    out_whole = out_whole.reshape(4 * cols, depth)
    down_half = down_half.reshape(2 * units, depth)

    branch_a = dot(heads, out_whole)

    resid = resid_low.astype(f32)
    out_a, unit_1, inverse_1 = norm_forward(branch_a, gains[1], shifts[1])
    middle = resid + out_a
    normed_f, unit_2, inverse_2 = norm_forward(middle, gains[2], shifts[2])
    own_f = normed_f.astype(bf16)
    pair_f = jnp.concatenate([own_f, across(own_f, "b")], axis=0)
    hidden = dot(pair_f, up_half)
    cube = 0.7978845608028654 * (hidden + 0.044715 * hidden * hidden * hidden)
    bend = jnp.tanh(cube)
    active = (0.5 * hidden * (1.0 + bend)).astype(bf16)
    slope = 0.5 * (1.0 + bend) + 0.5 * hidden * (1.0 - bend * bend) * 0.7978845608028654 * (
        1.0 + 3 * 0.044715 * hidden * hidden
    )
    slope = slope.astype(bf16)
    branch_f = dot(active[part:], down_half).astype(bf16)
    branch_f = dot(active[:part], down_half) + across(branch_f, "b").astype(f32)
    out_f, unit_3, inverse_3 = norm_forward(branch_f, gains[3], shifts[3])
    output = (middle + out_f).astype(bf16)

    picks = (
        corpus_ids[:, None] == jnp.arange(corpus_weight.shape[0], dtype=jnp.int32)[None, :]
    ).astype(f32)
    row_scale = turn(jnp.dot(picks, corpus_weight, precision=lax.Precision.HIGHEST))
    grad_final = cotangent_low.astype(f32) * row_scale[:, None]
    back_3, gain_3, shift_3 = norm_backward(grad_final, unit_3, inverse_3, gains[3])
    own_g = back_3.astype(bf16)
    pair_g = jnp.concatenate([own_g, across(own_g, "b")], axis=0)
    grad_active = dot(pair_g, down_half, NT)
    grad_hidden = (slope.astype(f32) * grad_active).astype(bf16)
    grad_f = dot(grad_hidden[part:], up_half, NT).astype(bf16)
    grad_f = dot(grad_hidden[:part], up_half, NT) + across(grad_f, "b").astype(f32)
    back_2, gain_2, shift_2 = norm_backward(grad_f, unit_2, inverse_2, gains[2])
    grad_middle = grad_final + back_2
    back_1, gain_1, shift_1 = norm_backward(grad_middle, unit_1, inverse_1, gains[1])
    grad_a = back_1.astype(bf16)
    grad_attended = dot(grad_a, out_whole, NT).astype(bf16)

    none = jnp.zeros_like(gain_1)
    norms = jnp.stack([none, gain_1, gain_2, gain_3, none, shift_1, shift_2, shift_3])
    norm_grads, input_grad, output, qkv_grad, up_grad, out_grad, down_grad = back(
        q,
        k,
        v,
        attended,
        lse,
        cosine,
        sine,
        gains[0],
        norms,
        grad_attended,
        output,
        pair_f,
        pair_g,
        grad_hidden,
        active,
        heads,
        grad_a,
        whole_a,
        w_attn,
        resid_low,
        grad_middle,
        groups,
    )
    input_grad = input_grad.astype(f32)
    qkv_grad = qkv_grad.reshape(depth, 3, cols).astype(f32)
    up_grad = up_grad.reshape(depth, units).astype(f32)
    out_grad = out_grad.reshape(cols, depth).astype(f32)
    down_grad = down_grad.reshape(units, depth).astype(f32)
    return (
        output[None],
        input_grad[None],
        qkv_grad,
        out_grad,
        up_grad,
        down_grad,
        norm_grads[:4],
        norm_grads[4:],
    )


def solution(mesh):
    rows, parts = mesh.shape["dp"], mesh.shape["mp"]
    bits = (rows // 2).bit_length() - 1
    assert parts == 4 and rows == 2 ** (bits + 1)
    groups = tuple(f"g{i}" for i in range(bits))
    fine = Mesh(mesh.devices.reshape((2,) * (bits + 3)), groups + ("b", "h", "l"))
    dp, mp = groups + ("b",), ("h", "l")
    placed = (
        P(dp, mp, None),
        P(None, None, mp),
        P(mp, None),
        P(None, mp),
        P(mp, None),
        P(),
        P(),
        P(dp, mp, None),
        P(dp),
        P(),
    )
    return jax.shard_map(
        functools.partial(on_device, groups=groups),
        mesh=fine,
        in_specs=placed,
        out_specs=(
            P(dp, mp, None),
            P(dp, mp, None),
            P(None, None, mp),
            P(mp, None),
            P(None, mp),
            P(mp, None),
            P(),
            P(),
        ),
        check_vma=False,
    )
```

```python
import functools

import jax
import jax.numpy as jnp
import numpy as np
from jax import lax
from jax.experimental import pallas as pl
from jax.experimental.pallas import tpu as pltpu
from jax.sharding import Mesh, PartitionSpec as P

HEAD_DIM = 64
BLOCK = 512
EPS = 1e-05
LOG2E = 1.4426950408889634
NN = (((1,), (0,)), ((), ()))
NT = (((1,), (1,)), ((), ()))
TN = (((0,), (0,)), ((), ()))
f32 = jnp.float32
bf16 = jnp.bfloat16


def head_lanes(shape, head):
    return lax.broadcasted_iota(jnp.int32, shape, 1) // HEAD_DIM == head


def swap_halves(value, sign):
    half = HEAD_DIM // 2
    width = value.shape[1]
    first = (lax.broadcasted_iota(jnp.int32, value.shape, 1) // half) % 2 == 0
    return jnp.where(
        first, sign * pltpu.roll(value, width - half, 1), -sign * pltpu.roll(value, half, 1)
    )


MESH = pl.DeviceIdType.MESH
BACK_PLAN = {
    "front": "s1 s2",
    0: "a1 s3",
    1: "a2",
    3: "b1 r1",
    4: "s4",
    6: "a3",
    7: "b2 r2",
    9: "b3 r3",
    "x0": "a4",
    "x3": "b4 r4 end",
}
FRONT_PLAN = {
    "own": "ring",
    "near": "one",
    0: "1a",
    1: "two 1b",
    2: "2a three",
    3: "2b 3a",
    "rest": "3b",
}


class Copies:
    def __init__(self, send, recv):
        self.send, self.recv, self.made = send, recv, {}

    def describe(self, name):
        n, build = self.made[name]
        source, target, device = build()
        return pltpu.make_async_remote_copy(
            src_ref=source,
            dst_ref=target,
            send_sem=self.send.at[n],
            recv_sem=self.recv.at[n],
            device_id=device,
            device_id_type=MESH,
        )

    def plan(self, name, build):
        self.made[name] = (len(self.made), build)

    def start(self, name, build=None):
        if build is not None:
            self.plan(name, build)
        self.describe(name).start()

    def arrived(self, name):
        self.describe(name).wait_recv()

    def sent(self, name):
        self.describe(name).wait_send()

    def drain(self, but=()):
        for name in self.made:
            if name not in but:
                self.sent(name)


def flip(axis):
    return {axis: 1 - lax.axis_index(axis)}


def next_layer(step):
    at = lax.rem(2 * lax.axis_index("h") + lax.axis_index("l") + step, 4)
    return {"h": at // 2, "l": lax.rem(at, 2)}


def add_into(total, term, rows=64):
    lead, count = total.shape[:-2], total.shape[-2]
    step = next(n for n in (rows, 32, 16, 8) if count % n == 0)

    @pl.loop(0, count // step)
    def _(i):
        at = pl.ds(pl.multiple_of(i * step, step), step)
        for index in np.ndindex(*lead):
            total[index + (at,)] = (
                total[index + (at,)].astype(f32) + term[index + (at,)].astype(f32)
            ).astype(bf16)


def exclusive(a, b):
    return a + b - 2 * a * b


def forward_branch(last, heads, rows, q_ref, k_ref, v_ref, o_ref, lse_ref):
    width = q_ref.shape[1]
    n = (last + 1) * rows
    block = pl.ds(last * rows, rows)
    acc = jnp.zeros((rows, width), f32)
    logs = jnp.zeros((rows, width), f32)
    for h in range(heads):
        mine = head_lanes((rows, width), h)
        qm = jnp.where(mine, q_ref[block], jnp.zeros((), bf16))
        s = lax.dot_general(qm, k_ref[:n], NT, preferred_element_type=f32)
        row = lax.broadcasted_iota(jnp.int32, (rows, rows), 0)
        column = lax.broadcasted_iota(jnp.int32, (rows, rows), 1)
        tail = jnp.where(column <= row, s[:, n - rows :], -1e30)
        top = jnp.max(tail, axis=1, keepdims=True)
        if last:
            top = jnp.maximum(top, jnp.max(s[:, : n - rows], axis=1, keepdims=True))
        top = top * LOG2E
        vm = jnp.where(head_lanes((n, width), h), v_ref[:n], jnp.ones((), bf16))
        low = jnp.exp2(tail * LOG2E - top).astype(bf16)
        out = lax.dot_general(low, vm[n - rows :], NN, preferred_element_type=f32)
        if last:
            low = jnp.exp2(s[:, : n - rows] * LOG2E - top).astype(bf16)
            out = out + lax.dot_general(low, vm[: n - rows], NN, preferred_element_type=f32)
        total = pltpu.roll(out, HEAD_DIM, 1)
        acc = jnp.where(mine, out / total, acc)
        logs = jnp.where(mine, top + jnp.log2(total), logs)
    o_ref[block] = acc.astype(bf16)
    lane = lax.broadcasted_iota(jnp.int32, (8, width), 1)
    pick = (lane == HEAD_DIM * lax.broadcasted_iota(jnp.int32, (8, width), 0)).astype(f32)
    lse_ref[:, block] = lax.dot_general(
        pick, logs, NT, precision=lax.Precision.HIGHEST, preferred_element_type=f32
    )


def front_kernel(*refs, groups, chunks):
    (
        tok_ref, cot_ref, wq_ref, up_ref, out_ref, down_ref, gain_ref, shift_ref, cos_ref, sin_ref,
        q_ref, k_ref, v_ref, whole_ref, o_ref, lse_ref,
        heads_ref, tok_home, cot_home, w_home, up_all, out_all, down_all,
        row, w_att, bounce_up, bounce_out, bounce_down, bounce_cot,
        send, recv, local, head_send, head_recv,
    ) = refs
    bits = len(groups)
    part = tok_ref.shape[0]
    depth = tok_ref.shape[1]
    width = q_ref.shape[1]
    heads = width // HEAD_DIM
    core, half, near = lax.axis_index("b"), lax.axis_index("h"), lax.axis_index("l")
    group = [lax.axis_index(axis) for axis in groups]
    layer = 2 * half + near
    place = 2 * core + near
    stays = core == half
    moves = core != half
    partner = {"b": half, "h": core}
    copies = Copies(send, recv)
    locals_made, here = [], []

    def copy_here(source, target):
        copy = pltpu.make_async_copy(source, target, local.at[len(locals_made)])
        locals_made.append(copy)
        here.append(copy)
        copy.start()

    barrier = pltpu.get_barrier_semaphore()
    friends = [flip(axis) for axis in groups + ("b",)] + [next_layer(1), next_layer(3)]
    friends += [flip("l"), {"b": 1 - core, "l": 1 - near}]
    for friend in friends:
        pl.semaphore_signal(barrier, inc=1, device_id=friend, device_id_type=MESH)

    @pl.when(moves)
    def _():
        pl.semaphore_signal(barrier, inc=1, device_id=partner, device_id_type=MESH)
        pl.semaphore_wait(barrier, len(friends) + 1)

    @pl.when(stays)
    def _():
        pl.semaphore_wait(barrier, len(friends))

    size = part // chunks

    def piece(c):
        return pl.ds(c * size, size)

    weights = (up_ref, out_ref, down_ref)
    orders = [tuple(range(bits)), tuple(range(bits)), tuple(reversed(range(bits)))]
    slab = up_ref.shape[-1] // 2

    def slot(a, shard, at):
        if a == 0:
            return up_all.at[at + (slice(None), pl.ds(pl.multiple_of(shard * slab, slab), slab))]
        if a == 1:
            return out_all.at[(shard, core) + at]
        return down_all.at[(shard,) + at]

    def held(a, at):
        if a == 0:
            return up_ref.at[at + (slice(None), pl.ds(pl.multiple_of(core * slab, slab), slab))]
        return weights[a].at[(core,) + at]

    def shard(k):
        return lax.rem(layer + 4 - k, 4)

    def ring_send(step):
        for a in range(3):

            def build(a=a):
                at = tuple(group)
                spot = slot(a, shard(step - 1), at)
                return (held(a, at) if step == 1 else spot, spot, next_layer(1))

            copies.start(("ring", a, step), build)

    def ring_wait(step):
        for a in range(3):
            copies.arrived(("ring", a, step))

    def plane_send(k, stage):
        for a in range(3):

            def build(a=a):
                order = orders[a]
                at = tuple(
                    group[axis] if order.index(axis) >= stage else slice(None)
                    for axis in range(bits)
                )
                spot = slot(a, shard(k), at)
                return (spot, spot, flip(groups[order[stage]]))

            copies.start(("plane", a, k, stage), build)

    def plane_wait(k, stage):
        for a in range(3):
            copies.arrived(("plane", a, k, stage))

    def core_send(k):
        def build():
            spot = slot(1, shard(k), (slice(None),) * bits)
            return (spot, spot, flip("b"))

        copies.start(("core", k), build)

    def plane_next(k, stage):
        plane_wait(k, stage)
        if stage + 1 < bits:
            plane_send(k, stage + 1)
        else:
            core_send(k)

    def inner_stages(k):
        for stage in range(1, bits):
            plane_next(k, stage)

    def arrive(k):
        ring_wait(k)
        if k < 3:
            ring_send(k + 1)
        plane_send(k, 0)

    steps = {
        "ring": lambda: ring_send(1),
        "one": lambda: arrive(1),
        "two": lambda: arrive(2),
        "three": lambda: arrive(3),
        "1a": lambda: plane_next(1, 0),
        "1b": lambda: inner_stages(1),
        "2a": lambda: plane_next(2, 0),
        "2b": lambda: inner_stages(2),
        "3a": lambda: plane_next(3, 0),
        "3b": lambda: inner_stages(3),
    }

    def weights_at(point):
        for name in FRONT_PLAN.get(point, "").split():
            steps[name]()

    everything = (slice(None),) * bits
    bounces = [
        (held(0, everything), bounce_up, slot(0, layer, everything)),
        (out_ref, bounce_out, out_all.at[layer]),
        (held(2, everything), bounce_down, slot(2, layer, everything)),
    ]
    inward = []
    for source, buffer, _ in bounces:
        copy = pltpu.make_async_copy(source, buffer, local.at[len(locals_made)])
        locals_made.append(copy)
        inward.append(copy)
        copy.start()

    weights_at("start")
    own = [
        pltpu.make_async_copy(
            tok_ref.at[piece(c)], row.at[place, piece(c)], local.at[len(locals_made) + c]
        )
        for c in range(chunks)
    ]
    locals_made.extend(own)
    turned = [("turn", c) for c in range(chunks)]
    for c in range(chunks):
        copies.plan(
            turned[c],
            lambda c=c: (tok_ref.at[piece(c)], row.at[layer, piece(c)], partner),
        )
    w_here = pltpu.make_async_copy(wq_ref, w_att, local.at[len(locals_made)])
    locals_made.append(w_here)
    copies.plan("wturn", lambda: (wq_ref.at[tuple(group)], w_att.at[tuple(group)], partner))
    cot_in = pltpu.make_async_copy(cot_ref, bounce_cot, local.at[len(locals_made)])
    locals_made.append(cot_in)
    cot_here = pltpu.make_async_copy(bounce_cot, cot_home, local.at[len(locals_made)])
    locals_made.append(cot_here)
    copies.plan("cot", lambda: (cot_ref, cot_home, partner))

    @pl.when(moves)
    def _():
        for c in range(chunks):
            copies.start(turned[c])
        copies.start("wturn")

    @pl.when(stays)
    def _():
        for c in range(chunks):
            own[c].start()
        w_here.start()
        cot_in.start()

    for c in range(chunks):
        pl.when(moves)(functools.partial(copies.arrived, turned[c]))
        pl.when(stays)(own[c].wait)
        for name, axis in (("near", "l"), ("core own", "b")):
            copies.start(
                (name, c),
                lambda c=c, axis=axis: (
                    row.at[place, piece(c)],
                    row.at[place, piece(c)],
                    flip(axis),
                ),
            )
    copy_here(row.at[place], tok_home)
    for copy in inward:
        copy.wait()
    for _, buffer, target in bounces:
        copy_here(buffer, target)
    weights_at("own")

    @pl.when(stays)
    def _():
        w_here.wait()

    parts = [pl.ds(i * (w_att.shape[-2] // 2), w_att.shape[-2] // 2) for i in range(2)]
    w_orders = [orders[0], orders[2]]
    for stage in range(bits):
        for i in range(2):

            def build(stage=stage, i=i):
                order = w_orders[i]
                at = tuple(
                    group[axis] if order.index(axis) >= stage else slice(None)
                    for axis in range(bits)
                )
                spot = w_att.at[at + (parts[i],)]
                return (spot, spot, flip(groups[order[stage]]))

            copies.plan(("w", stage, i), build)

    @pl.when(moves)
    def _():
        copies.arrived("wturn")
        for stage in range(bits):
            for i in range(2):
                copies.start(("w", stage, i))
            for i in range(2):
                copies.arrived(("w", stage, i))

    copy_here(w_att, w_home)
    near_block = 2 * core + 1 - near

    def pass_on():
        for c in range(chunks):
            copies.arrived(("near", c))
            copies.start(
                ("core near", c),
                lambda c=c: (row.at[near_block, piece(c)], row.at[near_block, piece(c)], flip("b")),
            )
        weights_at("near")

    def wait_all(name):
        def run():
            for c in range(chunks):
                copies.arrived((name, c))

        return run

    @pl.loop(0, 4)
    def _(r):
        far_core, far_near = lax.rem(r, 2), r // 2
        block = 2 * exclusive(core, far_core) + exclusive(near, far_near)
        pl.when(r == 1)(wait_all("core own"))
        pl.when(r == 2)(pass_on)
        pl.when(r == 3)(wait_all("core near"))

        @pl.loop(0, 2)
        def _(c):
            rows = part // 2
            inside = pl.ds(pl.multiple_of(c * rows, rows), rows)
            at = pl.ds(pl.multiple_of(block * part + c * rows, rows), rows)
            value = row[block, inside].astype(f32)
            center = value - jnp.mean(value, axis=1, keepdims=True)
            inverse = lax.rsqrt(jnp.mean(center * center, axis=1, keepdims=True) + EPS)
            normed = (center * inverse * gain_ref[0:1] + shift_ref[0:1]).astype(bf16)
            whole_ref[at] = normed
            w = w_att[...].reshape(depth, 3 * width)
            mixed = jnp.dot(normed, w, preferred_element_type=f32)
            cosine = jnp.concatenate([cos_ref[at]] * (width // 128), axis=1)
            sine = jnp.concatenate([sin_ref[at]] * (width // 128), axis=1)
            query, key = mixed[:, :width], mixed[:, width : 2 * width]
            query = HEAD_DIM ** (-0.5) * (query * cosine + swap_halves(query, -1.0) * sine)
            q_ref[at] = query.astype(bf16)
            k_ref[at] = (key * cosine + swap_halves(key, -1.0) * sine).astype(bf16)
            v_ref[at] = mixed[:, 2 * width :].astype(bf16)

    def head_copy(mask):
        far_core, far_near = mask // 2, lax.rem(mask, 2)
        to_core, to_near = exclusive(core, far_core), exclusive(near, far_near)
        block = 2 * to_core + to_near
        rows = pl.ds(pl.multiple_of(block * part, part), part)
        columns = pl.ds(pl.multiple_of(place * width, width), width)
        return pltpu.make_async_remote_copy(
            src_ref=o_ref.at[rows],
            dst_ref=heads_ref.at[:, columns],
            send_sem=head_send.at[mask],
            recv_sem=head_recv.at[mask],
            device_id={"b": to_core, "l": to_near},
            device_id_type=MESH,
        )

    @pl.loop(0, 4)
    def _(r):
        far_core, far_near = 1 - lax.rem(r, 2), 1 - r // 2
        mask = 2 * far_core + far_near
        block = 2 * exclusive(core, far_core) + exclusive(near, far_near)
        for n in range(4):
            pl.when(r == n)(functools.partial(weights_at, n))
        for i in range(4):
            pl.when(block == i)(
                functools.partial(
                    forward_branch, i, heads, part, q_ref, k_ref, v_ref, o_ref, lse_ref
                )
            )

        @pl.when(r < 3)
        def _():
            head_copy(mask).start()

    copy_here(
        o_ref.at[pl.ds(pl.multiple_of(place * part, part), part)],
        heads_ref.at[:, pl.ds(pl.multiple_of(place * width, width), width)],
    )

    @pl.when(moves)
    def _():
        copies.start("cot")

    @pl.when(stays)
    def _():
        cot_in.wait()
        cot_here.start()

    weights_at("rest")
    for mask in (1, 2, 3):
        copy = head_copy(jnp.int32(mask))
        copy.wait_send()
        copy.wait_recv()
    for k in (1, 2, 3):
        copies.arrived(("core", k))
    sometimes = turned + ["wturn", "cot"] + [("w", s, i) for s in range(bits) for i in range(2)]

    @pl.when(moves)
    def _():
        copies.arrived("cot")
        for name in sometimes:
            copies.sent(name)

    @pl.when(stays)
    def _():
        cot_here.wait()

    for copy in here:
        copy.wait()
    copies.drain(sometimes)


def front(tok, cot, wq, up, out, down, gain, shift, cosine, sine, groups, chunks=2):
    part, depth = tok.shape
    length = 4 * part
    width = wq.shape[-1] // 3
    bits = len(groups)
    vmem = pl.BlockSpec(memory_space=pltpu.VMEM)
    anywhere = pl.BlockSpec(memory_space=pl.ANY)

    def shape(*dims):
        return jax.ShapeDtypeStruct(dims, bf16)

    n = 2 * chunks + 2 + 3 * chunks + 2 * bits + 3 * 3 + 9 * bits + 3 + 4
    return pl.pallas_call(
        functools.partial(front_kernel, groups=groups, chunks=chunks),
        out_shape=(
            shape(length, width),
            shape(length, width),
            shape(length, width),
            shape(length, depth),
            shape(length, width),
            jax.ShapeDtypeStruct((8, length), f32),
            shape(part, depth),
            shape(part, depth),
            shape(part, depth),
            shape(*wq.shape),
            shape(*up.shape[:-1], 2 * up.shape[-1]),
            shape(4, *out.shape),
            shape(4, *down.shape[1:]),
        ),
        in_specs=[anywhere] * 6 + [vmem] * 4,
        out_specs=(vmem,) * 6 + (anywhere,) * 7,
        scratch_shapes=[
            pltpu.VMEM((4, part, depth), bf16),
            pltpu.VMEM(wq.shape, bf16),
            pltpu.VMEM(up.shape[:-1] + (up.shape[-1] // 2,), bf16),
            pltpu.VMEM(out.shape, bf16),
            pltpu.VMEM(down.shape[1:], bf16),
            pltpu.VMEM((part, depth), bf16),
            pltpu.SemaphoreType.DMA((n,)),
            pltpu.SemaphoreType.DMA((n,)),
            pltpu.SemaphoreType.DMA((32,)),
            pltpu.SemaphoreType.DMA((4,)),
            pltpu.SemaphoreType.DMA((4,)),
        ],
        compiler_params=pltpu.CompilerParams(
            vmem_limit_bytes=58 * 2**20, collective_id=2, has_side_effects=True
        ),
        cost_estimate=pl.CostEstimate(
            flops=100_000_000_000, bytes_accessed=32 * 2**20, transcendentals=0
        ),
    )(tok, cot, wq, up, out, down, gain, shift, cosine, sine)

def back_kernel(*refs, groups, rows, chunks):
    (
        q_ref, k_ref, v_ref, o_ref, lse_ref, cos_ref, sin_ref, gain_ref, norms_ref,
        da_ref, low_ref, inputs_ref, branches_ref, hidden_ref, active_ref, heads_ref, branch_ref,
        whole_ref, w_ref, resid_ref, middle_ref,
        gains_out, shifts_out, grad_home, low_home, qkv_all, up_all, out_all, down_all,
        up_ref, out_ref, down_ref,
        out_part, out_in, up_tile, down_tile, turned,
        do, dq, dk, dv, delta, mixed, whole, w, resid, middle,
        sent, from_core, from_near, grad_x, grad_low, qkv_sum, qkv_core, norm_sum, norm_in,
        *rest,
    ) = refs
    bits = len(groups)
    terms = (up_ref, out_ref, down_ref)
    partial = [[rest[3 * s + a] for s in range(bits)] for a in range(3)]
    rest = rest[3 * bits :]
    passing, staged, rest = rest[:3], rest[3:6], rest[6:]
    qkv_in, (send, recv, local) = rest[:bits], rest[bits:]
    copies = Copies(send, recv)
    group = [lax.axis_index(axis) for axis in groups]
    core, half, near = lax.axis_index("b"), lax.axis_index("h"), lax.axis_index("l")
    layer = 2 * half + near
    place = 2 * core + near
    moves, stays = core != half, core == half
    partner = {"b": half, "h": core}
    orders = [tuple(range(bits)), tuple(range(bits)), tuple(reversed(range(bits)))]
    part, depth = da_ref.shape
    length, width = q_ref.shape
    heads = width // HEAD_DIM
    blocks = length // rows
    slab = up_ref.shape[-1] // 4
    quarter = depth // 2**bits
    all_local = [0]

    def local_copy(source, target):
        n = all_local[0]
        all_local[0] += 1
        return pltpu.make_async_copy(source, target, local.at[n])

    def columns(which, size):
        return pl.ds(pl.multiple_of(which * size, size), size)

    def shard(k):
        return lax.rem(layer + 4 - k, 4)

    def term(a, k, at):
        if a == 0:
            return up_ref.at[at + (slice(None), columns(shard(k), slab))]
        return terms[a].at[(shard(k),) + at]

    def result(a, at):
        if a == 0:
            return up_all.at[at + (slice(None), columns(core, slab))]
        return (None, out_all, down_all)[a].at[(core,) + at]

    def split(order, stage, side):
        at = []
        for axis in range(bits):
            when = order.index(axis)
            if when == stage:
                at.append(group[axis] if side == 0 else 1 - group[axis])
            elif when > stage:
                at.append(slice(None))
        return tuple(at)

    def source(a, k, stage, side):
        at = split(orders[a], stage, side)
        if stage == 0:
            return term(a, k, at) if side else staged[a].at[k % 2]
        return partial[a][stage - 1].at[(k % 4,) + at]

    loads = {}

    def plane_send(k, stage):
        for a in range(3):
            copies.start(
                ("plane", a, k, stage),
                lambda a=a: (
                    source(a, k, stage, 1),
                    partial[a][stage].at[k % 4],
                    flip(groups[orders[a][stage]]),
                ),
            )
            if stage == 0:
                loads[a, k] = local_copy(term(a, k, split(orders[a], 0, 0)), staged[a].at[k % 2])
                loads[a, k].start()

    def plane_add(k, stage):
        for a in range(3):
            copies.arrived(("plane", a, k, stage))
            if stage == 0:
                loads[a, k].wait()
            add_into(partial[a][stage].at[k % 4], source(a, k, stage, 0))

    def plane_step(k, stage):
        plane_add(k, stage)
        if stage + 1 < bits:
            plane_send(k, stage + 1)

    def ring_send(step):
        for a in range(3):
            held = partial[a][bits - 1].at[1] if step == 1 else passing[a].at[step - 2]
            target = passing[a].at[step - 1]
            copies.start(
                ("ring", a, step), lambda held=held, target=target: (held, target, next_layer(1))
            )

    def ring_add(step):
        for a in range(3):
            copies.arrived(("ring", a, step))
            add_into(passing[a].at[step - 1], partial[a][bits - 1].at[(step + 1) % 4])

    def gather_send(stage):
        for a in range(3):
            order = orders[a]
            at = tuple(
                group[axis] if order.index(axis) >= stage else slice(None) for axis in range(bits)
            )
            held = passing[a].at[2] if stage == 0 else result(a, at)
            spot, axis = result(a, at), groups[order[stage]]
            copies.start(
                ("gather", a, stage),
                lambda held=held, spot=spot, axis=axis: (held, spot, flip(axis)),
            )

    def brought(order, stage):
        at = []
        for axis in range(bits):
            when = order.index(axis)
            if stage == 0 or when > stage - 1:
                at.append(group[axis])
            elif when == stage - 1:
                at.append(1 - group[axis])
            else:
                at.append(slice(None))
        return tuple(at)

    def core_send(stage):
        for a in range(3):
            spot = result(a, brought(orders[a], stage))
            held = passing[a].at[2] if stage == 0 else spot
            copies.start(("core", a, stage), lambda held=held, spot=spot: (held, spot, flip("b")))

    barrier = pltpu.get_barrier_semaphore()
    friends = [flip(axis) for axis in groups + ("b", "h", "l")] + [next_layer(1), next_layer(3)]
    friends += [{"b": 1 - core, "l": 1 - near}]
    for friend in friends:
        pl.semaphore_signal(barrier, inc=1, device_id=friend, device_id_type=MESH)

    @pl.when(moves)
    def _():
        pl.semaphore_signal(barrier, inc=1, device_id=partner, device_id_type=MESH)
        pl.semaphore_wait(barrier, len(friends) + 1)

    @pl.when(stays)
    def _():
        pl.semaphore_wait(barrier, len(friends))

    for mask in (3, 1, 2):
        to_core, to_near = exclusive(core, mask // 2), exclusive(near, mask % 2)

        def build(to_core=to_core, to_near=to_near):
            return (
                da_ref.at[:, columns(2 * to_core + to_near, width)],
                do.at[columns(place, part)],
                {"b": to_core, "l": to_near},
            )

        copies.start(("heads", mask), build)
    own_heads = local_copy(da_ref.at[:, columns(place, width)], do.at[columns(place, part)])
    own_heads.start()
    low_in = local_copy(low_ref, grad_low)
    low_here = local_copy(grad_low, low_home)
    copies.plan("low", lambda: (low_ref, low_home, partner))
    pl.when(moves)(functools.partial(copies.start, "low"))
    pl.when(stays)(low_in.start)

    pieces = 2
    thin = slab // pieces
    pair = whole.shape[0] // 2
    units = [local_copy(inputs_ref, whole.at[:pair]), local_copy(branches_ref, whole.at[pair:])]
    units += [local_copy(heads_ref, sent.at[0]), local_copy(branch_ref, sent.at[1])]
    for copy in units:
        copy.start()

    def hidden_load(u):
        spot = columns(pieces * shard(1 + u // pieces) + lax.rem(u, pieces), thin)
        at = columns(lax.rem(u, 3), thin)
        semaphore = hidden_local + 2 * lax.rem(u, 3)
        return (
            pltpu.make_async_copy(
                hidden_ref.at[:, spot], mixed.at[:pair, at], local.at[semaphore]
            ),
            pltpu.make_async_copy(
                active_ref.at[:, spot], mixed.at[pair:, at], local.at[semaphore + 1]
            ),
        )

    hidden_local = all_local[0]
    all_local[0] += 6
    for u in range(2):
        for copy in hidden_load(jnp.int32(u)):
            copy.start()
    for copy in units:
        copy.wait()
    @pl.loop(0, 4)
    def _(s):
        block = lax.dot_general(
            sent[0, :, columns(s, width)], sent[1], TN, preferred_element_type=f32
        ).astype(bf16)
        out_part[s] = block.reshape(out_part.shape[1:])

    @pl.loop(0, 4)
    def _(c):
        turned[columns(c, depth // 4)] = whole[:pair, columns(c, depth // 4)].T

    copies.start("out core", lambda: (out_part.at[:, 1 - core], out_in, flip("b")))
    def shard_gradients(k):
        @pl.loop(0, pieces)
        def _(n):
            u = pieces * (k - 1) + n
            for copy in hidden_load(u):
                copy.wait()

            @pl.when(u + 2 < 4 * pieces)
            def _():
                for copy in hidden_load(u + 2):
                    copy.start()

            buffer = columns(lax.rem(u, 3), thin)

            @pl.loop(0, 2**bits)
            def _(c):
                slot = tuple(lax.rem(c // 2 ** (bits - 1 - i), 2) for i in range(bits))
                up_tile[(n,) + slot] = jnp.dot(
                    turned[columns(c, quarter)],
                    mixed[:pair, buffer],
                    preferred_element_type=f32,
                ).astype(bf16)

            block = lax.dot_general(
                mixed[pair:, buffer], whole[pair:], TN, preferred_element_type=f32
            )
            down_tile[n] = block.astype(bf16).reshape(down_tile.shape[1:])

        if k == 1:
            copies.arrived("out core")

            @pl.loop(0, 4)
            def _(s):
                out_in[s] = (out_in[s].astype(f32) + out_part[s, core].astype(f32)).astype(bf16)

            put = local_copy(out_in, out_ref)
            put.start()
            put.wait()
        made = []
        for u in range(pieces):
            spot = (slice(None),) * (bits + 1) + (columns(pieces * shard(k) + u, thin),)
            made.append(local_copy(up_tile.at[u], up_ref.at[spot]))
            made.append(local_copy(down_tile.at[u], down_ref.at[shard(k), u]))
        for copy in made:
            copy.start()
        for copy in made:
            copy.wait()

    whole_load = local_copy(whole_ref, whole)

    def begin(k):
        shard_gradients(k)
        if k == 4:
            whole_load.start()
        plane_send(k, 0)

    def last_stages(k):
        for stage in range(1, bits):
            plane_step(k, stage)

    def ring(step):
        if step > 1:
            ring_add(step - 1)
        if step < 4:
            ring_send(step)

    own = [local_copy(passing[a].at[2], result(a, tuple(group))) for a in range(3)]

    def finish():
        core_send(0)
        gather_send(0)
        for copy in own:
            copy.start()

    kinds = {"s": begin, "a": lambda k: plane_step(k, 0), "b": last_stages, "r": ring}

    def sums_at(point):
        for name in BACK_PLAN.get(point, "").split():
            if name == "end":
                finish()
            else:
                kinds[name[0]](int(name[1]))

    sums_at("front")
    early = [
        local_copy(w_ref, w),
        local_copy(resid_ref, resid),
        local_copy(middle_ref, middle),
    ]
    for copy in early:
        copy.start()

    @pl.when(stays)
    def _():
        low_in.wait()
        low_here.start()

    for total in (dq, dk, dv):
        total[...] = jnp.zeros_like(total)
    own_heads.wait()
    for mask in (2, 1, 3):
        copies.arrived(("heads", mask))

    lane_head = lax.broadcasted_iota(jnp.int32, (8, width), 1) // HEAD_DIM
    marks = (lane_head == lax.broadcasted_iota(jnp.int32, (8, width), 0)).astype(f32)

    def span(i):
        return pl.ds(pl.multiple_of(i * rows, rows), rows)

    @pl.loop(0, blocks)
    def _(i):
        product = do[span(i)].astype(f32) * o_ref[span(i)].astype(f32)
        delta[:, span(i)] = lax.dot_general(
            marks, product, NT, precision=lax.Precision.HIGHEST, preferred_element_type=f32
        )

    def tile(i, j):
        at, to = span(i), span(j)
        keys, values = k_ref[to], v_ref[to]
        queries, grads = q_ref[at], do[at]
        dkj, dvj, dqi = dk[to], dv[to], dq[at]
        zero = jnp.zeros((), bf16)
        key = j * rows + lax.broadcasted_iota(jnp.int32, (rows, rows), 0)
        query = i * rows + lax.broadcasted_iota(jnp.int32, (rows, rows), 1)
        allowed = key <= query
        for h in range(heads):
            mine = head_lanes((rows, width), h)
            qm = jnp.where(mine, queries, zero)
            dom = jnp.where(mine, grads, zero)
            km = jnp.where(mine, keys, zero)
            st = lax.dot_general(keys, qm, NT, preferred_element_type=f32)
            pt = jnp.where(allowed, jnp.exp2(st * LOG2E - lse_ref[h : h + 1, at]), 0.0)
            dpt = lax.dot_general(values, dom, NT, preferred_element_type=f32)
            dst = (pt * (dpt - delta[h : h + 1, at])).astype(bf16)
            dvj = dvj + jnp.dot(pt.astype(bf16), dom, preferred_element_type=f32)
            dkj = dkj + jnp.dot(dst, qm, preferred_element_type=f32)
            dqi = dqi + lax.dot_general(dst, km, TN, preferred_element_type=f32)
        dq[at], dk[to], dv[to] = dqi, dkj, dvj

    count = blocks * (blocks + 1) // 2

    def tiles(low, high):
        @pl.loop(low, high)
        def _(t):
            i = jnp.int32(0)
            for n in range(1, blocks):
                i = i + (t >= n * (n + 1) // 2).astype(jnp.int32)
            tile(i, t - i * (i + 1) // 2)

    low = 0
    for point in range(10):
        when = point * count // 10
        if point in BACK_PLAN:
            if when > low:
                tiles(low, when)
            sums_at(point)
            low = when
    tiles(low, count)

    def turn_back(grad, at):
        cosine = jnp.concatenate([cos_ref[at]] * (width // 128), axis=1)
        sine = jnp.concatenate([sin_ref[at]] * (width // 128), axis=1)
        return grad * cosine + swap_halves(grad, 1.0) * sine

    @pl.loop(0, blocks)
    def _(i):
        at = span(i)
        mixed[at, :width] = (HEAD_DIM ** (-0.5) * turn_back(dq[at], at)).astype(bf16)
        mixed[at, width : 2 * width] = turn_back(dk[at], at).astype(bf16)
        mixed[at, 2 * width :] = dv[at].astype(bf16)

    for copy in early:
        copy.wait()
    size = part // chunks

    def input_part(block, c):
        at = pl.ds(pl.multiple_of(block * part + c * size, size), size)
        return lax.dot_general(
            mixed[at], w[...].reshape(depth, 3 * width), NT, preferred_element_type=f32
        )

    def inside(c):
        return pl.ds(pl.multiple_of(c * size, size), size)

    for slot in range(2):
        block = 2 * (1 - core) + (1 - near if slot == 0 else near)

        @pl.loop(0, chunks)
        def _(c):
            sent[slot, inside(c)] = input_part(block, c).astype(bf16)

        copies.start(
            ("x core", slot),
            lambda slot=slot: (sent.at[slot], from_core.at[slot], flip("b")),
        )
    sums_at("x0")
    copies.arrived(("x core", 0))
    for c in range(chunks):
        total = input_part(2 * core + 1 - near, c) + from_core[0, inside(c)].astype(f32)
        sent[2, inside(c)] = total.astype(bf16)
        copies.start(
            ("x near", c),
            lambda c=c: (sent.at[2, inside(c)], from_near.at[inside(c)], flip("l")),
        )
    sums_at("x1")
    whole_load.wait()
    side = quarter // 2
    for index in np.ndindex(*(2,) * bits):
        first = sum(bit << (bits - 1 - axis) for axis, bit in enumerate(index)) * quarter
        block = lax.dot_general(
            whole[:, first : first + quarter], mixed[...], TN, preferred_element_type=f32
        ).astype(bf16)
        for i in range(2):
            qkv_sum[index + (i,)] = block[i * side : (i + 1) * side]
    q_orders = [orders[0], orders[2]]

    def q_slot(i, stage, side):
        order = q_orders[i]
        at = []
        for axis in range(bits):
            when = order.index(axis)
            if when < stage:
                at.append(group[axis])
            elif when == stage:
                at.append(group[axis] if side == 0 else 1 - group[axis])
            else:
                at.append(slice(None))
        return qkv_sum.at[tuple(at) + (i,)]

    def q_send(stage):
        for i in range(2):
            copies.start(
                ("q", i, stage),
                lambda i=i: (
                    q_slot(i, stage, 1),
                    qkv_in[stage].at[i],
                    flip(groups[q_orders[i][stage]]),
                ),
            )

    def q_add(stage):
        for i in range(2):
            copies.arrived(("q", i, stage))
            add_into(q_slot(i, stage, 0), qkv_in[stage].at[i])

    q_send(0)
    sums_at("x2")
    copies.arrived(("x core", 1))

    @pl.loop(0, chunks)
    def _(c):
        grad_x[inside(c)] = input_part(place, c) + from_core[1, inside(c)].astype(f32)

    own_q = tuple(group)
    axes = groups + ("b", "h", "l")

    def norms_send(step):
        copies.start(("norms", step), lambda: (norm_sum, norm_in.at[step], flip(axes[step])))

    def norms_add(step):
        copies.arrived(("norms", step))
        copies.sent(("norms", step))
        norm_sum[...] += norm_in[step]

    pl.when(stays)(low_here.wait)
    norm_sum[...] = norms_ref[...]
    fine = min(128, size)

    def home(c):
        copies.arrived(("x near", c))

        @pl.loop(0, size // fine)
        def _(s):
            at = pl.ds(pl.multiple_of(c * size + s * fine, fine), fine)
            grad = grad_x[at] + from_near[at].astype(f32)
            value = resid[at].astype(f32)
            center = value - jnp.mean(value, axis=1, keepdims=True)
            inverse = lax.rsqrt(jnp.mean(center * center, axis=1, keepdims=True) + EPS)
            unit = center * inverse
            scaled = grad * gain_ref[0:1]
            back = inverse * (
                scaled
                - jnp.mean(scaled, axis=1, keepdims=True)
                - unit * jnp.mean(scaled * unit, axis=1, keepdims=True)
            )
            grad_low[at] = (middle[at] + back).astype(bf16)
            norm_sum[0:1] += jnp.sum(grad * unit, axis=0, keepdims=True)
            norm_sum[4:5] += jnp.sum(grad, axis=0, keepdims=True)

        copies.plan(
            ("home", c), lambda c=c: (grad_low.at[inside(c)], grad_home.at[inside(c)], partner)
        )
        pl.when(moves)(functools.partial(copies.start, ("home", c)))

    def gather_next(stage):
        for a in range(3):
            copies.arrived(("gather", a, stage))
        if stage + 1 < bits:
            gather_send(stage + 1)
        core_send(stage + 1)

    def q_spot(at):
        return qkv_all.at[at + (core,)]

    keep_q = local_copy(qkv_core.at[1, core], q_spot(own_q))
    def q_gather(stage):
        at = tuple(group[axis] if axis >= stage else slice(None) for axis in range(bits))
        held = qkv_core.at[1, core] if stage == 0 else q_spot(at)
        copies.start(("q gather", stage), lambda: (held, q_spot(at), flip(groups[stage])))

    def q_core_send(stage):
        spot = q_spot(brought(orders[0], stage))
        held = qkv_core.at[1, core] if stage == 0 else spot
        copies.start(("q both", stage), lambda: (held, spot, flip("b")))

    sums_at("x3")
    half_way = chunks // 2
    for c in range(half_way):
        home(c)
    sums_at("x4")
    for stage in range(bits):
        q_add(stage)
        if stage + 1 < bits:
            q_send(stage + 1)

    copies.plan("q turn", lambda: (qkv_sum.at[own_q], qkv_core.at[0], partner))
    pl.when(moves)(functools.partial(copies.start, "q turn"))
    sums_at("x5")
    for c in range(half_way, chunks):
        home(c)
    stay = [local_copy(grad_low, grad_home)]
    pl.when(stays)(stay[0].start)
    norms_send(0)
    sums_at("x6")
    for copy in own:
        copy.wait()
    gather_next(0)

    @pl.when(moves)
    def _():
        copies.arrived("q turn")

    @pl.when(stays)
    def _():
        qkv_core[0] = qkv_sum[own_q]

    copies.start("q core", lambda: (qkv_core.at[0, 1 - core], qkv_core.at[1, 1 - core], flip("b")))
    norms_add(0)
    norms_send(1)
    copies.arrived("q core")
    add_into(qkv_core.at[1, core], qkv_core.at[0, core])
    keep_q.start()
    q_gather(0)
    q_core_send(0)
    keep_q.wait()
    norms_add(1)
    norms_send(2)
    for stage in range(1, bits):
        gather_next(stage)
    for stage in range(bits):
        copies.arrived(("q gather", stage))
        if stage + 1 < bits:
            q_gather(stage + 1)
        q_core_send(stage + 1)
    for step in range(2, len(axes)):
        norms_add(step)
        if step + 1 < len(axes):
            norms_send(step + 1)
    gains_out[...] = norm_sum[0:4]
    shifts_out[...] = norm_sum[4:8]
    for stage in range(bits + 1):
        for a in range(3):
            copies.arrived(("core", a, stage))
        copies.arrived(("q both", stage))
    sometimes = ["q turn", "low"] + [("home", c) for c in range(chunks)]

    @pl.when(moves)
    def _():
        copies.arrived("low")
        for c in range(chunks):
            copies.arrived(("home", c))
        for name in sometimes:
            copies.sent(name)

    pl.when(stays)(stay[0].wait)
    copies.drain(sometimes + [("norms", step) for step in range(len(axes))])


def back(
    q, k, v, o, lse, cosine, sine, gain, norms, da, low, inputs, branches, hidden, active,
    heads, branch, whole, w, resid, middle, groups, rows=BLOCK, chunks=2,
):
    length, width = q.shape
    part, depth = da.shape
    bits = len(groups)
    slots = (2,) * bits
    slab = hidden.shape[1] // 4
    up_shape = slots + (depth // 2**bits, 4 * slab)
    out_shape = (4,) + slots + (width // 2 ** (bits + 1), depth)
    down_shape = (4,) + slots + (slab // 2**bits, depth)
    tails = (up_shape[-2:-1] + (slab,), out_shape[-2:], down_shape[-2:])
    vmem = pl.BlockSpec(memory_space=pltpu.VMEM)
    anywhere = pl.BlockSpec(memory_space=pl.ANY)
    quarter = depth // 2**bits
    q_tail = (quarter // 2, 3 * width)
    thin = slab // 2
    scratch = [
        pltpu.VMEM((4, 2) + out_shape[1:], bf16),
        pltpu.VMEM(out_shape, bf16),
        pltpu.VMEM((2,) + up_shape[:-1] + (thin,), bf16),
        pltpu.VMEM((2,) + down_shape[2:], bf16),
        pltpu.VMEM((depth, length // 2), bf16),
    ]
    scratch += [pltpu.VMEM((length, width), bf16)]
    scratch += [pltpu.VMEM((length, width), f32)] * 3 + [pltpu.VMEM((8, length), f32)]
    scratch += [
        pltpu.VMEM((length, 3 * width), bf16),
        pltpu.VMEM(whole.shape, bf16),
        pltpu.VMEM(w.shape, bf16),
        pltpu.VMEM((part, depth), bf16),
        pltpu.VMEM((part, depth), f32),
        pltpu.VMEM((3, part, depth), bf16),
        pltpu.VMEM((2, part, depth), bf16),
        pltpu.VMEM((part, depth), bf16),
        pltpu.VMEM((part, depth), f32),
        pltpu.VMEM((part, depth), bf16),
        pltpu.VMEM(slots + (2,) + q_tail, bf16),
        pltpu.VMEM((2, 2) + q_tail, bf16),
        pltpu.VMEM((8, depth), f32),
        pltpu.VMEM((bits + 3, 8, depth), f32),
    ]
    for stage in range(bits):
        for tail in tails:
            scratch.append(pltpu.VMEM((4,) + (2,) * (bits - 1 - stage) + tail, bf16))
    scratch += [pltpu.VMEM((3,) + tail, bf16) for tail in tails]
    scratch += [pltpu.VMEM((2,) + (2,) * (bits - 1) + tail, bf16) for tail in tails]
    scratch += [
        pltpu.VMEM((2,) + (2,) * (bits - 1 - stage) + q_tail, bf16) for stage in range(bits)
    ]
    n = 5 + 3 * (4 * bits + 3 + bits + bits + 1)
    n += 2 + chunks + 2 * bits + chunks + (bits + 3) + 2 + bits + bits + 1
    scratch += [pltpu.SemaphoreType.DMA((n,)), pltpu.SemaphoreType.DMA((n,))]
    scratch += [pltpu.SemaphoreType.DMA((64,))]
    return pl.pallas_call(
        functools.partial(back_kernel, groups=groups, rows=rows, chunks=chunks),
        out_shape=(
            jax.ShapeDtypeStruct((4, depth), f32),
            jax.ShapeDtypeStruct((4, depth), f32),
            jax.ShapeDtypeStruct((part, depth), bf16),
            jax.ShapeDtypeStruct((part, depth), bf16),
            jax.ShapeDtypeStruct(slots + (2,) + q_tail, bf16),
            jax.ShapeDtypeStruct(up_shape[:-1] + (2 * slab,), bf16),
            jax.ShapeDtypeStruct((2,) + out_shape[1:], bf16),
            jax.ShapeDtypeStruct((2,) + down_shape[1:], bf16),
            jax.ShapeDtypeStruct(up_shape, bf16),
            jax.ShapeDtypeStruct(out_shape, bf16),
            jax.ShapeDtypeStruct(down_shape, bf16),
        ),
        in_specs=[vmem] * 9 + [anywhere] * 12,
        out_specs=(vmem,) * 2 + (anywhere,) * 9,
        scratch_shapes=scratch,
        compiler_params=pltpu.CompilerParams(
            vmem_limit_bytes=63 * 2**20, collective_id=1, has_side_effects=True
        ),
        cost_estimate=pl.CostEstimate(
            flops=100_000_000_000, bytes_accessed=32 * 2**20, transcendentals=0
        ),
    )(
        q, k, v, o, lse, cosine, sine, gain, norms, da, low, inputs, branches, hidden, active, heads,
        branch, whole, w, resid, middle,
    )[:8]


def norm_forward(value, gain, shift):
    center = value - jnp.mean(value, axis=-1, keepdims=True)
    inverse = lax.rsqrt(jnp.mean(center * center, axis=-1, keepdims=True) + EPS)
    unit = center * inverse
    return (unit * gain + shift, unit, inverse)


def norm_backward(grad, unit, inverse, gain):
    scaled = grad * gain
    back = inverse * (
        scaled
        - jnp.mean(scaled, axis=-1, keepdims=True)
        - unit * jnp.mean(scaled * unit, axis=-1, keepdims=True)
    )
    return (back, jnp.sum(grad * unit, axis=0), jnp.sum(grad, axis=0))


def rotary_tables(length, width):
    half = HEAD_DIM // 2
    steps = (np.arange(width) % half).astype(np.float32) / np.float32(half)
    freqs = np.float32(10000.0) ** (-steps)
    angles = np.arange(length, dtype=np.float32)[:, None] * freqs[None, :]
    return (jnp.asarray(np.cos(angles)), jnp.asarray(np.sin(angles)))


SWAP = [(0, 1), (1, 0)]


def dot(left, right, dims=NN):
    return lax.dot_general(left, right, dims, preferred_element_type=f32)


def across(value, axis):
    return lax.ppermute(value, axis, SWAP)


def turn(value):
    return lax.ppermute(value, ("b", "h"), [(0, 0), (1, 2), (2, 1), (3, 3)])


def on_device(
    tokens,
    w_qkv,
    w_out,
    w_up,
    w_down,
    norm_gains,
    norm_shifts,
    cotangent,
    corpus_ids,
    corpus_weight,
    *,
    groups,
):
    _, part, depth = tokens.shape
    cols = w_qkv.shape[2]
    units = w_up.shape[1]
    core, half, near = lax.axis_index("b"), lax.axis_index("h"), lax.axis_index("l")
    length = 4 * part
    place = 2 * core + near
    group = jnp.int32(0)
    for axis in groups:
        group = 2 * group + lax.axis_index(axis)
    n_groups = 2 ** len(groups)
    stack = ("h", "l")
    cosine, sine = rotary_tables(length, 128)
    gains = [norm_gains[i : i + 1] for i in range(4)]
    shifts = [norm_shifts[i : i + 1] for i in range(4)]

    slots = (2,) * len(groups)
    q, k, v, whole_a, attended, lse, heads, resid_low, cotangent_low, w_attn, up_half, out_whole, down_half = front(
        tokens[0],
        cotangent[0],
        w_qkv.reshape(slots + (depth // n_groups, 3 * cols)),
        w_up.reshape(slots + (depth // n_groups, units)),
        w_out.reshape((2,) + slots + (cols // (2 * n_groups), depth)),
        w_down.reshape((2,) + slots + (units // (2 * n_groups), depth)),
        norm_gains,
        norm_shifts,
        cosine,
        sine,
        groups,
    )
    up_half = up_half.reshape(depth, 2 * units)
    out_whole = out_whole.reshape(4 * cols, depth)
    down_half = down_half.reshape(2 * units, depth)

    branch_a = dot(heads, out_whole)

    resid = resid_low.astype(f32)
    out_a, unit_1, inverse_1 = norm_forward(branch_a, gains[1], shifts[1])
    middle = resid + out_a
    normed_f, unit_2, inverse_2 = norm_forward(middle, gains[2], shifts[2])
    own_f = normed_f.astype(bf16)
    pair_f = jnp.concatenate([own_f, across(own_f, "b")], axis=0)
    hidden = dot(pair_f, up_half)
    cube = 0.7978845608028654 * (hidden + 0.044715 * hidden * hidden * hidden)
    bend = jnp.tanh(cube)
    active = (0.5 * hidden * (1.0 + bend)).astype(bf16)
    slope = 0.5 * (1.0 + bend) + 0.5 * hidden * (1.0 - bend * bend) * 0.7978845608028654 * (
        1.0 + 3 * 0.044715 * hidden * hidden
    )
    slope = slope.astype(bf16)
    branch_f = dot(active[part:], down_half).astype(bf16)
    branch_f = dot(active[:part], down_half) + across(branch_f, "b").astype(f32)
    out_f, unit_3, inverse_3 = norm_forward(branch_f, gains[3], shifts[3])
    output = (middle + out_f).astype(bf16)

    picks = (
        corpus_ids[:, None] == jnp.arange(corpus_weight.shape[0], dtype=jnp.int32)[None, :]
    ).astype(f32)
    row_scale = turn(jnp.dot(picks, corpus_weight, precision=lax.Precision.HIGHEST))
    grad_final = cotangent_low.astype(f32) * row_scale[:, None]
    back_3, gain_3, shift_3 = norm_backward(grad_final, unit_3, inverse_3, gains[3])
    own_g = back_3.astype(bf16)
    pair_g = jnp.concatenate([own_g, across(own_g, "b")], axis=0)
    grad_active = dot(pair_g, down_half, NT)
    grad_hidden = (slope.astype(f32) * grad_active).astype(bf16)
    grad_f = dot(grad_hidden[part:], up_half, NT).astype(bf16)
    grad_f = dot(grad_hidden[:part], up_half, NT) + across(grad_f, "b").astype(f32)
    back_2, gain_2, shift_2 = norm_backward(grad_f, unit_2, inverse_2, gains[2])
    grad_middle = grad_final + back_2
    back_1, gain_1, shift_1 = norm_backward(grad_middle, unit_1, inverse_1, gains[1])
    grad_a = back_1.astype(bf16)
    grad_attended = dot(grad_a, out_whole, NT).astype(bf16)

    none = jnp.zeros_like(gain_1)
    norms = jnp.stack([none, gain_1, gain_2, gain_3, none, shift_1, shift_2, shift_3])
    gain_grad, shift_grad, input_grad, output, qkv_grad, up_grad, out_grad, down_grad = back(
        q,
        k,
        v,
        attended,
        lse,
        cosine,
        sine,
        norm_gains,
        norms,
        grad_attended,
        output,
        pair_f,
        pair_g,
        grad_hidden,
        active,
        heads,
        grad_a,
        whole_a,
        w_attn,
        resid_low,
        grad_middle,
        groups,
    )
    input_grad = input_grad.astype(f32)
    qkv_grad = qkv_grad.reshape(depth, 3 * cols).astype(f32)
    qkv_grad = jnp.stack(jnp.split(qkv_grad, 3, axis=1), axis=1)
    up_grad = up_grad.reshape(depth, units).astype(f32)
    out_grad = out_grad.reshape(cols, depth).astype(f32)
    down_grad = down_grad.reshape(units, depth).astype(f32)
    return (
        output[None],
        input_grad[None],
        qkv_grad,
        out_grad,
        up_grad,
        down_grad,
        gain_grad,
        shift_grad,
    )


def solution(mesh):
    rows, parts = mesh.shape["dp"], mesh.shape["mp"]
    bits = (rows // 2).bit_length() - 1
    assert parts == 4 and rows == 2 ** (bits + 1)
    groups = tuple(f"g{i}" for i in range(bits))
    fine = Mesh(mesh.devices.reshape((2,) * (bits + 3)), groups + ("b", "h", "l"))
    dp, mp = groups + ("b",), ("h", "l")
    placed = (
        P(dp, mp, None),
        P(None, None, mp),
        P(mp, None),
        P(None, mp),
        P(mp, None),
        P(),
        P(),
        P(dp, mp, None),
        P(dp),
        P(),
    )
    return jax.shard_map(
        functools.partial(on_device, groups=groups),
        mesh=fine,
        in_specs=placed,
        out_specs=(
            P(dp, mp, None),
            P(dp, mp, None),
            P(None, None, mp),
            P(mp, None),
            P(None, mp),
            P(mp, None),
            P(),
            P(),
        ),
        check_vma=False,
    )
```

```python
import functools

import jax
import jax.numpy as jnp
import numpy as np
from jax import lax
from jax.experimental import pallas as pl
from jax.experimental.pallas import tpu as pltpu
from jax.sharding import Mesh, PartitionSpec as P

HEAD_DIM = 64
BLOCK = 512
EPS = 1e-05
LOG2E = 1.4426950408889634
NN = (((1,), (0,)), ((), ()))
NT = (((1,), (1,)), ((), ()))
TN = (((0,), (0,)), ((), ()))
f32 = jnp.float32
bf16 = jnp.bfloat16


def head_lanes(shape, head):
    return lax.broadcasted_iota(jnp.int32, shape, 1) // HEAD_DIM == head


def swap_halves(value, sign):
    half = HEAD_DIM // 2
    width = value.shape[1]
    first = (lax.broadcasted_iota(jnp.int32, value.shape, 1) // half) % 2 == 0
    return jnp.where(
        first, sign * pltpu.roll(value, width - half, 1), -sign * pltpu.roll(value, half, 1)
    )


MESH = pl.DeviceIdType.MESH
BACK_PLAN = {
    "front": "s1 s2",
    0: "a1 s3",
    1: "a2",
    3: "b1 r1",
    4: "s4",
    6: "a3",
    7: "b2 r2",
    9: "b3 r3",
    "x0": "a4",
    "x3": "b4 r4 end",
}
FRONT_PLAN = {
    "own": "ring",
    "near": "one",
    0: "1a",
    1: "two 1b",
    2: "2a three",
    3: "2b 3a",
    "rest": "3b",
}


class Copies:
    def __init__(self, send, recv):
        self.send, self.recv, self.made = send, recv, {}

    def describe(self, name):
        n, build = self.made[name]
        source, target, device = build()
        return pltpu.make_async_remote_copy(
            src_ref=source,
            dst_ref=target,
            send_sem=self.send.at[n],
            recv_sem=self.recv.at[n],
            device_id=device,
            device_id_type=MESH,
        )

    def plan(self, name, build):
        self.made[name] = (len(self.made), build)

    def start(self, name, build=None):
        if build is not None:
            self.plan(name, build)
        self.describe(name).start()

    def arrived(self, name):
        self.describe(name).wait_recv()

    def sent(self, name):
        self.describe(name).wait_send()

    def drain(self, but=()):
        for name in self.made:
            if name not in but:
                self.sent(name)


def flip(axis):
    return {axis: 1 - lax.axis_index(axis)}


def next_layer(step):
    at = lax.rem(2 * lax.axis_index("h") + lax.axis_index("l") + step, 4)
    return {"h": at // 2, "l": lax.rem(at, 2)}


def add_into(total, term, rows=64):
    lead, count = total.shape[:-2], total.shape[-2]
    step = next(n for n in (rows, 32, 16, 8) if count % n == 0)

    @pl.loop(0, count // step)
    def _(i):
        at = pl.ds(pl.multiple_of(i * step, step), step)
        for index in np.ndindex(*lead):
            total[index + (at,)] = (
                total[index + (at,)].astype(f32) + term[index + (at,)].astype(f32)
            ).astype(bf16)


def exclusive(a, b):
    return a + b - 2 * a * b


def forward_branch(last, heads, rows, q_ref, k_ref, v_ref, o_ref, lse_ref):
    width = q_ref.shape[1]
    n = (last + 1) * rows
    block = pl.ds(last * rows, rows)
    acc = jnp.zeros((rows, width), f32)
    logs = jnp.zeros((rows, width), f32)
    for h in range(heads):
        mine = head_lanes((rows, width), h)
        qm = jnp.where(mine, q_ref[block], jnp.zeros((), bf16))
        s = lax.dot_general(qm, k_ref[:n], NT, preferred_element_type=f32)
        row = lax.broadcasted_iota(jnp.int32, (rows, rows), 0)
        column = lax.broadcasted_iota(jnp.int32, (rows, rows), 1)
        tail = jnp.where(column <= row, s[:, n - rows :], -1e30)
        top = jnp.max(tail, axis=1, keepdims=True)
        if last:
            top = jnp.maximum(top, jnp.max(s[:, : n - rows], axis=1, keepdims=True))
        top = top * LOG2E
        vm = jnp.where(head_lanes((n, width), h), v_ref[:n], jnp.ones((), bf16))
        low = jnp.exp2(tail * LOG2E - top).astype(bf16)
        out = lax.dot_general(low, vm[n - rows :], NN, preferred_element_type=f32)
        if last:
            low = jnp.exp2(s[:, : n - rows] * LOG2E - top).astype(bf16)
            out = out + lax.dot_general(low, vm[: n - rows], NN, preferred_element_type=f32)
        total = pltpu.roll(out, HEAD_DIM, 1)
        acc = jnp.where(mine, out / total, acc)
        logs = jnp.where(mine, top + jnp.log2(total), logs)
    o_ref[block] = acc.astype(bf16)
    lane = lax.broadcasted_iota(jnp.int32, (8, width), 1)
    pick = (lane == HEAD_DIM * lax.broadcasted_iota(jnp.int32, (8, width), 0)).astype(f32)
    lse_ref[:, block] = lax.dot_general(
        pick, logs, NT, precision=lax.Precision.HIGHEST, preferred_element_type=f32
    )


def front_kernel(*refs, groups, chunks):
    (
        tok_ref, cot_ref, wq_ref, up_ref, out_ref, down_ref, gain_ref, shift_ref, cos_ref, sin_ref,
        q_ref, k_ref, v_ref, whole_ref, o_ref, lse_ref,
        heads_ref, tok_home, cot_home, w_home, up_all, out_all, down_all,
        row, w_att, bounce_up, bounce_out, bounce_down, bounce_cot,
        send, recv, local, head_send, head_recv,
    ) = refs
    bits = len(groups)
    part = tok_ref.shape[0]
    depth = tok_ref.shape[1]
    width = q_ref.shape[1]
    heads = width // HEAD_DIM
    core, half, near = lax.axis_index("b"), lax.axis_index("h"), lax.axis_index("l")
    group = [lax.axis_index(axis) for axis in groups]
    layer = 2 * half + near
    place = 2 * core + near
    stays = core == half
    moves = core != half
    partner = {"b": half, "h": core}
    copies = Copies(send, recv)
    locals_made, here = [], []

    def copy_here(source, target):
        copy = pltpu.make_async_copy(source, target, local.at[len(locals_made)])
        locals_made.append(copy)
        here.append(copy)
        copy.start()

    barrier = pltpu.get_barrier_semaphore()
    friends = [flip(axis) for axis in groups + ("b",)] + [next_layer(1), next_layer(3)]
    friends += [flip("l"), {"b": 1 - core, "l": 1 - near}]
    for friend in friends:
        pl.semaphore_signal(barrier, inc=1, device_id=friend, device_id_type=MESH)

    @pl.when(moves)
    def _():
        pl.semaphore_signal(barrier, inc=1, device_id=partner, device_id_type=MESH)
        pl.semaphore_wait(barrier, len(friends) + 1)

    @pl.when(stays)
    def _():
        pl.semaphore_wait(barrier, len(friends))

    size = part // chunks

    def piece(c):
        return pl.ds(c * size, size)

    weights = (up_ref, out_ref, down_ref)
    orders = [tuple(range(bits)), tuple(range(bits)), tuple(reversed(range(bits)))]
    slab = up_ref.shape[-1] // 2

    def slot(a, shard, at):
        if a == 0:
            return up_all.at[at + (slice(None), pl.ds(pl.multiple_of(shard * slab, slab), slab))]
        if a == 1:
            return out_all.at[(shard, core) + at]
        return down_all.at[(shard,) + at]

    def held(a, at):
        if a == 0:
            return up_ref.at[at + (slice(None), pl.ds(pl.multiple_of(core * slab, slab), slab))]
        return weights[a].at[(core,) + at]

    def shard(k):
        return lax.rem(layer + 4 - k, 4)

    def ring_send(step):
        for a in range(3):

            def build(a=a):
                at = tuple(group)
                spot = slot(a, shard(step - 1), at)
                return (held(a, at) if step == 1 else spot, spot, next_layer(1))

            copies.start(("ring", a, step), build)

    def ring_wait(step):
        for a in range(3):
            copies.arrived(("ring", a, step))

    def plane_send(k, stage):
        for a in range(3):

            def build(a=a):
                order = orders[a]
                at = tuple(
                    group[axis] if order.index(axis) >= stage else slice(None)
                    for axis in range(bits)
                )
                spot = slot(a, shard(k), at)
                return (spot, spot, flip(groups[order[stage]]))

            copies.start(("plane", a, k, stage), build)

    def plane_wait(k, stage):
        for a in range(3):
            copies.arrived(("plane", a, k, stage))

    def core_send(k):
        def build():
            spot = slot(1, shard(k), (slice(None),) * bits)
            return (spot, spot, flip("b"))

        copies.start(("core", k), build)

    def plane_next(k, stage):
        plane_wait(k, stage)
        if stage + 1 < bits:
            plane_send(k, stage + 1)
        else:
            core_send(k)

    def inner_stages(k):
        for stage in range(1, bits):
            plane_next(k, stage)

    def arrive(k):
        ring_wait(k)
        if k < 3:
            ring_send(k + 1)
        plane_send(k, 0)

    steps = {
        "ring": lambda: ring_send(1),
        "one": lambda: arrive(1),
        "two": lambda: arrive(2),
        "three": lambda: arrive(3),
        "1a": lambda: plane_next(1, 0),
        "1b": lambda: inner_stages(1),
        "2a": lambda: plane_next(2, 0),
        "2b": lambda: inner_stages(2),
        "3a": lambda: plane_next(3, 0),
        "3b": lambda: inner_stages(3),
    }

    def weights_at(point):
        for name in FRONT_PLAN.get(point, "").split():
            steps[name]()

    everything = (slice(None),) * bits
    bounces = [
        (held(0, everything), bounce_up, slot(0, layer, everything)),
        (out_ref, bounce_out, out_all.at[layer]),
        (held(2, everything), bounce_down, slot(2, layer, everything)),
    ]
    inward = []
    for source, buffer, _ in bounces:
        copy = pltpu.make_async_copy(source, buffer, local.at[len(locals_made)])
        locals_made.append(copy)
        inward.append(copy)
        copy.start()

    weights_at("start")
    own = [
        pltpu.make_async_copy(
            tok_ref.at[piece(c)], row.at[place, piece(c)], local.at[len(locals_made) + c]
        )
        for c in range(chunks)
    ]
    locals_made.extend(own)
    turned = [("turn", c) for c in range(chunks)]
    for c in range(chunks):
        copies.plan(
            turned[c],
            lambda c=c: (tok_ref.at[piece(c)], row.at[layer, piece(c)], partner),
        )
    w_here = pltpu.make_async_copy(wq_ref, w_att, local.at[len(locals_made)])
    locals_made.append(w_here)
    copies.plan("wturn", lambda: (wq_ref.at[tuple(group)], w_att.at[tuple(group)], partner))
    cot_in = pltpu.make_async_copy(cot_ref, bounce_cot, local.at[len(locals_made)])
    locals_made.append(cot_in)
    cot_here = pltpu.make_async_copy(bounce_cot, cot_home, local.at[len(locals_made)])
    locals_made.append(cot_here)
    copies.plan("cot", lambda: (cot_ref, cot_home, partner))

    @pl.when(moves)
    def _():
        for c in range(chunks):
            copies.start(turned[c])
        copies.start("wturn")

    @pl.when(stays)
    def _():
        for c in range(chunks):
            own[c].start()
        w_here.start()
        cot_in.start()

    for c in range(chunks):
        pl.when(moves)(functools.partial(copies.arrived, turned[c]))
        pl.when(stays)(own[c].wait)
        for name, axis in (("near", "l"), ("core own", "b")):
            copies.start(
                (name, c),
                lambda c=c, axis=axis: (
                    row.at[place, piece(c)],
                    row.at[place, piece(c)],
                    flip(axis),
                ),
            )
    copy_here(row.at[place], tok_home)
    for copy in inward:
        copy.wait()
    for _, buffer, target in bounces:
        copy_here(buffer, target)
    weights_at("own")

    @pl.when(stays)
    def _():
        w_here.wait()

    parts = [pl.ds(i * (w_att.shape[-2] // 2), w_att.shape[-2] // 2) for i in range(2)]
    w_orders = [orders[0], orders[2]]
    for stage in range(bits):
        for i in range(2):

            def build(stage=stage, i=i):
                order = w_orders[i]
                at = tuple(
                    group[axis] if order.index(axis) >= stage else slice(None)
                    for axis in range(bits)
                )
                spot = w_att.at[at + (parts[i],)]
                return (spot, spot, flip(groups[order[stage]]))

            copies.plan(("w", stage, i), build)

    @pl.when(moves)
    def _():
        copies.arrived("wturn")
        for stage in range(bits):
            for i in range(2):
                copies.start(("w", stage, i))
            for i in range(2):
                copies.arrived(("w", stage, i))

    copy_here(w_att, w_home)
    near_block = 2 * core + 1 - near

    def pass_on():
        for c in range(chunks):
            copies.arrived(("near", c))
            copies.start(
                ("core near", c),
                lambda c=c: (row.at[near_block, piece(c)], row.at[near_block, piece(c)], flip("b")),
            )
        weights_at("near")

    def wait_all(name):
        def run():
            for c in range(chunks):
                copies.arrived((name, c))

        return run

    @pl.loop(0, 4)
    def _(r):
        far_core, far_near = lax.rem(r, 2), r // 2
        block = 2 * exclusive(core, far_core) + exclusive(near, far_near)
        pl.when(r == 1)(wait_all("core own"))
        pl.when(r == 2)(pass_on)
        pl.when(r == 3)(wait_all("core near"))

        @pl.loop(0, 2)
        def _(c):
            rows = part // 2
            inside = pl.ds(pl.multiple_of(c * rows, rows), rows)
            at = pl.ds(pl.multiple_of(block * part + c * rows, rows), rows)
            value = row[block, inside].astype(f32)
            center = value - jnp.mean(value, axis=1, keepdims=True)
            inverse = lax.rsqrt(jnp.mean(center * center, axis=1, keepdims=True) + EPS)
            normed = (center * inverse * gain_ref[0:1] + shift_ref[0:1]).astype(bf16)
            whole_ref[at] = normed
            w = w_att[...].reshape(depth, 3 * width)
            mixed = jnp.dot(normed, w, preferred_element_type=f32)
            cosine = jnp.concatenate([cos_ref[at]] * (width // 128), axis=1)
            sine = jnp.concatenate([sin_ref[at]] * (width // 128), axis=1)
            query, key = mixed[:, :width], mixed[:, width : 2 * width]
            query = HEAD_DIM ** (-0.5) * (query * cosine + swap_halves(query, -1.0) * sine)
            q_ref[at] = query.astype(bf16)
            k_ref[at] = (key * cosine + swap_halves(key, -1.0) * sine).astype(bf16)
            v_ref[at] = mixed[:, 2 * width :].astype(bf16)

    def head_copy(mask):
        far_core, far_near = mask // 2, lax.rem(mask, 2)
        to_core, to_near = exclusive(core, far_core), exclusive(near, far_near)
        block = 2 * to_core + to_near
        rows = pl.ds(pl.multiple_of(block * part, part), part)
        columns = pl.ds(pl.multiple_of(place * width, width), width)
        return pltpu.make_async_remote_copy(
            src_ref=o_ref.at[rows],
            dst_ref=heads_ref.at[:, columns],
            send_sem=head_send.at[mask],
            recv_sem=head_recv.at[mask],
            device_id={"b": to_core, "l": to_near},
            device_id_type=MESH,
        )

    @pl.loop(0, 4)
    def _(r):
        far_core, far_near = 1 - lax.rem(r, 2), 1 - r // 2
        mask = 2 * far_core + far_near
        block = 2 * exclusive(core, far_core) + exclusive(near, far_near)
        for n in range(4):
            pl.when(r == n)(functools.partial(weights_at, n))
        for i in range(4):
            pl.when(block == i)(
                functools.partial(
                    forward_branch, i, heads, part, q_ref, k_ref, v_ref, o_ref, lse_ref
                )
            )

        @pl.when(r < 3)
        def _():
            head_copy(mask).start()

    copy_here(
        o_ref.at[pl.ds(pl.multiple_of(place * part, part), part)],
        heads_ref.at[:, pl.ds(pl.multiple_of(place * width, width), width)],
    )

    @pl.when(moves)
    def _():
        copies.start("cot")

    @pl.when(stays)
    def _():
        cot_in.wait()
        cot_here.start()

    weights_at("rest")
    for mask in (1, 2, 3):
        copy = head_copy(jnp.int32(mask))
        copy.wait_send()
        copy.wait_recv()
    for k in (1, 2, 3):
        copies.arrived(("core", k))
    sometimes = turned + ["wturn", "cot"] + [("w", s, i) for s in range(bits) for i in range(2)]

    @pl.when(moves)
    def _():
        copies.arrived("cot")
        for name in sometimes:
            copies.sent(name)

    @pl.when(stays)
    def _():
        cot_here.wait()

    for copy in here:
        copy.wait()
    copies.drain(sometimes)


def front(tok, cot, wq, up, out, down, gain, shift, cosine, sine, groups, chunks=2):
    part, depth = tok.shape
    length = 4 * part
    width = wq.shape[-1] // 3
    bits = len(groups)
    vmem = pl.BlockSpec(memory_space=pltpu.VMEM)
    anywhere = pl.BlockSpec(memory_space=pl.ANY)

    def shape(*dims):
        return jax.ShapeDtypeStruct(dims, bf16)

    n = 2 * chunks + 2 + 3 * chunks + 2 * bits + 3 * 3 + 9 * bits + 3 + 4
    return pl.pallas_call(
        functools.partial(front_kernel, groups=groups, chunks=chunks),
        out_shape=(
            shape(length, width),
            shape(length, width),
            shape(length, width),
            shape(length, depth),
            shape(length, width),
            jax.ShapeDtypeStruct((8, length), f32),
            shape(part, depth),
            shape(part, depth),
            shape(part, depth),
            shape(*wq.shape),
            shape(*up.shape[:-1], 2 * up.shape[-1]),
            shape(4, *out.shape),
            shape(4, *down.shape[1:]),
        ),
        in_specs=[anywhere] * 6 + [vmem] * 4,
        out_specs=(vmem,) * 6 + (anywhere,) * 7,
        scratch_shapes=[
            pltpu.VMEM((4, part, depth), bf16),
            pltpu.VMEM(wq.shape, bf16),
            pltpu.VMEM(up.shape[:-1] + (up.shape[-1] // 2,), bf16),
            pltpu.VMEM(out.shape, bf16),
            pltpu.VMEM(down.shape[1:], bf16),
            pltpu.VMEM((part, depth), bf16),
            pltpu.SemaphoreType.DMA((n,)),
            pltpu.SemaphoreType.DMA((n,)),
            pltpu.SemaphoreType.DMA((32,)),
            pltpu.SemaphoreType.DMA((4,)),
            pltpu.SemaphoreType.DMA((4,)),
        ],
        compiler_params=pltpu.CompilerParams(
            vmem_limit_bytes=58 * 2**20, collective_id=2, has_side_effects=True
        ),
        cost_estimate=pl.CostEstimate(
            flops=100_000_000_000, bytes_accessed=32 * 2**20, transcendentals=0
        ),
    )(tok, cot, wq, up, out, down, gain, shift, cosine, sine)

def back_kernel(*refs, groups, rows, chunks):
    (
        q_ref, k_ref, v_ref, o_ref, lse_ref, cos_ref, sin_ref, gain_ref, norms_ref,
        da_ref, low_ref, own_in, other_in, own_branch, other_branch, own_hidden, other_hidden, own_active, other_active,
        heads_ref, branch_ref,
        whole_ref, w_ref, resid_ref, middle_ref,
        gains_out, shifts_out, grad_home, low_home, qkv_all, up_all, out_all, down_all,
        up_ref, out_ref, down_ref,
        out_part, out_in, up_tile, down_tile, turned,
        do, dq, dk, dv, delta, mixed, whole, w, resid, middle,
        sent, from_core, from_near, grad_x, grad_low, qkv_sum, qkv_core, norm_sum, norm_in,
        *rest,
    ) = refs
    bits = len(groups)
    terms = (up_ref, out_ref, down_ref)
    partial = [[rest[3 * s + a] for s in range(bits)] for a in range(3)]
    rest = rest[3 * bits :]
    passing, staged, rest = rest[:3], rest[3:6], rest[6:]
    qkv_in, (send, recv, local) = rest[:bits], rest[bits:]
    copies = Copies(send, recv)
    group = [lax.axis_index(axis) for axis in groups]
    core, half, near = lax.axis_index("b"), lax.axis_index("h"), lax.axis_index("l")
    layer = 2 * half + near
    place = 2 * core + near
    moves, stays = core != half, core == half
    partner = {"b": half, "h": core}
    orders = [tuple(range(bits)), tuple(range(bits)), tuple(reversed(range(bits)))]
    part, depth = da_ref.shape
    length, width = q_ref.shape
    heads = width // HEAD_DIM
    blocks = length // rows
    slab = up_ref.shape[-1] // 4
    quarter = depth // 2**bits
    all_local = [0]

    def local_copy(source, target):
        n = all_local[0]
        all_local[0] += 1
        return pltpu.make_async_copy(source, target, local.at[n])

    def columns(which, size):
        return pl.ds(pl.multiple_of(which * size, size), size)

    def shard(k):
        return lax.rem(layer + 4 - k, 4)

    def term(a, k, at):
        if a == 0:
            return up_ref.at[at + (slice(None), columns(shard(k), slab))]
        return terms[a].at[(shard(k),) + at]

    def result(a, at):
        if a == 0:
            return up_all.at[at + (slice(None), columns(core, slab))]
        return (None, out_all, down_all)[a].at[(core,) + at]

    def split(order, stage, side):
        at = []
        for axis in range(bits):
            when = order.index(axis)
            if when == stage:
                at.append(group[axis] if side == 0 else 1 - group[axis])
            elif when > stage:
                at.append(slice(None))
        return tuple(at)

    def source(a, k, stage, side):
        at = split(orders[a], stage, side)
        if stage == 0:
            return term(a, k, at) if side else staged[a].at[k % 2]
        return partial[a][stage - 1].at[(k % 4,) + at]

    loads = {}

    def plane_send(k, stage):
        for a in range(3):
            copies.start(
                ("plane", a, k, stage),
                lambda a=a: (
                    source(a, k, stage, 1),
                    partial[a][stage].at[k % 4],
                    flip(groups[orders[a][stage]]),
                ),
            )
            if stage == 0:
                loads[a, k] = local_copy(term(a, k, split(orders[a], 0, 0)), staged[a].at[k % 2])
                loads[a, k].start()

    def plane_add(k, stage):
        for a in range(3):
            copies.arrived(("plane", a, k, stage))
            if stage == 0:
                loads[a, k].wait()
            add_into(partial[a][stage].at[k % 4], source(a, k, stage, 0))

    def plane_step(k, stage):
        plane_add(k, stage)
        if stage + 1 < bits:
            plane_send(k, stage + 1)

    def ring_send(step):
        for a in range(3):
            held = partial[a][bits - 1].at[1] if step == 1 else passing[a].at[step - 2]
            target = passing[a].at[step - 1]
            copies.start(
                ("ring", a, step), lambda held=held, target=target: (held, target, next_layer(1))
            )

    def ring_add(step):
        for a in range(3):
            copies.arrived(("ring", a, step))
            add_into(passing[a].at[step - 1], partial[a][bits - 1].at[(step + 1) % 4])

    def gather_send(stage):
        for a in range(3):
            order = orders[a]
            at = tuple(
                group[axis] if order.index(axis) >= stage else slice(None) for axis in range(bits)
            )
            held = passing[a].at[2] if stage == 0 else result(a, at)
            spot, axis = result(a, at), groups[order[stage]]
            copies.start(
                ("gather", a, stage),
                lambda held=held, spot=spot, axis=axis: (held, spot, flip(axis)),
            )

    def brought(order, stage):
        at = []
        for axis in range(bits):
            when = order.index(axis)
            if stage == 0 or when > stage - 1:
                at.append(group[axis])
            elif when == stage - 1:
                at.append(1 - group[axis])
            else:
                at.append(slice(None))
        return tuple(at)

    def core_send(stage):
        for a in range(3):
            spot = result(a, brought(orders[a], stage))
            held = passing[a].at[2] if stage == 0 else spot
            copies.start(("core", a, stage), lambda held=held, spot=spot: (held, spot, flip("b")))

    barrier = pltpu.get_barrier_semaphore()
    friends = [flip(axis) for axis in groups + ("b", "h", "l")] + [next_layer(1), next_layer(3)]
    friends += [{"b": 1 - core, "l": 1 - near}]
    for friend in friends:
        pl.semaphore_signal(barrier, inc=1, device_id=friend, device_id_type=MESH)

    @pl.when(moves)
    def _():
        pl.semaphore_signal(barrier, inc=1, device_id=partner, device_id_type=MESH)
        pl.semaphore_wait(barrier, len(friends) + 1)

    @pl.when(stays)
    def _():
        pl.semaphore_wait(barrier, len(friends))

    for mask in (3, 1, 2):
        to_core, to_near = exclusive(core, mask // 2), exclusive(near, mask % 2)

        def build(to_core=to_core, to_near=to_near):
            return (
                da_ref.at[:, columns(2 * to_core + to_near, width)],
                do.at[columns(place, part)],
                {"b": to_core, "l": to_near},
            )

        copies.start(("heads", mask), build)
    own_heads = local_copy(da_ref.at[:, columns(place, width)], do.at[columns(place, part)])
    own_heads.start()
    low_in = local_copy(low_ref, grad_low)
    low_here = local_copy(grad_low, low_home)
    copies.plan("low", lambda: (low_ref, low_home, partner))
    pl.when(moves)(functools.partial(copies.start, "low"))
    pl.when(stays)(low_in.start)

    pieces = 2
    thin = slab // pieces
    pair = whole.shape[0] // 2
    units = [
        local_copy(source, whole.at[pl.ds(n * part, part)])
        for n, source in enumerate((own_in, other_in, own_branch, other_branch))
    ]
    units += [local_copy(heads_ref, sent.at[0]), local_copy(branch_ref, sent.at[1])]
    for copy in units:
        copy.start()

    def hidden_load(u):
        spot = columns(pieces * shard(1 + u // pieces) + lax.rem(u, pieces), thin)
        at = columns(lax.rem(u, 3), thin)
        semaphore = hidden_local + 4 * lax.rem(u, 3)
        return [
            pltpu.make_async_copy(
                source.at[:, spot], mixed.at[pl.ds(n * part, part), at], local.at[semaphore + n]
            )
            for n, source in enumerate((own_hidden, other_hidden, own_active, other_active))
        ]

    hidden_local = all_local[0]
    all_local[0] += 12
    for u in range(2):
        for copy in hidden_load(jnp.int32(u)):
            copy.start()
    for copy in units:
        copy.wait()
    @pl.loop(0, 4)
    def _(s):
        block = lax.dot_general(
            sent[0, :, columns(s, width)], sent[1], TN, preferred_element_type=f32
        ).astype(bf16)
        out_part[s] = block.reshape(out_part.shape[1:])

    @pl.loop(0, 4)
    def _(c):
        turned[columns(c, depth // 4)] = whole[:pair, columns(c, depth // 4)].T

    copies.start("out core", lambda: (out_part.at[:, 1 - core], out_in, flip("b")))
    def shard_gradients(k):
        @pl.loop(0, pieces)
        def _(n):
            u = pieces * (k - 1) + n
            for copy in hidden_load(u):
                copy.wait()

            @pl.when(u + 2 < 4 * pieces)
            def _():
                for copy in hidden_load(u + 2):
                    copy.start()

            buffer = columns(lax.rem(u, 3), thin)

            @pl.loop(0, 2**bits)
            def _(c):
                slot = tuple(lax.rem(c // 2 ** (bits - 1 - i), 2) for i in range(bits))
                up_tile[(n,) + slot] = jnp.dot(
                    turned[columns(c, quarter)],
                    mixed[:pair, buffer],
                    preferred_element_type=f32,
                ).astype(bf16)

            block = lax.dot_general(
                mixed[pair:, buffer], whole[pair:], TN, preferred_element_type=f32
            )
            down_tile[n] = block.astype(bf16).reshape(down_tile.shape[1:])

        if k == 1:
            copies.arrived("out core")

            @pl.loop(0, 4)
            def _(s):
                out_in[s] = (out_in[s].astype(f32) + out_part[s, core].astype(f32)).astype(bf16)

            put = local_copy(out_in, out_ref)
            put.start()
            put.wait()
        made = []
        for u in range(pieces):
            spot = (slice(None),) * (bits + 1) + (columns(pieces * shard(k) + u, thin),)
            made.append(local_copy(up_tile.at[u], up_ref.at[spot]))
            made.append(local_copy(down_tile.at[u], down_ref.at[shard(k), u]))
        for copy in made:
            copy.start()
        for copy in made:
            copy.wait()

    whole_load = local_copy(whole_ref, whole)

    def begin(k):
        shard_gradients(k)
        if k == 4:
            whole_load.start()
        plane_send(k, 0)

    def last_stages(k):
        for stage in range(1, bits):
            plane_step(k, stage)

    def ring(step):
        if step > 1:
            ring_add(step - 1)
        if step < 4:
            ring_send(step)

    own = [local_copy(passing[a].at[2], result(a, tuple(group))) for a in range(3)]

    def finish():
        core_send(0)
        gather_send(0)
        for copy in own:
            copy.start()

    kinds = {"s": begin, "a": lambda k: plane_step(k, 0), "b": last_stages, "r": ring}

    def sums_at(point):
        for name in BACK_PLAN.get(point, "").split():
            if name == "end":
                finish()
            else:
                kinds[name[0]](int(name[1]))

    sums_at("front")
    early = [
        local_copy(w_ref, w),
        local_copy(resid_ref, resid),
        local_copy(middle_ref, middle),
    ]
    for copy in early:
        copy.start()

    @pl.when(stays)
    def _():
        low_in.wait()
        low_here.start()

    for total in (dq, dk, dv):
        total[...] = jnp.zeros_like(total)
    own_heads.wait()
    for mask in (2, 1, 3):
        copies.arrived(("heads", mask))

    lane_head = lax.broadcasted_iota(jnp.int32, (8, width), 1) // HEAD_DIM
    marks = (lane_head == lax.broadcasted_iota(jnp.int32, (8, width), 0)).astype(f32)

    def span(i):
        return pl.ds(pl.multiple_of(i * rows, rows), rows)

    @pl.loop(0, blocks)
    def _(i):
        product = do[span(i)].astype(f32) * o_ref[span(i)].astype(f32)
        delta[:, span(i)] = lax.dot_general(
            marks, product, NT, precision=lax.Precision.HIGHEST, preferred_element_type=f32
        )

    def tile(i, j):
        at, to = span(i), span(j)
        keys, values = k_ref[to], v_ref[to]
        queries, grads = q_ref[at], do[at]
        dkj, dvj, dqi = dk[to], dv[to], dq[at]
        zero = jnp.zeros((), bf16)
        key = j * rows + lax.broadcasted_iota(jnp.int32, (rows, rows), 0)
        query = i * rows + lax.broadcasted_iota(jnp.int32, (rows, rows), 1)
        allowed = key <= query
        for h in range(heads):
            mine = head_lanes((rows, width), h)
            qm = jnp.where(mine, queries, zero)
            dom = jnp.where(mine, grads, zero)
            km = jnp.where(mine, keys, zero)
            st = lax.dot_general(keys, qm, NT, preferred_element_type=f32)
            pt = jnp.where(allowed, jnp.exp2(st * LOG2E - lse_ref[h : h + 1, at]), 0.0)
            dpt = lax.dot_general(values, dom, NT, preferred_element_type=f32)
            dst = (pt * (dpt - delta[h : h + 1, at])).astype(bf16)
            dvj = dvj + jnp.dot(pt.astype(bf16), dom, preferred_element_type=f32)
            dkj = dkj + jnp.dot(dst, qm, preferred_element_type=f32)
            dqi = dqi + lax.dot_general(dst, km, TN, preferred_element_type=f32)
        dq[at], dk[to], dv[to] = dqi, dkj, dvj

    count = blocks * (blocks + 1) // 2

    def tiles(low, high):
        @pl.loop(low, high)
        def _(t):
            i = jnp.int32(0)
            for n in range(1, blocks):
                i = i + (t >= n * (n + 1) // 2).astype(jnp.int32)
            tile(i, t - i * (i + 1) // 2)

    low = 0
    for point in range(10):
        when = point * count // 10
        if point in BACK_PLAN:
            if when > low:
                tiles(low, when)
            sums_at(point)
            low = when
    tiles(low, count)

    def turn_back(grad, at):
        cosine = jnp.concatenate([cos_ref[at]] * (width // 128), axis=1)
        sine = jnp.concatenate([sin_ref[at]] * (width // 128), axis=1)
        return grad * cosine + swap_halves(grad, 1.0) * sine

    @pl.loop(0, blocks)
    def _(i):
        at = span(i)
        mixed[at, :width] = (HEAD_DIM ** (-0.5) * turn_back(dq[at], at)).astype(bf16)
        mixed[at, width : 2 * width] = turn_back(dk[at], at).astype(bf16)
        mixed[at, 2 * width :] = dv[at].astype(bf16)

    for copy in early:
        copy.wait()
    size = part // chunks

    def input_part(block, c):
        at = pl.ds(pl.multiple_of(block * part + c * size, size), size)
        return lax.dot_general(
            mixed[at], w[...].reshape(depth, 3 * width), NT, preferred_element_type=f32
        )

    def inside(c):
        return pl.ds(pl.multiple_of(c * size, size), size)

    for slot in range(2):
        block = 2 * (1 - core) + (1 - near if slot == 0 else near)

        @pl.loop(0, chunks)
        def _(c):
            sent[slot, inside(c)] = input_part(block, c).astype(bf16)

        copies.start(
            ("x core", slot),
            lambda slot=slot: (sent.at[slot], from_core.at[slot], flip("b")),
        )
    sums_at("x0")
    copies.arrived(("x core", 0))
    for c in range(chunks):
        total = input_part(2 * core + 1 - near, c) + from_core[0, inside(c)].astype(f32)
        sent[2, inside(c)] = total.astype(bf16)
        copies.start(
            ("x near", c),
            lambda c=c: (sent.at[2, inside(c)], from_near.at[inside(c)], flip("l")),
        )
    sums_at("x1")
    whole_load.wait()
    side = quarter // 2
    for index in np.ndindex(*(2,) * bits):
        first = sum(bit << (bits - 1 - axis) for axis, bit in enumerate(index)) * quarter
        block = lax.dot_general(
            whole[:, first : first + quarter], mixed[...], TN, preferred_element_type=f32
        ).astype(bf16)
        for i in range(2):
            qkv_sum[index + (i,)] = block[i * side : (i + 1) * side]
    q_orders = [orders[0], orders[2]]

    def q_slot(i, stage, side):
        order = q_orders[i]
        at = []
        for axis in range(bits):
            when = order.index(axis)
            if when < stage:
                at.append(group[axis])
            elif when == stage:
                at.append(group[axis] if side == 0 else 1 - group[axis])
            else:
                at.append(slice(None))
        return qkv_sum.at[tuple(at) + (i,)]

    def q_send(stage):
        for i in range(2):
            copies.start(
                ("q", i, stage),
                lambda i=i: (
                    q_slot(i, stage, 1),
                    qkv_in[stage].at[i],
                    flip(groups[q_orders[i][stage]]),
                ),
            )

    def q_add(stage):
        for i in range(2):
            copies.arrived(("q", i, stage))
            add_into(q_slot(i, stage, 0), qkv_in[stage].at[i])

    q_send(0)
    sums_at("x2")
    copies.arrived(("x core", 1))

    @pl.loop(0, chunks)
    def _(c):
        grad_x[inside(c)] = input_part(place, c) + from_core[1, inside(c)].astype(f32)

    own_q = tuple(group)
    axes = groups + ("b", "h", "l")

    def norms_send(step):
        copies.start(("norms", step), lambda: (norm_sum, norm_in.at[step], flip(axes[step])))

    def norms_add(step):
        copies.arrived(("norms", step))
        copies.sent(("norms", step))
        norm_sum[...] += norm_in[step]

    pl.when(stays)(low_here.wait)
    norm_sum[...] = norms_ref[...]
    fine = min(128, size)

    def home(c):
        copies.arrived(("x near", c))

        @pl.loop(0, size // fine)
        def _(s):
            at = pl.ds(pl.multiple_of(c * size + s * fine, fine), fine)
            grad = grad_x[at] + from_near[at].astype(f32)
            value = resid[at].astype(f32)
            center = value - jnp.mean(value, axis=1, keepdims=True)
            inverse = lax.rsqrt(jnp.mean(center * center, axis=1, keepdims=True) + EPS)
            unit = center * inverse
            scaled = grad * gain_ref[0:1]
            back = inverse * (
                scaled
                - jnp.mean(scaled, axis=1, keepdims=True)
                - unit * jnp.mean(scaled * unit, axis=1, keepdims=True)
            )
            grad_low[at] = (middle[at] + back).astype(bf16)
            norm_sum[0:1] += jnp.sum(grad * unit, axis=0, keepdims=True)
            norm_sum[4:5] += jnp.sum(grad, axis=0, keepdims=True)

        copies.plan(
            ("home", c), lambda c=c: (grad_low.at[inside(c)], grad_home.at[inside(c)], partner)
        )
        pl.when(moves)(functools.partial(copies.start, ("home", c)))

    def gather_next(stage):
        for a in range(3):
            copies.arrived(("gather", a, stage))
        if stage + 1 < bits:
            gather_send(stage + 1)
        core_send(stage + 1)

    def q_spot(at):
        return qkv_all.at[at + (core,)]

    keep_q = local_copy(qkv_core.at[1, core], q_spot(own_q))
    def q_gather(stage):
        at = tuple(group[axis] if axis >= stage else slice(None) for axis in range(bits))
        held = qkv_core.at[1, core] if stage == 0 else q_spot(at)
        copies.start(("q gather", stage), lambda: (held, q_spot(at), flip(groups[stage])))

    def q_core_send(stage):
        spot = q_spot(brought(orders[0], stage))
        held = qkv_core.at[1, core] if stage == 0 else spot
        copies.start(("q both", stage), lambda: (held, spot, flip("b")))

    sums_at("x3")
    half_way = chunks // 2
    for c in range(half_way):
        home(c)
    sums_at("x4")
    for stage in range(bits):
        q_add(stage)
        if stage + 1 < bits:
            q_send(stage + 1)

    copies.plan("q turn", lambda: (qkv_sum.at[own_q], qkv_core.at[0], partner))
    pl.when(moves)(functools.partial(copies.start, "q turn"))
    sums_at("x5")
    for c in range(half_way, chunks):
        home(c)
    stay = [local_copy(grad_low, grad_home)]
    pl.when(stays)(stay[0].start)
    norms_send(0)
    sums_at("x6")
    for copy in own:
        copy.wait()
    gather_next(0)

    @pl.when(moves)
    def _():
        copies.arrived("q turn")

    @pl.when(stays)
    def _():
        qkv_core[0] = qkv_sum[own_q]

    copies.start("q core", lambda: (qkv_core.at[0, 1 - core], qkv_core.at[1, 1 - core], flip("b")))
    norms_add(0)
    norms_send(1)
    copies.arrived("q core")
    add_into(qkv_core.at[1, core], qkv_core.at[0, core])
    keep_q.start()
    q_gather(0)
    q_core_send(0)
    keep_q.wait()
    norms_add(1)
    norms_send(2)
    for stage in range(1, bits):
        gather_next(stage)
    for stage in range(bits):
        copies.arrived(("q gather", stage))
        if stage + 1 < bits:
            q_gather(stage + 1)
        q_core_send(stage + 1)
    for step in range(2, len(axes)):
        norms_add(step)
        if step + 1 < len(axes):
            norms_send(step + 1)
    gains_out[...] = norm_sum[0:4]
    shifts_out[...] = norm_sum[4:8]
    for stage in range(bits + 1):
        for a in range(3):
            copies.arrived(("core", a, stage))
        copies.arrived(("q both", stage))
    sometimes = ["q turn", "low"] + [("home", c) for c in range(chunks)]

    @pl.when(moves)
    def _():
        copies.arrived("low")
        for c in range(chunks):
            copies.arrived(("home", c))
        for name in sometimes:
            copies.sent(name)

    pl.when(stays)(stay[0].wait)
    copies.drain(sometimes + [("norms", step) for step in range(len(axes))])


def back(
    q, k, v, o, lse, cosine, sine, gain, norms, da, low, own, other, heads, branch, whole, w, resid, middle, groups, rows=BLOCK, chunks=2,
):
    length, width = q.shape
    part, depth = da.shape
    bits = len(groups)
    slots = (2,) * bits
    slab = own[2].shape[1] // 4
    up_shape = slots + (depth // 2**bits, 4 * slab)
    out_shape = (4,) + slots + (width // 2 ** (bits + 1), depth)
    down_shape = (4,) + slots + (slab // 2**bits, depth)
    tails = (up_shape[-2:-1] + (slab,), out_shape[-2:], down_shape[-2:])
    vmem = pl.BlockSpec(memory_space=pltpu.VMEM)
    anywhere = pl.BlockSpec(memory_space=pl.ANY)
    quarter = depth // 2**bits
    q_tail = (quarter // 2, 3 * width)
    thin = slab // 2
    scratch = [
        pltpu.VMEM((4, 2) + out_shape[1:], bf16),
        pltpu.VMEM(out_shape, bf16),
        pltpu.VMEM((2,) + up_shape[:-1] + (thin,), bf16),
        pltpu.VMEM((2,) + down_shape[2:], bf16),
        pltpu.VMEM((depth, length // 2), bf16),
    ]
    scratch += [pltpu.VMEM((length, width), bf16)]
    scratch += [pltpu.VMEM((length, width), f32)] * 3 + [pltpu.VMEM((8, length), f32)]
    scratch += [
        pltpu.VMEM((length, 3 * width), bf16),
        pltpu.VMEM(whole.shape, bf16),
        pltpu.VMEM(w.shape, bf16),
        pltpu.VMEM((part, depth), bf16),
        pltpu.VMEM((part, depth), f32),
        pltpu.VMEM((3, part, depth), bf16),
        pltpu.VMEM((2, part, depth), bf16),
        pltpu.VMEM((part, depth), bf16),
        pltpu.VMEM((part, depth), f32),
        pltpu.VMEM((part, depth), bf16),
        pltpu.VMEM(slots + (2,) + q_tail, bf16),
        pltpu.VMEM((2, 2) + q_tail, bf16),
        pltpu.VMEM((8, depth), f32),
        pltpu.VMEM((bits + 3, 8, depth), f32),
    ]
    for stage in range(bits):
        for tail in tails:
            scratch.append(pltpu.VMEM((4,) + (2,) * (bits - 1 - stage) + tail, bf16))
    scratch += [pltpu.VMEM((3,) + tail, bf16) for tail in tails]
    scratch += [pltpu.VMEM((2,) + (2,) * (bits - 1) + tail, bf16) for tail in tails]
    scratch += [
        pltpu.VMEM((2,) + (2,) * (bits - 1 - stage) + q_tail, bf16) for stage in range(bits)
    ]
    n = 5 + 3 * (4 * bits + 3 + bits + bits + 1)
    n += 2 + chunks + 2 * bits + chunks + (bits + 3) + 2 + bits + bits + 1
    scratch += [pltpu.SemaphoreType.DMA((n,)), pltpu.SemaphoreType.DMA((n,))]
    scratch += [pltpu.SemaphoreType.DMA((64,))]
    return pl.pallas_call(
        functools.partial(back_kernel, groups=groups, rows=rows, chunks=chunks),
        out_shape=(
            jax.ShapeDtypeStruct((4, depth), f32),
            jax.ShapeDtypeStruct((4, depth), f32),
            jax.ShapeDtypeStruct((part, depth), bf16),
            jax.ShapeDtypeStruct((part, depth), bf16),
            jax.ShapeDtypeStruct(slots + (2,) + q_tail, bf16),
            jax.ShapeDtypeStruct(up_shape[:-1] + (2 * slab,), bf16),
            jax.ShapeDtypeStruct((2,) + out_shape[1:], bf16),
            jax.ShapeDtypeStruct((2,) + down_shape[1:], bf16),
            jax.ShapeDtypeStruct(up_shape, bf16),
            jax.ShapeDtypeStruct(out_shape, bf16),
            jax.ShapeDtypeStruct(down_shape, bf16),
        ),
        in_specs=[vmem] * 9 + [anywhere] * 16,
        out_specs=(vmem,) * 2 + (anywhere,) * 9,
        scratch_shapes=scratch,
        compiler_params=pltpu.CompilerParams(
            vmem_limit_bytes=63 * 2**20, collective_id=1, has_side_effects=True
        ),
        cost_estimate=pl.CostEstimate(
            flops=100_000_000_000, bytes_accessed=32 * 2**20, transcendentals=0
        ),
    )(
        q, k, v, o, lse, cosine, sine, gain, norms, da, low,
        own[0], other[0], own[1], other[1], own[2], other[2], own[3], other[3],
        heads, branch, whole, w, resid, middle,
    )[:8]


def norm_forward(value, gain, shift):
    center = value - jnp.mean(value, axis=-1, keepdims=True)
    inverse = lax.rsqrt(jnp.mean(center * center, axis=-1, keepdims=True) + EPS)
    unit = center * inverse
    return (unit * gain + shift, unit, inverse)


def norm_backward(grad, unit, inverse, gain):
    scaled = grad * gain
    back = inverse * (
        scaled
        - jnp.mean(scaled, axis=-1, keepdims=True)
        - unit * jnp.mean(scaled * unit, axis=-1, keepdims=True)
    )
    return (back, jnp.sum(grad * unit, axis=0), jnp.sum(grad, axis=0))


def rotary_tables(length, width):
    half = HEAD_DIM // 2
    steps = (np.arange(width) % half).astype(np.float32) / np.float32(half)
    freqs = np.float32(10000.0) ** (-steps)
    angles = np.arange(length, dtype=np.float32)[:, None] * freqs[None, :]
    return (jnp.asarray(np.cos(angles)), jnp.asarray(np.sin(angles)))


SWAP = [(0, 1), (1, 0)]


def dot(left, right, dims=NN):
    return lax.dot_general(left, right, dims, preferred_element_type=f32)


def across(value, axis):
    return lax.ppermute(value, axis, SWAP)


def turn(value):
    return lax.ppermute(value, ("b", "h"), [(0, 0), (1, 2), (2, 1), (3, 3)])


def on_device(
    tokens,
    w_qkv,
    w_out,
    w_up,
    w_down,
    norm_gains,
    norm_shifts,
    cotangent,
    corpus_ids,
    corpus_weight,
    *,
    groups,
):
    _, part, depth = tokens.shape
    cols = w_qkv.shape[2]
    units = w_up.shape[1]
    core, half, near = lax.axis_index("b"), lax.axis_index("h"), lax.axis_index("l")
    length = 4 * part
    place = 2 * core + near
    group = jnp.int32(0)
    for axis in groups:
        group = 2 * group + lax.axis_index(axis)
    n_groups = 2 ** len(groups)
    stack = ("h", "l")
    cosine, sine = rotary_tables(length, 128)
    gains = [norm_gains[i : i + 1] for i in range(4)]
    shifts = [norm_shifts[i : i + 1] for i in range(4)]

    slots = (2,) * len(groups)
    q, k, v, whole_a, attended, lse, heads, resid_low, cotangent_low, w_attn, up_half, out_whole, down_half = front(
        tokens[0],
        cotangent[0],
        jnp.concatenate([w_qkv[:, i] for i in range(3)], axis=1).reshape(
            slots + (depth // n_groups, 3 * cols)
        ),
        w_up.reshape(slots + (depth // n_groups, units)),
        w_out.reshape((2,) + slots + (cols // (2 * n_groups), depth)),
        w_down.reshape((2,) + slots + (units // (2 * n_groups), depth)),
        norm_gains,
        norm_shifts,
        cosine,
        sine,
        groups,
    )
    up_half = up_half.reshape(depth, 2 * units)
    out_whole = out_whole.reshape(4 * cols, depth)
    down_half = down_half.reshape(2 * units, depth)

    branch_a = dot(heads, out_whole)

    resid = resid_low.astype(f32)
    out_a, unit_1, inverse_1 = norm_forward(branch_a, gains[1], shifts[1])
    middle = resid + out_a
    normed_f, unit_2, inverse_2 = norm_forward(middle, gains[2], shifts[2])
    own_f = normed_f.astype(bf16)
    other_f = across(own_f, "b")

    def hidden_units(value):
        hidden = dot(value, up_half)
        bend = jnp.tanh(0.7978845608028654 * (hidden + 0.044715 * hidden * hidden * hidden))
        slope = 0.5 * (1.0 + bend) + 0.5 * hidden * (1.0 - bend * bend) * 0.7978845608028654 * (
            1.0 + 3 * 0.044715 * hidden * hidden
        )
        return (0.5 * hidden * (1.0 + bend)).astype(bf16), slope.astype(bf16)

    own_active, own_slope = hidden_units(own_f)
    other_active, other_slope = hidden_units(other_f)
    branch_f = across(dot(other_active, down_half).astype(bf16), "b")
    branch_f = dot(own_active, down_half) + branch_f.astype(f32)
    out_f, unit_3, inverse_3 = norm_forward(branch_f, gains[3], shifts[3])
    output = (middle + out_f).astype(bf16)

    picks = (
        corpus_ids[:, None] == jnp.arange(corpus_weight.shape[0], dtype=jnp.int32)[None, :]
    ).astype(f32)
    row_scale = turn(jnp.dot(picks, corpus_weight, precision=lax.Precision.HIGHEST))
    grad_final = cotangent_low.astype(f32) * row_scale[:, None]
    back_3, gain_3, shift_3 = norm_backward(grad_final, unit_3, inverse_3, gains[3])
    own_g = back_3.astype(bf16)
    other_g = across(own_g, "b")
    own_hidden = (own_slope.astype(f32) * dot(own_g, down_half, NT)).astype(bf16)
    other_hidden = (other_slope.astype(f32) * dot(other_g, down_half, NT)).astype(bf16)
    grad_f = across(dot(other_hidden, up_half, NT).astype(bf16), "b")
    grad_f = dot(own_hidden, up_half, NT) + grad_f.astype(f32)
    back_2, gain_2, shift_2 = norm_backward(grad_f, unit_2, inverse_2, gains[2])
    grad_middle = grad_final + back_2
    back_1, gain_1, shift_1 = norm_backward(grad_middle, unit_1, inverse_1, gains[1])
    grad_a = back_1.astype(bf16)
    grad_attended = dot(grad_a, out_whole, NT).astype(bf16)

    none = jnp.zeros_like(gain_1)
    norms = jnp.stack([none, gain_1, gain_2, gain_3, none, shift_1, shift_2, shift_3])
    gain_grad, shift_grad, input_grad, output, qkv_grad, up_grad, out_grad, down_grad = back(
        q,
        k,
        v,
        attended,
        lse,
        cosine,
        sine,
        norm_gains,
        norms,
        grad_attended,
        output,
        (own_f, own_g, own_hidden, own_active),
        (other_f, other_g, other_hidden, other_active),
        heads,
        grad_a,
        whole_a,
        w_attn,
        resid_low,
        grad_middle,
        groups,
    )
    input_grad = input_grad.astype(f32)
    qkv_grad = qkv_grad.reshape(depth, 3 * cols).astype(f32)
    qkv_grad = jnp.stack(jnp.split(qkv_grad, 3, axis=1), axis=1)
    up_grad = up_grad.reshape(depth, units).astype(f32)
    out_grad = out_grad.reshape(cols, depth).astype(f32)
    down_grad = down_grad.reshape(units, depth).astype(f32)
    return (
        output[None],
        input_grad[None],
        qkv_grad,
        out_grad,
        up_grad,
        down_grad,
        gain_grad,
        shift_grad,
    )


def solution(mesh):
    rows, parts = mesh.shape["dp"], mesh.shape["mp"]
    bits = (rows // 2).bit_length() - 1
    assert parts == 4 and rows == 2 ** (bits + 1)
    groups = tuple(f"g{i}" for i in range(bits))
    fine = Mesh(mesh.devices.reshape((2,) * (bits + 3)), groups + ("b", "h", "l"))
    dp, mp = groups + ("b",), ("h", "l")
    placed = (
        P(dp, mp, None),
        P(None, None, mp),
        P(mp, None),
        P(None, mp),
        P(mp, None),
        P(),
        P(),
        P(dp, mp, None),
        P(dp),
        P(),
    )
    return jax.shard_map(
        functools.partial(on_device, groups=groups),
        mesh=fine,
        in_specs=placed,
        out_specs=(
            P(dp, mp, None),
            P(dp, mp, None),
            P(None, None, mp),
            P(mp, None),
            P(None, mp),
            P(mp, None),
            P(),
            P(),
        ),
        check_vma=False,
    )
```

```python
import functools

import jax
import jax.numpy as jnp
import numpy as np
from jax import lax
from jax.experimental import pallas as pl
from jax.experimental.pallas import tpu as pltpu
from jax.sharding import Mesh, PartitionSpec as P

HEAD_DIM = 64
BLOCK = 512
EPS = 1e-05
LOG2E = 1.4426950408889634
NN = (((1,), (0,)), ((), ()))
NT = (((1,), (1,)), ((), ()))
TN = (((0,), (0,)), ((), ()))
f32 = jnp.float32
bf16 = jnp.bfloat16


def head_lanes(shape, head):
    return lax.broadcasted_iota(jnp.int32, shape, 1) // HEAD_DIM == head


def swap_halves(value, sign):
    half = HEAD_DIM // 2
    width = value.shape[1]
    first = (lax.broadcasted_iota(jnp.int32, value.shape, 1) // half) % 2 == 0
    return jnp.where(
        first, sign * pltpu.roll(value, width - half, 1), -sign * pltpu.roll(value, half, 1)
    )


MESH = pl.DeviceIdType.MESH
BACK_PLAN = {
    "front": "s1 s2",
    0: "a1 s3",
    1: "a2",
    3: "b1 r1",
    4: "s4",
    6: "a3",
    7: "b2 r2",
    9: "b3 r3",
    "x0": "a4",
    "x3": "b4 r4 end",
}
FRONT_PLAN = {
    "own": "ring",
    "near": "one",
    0: "1a",
    1: "two 1b",
    2: "2a three",
    3: "2b 3a",
    "rest": "3b",
}


class Copies:
    def __init__(self, send, recv):
        self.send, self.recv, self.made = send, recv, {}

    def describe(self, name):
        n, build = self.made[name]
        source, target, device = build()
        return pltpu.make_async_remote_copy(
            src_ref=source,
            dst_ref=target,
            send_sem=self.send.at[n],
            recv_sem=self.recv.at[n],
            device_id=device,
            device_id_type=MESH,
        )

    def plan(self, name, build):
        self.made[name] = (len(self.made), build)

    def start(self, name, build=None):
        if build is not None:
            self.plan(name, build)
        self.describe(name).start()

    def arrived(self, name):
        self.describe(name).wait_recv()

    def sent(self, name):
        self.describe(name).wait_send()

    def drain(self, but=()):
        for name in self.made:
            if name not in but:
                self.sent(name)


def flip(axis):
    return {axis: 1 - lax.axis_index(axis)}


def next_layer(step):
    at = lax.rem(2 * lax.axis_index("h") + lax.axis_index("l") + step, 4)
    return {"h": at // 2, "l": lax.rem(at, 2)}


def add_into(total, term, rows=64):
    lead, count = total.shape[:-2], total.shape[-2]
    step = next(n for n in (rows, 32, 16, 8) if count % n == 0)

    @pl.loop(0, count // step)
    def _(i):
        at = pl.ds(pl.multiple_of(i * step, step), step)
        for index in np.ndindex(*lead):
            total[index + (at,)] = (
                total[index + (at,)].astype(f32) + term[index + (at,)].astype(f32)
            ).astype(bf16)


def exclusive(a, b):
    return a + b - 2 * a * b


def forward_branch(last, heads, rows, q_ref, k_ref, v_ref, o_ref, lse_ref):
    width = q_ref.shape[1]
    n = (last + 1) * rows
    block = pl.ds(last * rows, rows)
    acc = jnp.zeros((rows, width), f32)
    logs = jnp.zeros((rows, width), f32)
    for h in range(heads):
        mine = head_lanes((rows, width), h)
        qm = jnp.where(mine, q_ref[block], jnp.zeros((), bf16))
        s = lax.dot_general(qm, k_ref[:n], NT, preferred_element_type=f32)
        row = lax.broadcasted_iota(jnp.int32, (rows, rows), 0)
        column = lax.broadcasted_iota(jnp.int32, (rows, rows), 1)
        tail = jnp.where(column <= row, s[:, n - rows :], -1e30)
        top = jnp.max(tail, axis=1, keepdims=True)
        if last:
            top = jnp.maximum(top, jnp.max(s[:, : n - rows], axis=1, keepdims=True))
        top = top * LOG2E
        vm = jnp.where(head_lanes((n, width), h), v_ref[:n], jnp.ones((), bf16))
        low = jnp.exp2(tail * LOG2E - top).astype(bf16)
        out = lax.dot_general(low, vm[n - rows :], NN, preferred_element_type=f32)
        if last:
            low = jnp.exp2(s[:, : n - rows] * LOG2E - top).astype(bf16)
            out = out + lax.dot_general(low, vm[: n - rows], NN, preferred_element_type=f32)
        total = pltpu.roll(out, HEAD_DIM, 1)
        acc = jnp.where(mine, out / total, acc)
        logs = jnp.where(mine, top + jnp.log2(total), logs)
    o_ref[block] = acc.astype(bf16)
    lane = lax.broadcasted_iota(jnp.int32, (8, width), 1)
    pick = (lane == HEAD_DIM * lax.broadcasted_iota(jnp.int32, (8, width), 0)).astype(f32)
    lse_ref[:, block] = lax.dot_general(
        pick, logs, NT, precision=lax.Precision.HIGHEST, preferred_element_type=f32
    )


def front_kernel(*refs, groups, chunks):
    (
        tok_ref, wq_ref, up_ref, out_ref, down_ref, gain_ref, shift_ref, cos_ref, sin_ref,
        q_ref, k_ref, v_ref, whole_ref, o_ref, lse_ref,
        heads_ref, tok_home, w_home, up_all, out_all, down_all,
        row, w_att, bounce_up, bounce_out, bounce_down,
        send, recv, local, head_send, head_recv,
    ) = refs
    bits = len(groups)
    part = tok_ref.shape[0]
    depth = tok_ref.shape[1]
    width = q_ref.shape[1]
    heads = width // HEAD_DIM
    core, half, near = lax.axis_index("b"), lax.axis_index("h"), lax.axis_index("l")
    group = [lax.axis_index(axis) for axis in groups]
    layer = 2 * half + near
    place = 2 * core + near
    stays = core == half
    moves = core != half
    partner = {"b": half, "h": core}
    copies = Copies(send, recv)
    locals_made, here = [], []

    def copy_here(source, target):
        copy = pltpu.make_async_copy(source, target, local.at[len(locals_made)])
        locals_made.append(copy)
        here.append(copy)
        copy.start()

    barrier = pltpu.get_barrier_semaphore()
    friends = [flip(axis) for axis in groups + ("b",)] + [next_layer(1), next_layer(3)]
    friends += [flip("l"), {"b": 1 - core, "l": 1 - near}]
    for friend in friends:
        pl.semaphore_signal(barrier, inc=1, device_id=friend, device_id_type=MESH)

    @pl.when(moves)
    def _():
        pl.semaphore_signal(barrier, inc=1, device_id=partner, device_id_type=MESH)
        pl.semaphore_wait(barrier, len(friends) + 1)

    @pl.when(stays)
    def _():
        pl.semaphore_wait(barrier, len(friends))

    size = part // chunks

    def piece(c):
        return pl.ds(c * size, size)

    weights = (up_ref, out_ref, down_ref)
    orders = [tuple(range(bits)), tuple(range(bits)), tuple(reversed(range(bits)))]
    slab = up_ref.shape[-1] // 2

    def slot(a, shard, at):
        if a == 0:
            return up_all.at[at + (slice(None), pl.ds(pl.multiple_of(shard * slab, slab), slab))]
        if a == 1:
            return out_all.at[(shard, core) + at]
        return down_all.at[(shard,) + at]

    def held(a, at):
        if a == 0:
            return up_ref.at[at + (slice(None), pl.ds(pl.multiple_of(core * slab, slab), slab))]
        return weights[a].at[(core,) + at]

    def shard(k):
        return lax.rem(layer + 4 - k, 4)

    def ring_send(step):
        for a in range(3):

            def build(a=a):
                at = tuple(group)
                spot = slot(a, shard(step - 1), at)
                return (held(a, at) if step == 1 else spot, spot, next_layer(1))

            copies.start(("ring", a, step), build)

    def ring_wait(step):
        for a in range(3):
            copies.arrived(("ring", a, step))

    def plane_send(k, stage):
        for a in range(3):

            def build(a=a):
                order = orders[a]
                at = tuple(
                    group[axis] if order.index(axis) >= stage else slice(None)
                    for axis in range(bits)
                )
                spot = slot(a, shard(k), at)
                return (spot, spot, flip(groups[order[stage]]))

            copies.start(("plane", a, k, stage), build)

    def plane_wait(k, stage):
        for a in range(3):
            copies.arrived(("plane", a, k, stage))

    def core_send(k):
        def build():
            spot = slot(1, shard(k), (slice(None),) * bits)
            return (spot, spot, flip("b"))

        copies.start(("core", k), build)

    def plane_next(k, stage):
        plane_wait(k, stage)
        if stage + 1 < bits:
            plane_send(k, stage + 1)
        else:
            core_send(k)

    def inner_stages(k):
        for stage in range(1, bits):
            plane_next(k, stage)

    def arrive(k):
        ring_wait(k)
        if k < 3:
            ring_send(k + 1)
        plane_send(k, 0)

    steps = {
        "ring": lambda: ring_send(1),
        "one": lambda: arrive(1),
        "two": lambda: arrive(2),
        "three": lambda: arrive(3),
        "1a": lambda: plane_next(1, 0),
        "1b": lambda: inner_stages(1),
        "2a": lambda: plane_next(2, 0),
        "2b": lambda: inner_stages(2),
        "3a": lambda: plane_next(3, 0),
        "3b": lambda: inner_stages(3),
    }

    def weights_at(point):
        for name in FRONT_PLAN.get(point, "").split():
            steps[name]()

    everything = (slice(None),) * bits
    bounces = [
        (held(0, everything), bounce_up, slot(0, layer, everything)),
        (out_ref, bounce_out, out_all.at[layer]),
        (held(2, everything), bounce_down, slot(2, layer, everything)),
    ]
    inward = []
    for source, buffer, _ in bounces:
        copy = pltpu.make_async_copy(source, buffer, local.at[len(locals_made)])
        locals_made.append(copy)
        inward.append(copy)
        copy.start()

    weights_at("start")
    own = [
        pltpu.make_async_copy(
            tok_ref.at[piece(c)], row.at[place, piece(c)], local.at[len(locals_made) + c]
        )
        for c in range(chunks)
    ]
    locals_made.extend(own)
    turned = [("turn", c) for c in range(chunks)]
    for c in range(chunks):
        copies.plan(
            turned[c],
            lambda c=c: (tok_ref.at[piece(c)], row.at[layer, piece(c)], partner),
        )
    w_here = pltpu.make_async_copy(wq_ref, w_att, local.at[len(locals_made)])
    locals_made.append(w_here)
    copies.plan("wturn", lambda: (wq_ref.at[tuple(group)], w_att.at[tuple(group)], partner))

    @pl.when(moves)
    def _():
        for c in range(chunks):
            copies.start(turned[c])
        copies.start("wturn")

    @pl.when(stays)
    def _():
        for c in range(chunks):
            own[c].start()
        w_here.start()

    for c in range(chunks):
        pl.when(moves)(functools.partial(copies.arrived, turned[c]))
        pl.when(stays)(own[c].wait)
        for name, axis in (("near", "l"), ("core own", "b")):
            copies.start(
                (name, c),
                lambda c=c, axis=axis: (
                    row.at[place, piece(c)],
                    row.at[place, piece(c)],
                    flip(axis),
                ),
            )
    copy_here(row.at[place], tok_home)
    for copy in inward:
        copy.wait()
    for _, buffer, target in bounces:
        copy_here(buffer, target)
    weights_at("own")

    @pl.when(stays)
    def _():
        w_here.wait()

    parts = [pl.ds(i * (w_att.shape[-2] // 2), w_att.shape[-2] // 2) for i in range(2)]
    w_orders = [orders[0], orders[2]]
    for stage in range(bits):
        for i in range(2):

            def build(stage=stage, i=i):
                order = w_orders[i]
                at = tuple(
                    group[axis] if order.index(axis) >= stage else slice(None)
                    for axis in range(bits)
                )
                spot = w_att.at[at + (parts[i],)]
                return (spot, spot, flip(groups[order[stage]]))

            copies.plan(("w", stage, i), build)

    @pl.when(moves)
    def _():
        copies.arrived("wturn")
        for stage in range(bits):
            for i in range(2):
                copies.start(("w", stage, i))
            for i in range(2):
                copies.arrived(("w", stage, i))

    copy_here(w_att, w_home)
    near_block = 2 * core + 1 - near

    def pass_on():
        for c in range(chunks):
            copies.arrived(("near", c))
            copies.start(
                ("core near", c),
                lambda c=c: (row.at[near_block, piece(c)], row.at[near_block, piece(c)], flip("b")),
            )
        weights_at("near")

    def wait_all(name):
        def run():
            for c in range(chunks):
                copies.arrived((name, c))

        return run

    @pl.loop(0, 4)
    def _(r):
        far_core, far_near = lax.rem(r, 2), r // 2
        block = 2 * exclusive(core, far_core) + exclusive(near, far_near)
        pl.when(r == 1)(wait_all("core own"))
        pl.when(r == 2)(pass_on)
        pl.when(r == 3)(wait_all("core near"))

        @pl.loop(0, 2)
        def _(c):
            rows = part // 2
            inside = pl.ds(pl.multiple_of(c * rows, rows), rows)
            at = pl.ds(pl.multiple_of(block * part + c * rows, rows), rows)
            value = row[block, inside].astype(f32)
            center = value - jnp.mean(value, axis=1, keepdims=True)
            inverse = lax.rsqrt(jnp.mean(center * center, axis=1, keepdims=True) + EPS)
            normed = (center * inverse * gain_ref[0:1] + shift_ref[0:1]).astype(bf16)
            whole_ref[at] = normed
            w = w_att[...].reshape(depth, 3 * width)
            mixed = jnp.dot(normed, w, preferred_element_type=f32)
            cosine = jnp.concatenate([cos_ref[at]] * (width // 128), axis=1)
            sine = jnp.concatenate([sin_ref[at]] * (width // 128), axis=1)
            query, key = mixed[:, :width], mixed[:, width : 2 * width]
            query = HEAD_DIM ** (-0.5) * (query * cosine + swap_halves(query, -1.0) * sine)
            q_ref[at] = query.astype(bf16)
            k_ref[at] = (key * cosine + swap_halves(key, -1.0) * sine).astype(bf16)
            v_ref[at] = mixed[:, 2 * width :].astype(bf16)

    def head_copy(mask):
        far_core, far_near = mask // 2, lax.rem(mask, 2)
        to_core, to_near = exclusive(core, far_core), exclusive(near, far_near)
        block = 2 * to_core + to_near
        rows = pl.ds(pl.multiple_of(block * part, part), part)
        columns = pl.ds(pl.multiple_of(place * width, width), width)
        return pltpu.make_async_remote_copy(
            src_ref=o_ref.at[rows],
            dst_ref=heads_ref.at[:, columns],
            send_sem=head_send.at[mask],
            recv_sem=head_recv.at[mask],
            device_id={"b": to_core, "l": to_near},
            device_id_type=MESH,
        )

    @pl.loop(0, 4)
    def _(r):
        far_core, far_near = 1 - lax.rem(r, 2), 1 - r // 2
        mask = 2 * far_core + far_near
        block = 2 * exclusive(core, far_core) + exclusive(near, far_near)
        for n in range(4):
            pl.when(r == n)(functools.partial(weights_at, n))
        for i in range(4):
            pl.when(block == i)(
                functools.partial(
                    forward_branch, i, heads, part, q_ref, k_ref, v_ref, o_ref, lse_ref
                )
            )

        @pl.when(r < 3)
        def _():
            head_copy(mask).start()

    copy_here(
        o_ref.at[pl.ds(pl.multiple_of(place * part, part), part)],
        heads_ref.at[:, pl.ds(pl.multiple_of(place * width, width), width)],
    )

    weights_at("rest")
    for mask in (1, 2, 3):
        copy = head_copy(jnp.int32(mask))
        copy.wait_send()
        copy.wait_recv()
    for k in (1, 2, 3):
        copies.arrived(("core", k))
    sometimes = turned + ["wturn"] + [("w", s, i) for s in range(bits) for i in range(2)]

    @pl.when(moves)
    def _():
        for name in sometimes:
            copies.sent(name)

    for copy in here:
        copy.wait()
    copies.drain(sometimes)


def front(tok, wq, up, out, down, gain, shift, cosine, sine, groups, chunks=2):
    part, depth = tok.shape
    length = 4 * part
    width = wq.shape[-1] // 3
    bits = len(groups)
    vmem = pl.BlockSpec(memory_space=pltpu.VMEM)
    anywhere = pl.BlockSpec(memory_space=pl.ANY)

    def shape(*dims):
        return jax.ShapeDtypeStruct(dims, bf16)

    n = 2 * chunks + 2 + 3 * chunks + 2 * bits + 3 * 3 + 9 * bits + 3 + 4
    return pl.pallas_call(
        functools.partial(front_kernel, groups=groups, chunks=chunks),
        out_shape=(
            shape(length, width),
            shape(length, width),
            shape(length, width),
            shape(length, depth),
            shape(length, width),
            jax.ShapeDtypeStruct((8, length), f32),
            shape(part, depth),
            shape(part, depth),
            shape(*wq.shape),
            shape(*up.shape[:-1], 2 * up.shape[-1]),
            shape(4, *out.shape),
            shape(4, *down.shape[1:]),
        ),
        in_specs=[anywhere] * 5 + [vmem] * 4,
        out_specs=(vmem,) * 6 + (anywhere,) * 6,
        scratch_shapes=[
            pltpu.VMEM((4, part, depth), bf16),
            pltpu.VMEM(wq.shape, bf16),
            pltpu.VMEM(up.shape[:-1] + (up.shape[-1] // 2,), bf16),
            pltpu.VMEM(out.shape, bf16),
            pltpu.VMEM(down.shape[1:], bf16),
            pltpu.SemaphoreType.DMA((n,)),
            pltpu.SemaphoreType.DMA((n,)),
            pltpu.SemaphoreType.DMA((32,)),
            pltpu.SemaphoreType.DMA((4,)),
            pltpu.SemaphoreType.DMA((4,)),
        ],
        compiler_params=pltpu.CompilerParams(
            vmem_limit_bytes=58 * 2**20, collective_id=2, has_side_effects=True
        ),
        cost_estimate=pl.CostEstimate(
            flops=100_000_000_000, bytes_accessed=32 * 2**20, transcendentals=0
        ),
    )(tok, wq, up, out, down, gain, shift, cosine, sine)

def back_kernel(*refs, groups, rows, chunks):
    (
        q_ref, k_ref, v_ref, o_ref, lse_ref, cos_ref, sin_ref, gain_ref, norms_ref,
        da_ref, low_ref, own_in, other_in, own_branch, other_branch, own_hidden, other_hidden, own_active, other_active,
        heads_ref, branch_ref,
        whole_ref, w_ref, resid_ref, middle_ref,
        gains_out, shifts_out, grad_home, low_home, qkv_all, up_all, out_all, down_all,
        up_ref, out_ref, down_ref,
        out_part, out_in, up_tile, down_tile, turned,
        do, dq, dk, dv, delta, mixed, whole, w, resid, middle,
        sent, from_core, from_near, grad_x, grad_low, qkv_sum, qkv_core, norm_sum, norm_in,
        *rest,
    ) = refs
    bits = len(groups)
    terms = (up_ref, out_ref, down_ref)
    partial = [[rest[3 * s + a] for s in range(bits)] for a in range(3)]
    rest = rest[3 * bits :]
    passing, staged, rest = rest[:3], rest[3:6], rest[6:]
    qkv_in, (send, recv, local) = rest[:bits], rest[bits:]
    copies = Copies(send, recv)
    group = [lax.axis_index(axis) for axis in groups]
    core, half, near = lax.axis_index("b"), lax.axis_index("h"), lax.axis_index("l")
    layer = 2 * half + near
    place = 2 * core + near
    moves, stays = core != half, core == half
    partner = {"b": half, "h": core}
    orders = [tuple(range(bits)), tuple(range(bits)), tuple(reversed(range(bits)))]
    part, depth = da_ref.shape
    length, width = q_ref.shape
    heads = width // HEAD_DIM
    blocks = length // rows
    slab = up_ref.shape[-1] // 4
    quarter = depth // 2**bits
    all_local = [0]

    def local_copy(source, target):
        n = all_local[0]
        all_local[0] += 1
        return pltpu.make_async_copy(source, target, local.at[n])

    def columns(which, size):
        return pl.ds(pl.multiple_of(which * size, size), size)

    def shard(k):
        return lax.rem(layer + 4 - k, 4)

    def term(a, k, at):
        if a == 0:
            return up_ref.at[at + (slice(None), columns(shard(k), slab))]
        return terms[a].at[(shard(k),) + at]

    def result(a, at):
        if a == 0:
            return up_all.at[at + (slice(None), columns(core, slab))]
        return (None, out_all, down_all)[a].at[(core,) + at]

    def split(order, stage, side):
        at = []
        for axis in range(bits):
            when = order.index(axis)
            if when == stage:
                at.append(group[axis] if side == 0 else 1 - group[axis])
            elif when > stage:
                at.append(slice(None))
        return tuple(at)

    def source(a, k, stage, side):
        at = split(orders[a], stage, side)
        if stage == 0:
            return term(a, k, at) if side else staged[a].at[k % 2]
        return partial[a][stage - 1].at[(k % 4,) + at]

    loads = {}

    def plane_send(k, stage):
        for a in range(3):
            copies.start(
                ("plane", a, k, stage),
                lambda a=a: (
                    source(a, k, stage, 1),
                    partial[a][stage].at[k % 4],
                    flip(groups[orders[a][stage]]),
                ),
            )
            if stage == 0:
                loads[a, k] = local_copy(term(a, k, split(orders[a], 0, 0)), staged[a].at[k % 2])
                loads[a, k].start()

    def plane_add(k, stage):
        for a in range(3):
            copies.arrived(("plane", a, k, stage))
            if stage == 0:
                loads[a, k].wait()
            add_into(partial[a][stage].at[k % 4], source(a, k, stage, 0))

    def plane_step(k, stage):
        plane_add(k, stage)
        if stage + 1 < bits:
            plane_send(k, stage + 1)

    def ring_send(step):
        for a in range(3):
            held = partial[a][bits - 1].at[1] if step == 1 else passing[a].at[step - 2]
            target = passing[a].at[step - 1]
            copies.start(
                ("ring", a, step), lambda held=held, target=target: (held, target, next_layer(1))
            )

    def ring_add(step):
        for a in range(3):
            copies.arrived(("ring", a, step))
            add_into(passing[a].at[step - 1], partial[a][bits - 1].at[(step + 1) % 4])

    def gather_send(stage):
        for a in range(3):
            order = orders[a]
            at = tuple(
                group[axis] if order.index(axis) >= stage else slice(None) for axis in range(bits)
            )
            held = passing[a].at[2] if stage == 0 else result(a, at)
            spot, axis = result(a, at), groups[order[stage]]
            copies.start(
                ("gather", a, stage),
                lambda held=held, spot=spot, axis=axis: (held, spot, flip(axis)),
            )

    def brought(order, stage):
        at = []
        for axis in range(bits):
            when = order.index(axis)
            if stage == 0 or when > stage - 1:
                at.append(group[axis])
            elif when == stage - 1:
                at.append(1 - group[axis])
            else:
                at.append(slice(None))
        return tuple(at)

    def core_send(stage):
        for a in range(3):
            spot = result(a, brought(orders[a], stage))
            held = passing[a].at[2] if stage == 0 else spot
            copies.start(("core", a, stage), lambda held=held, spot=spot: (held, spot, flip("b")))

    barrier = pltpu.get_barrier_semaphore()
    friends = [flip(axis) for axis in groups + ("b", "h", "l")] + [next_layer(1), next_layer(3)]
    friends += [{"b": 1 - core, "l": 1 - near}]
    for friend in friends:
        pl.semaphore_signal(barrier, inc=1, device_id=friend, device_id_type=MESH)

    @pl.when(moves)
    def _():
        pl.semaphore_signal(barrier, inc=1, device_id=partner, device_id_type=MESH)
        pl.semaphore_wait(barrier, len(friends) + 1)

    @pl.when(stays)
    def _():
        pl.semaphore_wait(barrier, len(friends))

    for mask in (3, 1, 2):
        to_core, to_near = exclusive(core, mask // 2), exclusive(near, mask % 2)

        def build(to_core=to_core, to_near=to_near):
            return (
                da_ref.at[:, columns(2 * to_core + to_near, width)],
                do.at[columns(place, part)],
                {"b": to_core, "l": to_near},
            )

        copies.start(("heads", mask), build)
    own_heads = local_copy(da_ref.at[:, columns(place, width)], do.at[columns(place, part)])
    own_heads.start()
    low_in = local_copy(low_ref, grad_low)
    low_here = local_copy(grad_low, low_home)
    copies.plan("low", lambda: (low_ref, low_home, partner))
    pl.when(moves)(functools.partial(copies.start, "low"))
    pl.when(stays)(low_in.start)

    pieces = 2
    thin = slab // pieces
    pair = whole.shape[0] // 2
    units = [
        local_copy(source, whole.at[pl.ds(n * part, part)])
        for n, source in enumerate((own_in, other_in, own_branch, other_branch))
    ]
    units += [local_copy(heads_ref, sent.at[0]), local_copy(branch_ref, sent.at[1])]
    for copy in units:
        copy.start()

    def hidden_load(u):
        spot = columns(pieces * shard(1 + u // pieces) + lax.rem(u, pieces), thin)
        at = columns(lax.rem(u, 3), thin)
        semaphore = hidden_local + 4 * lax.rem(u, 3)
        return [
            pltpu.make_async_copy(
                source.at[:, spot], mixed.at[pl.ds(n * part, part), at], local.at[semaphore + n]
            )
            for n, source in enumerate((own_hidden, other_hidden, own_active, other_active))
        ]

    hidden_local = all_local[0]
    all_local[0] += 12
    for u in range(2):
        for copy in hidden_load(jnp.int32(u)):
            copy.start()
    for copy in units:
        copy.wait()
    @pl.loop(0, 4)
    def _(s):
        block = lax.dot_general(
            sent[0, :, columns(s, width)], sent[1], TN, preferred_element_type=f32
        ).astype(bf16)
        out_part[s] = block.reshape(out_part.shape[1:])

    @pl.loop(0, 4)
    def _(c):
        turned[columns(c, depth // 4)] = whole[:pair, columns(c, depth // 4)].T

    copies.start("out core", lambda: (out_part.at[:, 1 - core], out_in, flip("b")))
    def shard_gradients(k):
        @pl.loop(0, pieces)
        def _(n):
            u = pieces * (k - 1) + n
            for copy in hidden_load(u):
                copy.wait()

            @pl.when(u + 2 < 4 * pieces)
            def _():
                for copy in hidden_load(u + 2):
                    copy.start()

            buffer = columns(lax.rem(u, 3), thin)

            @pl.loop(0, 2**bits)
            def _(c):
                slot = tuple(lax.rem(c // 2 ** (bits - 1 - i), 2) for i in range(bits))
                up_tile[(n,) + slot] = jnp.dot(
                    turned[columns(c, quarter)],
                    mixed[:pair, buffer],
                    preferred_element_type=f32,
                ).astype(bf16)

            block = lax.dot_general(
                mixed[pair:, buffer], whole[pair:], TN, preferred_element_type=f32
            )
            down_tile[n] = block.astype(bf16).reshape(down_tile.shape[1:])

        if k == 1:
            copies.arrived("out core")

            @pl.loop(0, 4)
            def _(s):
                out_in[s] = (out_in[s].astype(f32) + out_part[s, core].astype(f32)).astype(bf16)

            put = local_copy(out_in, out_ref)
            put.start()
            put.wait()
        made = []
        for u in range(pieces):
            spot = (slice(None),) * (bits + 1) + (columns(pieces * shard(k) + u, thin),)
            made.append(local_copy(up_tile.at[u], up_ref.at[spot]))
            made.append(local_copy(down_tile.at[u], down_ref.at[shard(k), u]))
        for copy in made:
            copy.start()
        for copy in made:
            copy.wait()

    whole_load = local_copy(whole_ref, whole)

    def begin(k):
        shard_gradients(k)
        if k == 4:
            whole_load.start()
        plane_send(k, 0)

    def last_stages(k):
        for stage in range(1, bits):
            plane_step(k, stage)

    def ring(step):
        if step > 1:
            ring_add(step - 1)
        if step < 4:
            ring_send(step)

    own = [local_copy(passing[a].at[2], result(a, tuple(group))) for a in range(3)]

    def finish():
        core_send(0)
        gather_send(0)
        for copy in own:
            copy.start()

    kinds = {"s": begin, "a": lambda k: plane_step(k, 0), "b": last_stages, "r": ring}

    def sums_at(point):
        for name in BACK_PLAN.get(point, "").split():
            if name == "end":
                finish()
            else:
                kinds[name[0]](int(name[1]))

    sums_at("front")
    early = [
        local_copy(w_ref, w),
        local_copy(resid_ref, resid),
        local_copy(middle_ref, middle),
    ]
    for copy in early:
        copy.start()

    @pl.when(stays)
    def _():
        low_in.wait()
        low_here.start()

    for total in (dq, dk, dv):
        total[...] = jnp.zeros_like(total)
    own_heads.wait()
    for mask in (2, 1, 3):
        copies.arrived(("heads", mask))

    lane_head = lax.broadcasted_iota(jnp.int32, (8, width), 1) // HEAD_DIM
    marks = (lane_head == lax.broadcasted_iota(jnp.int32, (8, width), 0)).astype(f32)

    def span(i):
        return pl.ds(pl.multiple_of(i * rows, rows), rows)

    @pl.loop(0, blocks)
    def _(i):
        product = do[span(i)].astype(f32) * o_ref[span(i)].astype(f32)
        delta[:, span(i)] = lax.dot_general(
            marks, product, NT, precision=lax.Precision.HIGHEST, preferred_element_type=f32
        )

    def tile(i, j):
        at, to = span(i), span(j)
        keys, values = k_ref[to], v_ref[to]
        queries, grads = q_ref[at], do[at]
        dkj, dvj, dqi = dk[to], dv[to], dq[at]
        zero = jnp.zeros((), bf16)
        key = j * rows + lax.broadcasted_iota(jnp.int32, (rows, rows), 0)
        query = i * rows + lax.broadcasted_iota(jnp.int32, (rows, rows), 1)
        allowed = key <= query
        for h in range(heads):
            mine = head_lanes((rows, width), h)
            qm = jnp.where(mine, queries, zero)
            dom = jnp.where(mine, grads, zero)
            km = jnp.where(mine, keys, zero)
            st = lax.dot_general(keys, qm, NT, preferred_element_type=f32)
            pt = jnp.where(allowed, jnp.exp2(st * LOG2E - lse_ref[h : h + 1, at]), 0.0)
            dpt = lax.dot_general(values, dom, NT, preferred_element_type=f32)
            dst = (pt * (dpt - delta[h : h + 1, at])).astype(bf16)
            dvj = dvj + jnp.dot(pt.astype(bf16), dom, preferred_element_type=f32)
            dkj = dkj + jnp.dot(dst, qm, preferred_element_type=f32)
            dqi = dqi + lax.dot_general(dst, km, TN, preferred_element_type=f32)
        dq[at], dk[to], dv[to] = dqi, dkj, dvj

    count = blocks * (blocks + 1) // 2

    def tiles(low, high):
        @pl.loop(low, high)
        def _(t):
            i = jnp.int32(0)
            for n in range(1, blocks):
                i = i + (t >= n * (n + 1) // 2).astype(jnp.int32)
            tile(i, t - i * (i + 1) // 2)

    low = 0
    for point in range(10):
        when = point * count // 10
        if point in BACK_PLAN:
            if when > low:
                tiles(low, when)
            sums_at(point)
            low = when
    tiles(low, count)

    def turn_back(grad, at):
        cosine = jnp.concatenate([cos_ref[at]] * (width // 128), axis=1)
        sine = jnp.concatenate([sin_ref[at]] * (width // 128), axis=1)
        return grad * cosine + swap_halves(grad, 1.0) * sine

    @pl.loop(0, blocks)
    def _(i):
        at = span(i)
        mixed[at, :width] = (HEAD_DIM ** (-0.5) * turn_back(dq[at], at)).astype(bf16)
        mixed[at, width : 2 * width] = turn_back(dk[at], at).astype(bf16)
        mixed[at, 2 * width :] = dv[at].astype(bf16)

    for copy in early:
        copy.wait()
    size = part // chunks

    def input_part(block, c):
        at = pl.ds(pl.multiple_of(block * part + c * size, size), size)
        return lax.dot_general(
            mixed[at], w[...].reshape(depth, 3 * width), NT, preferred_element_type=f32
        )

    def inside(c):
        return pl.ds(pl.multiple_of(c * size, size), size)

    for slot in range(2):
        block = 2 * (1 - core) + (1 - near if slot == 0 else near)

        @pl.loop(0, chunks)
        def _(c):
            sent[slot, inside(c)] = input_part(block, c).astype(bf16)

        copies.start(
            ("x core", slot),
            lambda slot=slot: (sent.at[slot], from_core.at[slot], flip("b")),
        )
    sums_at("x0")
    copies.arrived(("x core", 0))
    for c in range(chunks):
        total = input_part(2 * core + 1 - near, c) + from_core[0, inside(c)].astype(f32)
        sent[2, inside(c)] = total.astype(bf16)
        copies.start(
            ("x near", c),
            lambda c=c: (sent.at[2, inside(c)], from_near.at[inside(c)], flip("l")),
        )
    sums_at("x1")
    whole_load.wait()
    side = quarter // 2
    for index in np.ndindex(*(2,) * bits):
        first = sum(bit << (bits - 1 - axis) for axis, bit in enumerate(index)) * quarter
        block = lax.dot_general(
            whole[:, first : first + quarter], mixed[...], TN, preferred_element_type=f32
        ).astype(bf16)
        for i in range(2):
            qkv_sum[index + (i,)] = block[i * side : (i + 1) * side]
    q_orders = [orders[0], orders[2]]

    def q_slot(i, stage, side):
        order = q_orders[i]
        at = []
        for axis in range(bits):
            when = order.index(axis)
            if when < stage:
                at.append(group[axis])
            elif when == stage:
                at.append(group[axis] if side == 0 else 1 - group[axis])
            else:
                at.append(slice(None))
        return qkv_sum.at[tuple(at) + (i,)]

    def q_send(stage):
        for i in range(2):
            copies.start(
                ("q", i, stage),
                lambda i=i: (
                    q_slot(i, stage, 1),
                    qkv_in[stage].at[i],
                    flip(groups[q_orders[i][stage]]),
                ),
            )

    def q_add(stage):
        for i in range(2):
            copies.arrived(("q", i, stage))
            add_into(q_slot(i, stage, 0), qkv_in[stage].at[i])

    q_send(0)
    sums_at("x2")
    copies.arrived(("x core", 1))

    @pl.loop(0, chunks)
    def _(c):
        grad_x[inside(c)] = input_part(place, c) + from_core[1, inside(c)].astype(f32)

    own_q = tuple(group)
    axes = groups + ("b", "h", "l")

    def norms_send(step):
        copies.start(("norms", step), lambda: (norm_sum, norm_in.at[step], flip(axes[step])))

    def norms_add(step):
        copies.arrived(("norms", step))
        copies.sent(("norms", step))
        norm_sum[...] += norm_in[step]

    pl.when(stays)(low_here.wait)
    norm_sum[...] = norms_ref[...]
    fine = min(128, size)

    def home(c):
        copies.arrived(("x near", c))

        @pl.loop(0, size // fine)
        def _(s):
            at = pl.ds(pl.multiple_of(c * size + s * fine, fine), fine)
            grad = grad_x[at] + from_near[at].astype(f32)
            value = resid[at].astype(f32)
            center = value - jnp.mean(value, axis=1, keepdims=True)
            inverse = lax.rsqrt(jnp.mean(center * center, axis=1, keepdims=True) + EPS)
            unit = center * inverse
            scaled = grad * gain_ref[0:1]
            back = inverse * (
                scaled
                - jnp.mean(scaled, axis=1, keepdims=True)
                - unit * jnp.mean(scaled * unit, axis=1, keepdims=True)
            )
            grad_low[at] = (middle[at] + back).astype(bf16)
            norm_sum[0:1] += jnp.sum(grad * unit, axis=0, keepdims=True)
            norm_sum[4:5] += jnp.sum(grad, axis=0, keepdims=True)

        copies.plan(
            ("home", c), lambda c=c: (grad_low.at[inside(c)], grad_home.at[inside(c)], partner)
        )
        pl.when(moves)(functools.partial(copies.start, ("home", c)))

    def gather_next(stage):
        for a in range(3):
            copies.arrived(("gather", a, stage))
        if stage + 1 < bits:
            gather_send(stage + 1)
        core_send(stage + 1)

    def q_spot(at):
        return qkv_all.at[at + (core,)]

    keep_q = local_copy(qkv_core.at[1, core], q_spot(own_q))
    def q_gather(stage):
        at = tuple(group[axis] if axis >= stage else slice(None) for axis in range(bits))
        held = qkv_core.at[1, core] if stage == 0 else q_spot(at)
        copies.start(("q gather", stage), lambda: (held, q_spot(at), flip(groups[stage])))

    def q_core_send(stage):
        spot = q_spot(brought(orders[0], stage))
        held = qkv_core.at[1, core] if stage == 0 else spot
        copies.start(("q both", stage), lambda: (held, spot, flip("b")))

    sums_at("x3")
    half_way = chunks // 2
    for c in range(half_way):
        home(c)
    sums_at("x4")
    for stage in range(bits):
        q_add(stage)
        if stage + 1 < bits:
            q_send(stage + 1)

    copies.plan("q turn", lambda: (qkv_sum.at[own_q], qkv_core.at[0], partner))
    pl.when(moves)(functools.partial(copies.start, "q turn"))
    sums_at("x5")
    for c in range(half_way, chunks):
        home(c)
    stay = [local_copy(grad_low, grad_home)]
    pl.when(stays)(stay[0].start)
    norms_send(0)
    sums_at("x6")
    for copy in own:
        copy.wait()
    gather_next(0)

    @pl.when(moves)
    def _():
        copies.arrived("q turn")

    @pl.when(stays)
    def _():
        qkv_core[0] = qkv_sum[own_q]

    copies.start("q core", lambda: (qkv_core.at[0, 1 - core], qkv_core.at[1, 1 - core], flip("b")))
    norms_add(0)
    norms_send(1)
    copies.arrived("q core")
    add_into(qkv_core.at[1, core], qkv_core.at[0, core])
    keep_q.start()
    q_gather(0)
    q_core_send(0)
    keep_q.wait()
    norms_add(1)
    norms_send(2)
    for stage in range(1, bits):
        gather_next(stage)
    for stage in range(bits):
        copies.arrived(("q gather", stage))
        if stage + 1 < bits:
            q_gather(stage + 1)
        q_core_send(stage + 1)
    for step in range(2, len(axes)):
        norms_add(step)
        if step + 1 < len(axes):
            norms_send(step + 1)
    gains_out[...] = norm_sum[0:4]
    shifts_out[...] = norm_sum[4:8]
    for stage in range(bits + 1):
        for a in range(3):
            copies.arrived(("core", a, stage))
        copies.arrived(("q both", stage))
    sometimes = ["q turn", "low"] + [("home", c) for c in range(chunks)]

    @pl.when(moves)
    def _():
        copies.arrived("low")
        for c in range(chunks):
            copies.arrived(("home", c))
        for name in sometimes:
            copies.sent(name)

    pl.when(stays)(stay[0].wait)
    copies.drain(sometimes + [("norms", step) for step in range(len(axes))])


def back(
    q, k, v, o, lse, cosine, sine, gain, norms, da, low, own, other, heads, branch, whole, w, resid, middle, groups, rows=BLOCK, chunks=2,
):
    length, width = q.shape
    part, depth = da.shape
    bits = len(groups)
    slots = (2,) * bits
    slab = own[2].shape[1] // 4
    up_shape = slots + (depth // 2**bits, 4 * slab)
    out_shape = (4,) + slots + (width // 2 ** (bits + 1), depth)
    down_shape = (4,) + slots + (slab // 2**bits, depth)
    tails = (up_shape[-2:-1] + (slab,), out_shape[-2:], down_shape[-2:])
    vmem = pl.BlockSpec(memory_space=pltpu.VMEM)
    anywhere = pl.BlockSpec(memory_space=pl.ANY)
    quarter = depth // 2**bits
    q_tail = (quarter // 2, 3 * width)
    thin = slab // 2
    scratch = [
        pltpu.VMEM((4, 2) + out_shape[1:], bf16),
        pltpu.VMEM(out_shape, bf16),
        pltpu.VMEM((2,) + up_shape[:-1] + (thin,), bf16),
        pltpu.VMEM((2,) + down_shape[2:], bf16),
        pltpu.VMEM((depth, length // 2), bf16),
    ]
    scratch += [pltpu.VMEM((length, width), bf16)]
    scratch += [pltpu.VMEM((length, width), f32)] * 3 + [pltpu.VMEM((8, length), f32)]
    scratch += [
        pltpu.VMEM((length, 3 * width), bf16),
        pltpu.VMEM(whole.shape, bf16),
        pltpu.VMEM(w.shape, bf16),
        pltpu.VMEM((part, depth), bf16),
        pltpu.VMEM((part, depth), f32),
        pltpu.VMEM((3, part, depth), bf16),
        pltpu.VMEM((2, part, depth), bf16),
        pltpu.VMEM((part, depth), bf16),
        pltpu.VMEM((part, depth), f32),
        pltpu.VMEM((part, depth), bf16),
        pltpu.VMEM(slots + (2,) + q_tail, bf16),
        pltpu.VMEM((2, 2) + q_tail, bf16),
        pltpu.VMEM((8, depth), f32),
        pltpu.VMEM((bits + 3, 8, depth), f32),
    ]
    for stage in range(bits):
        for tail in tails:
            scratch.append(pltpu.VMEM((4,) + (2,) * (bits - 1 - stage) + tail, bf16))
    scratch += [pltpu.VMEM((3,) + tail, bf16) for tail in tails]
    scratch += [pltpu.VMEM((2,) + (2,) * (bits - 1) + tail, bf16) for tail in tails]
    scratch += [
        pltpu.VMEM((2,) + (2,) * (bits - 1 - stage) + q_tail, bf16) for stage in range(bits)
    ]
    n = 5 + 3 * (4 * bits + 3 + bits + bits + 1)
    n += 2 + chunks + 2 * bits + chunks + (bits + 3) + 2 + bits + bits + 1
    scratch += [pltpu.SemaphoreType.DMA((n,)), pltpu.SemaphoreType.DMA((n,))]
    scratch += [pltpu.SemaphoreType.DMA((64,))]
    return pl.pallas_call(
        functools.partial(back_kernel, groups=groups, rows=rows, chunks=chunks),
        out_shape=(
            jax.ShapeDtypeStruct((4, depth), f32),
            jax.ShapeDtypeStruct((4, depth), f32),
            jax.ShapeDtypeStruct((part, depth), bf16),
            jax.ShapeDtypeStruct((part, depth), bf16),
            jax.ShapeDtypeStruct(slots + (2,) + q_tail, bf16),
            jax.ShapeDtypeStruct(up_shape[:-1] + (2 * slab,), bf16),
            jax.ShapeDtypeStruct((2,) + out_shape[1:], bf16),
            jax.ShapeDtypeStruct((2,) + down_shape[1:], bf16),
            jax.ShapeDtypeStruct(up_shape, bf16),
            jax.ShapeDtypeStruct(out_shape, bf16),
            jax.ShapeDtypeStruct(down_shape, bf16),
        ),
        in_specs=[vmem] * 9 + [anywhere] * 16,
        out_specs=(vmem,) * 2 + (anywhere,) * 9,
        scratch_shapes=scratch,
        compiler_params=pltpu.CompilerParams(
            vmem_limit_bytes=63 * 2**20, collective_id=1, has_side_effects=True
        ),
        cost_estimate=pl.CostEstimate(
            flops=100_000_000_000, bytes_accessed=32 * 2**20, transcendentals=0
        ),
    )(
        q, k, v, o, lse, cosine, sine, gain, norms, da, low,
        own[0], other[0], own[1], other[1], own[2], other[2], own[3], other[3],
        heads, branch, whole, w, resid, middle,
    )[:8]


def norm_forward(value, gain, shift):
    center = value - jnp.mean(value, axis=-1, keepdims=True)
    inverse = lax.rsqrt(jnp.mean(center * center, axis=-1, keepdims=True) + EPS)
    unit = center * inverse
    return (unit * gain + shift, unit, inverse)


def norm_backward(grad, unit, inverse, gain):
    scaled = grad * gain
    back = inverse * (
        scaled
        - jnp.mean(scaled, axis=-1, keepdims=True)
        - unit * jnp.mean(scaled * unit, axis=-1, keepdims=True)
    )
    return (back, jnp.sum(grad * unit, axis=0), jnp.sum(grad, axis=0))


def rotary_tables(length, width):
    half = HEAD_DIM // 2
    steps = (np.arange(width) % half).astype(np.float32) / np.float32(half)
    freqs = np.float32(10000.0) ** (-steps)
    angles = np.arange(length, dtype=np.float32)[:, None] * freqs[None, :]
    return (jnp.asarray(np.cos(angles)), jnp.asarray(np.sin(angles)))


SWAP = [(0, 1), (1, 0)]


def dot(left, right, dims=NN):
    return lax.dot_general(left, right, dims, preferred_element_type=f32)


def across(value, axis):
    return lax.ppermute(value, axis, SWAP)


def turn(value):
    return lax.ppermute(value, ("b", "h"), [(0, 0), (1, 2), (2, 1), (3, 3)])


def on_device(
    tokens,
    w_qkv,
    w_out,
    w_up,
    w_down,
    norm_gains,
    norm_shifts,
    cotangent,
    corpus_ids,
    corpus_weight,
    *,
    groups,
):
    _, part, depth = tokens.shape
    cols = w_qkv.shape[2]
    units = w_up.shape[1]
    core, half, near = lax.axis_index("b"), lax.axis_index("h"), lax.axis_index("l")
    length = 4 * part
    place = 2 * core + near
    group = jnp.int32(0)
    for axis in groups:
        group = 2 * group + lax.axis_index(axis)
    n_groups = 2 ** len(groups)
    stack = ("h", "l")
    cosine, sine = rotary_tables(length, 128)
    gains = [norm_gains[i : i + 1] for i in range(4)]
    shifts = [norm_shifts[i : i + 1] for i in range(4)]

    slots = (2,) * len(groups)
    q, k, v, whole_a, attended, lse, heads, resid_low, w_attn, up_half, out_whole, down_half = front(
        tokens[0],
        jnp.concatenate([w_qkv[:, i] for i in range(3)], axis=1).reshape(
            slots + (depth // n_groups, 3 * cols)
        ),
        w_up.reshape(slots + (depth // n_groups, units)),
        w_out.reshape((2,) + slots + (cols // (2 * n_groups), depth)),
        w_down.reshape((2,) + slots + (units // (2 * n_groups), depth)),
        norm_gains,
        norm_shifts,
        cosine,
        sine,
        groups,
    )
    up_half = up_half.reshape(depth, 2 * units)
    out_whole = out_whole.reshape(4 * cols, depth)
    down_half = down_half.reshape(2 * units, depth)

    cotangent_low, heads = lax.optimization_barrier((cotangent[0], heads))
    cotangent_low = turn(cotangent_low)
    branch_a = dot(heads, out_whole)

    resid = resid_low.astype(f32)
    out_a, unit_1, inverse_1 = norm_forward(branch_a, gains[1], shifts[1])
    middle = resid + out_a
    normed_f, unit_2, inverse_2 = norm_forward(middle, gains[2], shifts[2])
    own_f = normed_f.astype(bf16)
    other_f = across(own_f, "b")

    def hidden_units(value):
        hidden = dot(value, up_half)
        bend = jnp.tanh(0.7978845608028654 * (hidden + 0.044715 * hidden * hidden * hidden))
        slope = 0.5 * (1.0 + bend) + 0.5 * hidden * (1.0 - bend * bend) * 0.7978845608028654 * (
            1.0 + 3 * 0.044715 * hidden * hidden
        )
        return (0.5 * hidden * (1.0 + bend)).astype(bf16), slope.astype(bf16)

    own_active, own_slope = hidden_units(own_f)
    other_active, other_slope = hidden_units(other_f)
    branch_f = across(dot(other_active, down_half).astype(bf16), "b")
    branch_f = dot(own_active, down_half) + branch_f.astype(f32)
    out_f, unit_3, inverse_3 = norm_forward(branch_f, gains[3], shifts[3])
    output = (middle + out_f).astype(bf16)

    picks = (
        corpus_ids[:, None] == jnp.arange(corpus_weight.shape[0], dtype=jnp.int32)[None, :]
    ).astype(f32)
    row_scale = turn(jnp.dot(picks, corpus_weight, precision=lax.Precision.HIGHEST))
    grad_final = cotangent_low.astype(f32) * row_scale[:, None]
    back_3, gain_3, shift_3 = norm_backward(grad_final, unit_3, inverse_3, gains[3])
    own_g = back_3.astype(bf16)
    other_g = across(own_g, "b")
    own_hidden = (own_slope.astype(f32) * dot(own_g, down_half, NT)).astype(bf16)
    other_hidden = (other_slope.astype(f32) * dot(other_g, down_half, NT)).astype(bf16)
    grad_f = across(dot(other_hidden, up_half, NT).astype(bf16), "b")
    grad_f = dot(own_hidden, up_half, NT) + grad_f.astype(f32)
    back_2, gain_2, shift_2 = norm_backward(grad_f, unit_2, inverse_2, gains[2])
    grad_middle = grad_final + back_2
    back_1, gain_1, shift_1 = norm_backward(grad_middle, unit_1, inverse_1, gains[1])
    grad_a = back_1.astype(bf16)
    grad_attended = dot(grad_a, out_whole, NT).astype(bf16)

    none = jnp.zeros_like(gain_1)
    norms = jnp.stack([none, gain_1, gain_2, gain_3, none, shift_1, shift_2, shift_3])
    gain_grad, shift_grad, input_grad, output, qkv_grad, up_grad, out_grad, down_grad = back(
        q,
        k,
        v,
        attended,
        lse,
        cosine,
        sine,
        norm_gains,
        norms,
        grad_attended,
        output,
        (own_f, own_g, own_hidden, own_active),
        (other_f, other_g, other_hidden, other_active),
        heads,
        grad_a,
        whole_a,
        w_attn,
        resid_low,
        grad_middle,
        groups,
    )
    input_grad = input_grad.astype(f32)
    qkv_grad = qkv_grad.reshape(depth, 3 * cols).astype(f32)
    qkv_grad = jnp.stack(jnp.split(qkv_grad, 3, axis=1), axis=1)
    up_grad = up_grad.reshape(depth, units).astype(f32)
    out_grad = out_grad.reshape(cols, depth).astype(f32)
    down_grad = down_grad.reshape(units, depth).astype(f32)
    return (
        output[None],
        input_grad[None],
        qkv_grad,
        out_grad,
        up_grad,
        down_grad,
        gain_grad,
        shift_grad,
    )


def solution(mesh):
    rows, parts = mesh.shape["dp"], mesh.shape["mp"]
    bits = (rows // 2).bit_length() - 1
    assert parts == 4 and rows == 2 ** (bits + 1)
    groups = tuple(f"g{i}" for i in range(bits))
    fine = Mesh(mesh.devices.reshape((2,) * (bits + 3)), groups + ("b", "h", "l"))
    dp, mp = groups + ("b",), ("h", "l")
    placed = (
        P(dp, mp, None),
        P(None, None, mp),
        P(mp, None),
        P(None, mp),
        P(mp, None),
        P(),
        P(),
        P(dp, mp, None),
        P(dp),
        P(),
    )
    return jax.shard_map(
        functools.partial(on_device, groups=groups),
        mesh=fine,
        in_specs=placed,
        out_specs=(
            P(dp, mp, None),
            P(dp, mp, None),
            P(None, None, mp),
            P(mp, None),
            P(None, mp),
            P(mp, None),
            P(),
            P(),
        ),
        check_vma=False,
    )
```

```python
import functools

import jax
import jax.numpy as jnp
import numpy as np
from jax import lax
from jax.experimental import pallas as pl
from jax.experimental.pallas import tpu as pltpu
from jax.sharding import Mesh, PartitionSpec as P

HEAD_DIM = 64
BLOCK = 512
EPS = 1e-05
LOG2E = 1.4426950408889634
NN = (((1,), (0,)), ((), ()))
NT = (((1,), (1,)), ((), ()))
TN = (((0,), (0,)), ((), ()))
f32 = jnp.float32
bf16 = jnp.bfloat16


def head_lanes(shape, head):
    return lax.broadcasted_iota(jnp.int32, shape, 1) // HEAD_DIM == head


def swap_halves(value, sign):
    half = HEAD_DIM // 2
    width = value.shape[1]
    first = (lax.broadcasted_iota(jnp.int32, value.shape, 1) // half) % 2 == 0
    return jnp.where(
        first, sign * pltpu.roll(value, width - half, 1), -sign * pltpu.roll(value, half, 1)
    )


MESH = pl.DeviceIdType.MESH
BACK_PLAN = {
    "front": "s1 s2",
    0: "a1 s3",
    1: "a2",
    3: "b1 r1",
    4: "s4",
    6: "a3",
    7: "b2 r2",
    9: "b3 r3",
    "x0": "a4",
    "x3": "b4 r4 end",
}
FRONT_PLAN = {
    "own": "ring",
    "near": "one",
    0: "1a two",
    1: "1b",
    2: "2a three",
    3: "2b",
    "rest": "3a 3b",
}


class Copies:
    def __init__(self, send, recv):
        self.send, self.recv, self.made = send, recv, {}

    def describe(self, name):
        n, build = self.made[name]
        source, target, device = build()
        return pltpu.make_async_remote_copy(
            src_ref=source,
            dst_ref=target,
            send_sem=self.send.at[n],
            recv_sem=self.recv.at[n],
            device_id=device,
            device_id_type=MESH,
        )

    def plan(self, name, build):
        self.made[name] = (len(self.made), build)

    def start(self, name, build=None):
        if build is not None:
            self.plan(name, build)
        self.describe(name).start()

    def arrived(self, name):
        self.describe(name).wait_recv()

    def sent(self, name):
        self.describe(name).wait_send()

    def drain(self, but=()):
        for name in self.made:
            if name not in but:
                self.sent(name)


def flip(axis):
    return {axis: 1 - lax.axis_index(axis)}


def next_layer(step):
    at = lax.rem(2 * lax.axis_index("h") + lax.axis_index("l") + step, 4)
    return {"h": at // 2, "l": lax.rem(at, 2)}


def add_into(total, term, rows=64):
    lead, count = total.shape[:-2], total.shape[-2]
    step = next(n for n in (rows, 32, 16, 8) if count % n == 0)

    @pl.loop(0, count // step)
    def _(i):
        at = pl.ds(pl.multiple_of(i * step, step), step)
        for index in np.ndindex(*lead):
            total[index + (at,)] = (
                total[index + (at,)].astype(f32) + term[index + (at,)].astype(f32)
            ).astype(bf16)


def exclusive(a, b):
    return a + b - 2 * a * b


def forward_branch(last, heads, rows, q_ref, k_ref, v_ref, o_ref, lse_ref):
    width = q_ref.shape[1]
    n = (last + 1) * rows
    block = pl.ds(last * rows, rows)
    acc = jnp.zeros((rows, width), f32)
    logs = jnp.zeros((rows, width), f32)
    for h in range(heads):
        mine = head_lanes((rows, width), h)
        qm = jnp.where(mine, q_ref[block], jnp.zeros((), bf16))
        s = lax.dot_general(qm, k_ref[:n], NT, preferred_element_type=f32)
        row = lax.broadcasted_iota(jnp.int32, (rows, rows), 0)
        column = lax.broadcasted_iota(jnp.int32, (rows, rows), 1)
        tail = jnp.where(column <= row, s[:, n - rows :], -1e30)
        top = jnp.max(tail, axis=1, keepdims=True)
        if last:
            top = jnp.maximum(top, jnp.max(s[:, : n - rows], axis=1, keepdims=True))
        top = top * LOG2E
        vm = jnp.where(head_lanes((n, width), h), v_ref[:n], jnp.ones((), bf16))
        low = jnp.exp2(tail * LOG2E - top).astype(bf16)
        out = lax.dot_general(low, vm[n - rows :], NN, preferred_element_type=f32)
        if last:
            low = jnp.exp2(s[:, : n - rows] * LOG2E - top).astype(bf16)
            out = out + lax.dot_general(low, vm[: n - rows], NN, preferred_element_type=f32)
        total = pltpu.roll(out, HEAD_DIM, 1)
        acc = jnp.where(mine, out / total, acc)
        logs = jnp.where(mine, top + jnp.log2(total), logs)
    o_ref[block] = acc.astype(bf16)
    lane = lax.broadcasted_iota(jnp.int32, (8, width), 1)
    pick = (lane == HEAD_DIM * lax.broadcasted_iota(jnp.int32, (8, width), 0)).astype(f32)
    lse_ref[:, block] = lax.dot_general(
        pick, logs, NT, precision=lax.Precision.HIGHEST, preferred_element_type=f32
    )


def front_kernel(*refs, groups, chunks):
    (
        tok_ref, cot_ref, wq_ref, up_ref, out_ref, down_ref, gain_ref, shift_ref, cos_ref, sin_ref,
        q_ref, k_ref, v_ref, whole_ref, o_ref, lse_ref,
        heads_ref, tok_home, cot_home, w_home, up_all, out_all, down_all,
        row, w_att, bounce_up, bounce_out, bounce_down, bounce_cot,
        send, recv, local, head_send, head_recv,
    ) = refs
    bits = len(groups)
    part = tok_ref.shape[0]
    depth = tok_ref.shape[1]
    width = q_ref.shape[1]
    heads = width // HEAD_DIM
    core, half, near = lax.axis_index("b"), lax.axis_index("h"), lax.axis_index("l")
    group = [lax.axis_index(axis) for axis in groups]
    layer = 2 * half + near
    place = 2 * core + near
    stays = core == half
    moves = core != half
    partner = {"b": half, "h": core}
    copies = Copies(send, recv)
    locals_made, here = [], []

    def copy_here(source, target):
        copy = pltpu.make_async_copy(source, target, local.at[len(locals_made)])
        locals_made.append(copy)
        here.append(copy)
        copy.start()

    barrier = pltpu.get_barrier_semaphore()
    friends = [flip(axis) for axis in groups + ("b",)] + [next_layer(1), next_layer(3)]
    friends += [flip("l"), {"b": 1 - core, "l": 1 - near}]
    for friend in friends:
        pl.semaphore_signal(barrier, inc=1, device_id=friend, device_id_type=MESH)

    @pl.when(moves)
    def _():
        pl.semaphore_signal(barrier, inc=1, device_id=partner, device_id_type=MESH)
        pl.semaphore_wait(barrier, len(friends) + 1)

    @pl.when(stays)
    def _():
        pl.semaphore_wait(barrier, len(friends))

    size = part // chunks

    def piece(c):
        return pl.ds(c * size, size)

    weights = (up_ref, out_ref, down_ref)
    orders = [tuple(range(bits)), tuple(range(bits)), tuple(reversed(range(bits)))]
    slab = up_ref.shape[-1] // 2

    def slot(a, shard, at):
        if a == 0:
            return up_all.at[at + (slice(None), pl.ds(pl.multiple_of(shard * slab, slab), slab))]
        if a == 1:
            return out_all.at[(shard, core) + at]
        return down_all.at[(shard,) + at]

    def held(a, at):
        if a == 0:
            return up_ref.at[at + (slice(None), pl.ds(pl.multiple_of(core * slab, slab), slab))]
        return weights[a].at[(core,) + at]

    def shard(k):
        return lax.rem(layer + 4 - k, 4)

    def ring_send(step):
        for a in range(3):

            def build(a=a):
                at = tuple(group)
                spot = slot(a, shard(step - 1), at)
                return (held(a, at) if step == 1 else spot, spot, next_layer(1))

            copies.start(("ring", a, step), build)

    def ring_wait(step):
        for a in range(3):
            copies.arrived(("ring", a, step))

    def plane_send(k, stage):
        for a in range(3):

            def build(a=a):
                order = orders[a]
                at = tuple(
                    group[axis] if order.index(axis) >= stage else slice(None)
                    for axis in range(bits)
                )
                spot = slot(a, shard(k), at)
                return (spot, spot, flip(groups[order[stage]]))

            copies.start(("plane", a, k, stage), build)

    def plane_wait(k, stage):
        for a in range(3):
            copies.arrived(("plane", a, k, stage))

    def core_send(k):
        def build():
            spot = slot(1, shard(k), (slice(None),) * bits)
            return (spot, spot, flip("b"))

        copies.start(("core", k), build)

    def plane_next(k, stage):
        plane_wait(k, stage)
        if stage + 1 < bits:
            plane_send(k, stage + 1)
        else:
            core_send(k)

    def inner_stages(k):
        for stage in range(1, bits):
            plane_next(k, stage)

    def arrive(k):
        ring_wait(k)
        if k < 3:
            ring_send(k + 1)
        plane_send(k, 0)

    steps = {
        "ring": lambda: ring_send(1),
        "one": lambda: arrive(1),
        "two": lambda: arrive(2),
        "three": lambda: arrive(3),
        "1a": lambda: plane_next(1, 0),
        "1b": lambda: inner_stages(1),
        "2a": lambda: plane_next(2, 0),
        "2b": lambda: inner_stages(2),
        "3a": lambda: plane_next(3, 0),
        "3b": lambda: inner_stages(3),
    }

    def weights_at(point):
        for name in FRONT_PLAN.get(point, "").split():
            steps[name]()

    everything = (slice(None),) * bits
    bounces = [
        (held(0, everything), bounce_up, slot(0, layer, everything)),
        (out_ref, bounce_out, out_all.at[layer]),
        (held(2, everything), bounce_down, slot(2, layer, everything)),
    ]
    inward = []
    for source, buffer, _ in bounces:
        copy = pltpu.make_async_copy(source, buffer, local.at[len(locals_made)])
        locals_made.append(copy)
        inward.append(copy)
        copy.start()

    weights_at("start")
    own = [
        pltpu.make_async_copy(
            tok_ref.at[piece(c)], row.at[place, piece(c)], local.at[len(locals_made) + c]
        )
        for c in range(chunks)
    ]
    locals_made.extend(own)
    turned = [("turn", c) for c in range(chunks)]
    for c in range(chunks):
        copies.plan(
            turned[c],
            lambda c=c: (tok_ref.at[piece(c)], row.at[layer, piece(c)], partner),
        )
    w_here = pltpu.make_async_copy(wq_ref, w_att, local.at[len(locals_made)])
    locals_made.append(w_here)
    copies.plan("wturn", lambda: (wq_ref.at[tuple(group)], w_att.at[tuple(group)], partner))
    cot_in = pltpu.make_async_copy(cot_ref, bounce_cot, local.at[len(locals_made)])
    locals_made.append(cot_in)
    cot_here = pltpu.make_async_copy(bounce_cot, cot_home, local.at[len(locals_made)])
    locals_made.append(cot_here)
    copies.plan("cot", lambda: (cot_ref, cot_home, partner))

    @pl.when(moves)
    def _():
        for c in range(chunks):
            copies.start(turned[c])
        copies.start("wturn")

    @pl.when(stays)
    def _():
        for c in range(chunks):
            own[c].start()
        w_here.start()
        cot_in.start()

    for c in range(chunks):
        pl.when(moves)(functools.partial(copies.arrived, turned[c]))
        pl.when(stays)(own[c].wait)
        for name, axis in (("near", "l"), ("core own", "b")):
            copies.start(
                (name, c),
                lambda c=c, axis=axis: (
                    row.at[place, piece(c)],
                    row.at[place, piece(c)],
                    flip(axis),
                ),
            )
    copy_here(row.at[place], tok_home)
    for copy in inward:
        copy.wait()
    for _, buffer, target in bounces:
        copy_here(buffer, target)
    weights_at("own")

    @pl.when(stays)
    def _():
        w_here.wait()

    parts = [pl.ds(i * (w_att.shape[-2] // 2), w_att.shape[-2] // 2) for i in range(2)]
    w_orders = [orders[0], orders[2]]
    for stage in range(bits):
        for i in range(2):

            def build(stage=stage, i=i):
                order = w_orders[i]
                at = tuple(
                    group[axis] if order.index(axis) >= stage else slice(None)
                    for axis in range(bits)
                )
                spot = w_att.at[at + (parts[i],)]
                return (spot, spot, flip(groups[order[stage]]))

            copies.plan(("w", stage, i), build)

    @pl.when(moves)
    def _():
        copies.arrived("wturn")
        for stage in range(bits):
            for i in range(2):
                copies.start(("w", stage, i))
            for i in range(2):
                copies.arrived(("w", stage, i))

    copy_here(w_att, w_home)
    near_block = 2 * core + 1 - near

    def pass_on():
        for c in range(chunks):
            copies.arrived(("near", c))
            copies.start(
                ("core near", c),
                lambda c=c: (row.at[near_block, piece(c)], row.at[near_block, piece(c)], flip("b")),
            )
        weights_at("near")

    def wait_all(name):
        def run():
            for c in range(chunks):
                copies.arrived((name, c))

        return run

    @pl.loop(0, 4)
    def _(r):
        far_core, far_near = lax.rem(r, 2), r // 2
        block = 2 * exclusive(core, far_core) + exclusive(near, far_near)
        pl.when(r == 1)(wait_all("core own"))
        pl.when(r == 2)(pass_on)
        pl.when(r == 3)(wait_all("core near"))

        @pl.loop(0, 2)
        def _(c):
            rows = part // 2
            inside = pl.ds(pl.multiple_of(c * rows, rows), rows)
            at = pl.ds(pl.multiple_of(block * part + c * rows, rows), rows)
            value = row[block, inside].astype(f32)
            center = value - jnp.mean(value, axis=1, keepdims=True)
            inverse = lax.rsqrt(jnp.mean(center * center, axis=1, keepdims=True) + EPS)
            normed = (center * inverse * gain_ref[0:1] + shift_ref[0:1]).astype(bf16)
            whole_ref[at] = normed
            w = w_att[...].reshape(depth, 3 * width)
            mixed = jnp.dot(normed, w, preferred_element_type=f32)
            cosine = jnp.concatenate([cos_ref[at]] * (width // 128), axis=1)
            sine = jnp.concatenate([sin_ref[at]] * (width // 128), axis=1)
            query, key = mixed[:, :width], mixed[:, width : 2 * width]
            query = HEAD_DIM ** (-0.5) * (query * cosine + swap_halves(query, -1.0) * sine)
            q_ref[at] = query.astype(bf16)
            k_ref[at] = (key * cosine + swap_halves(key, -1.0) * sine).astype(bf16)
            v_ref[at] = mixed[:, 2 * width :].astype(bf16)

    def head_copy(mask):
        far_core, far_near = mask // 2, lax.rem(mask, 2)
        to_core, to_near = exclusive(core, far_core), exclusive(near, far_near)
        block = 2 * to_core + to_near
        rows = pl.ds(pl.multiple_of(block * part, part), part)
        columns = pl.ds(pl.multiple_of(place * width, width), width)
        return pltpu.make_async_remote_copy(
            src_ref=o_ref.at[rows],
            dst_ref=heads_ref.at[:, columns],
            send_sem=head_send.at[mask],
            recv_sem=head_recv.at[mask],
            device_id={"b": to_core, "l": to_near},
            device_id_type=MESH,
        )

    @pl.loop(0, 4)
    def _(r):
        far_core, far_near = 1 - lax.rem(r, 2), 1 - r // 2
        mask = 2 * far_core + far_near
        block = 2 * exclusive(core, far_core) + exclusive(near, far_near)
        for n in range(4):
            pl.when(r == n)(functools.partial(weights_at, n))
        for i in range(4):
            pl.when(block == i)(
                functools.partial(
                    forward_branch, i, heads, part, q_ref, k_ref, v_ref, o_ref, lse_ref
                )
            )

        @pl.when(r < 3)
        def _():
            head_copy(mask).start()

    copy_here(
        o_ref.at[pl.ds(pl.multiple_of(place * part, part), part)],
        heads_ref.at[:, pl.ds(pl.multiple_of(place * width, width), width)],
    )

    @pl.when(moves)
    def _():
        copies.start("cot")

    @pl.when(stays)
    def _():
        cot_in.wait()
        cot_here.start()

    weights_at("rest")
    for mask in (1, 2, 3):
        copy = head_copy(jnp.int32(mask))
        copy.wait_send()
        copy.wait_recv()
    for k in (1, 2, 3):
        copies.arrived(("core", k))
    sometimes = turned + ["wturn", "cot"] + [("w", s, i) for s in range(bits) for i in range(2)]

    @pl.when(moves)
    def _():
        copies.arrived("cot")
        for name in sometimes:
            copies.sent(name)

    @pl.when(stays)
    def _():
        cot_here.wait()

    for copy in here:
        copy.wait()
    copies.drain(sometimes)


def front(tok, cot, wq, up, out, down, gain, shift, cosine, sine, groups, chunks=2):
    part, depth = tok.shape
    length = 4 * part
    width = wq.shape[-1] // 3
    bits = len(groups)
    vmem = pl.BlockSpec(memory_space=pltpu.VMEM)
    anywhere = pl.BlockSpec(memory_space=pl.ANY)

    def shape(*dims):
        return jax.ShapeDtypeStruct(dims, bf16)

    n = 2 * chunks + 2 + 3 * chunks + 2 * bits + 3 * 3 + 9 * bits + 3 + 4
    return pl.pallas_call(
        functools.partial(front_kernel, groups=groups, chunks=chunks),
        out_shape=(
            shape(length, width),
            shape(length, width),
            shape(length, width),
            shape(length, depth),
            shape(length, width),
            jax.ShapeDtypeStruct((8, length), f32),
            shape(part, depth),
            shape(part, depth),
            shape(part, depth),
            shape(*wq.shape),
            shape(*up.shape[:-1], 2 * up.shape[-1]),
            shape(4, *out.shape),
            shape(4, *down.shape[1:]),
        ),
        in_specs=[anywhere] * 6 + [vmem] * 4,
        out_specs=(vmem,) * 6 + (anywhere,) * 7,
        scratch_shapes=[
            pltpu.VMEM((4, part, depth), bf16),
            pltpu.VMEM(wq.shape, bf16),
            pltpu.VMEM(up.shape[:-1] + (up.shape[-1] // 2,), bf16),
            pltpu.VMEM(out.shape, bf16),
            pltpu.VMEM(down.shape[1:], bf16),
            pltpu.VMEM((part, depth), bf16),
            pltpu.SemaphoreType.DMA((n,)),
            pltpu.SemaphoreType.DMA((n,)),
            pltpu.SemaphoreType.DMA((32,)),
            pltpu.SemaphoreType.DMA((4,)),
            pltpu.SemaphoreType.DMA((4,)),
        ],
        compiler_params=pltpu.CompilerParams(
            vmem_limit_bytes=58 * 2**20, collective_id=2, has_side_effects=True
        ),
        cost_estimate=pl.CostEstimate(
            flops=100_000_000_000, bytes_accessed=32 * 2**20, transcendentals=0
        ),
    )(tok, cot, wq, up, out, down, gain, shift, cosine, sine)

def back_kernel(*refs, groups, rows, chunks):
    (
        q_ref, k_ref, v_ref, o_ref, lse_ref, cos_ref, sin_ref, gain_ref, norms_ref,
        da_ref, low_ref, own_in, other_in, own_branch, other_branch, own_hidden, other_hidden, own_active, other_active,
        heads_ref, branch_ref,
        whole_ref, w_ref, resid_ref, middle_ref,
        gains_out, shifts_out, grad_home, low_home, qkv_all, up_all, out_all, down_all,
        up_ref, out_ref, down_ref,
        out_part, out_in, up_tile, down_tile, turned,
        do, dq, dk, dv, delta, mixed, whole, w, resid, middle,
        sent, from_core, from_near, grad_x, grad_low, qkv_sum, qkv_core, norm_sum, norm_in,
        *rest,
    ) = refs
    bits = len(groups)
    terms = (up_ref, out_ref, down_ref)
    partial = [[rest[3 * s + a] for s in range(bits)] for a in range(3)]
    rest = rest[3 * bits :]
    passing, staged, rest = rest[:3], rest[3:6], rest[6:]
    qkv_in, (send, recv, local) = rest[:bits], rest[bits:]
    copies = Copies(send, recv)
    group = [lax.axis_index(axis) for axis in groups]
    core, half, near = lax.axis_index("b"), lax.axis_index("h"), lax.axis_index("l")
    layer = 2 * half + near
    place = 2 * core + near
    moves, stays = core != half, core == half
    partner = {"b": half, "h": core}
    orders = [tuple(range(bits)), tuple(range(bits)), tuple(reversed(range(bits)))]
    part, depth = da_ref.shape
    length, width = q_ref.shape
    heads = width // HEAD_DIM
    blocks = length // rows
    slab = up_ref.shape[-1] // 4
    quarter = depth // 2**bits
    all_local = [0]

    def local_copy(source, target):
        n = all_local[0]
        all_local[0] += 1
        return pltpu.make_async_copy(source, target, local.at[n])

    def columns(which, size):
        return pl.ds(pl.multiple_of(which * size, size), size)

    def shard(k):
        return lax.rem(layer + 4 - k, 4)

    def term(a, k, at):
        if a == 0:
            return up_ref.at[at + (slice(None), columns(shard(k), slab))]
        return terms[a].at[(shard(k),) + at]

    def result(a, at):
        if a == 0:
            return up_all.at[at + (slice(None), columns(core, slab))]
        return (None, out_all, down_all)[a].at[(core,) + at]

    def split(order, stage, side):
        at = []
        for axis in range(bits):
            when = order.index(axis)
            if when == stage:
                at.append(group[axis] if side == 0 else 1 - group[axis])
            elif when > stage:
                at.append(slice(None))
        return tuple(at)

    def source(a, k, stage, side):
        at = split(orders[a], stage, side)
        if stage == 0:
            return term(a, k, at) if side else staged[a].at[k % 2]
        return partial[a][stage - 1].at[(k % 4,) + at]

    loads = {}

    def plane_send(k, stage):
        for a in range(3):
            copies.start(
                ("plane", a, k, stage),
                lambda a=a: (
                    source(a, k, stage, 1),
                    partial[a][stage].at[k % 4],
                    flip(groups[orders[a][stage]]),
                ),
            )
            if stage == 0:
                loads[a, k] = local_copy(term(a, k, split(orders[a], 0, 0)), staged[a].at[k % 2])
                loads[a, k].start()

    def plane_add(k, stage):
        for a in range(3):
            copies.arrived(("plane", a, k, stage))
            if stage == 0:
                loads[a, k].wait()
            add_into(partial[a][stage].at[k % 4], source(a, k, stage, 0))

    def plane_step(k, stage):
        plane_add(k, stage)
        if stage + 1 < bits:
            plane_send(k, stage + 1)

    def ring_send(step):
        for a in range(3):
            held = partial[a][bits - 1].at[1] if step == 1 else passing[a].at[step - 2]
            target = passing[a].at[step - 1]
            copies.start(
                ("ring", a, step), lambda held=held, target=target: (held, target, next_layer(1))
            )

    def ring_add(step):
        for a in range(3):
            copies.arrived(("ring", a, step))
            add_into(passing[a].at[step - 1], partial[a][bits - 1].at[(step + 1) % 4])

    def gather_send(stage):
        for a in range(3):
            order = orders[a]
            at = tuple(
                group[axis] if order.index(axis) >= stage else slice(None) for axis in range(bits)
            )
            held = passing[a].at[2] if stage == 0 else result(a, at)
            spot, axis = result(a, at), groups[order[stage]]
            copies.start(
                ("gather", a, stage),
                lambda held=held, spot=spot, axis=axis: (held, spot, flip(axis)),
            )

    def brought(order, stage):
        at = []
        for axis in range(bits):
            when = order.index(axis)
            if stage == 0 or when > stage - 1:
                at.append(group[axis])
            elif when == stage - 1:
                at.append(1 - group[axis])
            else:
                at.append(slice(None))
        return tuple(at)

    def core_send(stage):
        for a in range(3):
            spot = result(a, brought(orders[a], stage))
            held = passing[a].at[2] if stage == 0 else spot
            copies.start(("core", a, stage), lambda held=held, spot=spot: (held, spot, flip("b")))

    barrier = pltpu.get_barrier_semaphore()
    friends = [flip(axis) for axis in groups + ("b", "h", "l")] + [next_layer(1), next_layer(3)]
    friends += [{"b": 1 - core, "l": 1 - near}]
    for friend in friends:
        pl.semaphore_signal(barrier, inc=1, device_id=friend, device_id_type=MESH)

    @pl.when(moves)
    def _():
        pl.semaphore_signal(barrier, inc=1, device_id=partner, device_id_type=MESH)
        pl.semaphore_wait(barrier, len(friends) + 1)

    @pl.when(stays)
    def _():
        pl.semaphore_wait(barrier, len(friends))

    for mask in (3, 1, 2):
        to_core, to_near = exclusive(core, mask // 2), exclusive(near, mask % 2)

        def build(to_core=to_core, to_near=to_near):
            return (
                da_ref.at[:, columns(2 * to_core + to_near, width)],
                do.at[columns(place, part)],
                {"b": to_core, "l": to_near},
            )

        copies.start(("heads", mask), build)
    own_heads = local_copy(da_ref.at[:, columns(place, width)], do.at[columns(place, part)])
    own_heads.start()
    low_in = local_copy(low_ref, grad_low)
    low_here = local_copy(grad_low, low_home)
    copies.plan("low", lambda: (low_ref, low_home, partner))
    pl.when(moves)(functools.partial(copies.start, "low"))
    pl.when(stays)(low_in.start)

    pieces = 2
    thin = slab // pieces
    pair = whole.shape[0] // 2
    units = [
        local_copy(source, whole.at[pl.ds(n * part, part)])
        for n, source in enumerate((own_in, other_in, own_branch, other_branch))
    ]
    units += [local_copy(heads_ref, sent.at[0]), local_copy(branch_ref, sent.at[1])]
    for copy in units:
        copy.start()

    def hidden_load(u):
        spot = columns(pieces * shard(1 + u // pieces) + lax.rem(u, pieces), thin)
        at = columns(lax.rem(u, 3), thin)
        semaphore = hidden_local + 4 * lax.rem(u, 3)
        return [
            pltpu.make_async_copy(
                source.at[:, spot], mixed.at[pl.ds(n * part, part), at], local.at[semaphore + n]
            )
            for n, source in enumerate((own_hidden, other_hidden, own_active, other_active))
        ]

    hidden_local = all_local[0]
    all_local[0] += 12
    for u in range(2):
        for copy in hidden_load(jnp.int32(u)):
            copy.start()
    for copy in units:
        copy.wait()
    @pl.loop(0, 4)
    def _(s):
        block = lax.dot_general(
            sent[0, :, columns(s, width)], sent[1], TN, preferred_element_type=f32
        ).astype(bf16)
        out_part[s] = block.reshape(out_part.shape[1:])

    @pl.loop(0, 4)
    def _(c):
        turned[columns(c, depth // 4)] = whole[:pair, columns(c, depth // 4)].T

    copies.start("out core", lambda: (out_part.at[:, 1 - core], out_in, flip("b")))
    def shard_gradients(k):
        @pl.loop(0, pieces)
        def _(n):
            u = pieces * (k - 1) + n
            for copy in hidden_load(u):
                copy.wait()

            @pl.when(u + 2 < 4 * pieces)
            def _():
                for copy in hidden_load(u + 2):
                    copy.start()

            buffer = columns(lax.rem(u, 3), thin)

            @pl.loop(0, 2**bits)
            def _(c):
                slot = tuple(lax.rem(c // 2 ** (bits - 1 - i), 2) for i in range(bits))
                up_tile[(n,) + slot] = jnp.dot(
                    turned[columns(c, quarter)],
                    mixed[:pair, buffer],
                    preferred_element_type=f32,
                ).astype(bf16)

            block = lax.dot_general(
                mixed[pair:, buffer], whole[pair:], TN, preferred_element_type=f32
            )
            down_tile[n] = block.astype(bf16).reshape(down_tile.shape[1:])

        if k == 1:
            copies.arrived("out core")

            @pl.loop(0, 4)
            def _(s):
                out_in[s] = (out_in[s].astype(f32) + out_part[s, core].astype(f32)).astype(bf16)

            put = local_copy(out_in, out_ref)
            put.start()
            put.wait()
        made = []
        for u in range(pieces):
            spot = (slice(None),) * (bits + 1) + (columns(pieces * shard(k) + u, thin),)
            made.append(local_copy(up_tile.at[u], up_ref.at[spot]))
            made.append(local_copy(down_tile.at[u], down_ref.at[shard(k), u]))
        for copy in made:
            copy.start()
        for copy in made:
            copy.wait()

    whole_load = local_copy(whole_ref, whole)

    def begin(k):
        shard_gradients(k)
        if k == 4:
            whole_load.start()
        plane_send(k, 0)

    def last_stages(k):
        for stage in range(1, bits):
            plane_step(k, stage)

    def ring(step):
        if step > 1:
            ring_add(step - 1)
        if step < 4:
            ring_send(step)

    own = [local_copy(passing[a].at[2], result(a, tuple(group))) for a in range(3)]

    def finish():
        core_send(0)
        gather_send(0)
        for copy in own:
            copy.start()

    kinds = {"s": begin, "a": lambda k: plane_step(k, 0), "b": last_stages, "r": ring}

    def sums_at(point):
        for name in BACK_PLAN.get(point, "").split():
            if name == "end":
                finish()
            else:
                kinds[name[0]](int(name[1]))

    sums_at("front")
    early = [
        local_copy(w_ref, w),
        local_copy(resid_ref, resid),
        local_copy(middle_ref, middle),
    ]
    for copy in early:
        copy.start()

    @pl.when(stays)
    def _():
        low_in.wait()
        low_here.start()

    for total in (dq, dk, dv):
        total[...] = jnp.zeros_like(total)
    own_heads.wait()
    for mask in (2, 1, 3):
        copies.arrived(("heads", mask))

    lane_head = lax.broadcasted_iota(jnp.int32, (8, width), 1) // HEAD_DIM
    marks = (lane_head == lax.broadcasted_iota(jnp.int32, (8, width), 0)).astype(f32)

    def span(i):
        return pl.ds(pl.multiple_of(i * rows, rows), rows)

    @pl.loop(0, blocks)
    def _(i):
        product = do[span(i)].astype(f32) * o_ref[span(i)].astype(f32)
        delta[:, span(i)] = lax.dot_general(
            marks, product, NT, precision=lax.Precision.HIGHEST, preferred_element_type=f32
        )

    def tile(i, j):
        at, to = span(i), span(j)
        keys, values = k_ref[to], v_ref[to]
        queries, grads = q_ref[at], do[at]
        dkj, dvj, dqi = dk[to], dv[to], dq[at]
        zero = jnp.zeros((), bf16)
        key = j * rows + lax.broadcasted_iota(jnp.int32, (rows, rows), 0)
        query = i * rows + lax.broadcasted_iota(jnp.int32, (rows, rows), 1)
        allowed = key <= query
        for h in range(heads):
            mine = head_lanes((rows, width), h)
            qm = jnp.where(mine, queries, zero)
            dom = jnp.where(mine, grads, zero)
            km = jnp.where(mine, keys, zero)
            st = lax.dot_general(keys, qm, NT, preferred_element_type=f32)
            pt = jnp.where(allowed, jnp.exp2(st * LOG2E - lse_ref[h : h + 1, at]), 0.0)
            dpt = lax.dot_general(values, dom, NT, preferred_element_type=f32)
            dst = (pt * (dpt - delta[h : h + 1, at])).astype(bf16)
            dvj = dvj + jnp.dot(pt.astype(bf16), dom, preferred_element_type=f32)
            dkj = dkj + jnp.dot(dst, qm, preferred_element_type=f32)
            dqi = dqi + lax.dot_general(dst, km, TN, preferred_element_type=f32)
        dq[at], dk[to], dv[to] = dqi, dkj, dvj

    count = blocks * (blocks + 1) // 2

    def tiles(low, high):
        @pl.loop(low, high)
        def _(t):
            i = jnp.int32(0)
            for n in range(1, blocks):
                i = i + (t >= n * (n + 1) // 2).astype(jnp.int32)
            tile(i, t - i * (i + 1) // 2)

    low = 0
    for point in range(10):
        when = point * count // 10
        if point in BACK_PLAN:
            if when > low:
                tiles(low, when)
            sums_at(point)
            low = when
    tiles(low, count)

    def turn_back(grad, at):
        cosine = jnp.concatenate([cos_ref[at]] * (width // 128), axis=1)
        sine = jnp.concatenate([sin_ref[at]] * (width // 128), axis=1)
        return grad * cosine + swap_halves(grad, 1.0) * sine

    @pl.loop(0, blocks)
    def _(i):
        at = span(i)
        mixed[at, :width] = (HEAD_DIM ** (-0.5) * turn_back(dq[at], at)).astype(bf16)
        mixed[at, width : 2 * width] = turn_back(dk[at], at).astype(bf16)
        mixed[at, 2 * width :] = dv[at].astype(bf16)

    for copy in early:
        copy.wait()
    size = part // chunks

    def input_part(block, c):
        at = pl.ds(pl.multiple_of(block * part + c * size, size), size)
        return lax.dot_general(
            mixed[at], w[...].reshape(depth, 3 * width), NT, preferred_element_type=f32
        )

    def inside(c):
        return pl.ds(pl.multiple_of(c * size, size), size)

    for slot in range(2):
        block = 2 * (1 - core) + (1 - near if slot == 0 else near)

        @pl.loop(0, chunks)
        def _(c):
            sent[slot, inside(c)] = input_part(block, c).astype(bf16)

        copies.start(
            ("x core", slot),
            lambda slot=slot: (sent.at[slot], from_core.at[slot], flip("b")),
        )
    sums_at("x0")
    copies.arrived(("x core", 0))
    for c in range(chunks):
        total = input_part(2 * core + 1 - near, c) + from_core[0, inside(c)].astype(f32)
        sent[2, inside(c)] = total.astype(bf16)
        copies.start(
            ("x near", c),
            lambda c=c: (sent.at[2, inside(c)], from_near.at[inside(c)], flip("l")),
        )
    sums_at("x1")
    whole_load.wait()
    side = quarter // 2
    for index in np.ndindex(*(2,) * bits):
        first = sum(bit << (bits - 1 - axis) for axis, bit in enumerate(index)) * quarter
        block = lax.dot_general(
            whole[:, first : first + quarter], mixed[...], TN, preferred_element_type=f32
        ).astype(bf16)
        for i in range(2):
            qkv_sum[index + (i,)] = block[i * side : (i + 1) * side]
    q_orders = [orders[0], orders[2]]

    def q_slot(i, stage, side):
        order = q_orders[i]
        at = []
        for axis in range(bits):
            when = order.index(axis)
            if when < stage:
                at.append(group[axis])
            elif when == stage:
                at.append(group[axis] if side == 0 else 1 - group[axis])
            else:
                at.append(slice(None))
        return qkv_sum.at[tuple(at) + (i,)]

    def q_send(stage):
        for i in range(2):
            copies.start(
                ("q", i, stage),
                lambda i=i: (
                    q_slot(i, stage, 1),
                    qkv_in[stage].at[i],
                    flip(groups[q_orders[i][stage]]),
                ),
            )

    def q_add(stage):
        for i in range(2):
            copies.arrived(("q", i, stage))
            add_into(q_slot(i, stage, 0), qkv_in[stage].at[i])

    q_send(0)
    sums_at("x2")
    copies.arrived(("x core", 1))

    @pl.loop(0, chunks)
    def _(c):
        grad_x[inside(c)] = input_part(place, c) + from_core[1, inside(c)].astype(f32)

    own_q = tuple(group)
    axes = groups + ("b", "h", "l")

    def norms_send(step):
        copies.start(("norms", step), lambda: (norm_sum, norm_in.at[step], flip(axes[step])))

    def norms_add(step):
        copies.arrived(("norms", step))
        copies.sent(("norms", step))
        norm_sum[...] += norm_in[step]

    pl.when(stays)(low_here.wait)
    norm_sum[...] = norms_ref[...]
    fine = min(128, size)

    def home(c):
        copies.arrived(("x near", c))

        @pl.loop(0, size // fine)
        def _(s):
            at = pl.ds(pl.multiple_of(c * size + s * fine, fine), fine)
            grad = grad_x[at] + from_near[at].astype(f32)
            value = resid[at].astype(f32)
            center = value - jnp.mean(value, axis=1, keepdims=True)
            inverse = lax.rsqrt(jnp.mean(center * center, axis=1, keepdims=True) + EPS)
            unit = center * inverse
            scaled = grad * gain_ref[0:1]
            back = inverse * (
                scaled
                - jnp.mean(scaled, axis=1, keepdims=True)
                - unit * jnp.mean(scaled * unit, axis=1, keepdims=True)
            )
            grad_low[at] = (middle[at] + back).astype(bf16)
            norm_sum[0:1] += jnp.sum(grad * unit, axis=0, keepdims=True)
            norm_sum[4:5] += jnp.sum(grad, axis=0, keepdims=True)

        copies.plan(
            ("home", c), lambda c=c: (grad_low.at[inside(c)], grad_home.at[inside(c)], partner)
        )
        pl.when(moves)(functools.partial(copies.start, ("home", c)))

    def gather_next(stage):
        for a in range(3):
            copies.arrived(("gather", a, stage))
        if stage + 1 < bits:
            gather_send(stage + 1)
        core_send(stage + 1)

    def q_spot(at):
        return qkv_all.at[at + (core,)]

    keep_q = local_copy(qkv_core.at[1, core], q_spot(own_q))
    def q_gather(stage):
        at = tuple(group[axis] if axis >= stage else slice(None) for axis in range(bits))
        held = qkv_core.at[1, core] if stage == 0 else q_spot(at)
        copies.start(("q gather", stage), lambda: (held, q_spot(at), flip(groups[stage])))

    def q_core_send(stage):
        spot = q_spot(brought(orders[0], stage))
        held = qkv_core.at[1, core] if stage == 0 else spot
        copies.start(("q both", stage), lambda: (held, spot, flip("b")))

    sums_at("x3")
    half_way = chunks // 2
    for c in range(half_way):
        home(c)
    sums_at("x4")
    for stage in range(bits):
        q_add(stage)
        if stage + 1 < bits:
            q_send(stage + 1)

    copies.plan("q turn", lambda: (qkv_sum.at[own_q], qkv_core.at[0], partner))
    pl.when(moves)(functools.partial(copies.start, "q turn"))
    sums_at("x5")
    for c in range(half_way, chunks):
        home(c)
    stay = [local_copy(grad_low, grad_home)]
    pl.when(stays)(stay[0].start)
    norms_send(0)
    sums_at("x6")
    for copy in own:
        copy.wait()
    gather_next(0)

    @pl.when(moves)
    def _():
        copies.arrived("q turn")

    @pl.when(stays)
    def _():
        qkv_core[0] = qkv_sum[own_q]

    copies.start("q core", lambda: (qkv_core.at[0, 1 - core], qkv_core.at[1, 1 - core], flip("b")))
    norms_add(0)
    norms_send(1)
    copies.arrived("q core")
    add_into(qkv_core.at[1, core], qkv_core.at[0, core])
    keep_q.start()
    q_gather(0)
    q_core_send(0)
    keep_q.wait()
    norms_add(1)
    norms_send(2)
    for stage in range(1, bits):
        gather_next(stage)
    for stage in range(bits):
        copies.arrived(("q gather", stage))
        if stage + 1 < bits:
            q_gather(stage + 1)
        q_core_send(stage + 1)
    for step in range(2, len(axes)):
        norms_add(step)
        if step + 1 < len(axes):
            norms_send(step + 1)
    gains_out[...] = norm_sum[0:4]
    shifts_out[...] = norm_sum[4:8]
    for stage in range(bits + 1):
        for a in range(3):
            copies.arrived(("core", a, stage))
        copies.arrived(("q both", stage))
    sometimes = ["q turn", "low"] + [("home", c) for c in range(chunks)]

    @pl.when(moves)
    def _():
        copies.arrived("low")
        for c in range(chunks):
            copies.arrived(("home", c))
        for name in sometimes:
            copies.sent(name)

    pl.when(stays)(stay[0].wait)
    copies.drain(sometimes + [("norms", step) for step in range(len(axes))])


def back(
    q, k, v, o, lse, cosine, sine, gain, norms, da, low, own, other, heads, branch, whole, w, resid, middle, groups, rows=BLOCK, chunks=2,
):
    length, width = q.shape
    part, depth = da.shape
    bits = len(groups)
    slots = (2,) * bits
    slab = own[2].shape[1] // 4
    up_shape = slots + (depth // 2**bits, 4 * slab)
    out_shape = (4,) + slots + (width // 2 ** (bits + 1), depth)
    down_shape = (4,) + slots + (slab // 2**bits, depth)
    tails = (up_shape[-2:-1] + (slab,), out_shape[-2:], down_shape[-2:])
    vmem = pl.BlockSpec(memory_space=pltpu.VMEM)
    anywhere = pl.BlockSpec(memory_space=pl.ANY)
    quarter = depth // 2**bits
    q_tail = (quarter // 2, 3 * width)
    thin = slab // 2
    scratch = [
        pltpu.VMEM((4, 2) + out_shape[1:], bf16),
        pltpu.VMEM(out_shape, bf16),
        pltpu.VMEM((2,) + up_shape[:-1] + (thin,), bf16),
        pltpu.VMEM((2,) + down_shape[2:], bf16),
        pltpu.VMEM((depth, length // 2), bf16),
    ]
    scratch += [pltpu.VMEM((length, width), bf16)]
    scratch += [pltpu.VMEM((length, width), f32)] * 3 + [pltpu.VMEM((8, length), f32)]
    scratch += [
        pltpu.VMEM((length, 3 * width), bf16),
        pltpu.VMEM(whole.shape, bf16),
        pltpu.VMEM(w.shape, bf16),
        pltpu.VMEM((part, depth), bf16),
        pltpu.VMEM((part, depth), f32),
        pltpu.VMEM((3, part, depth), bf16),
        pltpu.VMEM((2, part, depth), bf16),
        pltpu.VMEM((part, depth), bf16),
        pltpu.VMEM((part, depth), f32),
        pltpu.VMEM((part, depth), bf16),
        pltpu.VMEM(slots + (2,) + q_tail, bf16),
        pltpu.VMEM((2, 2) + q_tail, bf16),
        pltpu.VMEM((8, depth), f32),
        pltpu.VMEM((bits + 3, 8, depth), f32),
    ]
    for stage in range(bits):
        for tail in tails:
            scratch.append(pltpu.VMEM((4,) + (2,) * (bits - 1 - stage) + tail, bf16))
    scratch += [pltpu.VMEM((3,) + tail, bf16) for tail in tails]
    scratch += [pltpu.VMEM((2,) + (2,) * (bits - 1) + tail, bf16) for tail in tails]
    scratch += [
        pltpu.VMEM((2,) + (2,) * (bits - 1 - stage) + q_tail, bf16) for stage in range(bits)
    ]
    n = 5 + 3 * (4 * bits + 3 + bits + bits + 1)
    n += 2 + chunks + 2 * bits + chunks + (bits + 3) + 2 + bits + bits + 1
    scratch += [pltpu.SemaphoreType.DMA((n,)), pltpu.SemaphoreType.DMA((n,))]
    scratch += [pltpu.SemaphoreType.DMA((64,))]
    return pl.pallas_call(
        functools.partial(back_kernel, groups=groups, rows=rows, chunks=chunks),
        out_shape=(
            jax.ShapeDtypeStruct((4, depth), f32),
            jax.ShapeDtypeStruct((4, depth), f32),
            jax.ShapeDtypeStruct((part, depth), bf16),
            jax.ShapeDtypeStruct((part, depth), bf16),
            jax.ShapeDtypeStruct(slots + (2,) + q_tail, bf16),
            jax.ShapeDtypeStruct(up_shape[:-1] + (2 * slab,), bf16),
            jax.ShapeDtypeStruct((2,) + out_shape[1:], bf16),
            jax.ShapeDtypeStruct((2,) + down_shape[1:], bf16),
            jax.ShapeDtypeStruct(up_shape, bf16),
            jax.ShapeDtypeStruct(out_shape, bf16),
            jax.ShapeDtypeStruct(down_shape, bf16),
        ),
        in_specs=[vmem] * 9 + [anywhere] * 16,
        out_specs=(vmem,) * 2 + (anywhere,) * 9,
        scratch_shapes=scratch,
        compiler_params=pltpu.CompilerParams(
            vmem_limit_bytes=63 * 2**20, collective_id=1, has_side_effects=True
        ),
        cost_estimate=pl.CostEstimate(
            flops=100_000_000_000, bytes_accessed=32 * 2**20, transcendentals=0
        ),
    )(
        q, k, v, o, lse, cosine, sine, gain, norms, da, low,
        own[0], other[0], own[1], other[1], own[2], other[2], own[3], other[3],
        heads, branch, whole, w, resid, middle,
    )[:8]


def norm_forward(value, gain, shift):
    center = value - jnp.mean(value, axis=-1, keepdims=True)
    inverse = lax.rsqrt(jnp.mean(center * center, axis=-1, keepdims=True) + EPS)
    unit = center * inverse
    return (unit * gain + shift, unit, inverse)


def norm_backward(grad, unit, inverse, gain):
    scaled = grad * gain
    back = inverse * (
        scaled
        - jnp.mean(scaled, axis=-1, keepdims=True)
        - unit * jnp.mean(scaled * unit, axis=-1, keepdims=True)
    )
    return (back, jnp.sum(grad * unit, axis=0), jnp.sum(grad, axis=0))


def rotary_tables(length, width):
    half = HEAD_DIM // 2
    steps = (np.arange(width) % half).astype(np.float32) / np.float32(half)
    freqs = np.float32(10000.0) ** (-steps)
    angles = np.arange(length, dtype=np.float32)[:, None] * freqs[None, :]
    return (jnp.asarray(np.cos(angles)), jnp.asarray(np.sin(angles)))


SWAP = [(0, 1), (1, 0)]


def dot(left, right, dims=NN):
    return lax.dot_general(left, right, dims, preferred_element_type=f32)


def across(value, axis):
    return lax.ppermute(value, axis, SWAP)


def turn(value):
    return lax.ppermute(value, ("b", "h"), [(0, 0), (1, 2), (2, 1), (3, 3)])


def on_device(
    tokens,
    w_qkv,
    w_out,
    w_up,
    w_down,
    norm_gains,
    norm_shifts,
    cotangent,
    corpus_ids,
    corpus_weight,
    *,
    groups,
):
    _, part, depth = tokens.shape
    cols = w_qkv.shape[2]
    units = w_up.shape[1]
    core, half, near = lax.axis_index("b"), lax.axis_index("h"), lax.axis_index("l")
    length = 4 * part
    place = 2 * core + near
    group = jnp.int32(0)
    for axis in groups:
        group = 2 * group + lax.axis_index(axis)
    n_groups = 2 ** len(groups)
    stack = ("h", "l")
    cosine, sine = rotary_tables(length, 128)
    gains = [norm_gains[i : i + 1] for i in range(4)]
    shifts = [norm_shifts[i : i + 1] for i in range(4)]

    slots = (2,) * len(groups)
    q, k, v, whole_a, attended, lse, heads, resid_low, cotangent_low, w_attn, up_half, out_whole, down_half = front(
        tokens[0],
        cotangent[0],
        jnp.concatenate([w_qkv[:, i] for i in range(3)], axis=1).reshape(
            slots + (depth // n_groups, 3 * cols)
        ),
        w_up.reshape(slots + (depth // n_groups, units)),
        w_out.reshape((2,) + slots + (cols // (2 * n_groups), depth)),
        w_down.reshape((2,) + slots + (units // (2 * n_groups), depth)),
        norm_gains,
        norm_shifts,
        cosine,
        sine,
        groups,
    )
    up_half = up_half.reshape(depth, 2 * units)
    out_whole = out_whole.reshape(4 * cols, depth)
    down_half = down_half.reshape(2 * units, depth)

    branch_a = dot(heads, out_whole)

    resid = resid_low.astype(f32)
    out_a, unit_1, inverse_1 = norm_forward(branch_a, gains[1], shifts[1])
    middle = resid + out_a
    normed_f, unit_2, inverse_2 = norm_forward(middle, gains[2], shifts[2])
    own_f = normed_f.astype(bf16)
    other_f = across(own_f, "b")

    def hidden_units(value):
        hidden = dot(value, up_half)
        bend = jnp.tanh(0.7978845608028654 * (hidden + 0.044715 * hidden * hidden * hidden))
        slope = 0.5 * (1.0 + bend) + 0.5 * hidden * (1.0 - bend * bend) * 0.7978845608028654 * (
            1.0 + 3 * 0.044715 * hidden * hidden
        )
        return (0.5 * hidden * (1.0 + bend)).astype(bf16), slope.astype(bf16)

    own_active, own_slope = hidden_units(own_f)
    other_active, other_slope = hidden_units(other_f)
    branch_f = across(dot(other_active, down_half).astype(bf16), "b")
    branch_f = dot(own_active, down_half) + branch_f.astype(f32)
    out_f, unit_3, inverse_3 = norm_forward(branch_f, gains[3], shifts[3])
    output = (middle + out_f).astype(bf16)

    picks = (
        corpus_ids[:, None] == jnp.arange(corpus_weight.shape[0], dtype=jnp.int32)[None, :]
    ).astype(f32)
    row_scale = turn(jnp.dot(picks, corpus_weight, precision=lax.Precision.HIGHEST))
    grad_final = cotangent_low.astype(f32) * row_scale[:, None]
    back_3, gain_3, shift_3 = norm_backward(grad_final, unit_3, inverse_3, gains[3])
    own_g = back_3.astype(bf16)
    other_g = across(own_g, "b")
    own_hidden = (own_slope.astype(f32) * dot(own_g, down_half, NT)).astype(bf16)
    other_hidden = (other_slope.astype(f32) * dot(other_g, down_half, NT)).astype(bf16)
    grad_f = across(dot(other_hidden, up_half, NT).astype(bf16), "b")
    grad_f = dot(own_hidden, up_half, NT) + grad_f.astype(f32)
    back_2, gain_2, shift_2 = norm_backward(grad_f, unit_2, inverse_2, gains[2])
    grad_middle = grad_final + back_2
    back_1, gain_1, shift_1 = norm_backward(grad_middle, unit_1, inverse_1, gains[1])
    grad_a = back_1.astype(bf16)
    grad_attended = dot(grad_a, out_whole, NT).astype(bf16)

    none = jnp.zeros_like(gain_1)
    norms = jnp.stack([none, gain_1, gain_2, gain_3, none, shift_1, shift_2, shift_3])
    gain_grad, shift_grad, input_grad, output, qkv_grad, up_grad, out_grad, down_grad = back(
        q,
        k,
        v,
        attended,
        lse,
        cosine,
        sine,
        norm_gains,
        norms,
        grad_attended,
        output,
        (own_f, own_g, own_hidden, own_active),
        (other_f, other_g, other_hidden, other_active),
        heads,
        grad_a,
        whole_a,
        w_attn,
        resid_low,
        grad_middle,
        groups,
    )
    input_grad = input_grad.astype(f32)
    qkv_grad = qkv_grad.reshape(depth, 3 * cols).astype(f32)
    qkv_grad = jnp.stack(jnp.split(qkv_grad, 3, axis=1), axis=1)
    up_grad = up_grad.reshape(depth, units).astype(f32)
    out_grad = out_grad.reshape(cols, depth).astype(f32)
    down_grad = down_grad.reshape(units, depth).astype(f32)
    return (
        output[None],
        input_grad[None],
        qkv_grad,
        out_grad,
        up_grad,
        down_grad,
        gain_grad,
        shift_grad,
    )


def solution(mesh):
    rows, parts = mesh.shape["dp"], mesh.shape["mp"]
    bits = (rows // 2).bit_length() - 1
    assert parts == 4 and rows == 2 ** (bits + 1)
    groups = tuple(f"g{i}" for i in range(bits))
    fine = Mesh(mesh.devices.reshape((2,) * (bits + 3)), groups + ("b", "h", "l"))
    dp, mp = groups + ("b",), ("h", "l")
    placed = (
        P(dp, mp, None),
        P(None, None, mp),
        P(mp, None),
        P(None, mp),
        P(mp, None),
        P(),
        P(),
        P(dp, mp, None),
        P(dp),
        P(),
    )
    return jax.shard_map(
        functools.partial(on_device, groups=groups),
        mesh=fine,
        in_specs=placed,
        out_specs=(
            P(dp, mp, None),
            P(dp, mp, None),
            P(None, None, mp),
            P(mp, None),
            P(None, mp),
            P(mp, None),
            P(),
            P(),
        ),
        check_vma=False,
    )
```
